32 devices in a mesh: batch: 8 (over y, x, core), seq: 4 (over z).
Axes of the slice: x: 2, y: 2, z: 4, core: 2. Of those that a mesh axis runs over, the one named last changes fastest.
Arguments:
- tokens: bfloat16 [8, 1024, 1024], P('batch', 'seq'), may hold values from -6 to 6
- norm_gain1: float32 [1024], replicated, may hold values from 0.1 to 1.9
- w_in: bfloat16 [1024, 3072], replicated, may hold values from -0.1875 to 0.1875
- short_kernel: bfloat16 [3, 3072], replicated, may hold values from -1 to 1
- filt_w1: float32 [33, 64], replicated, may hold values from -1.75 to 1.75
- filt_w2: float32 [64, 64], replicated, may hold values from -1 to 1
- filt_w3: float32 [64, 1024], replicated, may hold values from -0.046875 to 0.046875
- decay_rate: float32 [1024], replicated, may hold values from 0 to 1, as said below
- conv_bias: float32 [1024], replicated, may hold values from -4 to 4
- w_out: bfloat16 [1024, 1024], replicated, may hold values from -0.1875 to 0.1875
- norm_gain2: float32 [1024], replicated, may hold values from 0.1 to 1.9
- w_up: bfloat16 [1024, 4096], replicated, may hold values from -0.1875 to 0.1875
- w_down: bfloat16 [4096, 1024], replicated, may hold values from -0.09375 to 0.09375
- cotangent: bfloat16 [8, 1024, 1024], P('batch', 'seq'), may hold values from -6 to 6
Outputs:
- layer_out: bfloat16 [8, 1024, 1024], P('batch', 'seq')
- tokens_grad: float32 [8, 1024, 1024], P('batch', 'seq')
- grad_gain1: float32 [1024], P(('batch', 'seq'))
- grad_w_in: float32 [1024, 3072], P(('batch', 'seq'))
- grad_short: float32 [3, 3072], P(None, ('batch', 'seq'))
- grad_filt_w1: float32 [33, 64], replicated
- grad_filt_w2: float32 [64, 64], replicated
- grad_filt_w3: float32 [64, 1024], P(None, ('batch', 'seq'))
- grad_conv_bias: float32 [1024], P(('batch', 'seq'))
- grad_w_out: float32 [1024, 1024], P(('batch', 'seq'))
- grad_gain2: float32 [1024], P(('batch', 'seq'))
- grad_w_up: float32 [1024, 4096], P(('batch', 'seq'))
- grad_w_down: float32 [4096, 1024], P(('batch', 'seq'))
The draws below stay inside these ranges and needn't reach their ends.
Inputs may be any that keep to these rules, and one draw needn't show every extreme that they name: `decay_rate`: positive per-lag decay rates.
All inputs are finite; a program needn't handle non-finite values.
Results may differ from the reference program's by a relative error of at most 0.012.
Values may be sent and summed in bfloat16 or wider, within the bound.
A program may use at most 256 MiB of HBM per device.

```python
import math
import jax
import jax.numpy as jnp
from jax import lax

D = 1024
FF = 4096
FILT = 64
EMB = 33
SEQ_LEN = 1024
SEQS = 8


def draw_decay_rate(key, part):
    key = jax.random.fold_in(key, 11)
    uniform_draw = jax.random.uniform(key, (D,), jnp.float32)
    lower = math.log(0.3 / SEQ_LEN)
    upper = math.log(1.0 / 12.0)
    return jnp.exp(lower + (upper - lower) * uniform_draw)


def spiked(values, own_key, source, target, parts, factor):
    def block_of(position):
        return (jnp.arange(values.shape[position]) // (values.shape[position] // parts)).reshape((-1,) + (1,) * (values.ndim - 1 - position))

    near = jax.random.permutation(own_key, parts)[block_of(target)]
    second = (block_of(target) + parts // 2) % parts
    return jnp.where((block_of(source) == near) | (block_of(source) == second), factor * values, values)


def block_scale(key, dims, split, smallest, largest):
    level = 1.0
    for axis_at, shards_of in split:
        draws = jax.random.uniform(jax.random.fold_in(jax.random.fold_in(key, 6), axis_at), (shards_of,), jnp.float32, smallest / len(split), largest / len(split))
        level = level * jnp.repeat(jnp.exp(draws), dims[axis_at] // shards_of).reshape((-1,) + (1,) * (len(dims) - 1 - axis_at))
    return level


def scatter_about(own_key, extent, spread, reach, cuts=(), dtype=jnp.bfloat16):
    factor_of = block_scale(own_key, extent, cuts, -0.22, 0.18) if cuts else 1.0
    entries = jax.random.normal(own_key, extent, jnp.float32) * spread * factor_of
    return jnp.minimum(jnp.maximum(entries, -reach), reach).astype(dtype)


def bell_draw_with(stream_key, extent, deviation, most, shards, heavy, kind=jnp.bfloat16):
    values = deviation * jax.random.normal(stream_key, extent, jnp.float32)
    if shards:
        values = values * block_scale(stream_key, extent, shards, -0.22, 0.18)
    return jnp.clip(spiked(values, jax.random.fold_in(stream_key, 3), *heavy), -most, most).astype(kind)


def setup_inputs(seed: int = 0) -> dict:
    arg_keys = jax.random.split(jax.random.key(seed), 15)
    return {
        "tokens": bell_draw_with(arg_keys[0], (SEQS, SEQ_LEN, D), 1.0, 6.0, ((0, 8), (1, 4)), (1, 2, 4, 2.0)),
        "norm_gain1": jnp.clip(1.0 + 0.18 * jax.random.normal(arg_keys[1], (D,), jnp.float32), 0.1, 1.9),
        "w_in": scatter_about(arg_keys[2], (D, 3 * D), D ** -0.5, 0.1875),
        "short_kernel": jnp.clip(jax.random.uniform(arg_keys[3], (3, 3 * D), jnp.float32, -1.0, 1.0), -1.0, 1.0).astype(jnp.bfloat16),
        "filt_w1": scatter_about(arg_keys[4], (EMB, FILT), (EMB // 3) ** -0.5, 1.75, (), jnp.float32),
        "filt_w2": scatter_about(arg_keys[5], (FILT, FILT), (FILT // 2) ** -0.5, 1.0, (), jnp.float32),
        "filt_w3": scatter_about(arg_keys[6], (FILT, D), (16 * SEQ_LEN) ** -0.5, 0.046875, (), jnp.float32),
        "decay_rate": draw_decay_rate(jax.random.fold_in(arg_keys[14], 71), 0),
        "conv_bias": scatter_about(arg_keys[8], (D,), 1.0, 4.0, (), jnp.float32),
        "w_out": scatter_about(arg_keys[9], (D, D), D ** -0.5, 0.1875),
        "norm_gain2": jnp.clip(1.0 + 0.18 * jax.random.normal(arg_keys[10], (D,), jnp.float32), 0.1, 1.9),
        "w_up": scatter_about(arg_keys[11], (D, FF), D ** -0.5, 0.1875),
        "w_down": scatter_about(arg_keys[12], (FF, D), FF ** -0.5, 0.09375),
        "cotangent": scatter_about(arg_keys[13], (SEQS, SEQ_LEN, D), 1.0, 6.0, ((0, 8), (1, 4))),
    }


@jax.custom_vjp
def low(v):
    return lax.optimization_barrier(v.astype(jnp.bfloat16)).astype(jnp.float32)

@jax.custom_vjp
def low_back(v):
    return v

def low_keep(v):
    return (low(v), None)

def low_pass(kept, grad):
    return (grad,)

def back_keep(v):
    return (v, None)

def back_low(kept, grad):
    return (low(grad),)
low.defvjp(low_keep, low_pass)
low_back.defvjp(back_keep, back_low)

def layer_norm(values, gain):
    average = lax.optimization_barrier(jnp.mean(values, axis=-1, keepdims=True))
    centered = values - average
    spread_sq = lax.optimization_barrier(jnp.mean(centered * centered, axis=-1, keepdims=True))
    return centered * lax.rsqrt(spread_sq + 1e-05) * gain

def smooth_gelu(values):
    return jax.nn.gelu(values, approximate=True)

def filter_taps(w_first, w_second, w_third, decay_rate, seq_len):
    band_count = (w_first.shape[0] - 1) // 2
    lag_index = jnp.arange(seq_len).astype(jnp.float32)
    lag_scaled = lag_index / (seq_len - 1)
    lag_angle = lag_index * (2.0 * math.pi / seq_len)
    band_freq = 0.0001 + jnp.arange(band_count).astype(jnp.float32) * ((band_count - 1 - 0.0001) / (band_count - 1))
    phases = lag_angle[:, None] * band_freq[None, :]
    features = jnp.concatenate([lag_scaled[:, None], jnp.cos(phases), -jnp.sin(phases)], axis=1)
    hidden_one = jnp.sin(jnp.dot(features, w_first, precision=lax.Precision.HIGHEST, preferred_element_type=jnp.float32))
    hidden_two = jnp.sin(jnp.dot(hidden_one, w_second, precision=lax.Precision.HIGHEST, preferred_element_type=jnp.float32))
    filt_raw = jnp.dot(hidden_two, w_third, precision=lax.Precision.HIGHEST, preferred_element_type=jnp.float32)
    return filt_raw * jnp.exp(-decay_rate[None, :] * lag_index[:, None])

def product(values, weight):
    return jnp.einsum('std,de->ste', values, weight, precision=lax.Precision.HIGHEST)

def short_conv(projected, kernel):
    length = projected.shape[1]
    padded = jnp.pad(projected, ((0, 0), (2, 0), (0, 0)))
    return kernel[0] * padded[:, 2:] + kernel[1] * padded[:, 1:length + 1] + kernel[2] * padded[:, :length]

def causal_conv(filt_taps, signal):
    length = filt_taps.shape[0]
    spectrum = jnp.fft.rfft(signal, n=2 * length, axis=1) * jnp.fft.rfft(filt_taps, n=2 * length, axis=0)[None]
    return jnp.fft.irfft(spectrum, n=2 * length, axis=1)[:, :length]

def reference(tokens, norm_gain1, w_in, short_kernel, filt_w1, filt_w2, filt_w3, decay_rate, conv_bias, w_out, norm_gain2, w_up, w_down, cotangent):
    seq_len = tokens.shape[1]
    features_count = tokens.shape[2]

    def forward(inputs, gain_one, proj_in, kernel, w_first, w_second, w_third, long_bias, proj_out, gain_two, proj_up, proj_down):
        normed1 = low(layer_norm(inputs, gain_one))
        projected = low(low_back(product(normed1, proj_in)))
        mixed = short_conv(projected, kernel)
        gate_out = mixed[..., :features_count]
        gate_in = mixed[..., features_count:2 * features_count]
        values = mixed[..., 2 * features_count:]
        signal = low(values * gate_in)
        filt_taps = low(filter_taps(w_first, w_second, w_third, decay_rate, seq_len))
        long_out = low_back(causal_conv(filt_taps, signal) + long_bias * signal)
        gated = low(long_out * gate_out)
        residual1 = inputs + low_back(product(gated, proj_out))
        normed2 = low(layer_norm(residual1, gain_two))
        hidden = low(smooth_gelu(low_back(product(normed2, proj_up))))
        return residual1 + low_back(product(hidden, proj_down))
    result, pullback = jax.vjp(forward, tokens.astype(jnp.float32), norm_gain1, w_in.astype(jnp.float32), short_kernel.astype(jnp.float32), filt_w1, filt_w2, filt_w3, conv_bias, w_out.astype(jnp.float32), norm_gain2, w_up.astype(jnp.float32), w_down.astype(jnp.float32))
    gradients = pullback(cotangent.astype(jnp.float32))
    return (result.astype(jnp.bfloat16), gradients[0], gradients[1], gradients[2], gradients[3], gradients[4], gradients[5], gradients[6], gradients[7], gradients[8], gradients[9], gradients[10], gradients[11])
```

```python
import math

import jax
import jax.numpy as jnp
import ml_dtypes
import numpy as np
from jax import lax
from jax.experimental import pallas as pl
from jax.experimental.pallas import tpu as pltpu
from jax.sharding import PartitionSpec as P

F32 = jnp.float32
BF16 = jnp.bfloat16
HIGHEST = lax.Precision.HIGHEST
GELU_SCALE = math.sqrt(2.0 / math.pi)
GELU_CUBIC = 0.044715


def dot(left, right, contract, out=F32, precision=None):
    return lax.dot_general(
        left, right, (contract, ((), ())), precision=precision, preferred_element_type=F32
    ).astype(out)


def mm(left, right, **kw):
    return dot(left, right, ((1,), (0,)), **kw)


def mm_nt(left, right, **kw):
    return dot(left, right, ((1,), (1,)), **kw)


def mm_tn(left, right, **kw):
    return dot(left, right, ((0,), (0,)), **kw)


def shifted(value, axis, steps):
    count = lax.axis_size(axis)
    first, last = (max(0, -steps), min(count, count - steps))
    return lax.ppermute(value, axis, [(source, source + steps) for source in range(first, last)])


def exchange(value, axis, bit):
    count = lax.axis_size(axis)
    return lax.ppermute(value, axis, [(at, at ^ (1 << bit)) for at in range(count)])


def bits_of(axis):
    return lax.axis_size(axis).bit_length() - 1


def stage_order(swap):
    batch_bits, seq_bits = bits_of("batch"), bits_of("seq")
    rest = list(range(1, batch_bits))
    half = len(rest) // 2
    if swap:
        rest = rest[half:] + rest[:half]
    return [("batch", bit) for bit in [0] + rest] + [("seq", bit) for bit in range(seq_bits)]


def scatter_sum(partial, swap=False, wire=BF16):
    batch_bits, seq_bits = bits_of("batch"), bits_of("seq")
    dims = [("batch", bit) for bit in reversed(range(batch_bits))]
    dims += [("seq", bit) for bit in reversed(range(seq_bits))]
    rows = partial.shape[0] >> len(dims)
    value = partial.reshape((2,) * len(dims) + (rows,) + partial.shape[1:]).astype(wire)
    for axis, bit in stage_order(swap):
        at = dims.index((axis, bit))
        mine = (lax.axis_index(axis) >> bit) & 1
        keep = lax.dynamic_index_in_dim(value, mine, at, keepdims=False)
        send = lax.dynamic_index_in_dim(value, 1 - mine, at, keepdims=False)
        got = exchange(send, axis, bit)
        value = keep.astype(F32) + got.astype(F32)
        dims.pop(at)
        if dims:
            value = value.astype(wire)
    return value


def gather_batch(value):
    return lax.all_gather(value, "batch", axis=0, tiled=True)


def columns_batch(value):
    return lax.all_to_all(value, "batch", 1, 0, tiled=True)


def rows_sum(left_own, right_all):
    blocks = lax.axis_size("seq")
    part = mm_tn(left_own, right_all, out=BF16)
    got = lax.all_to_all(part.reshape(blocks, -1, part.shape[1]), "seq", 0, 0, tiled=True)
    return jnp.sum(got.astype(F32), axis=0)


def columns_sum(left_all, right_own):
    blocks, groups = lax.axis_size("seq"), lax.axis_size("batch")
    part = mm_tn(left_all, right_own, out=BF16)
    part = part.reshape(groups * blocks, -1, part.shape[1])
    got = lax.all_to_all(part, ("batch", "seq"), 0, 0, tiled=True)
    got = jnp.sum(got.reshape(groups, blocks, -1, part.shape[2]).astype(F32), axis=1)
    return got.transpose(1, 0, 2).reshape(got.shape[1], -1)


def all_sum(value):
    for axis, bit in stage_order(False):
        value = value + exchange(value, axis, bit)
    return value


def norm_parts(values):
    centered = values - jnp.mean(values, axis=-1, keepdims=True)
    inverse = lax.rsqrt(jnp.mean(centered * centered, axis=-1, keepdims=True) + 1e-05)
    return centered * inverse, inverse


def norm_back(grad, gain, xhat, inverse):
    scaled = grad * gain
    return (
        scaled
        - jnp.mean(scaled, axis=-1, keepdims=True)
        - xhat * jnp.mean(scaled * xhat, axis=-1, keepdims=True)
    ) * inverse


def transform_table(length):
    count = np.arange(length, dtype=np.int64)
    turns = (2 * count[:, None] + 1) * count[None, :] % (4 * length)
    angles = turns.astype(np.float64) * (2.0 * np.pi / (4 * length))
    table = np.concatenate([np.cos(angles), -np.sin(angles)], axis=0)
    return table.astype(np.float32).astype(ml_dtypes.bfloat16)


def lag_features(emb, length):
    bands = (emb - 1) // 2
    lag = np.arange(length, dtype=np.float64)
    freq = 1e-4 + np.arange(bands, dtype=np.float64) * ((bands - 1 - 1e-4) / (bands - 1))
    phases = (lag * (2.0 * np.pi / length))[:, None] * freq[None, :]
    return np.concatenate(
        [(lag / (length - 1))[:, None], np.cos(phases), -np.sin(phases)], axis=1
    ).astype(np.float32)


def to_channels(value):
    return lax.all_to_all(value, "seq", 1, 0, tiled=True)


def to_tokens(value):
    return lax.all_to_all(value, "seq", 0, 1, tiled=True)


def plain_layer(
    tokens,
    norm_gain1,
    w_in,
    short_kernel,
    filt_w1,
    filt_w2,
    filt_w3,
    decay_rate,
    conv_bias,
    w_out,
    norm_gain2,
    w_up,
    w_down,
    cotangent,
):
    num_seqs, block_len, width = tokens.shape
    assert num_seqs == 1
    blocks = lax.axis_size("seq")
    position = lax.axis_index("seq")
    seq_len = block_len * blocks
    own = width // blocks
    table = jnp.asarray(transform_table(seq_len))
    features = jnp.asarray(lag_features(filt_w1.shape[0], seq_len))
    cot = cotangent[0]
    cot_all = gather_batch(cot)
    inputs = tokens[0].astype(F32)

    xhat1, inverse1 = norm_parts(inputs)
    normed1 = (xhat1 * norm_gain1).astype(BF16)
    normed1_all = gather_batch(normed1)
    projected = mm(normed1, w_in, out=BF16)
    earlier = shifted(projected[block_len - 2 :], "seq", 1)
    extended = jnp.concatenate([earlier, projected], axis=0).astype(F32)
    taps3 = short_kernel.astype(F32)
    lags = [extended[2 - lag : 2 - lag + block_len] for lag in range(3)]
    mixed = taps3[0] * lags[0] + taps3[1] * lags[1] + taps3[2] * lags[2]
    gate_out = mixed[:, :width]
    gate_in = mixed[:, width : 2 * width]
    values = mixed[:, 2 * width :]
    signal = (values * gate_in).astype(BF16)

    w3_own = lax.dynamic_slice_in_dim(filt_w3, position * own, own, 1)
    decay_own = lax.dynamic_slice_in_dim(decay_rate, position * own, own, 0)
    angle1 = mm(features, filt_w1, precision=HIGHEST)
    hidden1, slope1 = jnp.sin(angle1), jnp.cos(angle1)
    angle2 = mm(hidden1, filt_w2, precision=HIGHEST)
    hidden2, slope2 = jnp.sin(angle2), jnp.cos(angle2)
    lag_index = jnp.arange(seq_len).astype(F32)
    fading = jnp.exp(-decay_own[None, :] * lag_index[:, None])
    taps = (mm(hidden2, w3_own, precision=HIGHEST) * fading).astype(BF16)
    taps_spec = mm(table, taps)
    taps_re, taps_im = taps_spec[:seq_len], taps_spec[seq_len:]

    signal_spec = mm(table, to_channels(signal))
    signal_re, signal_im = signal_spec[:seq_len], signal_spec[seq_len:]
    scale = 1.0 / seq_len

    def inverse_of(real, imag):
        both = (jnp.concatenate([real, imag], axis=0) * scale).astype(BF16)
        return mm_tn(table, both)

    conv = inverse_of(
        taps_re * signal_re - taps_im * signal_im, taps_re * signal_im + taps_im * signal_re
    )
    long_out = to_tokens(conv.astype(BF16)).astype(F32) + conv_bias * signal.astype(F32)
    gated = (long_out * gate_out).astype(BF16)
    gated_all = gather_batch(gated)
    residual1 = inputs + mm(gated, w_out)
    xhat2, inverse2 = norm_parts(residual1)
    normed2 = (xhat2 * norm_gain2).astype(BF16)
    normed2_all = gather_batch(normed2)
    pre = mm(normed2, w_up)
    bent = jnp.tanh(GELU_SCALE * (pre + GELU_CUBIC * pre * pre * pre))
    hidden = (0.5 * pre * (1.0 + bent)).astype(BF16)
    layer_out = (residual1 + mm(hidden, w_down)).astype(BF16)

    slope = 0.5 * (1.0 + bent) + 0.5 * pre * (1.0 - bent * bent) * GELU_SCALE * (
        1.0 + 3.0 * GELU_CUBIC * pre * pre
    )
    grad_pre = (mm_nt(cot, w_down) * slope).astype(BF16)
    grad_w_down = rows_sum(columns_batch(hidden), cot_all)
    grad_w_up = columns_sum(normed2_all, columns_batch(grad_pre))
    grad_norm2 = mm_nt(grad_pre, w_up)
    grad_gain2 = jnp.sum(grad_norm2 * xhat2, axis=0)
    grad_res = cot.astype(F32) + norm_back(grad_norm2, norm_gain2, xhat2, inverse2)
    grad_branch = grad_res.astype(BF16)
    grad_w_out = columns_sum(gated_all, columns_batch(grad_branch))
    grad_gated = mm_nt(grad_branch, w_out)
    grad_long = (grad_gated * gate_out).astype(BF16)
    grad_gate_out = grad_gated * long_out
    grad_bias = jnp.sum(grad_long.astype(F32) * signal.astype(F32), axis=0)

    grad_spec = mm(table, to_channels(grad_long))
    grad_re, grad_im = grad_spec[:seq_len], grad_spec[seq_len:]
    grad_conv = inverse_of(
        taps_re * grad_re + taps_im * grad_im, taps_re * grad_im - taps_im * grad_re
    )
    grad_signal = to_tokens(grad_conv.astype(BF16)).astype(F32) + conv_bias * grad_long.astype(F32)
    grad_taps = inverse_of(
        signal_re * grad_re + signal_im * grad_im, signal_re * grad_im - signal_im * grad_re
    )
    grad_filt = grad_taps * fading
    grad_w3_own = mm_tn(hidden2, grad_filt)
    grad_angle2 = mm_nt(grad_filt, w3_own) * slope2
    grad_w2 = mm_tn(hidden1, grad_angle2)
    grad_angle1 = mm_nt(grad_angle2, filt_w2) * slope1
    grad_w1 = mm_tn(features, grad_angle1)

    grad_mixed = jnp.concatenate(
        [grad_gate_out, grad_signal * values, grad_signal * gate_in], axis=1
    )
    later = shifted(grad_mixed[:2], "seq", -1)
    grad_ext = jnp.concatenate([grad_mixed, later], axis=0)
    grad_proj = (
        taps3[0] * grad_ext[:block_len]
        + taps3[1] * grad_ext[1 : block_len + 1]
        + taps3[2] * grad_ext[2:]
    ).astype(BF16)
    grad_short = jnp.stack([jnp.sum(grad_mixed * lag, axis=0) for lag in lags])
    grad_w_in = columns_sum(normed1_all, columns_batch(grad_proj))
    grad_norm1 = mm_nt(grad_proj, w_in)
    grad_gain1 = jnp.sum(grad_norm1 * xhat1, axis=0)
    tokens_grad = grad_res + norm_back(grad_norm1, norm_gain1, xhat1, inverse1)

    return layer_out[None], tokens_grad[None], small_sums(
        grad_gain1, grad_bias, grad_gain2, grad_short, grad_w1, grad_w2, grad_w3_own
    ), (grad_w_in, grad_w_out, grad_w_up, grad_w_down)


MESH = pl.DeviceIdType.MESH
KERNEL_VMEM = 63 * 1024 * 1024


def symmetric_tables(length):
    odd = 2 * np.arange(length, dtype=np.int64) + 1
    angles = (odd[:, None] * odd[None, :] % (8 * length)).astype(np.float64) * (
        np.pi / (4 * length)
    )
    phase = odd.astype(np.float64) * (np.pi / (4 * length))
    tables = [np.cos(angles), np.sin(angles)]
    tables = [t.astype(np.float32).astype(ml_dtypes.bfloat16) for t in tables]
    return tables, np.stack([np.cos(phase), np.sin(phase)], axis=1).astype(np.float32)


def sin_cos(x):
    turns = jnp.floor(x * (2.0 / np.pi) + 0.5)
    rest = ((x - turns * 1.5703125) - turns * 4.837512969970703e-4) - turns * 7.54978995489188e-8
    square = rest * rest
    sine = rest + rest * square * (
        -1.6666654611e-1 + square * (8.3321608736e-3 - square * 1.9515295891e-4)
    )
    cosine = (1.0 - 0.5 * square) + square * square * (
        4.166664568298827e-2 + square * (-1.388731625493765e-3 + square * 2.443315711809948e-5)
    )
    quarter = turns - 4.0 * jnp.floor(turns * 0.25)
    odd = (quarter == 1.0) | (quarter == 3.0)
    sin_sign = jnp.where(quarter >= 2.0, -1.0, 1.0)
    cos_sign = jnp.where((quarter == 1.0) | (quarter == 2.0), -1.0, 1.0)
    return sin_sign * jnp.where(odd, cosine, sine), cos_sign * jnp.where(odd, sine, cosine)


class Named:
    def __init__(self, names, refs):
        assert len(names) == len(refs)
        for name, ref in zip(names, refs):
            setattr(self, name, ref)


def kernel_plan(groups, blocks, tokens, width, hidden, filt, emb):
    length = tokens * blocks
    own = width // blocks
    ffc = hidden // groups
    share = width // groups
    rows_out = share // blocks
    inc = 3 * share
    chips = groups // 2
    down_rows = ffc // blocks
    net_at = -(-emb // 8) * 8
    net_rows = net_at + filt
    peers, zpeers = groups - 1, blocks - 1
    vm, hbm = pltpu.VMEM, pl.ANY
    inputs = dict(
        tokens=hbm, cot=hbm, w_in=hbm, w_out=hbm, w_up=hbm, w_down=hbm,
        cosine=hbm, sine=hbm, filt_w3=hbm, decay=hbm,
        gain1=vm, gain2=vm, bias=vm, short=vm, filt_w1=vm, filt_w2=vm,
        features_t=vm, phase=vm,
    )
    outputs = dict(
        layer_out=((tokens, width), BF16, hbm),
        tokens_grad=((tokens, width), F32, hbm),
        grad_w_in=((rows_out, 3 * width), F32, hbm),
        grad_w_out=((rows_out, width), F32, hbm),
        grad_w_up=((rows_out, hidden), F32, hbm),
        grad_w_down=((ffc // blocks, width), F32, hbm),
        grad_gain1=((1, rows_out), F32, vm),
        grad_gain2=((1, rows_out), F32, vm),
        grad_bias=((1, rows_out), F32, vm),
        grad_short=((3, 3 * rows_out), F32, vm),
        grad_w1=((emb, filt), F32, vm),
        grad_w2=((filt, filt), F32, vm),
        grad_w3=((filt, rows_out), F32, vm),
        cot_land=((2, groups // 2 * tokens, width), BF16, hbm),
        n1_land=((groups, width, tokens), BF16, hbm),
        n2_land=((groups, width, tokens), BF16, hbm),
    )
    dma = pltpu.SemaphoreType.DMA
    scratch = dict(
        tok=vm((tokens, width), BF16), cotv=vm((tokens, width), BF16),
        mean1=vm((tokens, 128), F32), inv1=vm((tokens, 128), F32),
        n1=vm((tokens, width), BF16), turn=vm((width, tokens), BF16),
        gated_turn=vm((width, tokens), BF16), gated_pair=vm((width // 2, 2 * tokens), BF16),
        hid_buf=vm((tokens, ffc), BF16), gmix=vm((tokens + 8, 3 * width), F32),
        win=vm((3, width, width), BF16), wout=vm((width, width), BF16),
        cs=vm((length, length), BF16), sn=vm((length, length), BF16),
        ext=vm((tokens + 16, 3 * width), BF16),
        halo_out=vm((16, 3 * width), BF16), halo_in=vm((16, 3 * width), BF16),
        gate_out=vm((tokens, width), F32),
        sig=vm((tokens, width), BF16), chan=vm((length, own), BF16),
        w3=vm((filt, own), F32), fade=vm((1, own), F32),
        h1=vm((filt, length), F32), s1=vm((filt, length), F32),
        h2=vm((filt, length), F32), s2=vm((filt, length), F32),
        sum_gain1=vm((1, width), F32), sum_gain2=vm((1, width), F32),
        sum_bias=vm((1, width), F32), sum_short=vm((3, 3 * width), F32),
        small_send=vm((groups, 16, share), F32), small_land=vm((groups, 16, share), F32),
        small_sum=vm((16, share), F32), small_z=vm((zpeers, 16, share), F32),
        short_all=vm((8, inc), F32),
        w12=vm((net_rows, 128), F32), w12_z=vm((zpeers, net_rows, 128), F32),
        w12_sum=vm((net_rows, 128), F32), w12_plane=vm((peers, net_rows, 128), F32),
        sum_w3=vm((filt, own), F32), w3_land=vm((peers, filt // groups, own), F32),
        w3_part=vm((filt // groups, own), F32), w3_all=vm((blocks, filt, own), F32),
        hre=vm((length, own), F32), him=vm((length, own), F32),
        xre=vm((length, own), F32), xim=vm((length, own), F32),
        yre=vm((length, own), BF16), yim=vm((length, own), BF16),
        qre=vm((length, own), BF16), qim=vm((length, own), BF16),
        conv_out=vm((length, own), BF16), conv_in=vm((blocks, tokens, own), BF16),
        long=vm((tokens, width), F32), half=vm((tokens, width), BF16),
        res=vm((tokens, width), F32), xhat2=vm((tokens, width), F32),
        inv2=vm((tokens, 128), F32), gn2=vm((tokens, width), F32),
        gres=vm((tokens, width), F32),
        hid_send=vm((groups, ffc, tokens), BF16), hid_own=vm((ffc, groups * tokens), BF16),
        pre_send=vm((groups, tokens, ffc), BF16), pre_own=vm((groups * tokens, ffc), BF16),
        gbr_pair=vm((2 * tokens, width), BF16),
        glong=vm((tokens, width), BF16),
        gproj=vm((tokens, 3 * width), BF16), gproj_own=vm((groups * tokens, inc), BF16),
        down_send=vm((2, down_rows, width), BF16), down_land=vm((2, down_rows, width), BF16),
        down_next=vm((down_rows, width), BF16), down_last=vm((down_rows, width), BF16),
        down_own=vm((down_rows, width), F32),
        up_send=vm((2, own, ffc), BF16), up_land=vm((2, own, ffc), BF16),
        up_next=vm((own, ffc), BF16), up_last=vm((own, ffc), BF16), up_own=vm((own, ffc), F32),
        in_send=vm((2, own, inc), BF16), in_land=vm((2, own, inc), BF16),
        in_next=vm((own, inc), BF16), in_last=vm((own, inc), BF16), in_own=vm((own, inc), F32),
        out_send=vm((chips - 1, share, width), BF16), out_land=vm((chips - 1, share, width), BF16),
        out_own=vm((share, width), F32),
        outz_send=vm((share, width), BF16), outz_land=vm((zpeers, rows_out, width), BF16),
        outz_own=vm((rows_out, width), F32),
        load_sem=dma((16,)),
        pool_sem=dma((groups,)),
        win_sem=dma((3,)),
        ffn_sem=dma((2, 2)),
        local_sem=dma((16,)),
        stage=vm((chips - 1, width, tokens), BF16), stage_sem=dma((chips - 1,)),
        ag_s=dma((3, groups - 1)), ag_r=dma((3, groups - 1)),
        halo_s=dma((2,)), halo_r=dma((2,)),
        za_s=dma((4, zpeers)), za_r=dma((4, zpeers)),
        pa_s=dma((3, peers)), pa_r=dma((3, peers)),
        cx_s=dma((2,)), cx_r=dma((2,)), wo_s=dma((2, chips - 1)), wo_r=dma((2, chips - 1)),
        rs_s=dma((3, 2)), rs_r=dma((3, 2)),
        sm_s=dma((4, peers)), sm_r=dma((4, peers)),
        sz_s=dma((3, zpeers)), sz_r=dma((3, zpeers)),
        tr_s=dma((2, peers)), tr_r=dma((2, peers)),
    )
    names = [*inputs, *outputs, *scratch]

    def kernel(*refs):
        r = Named(names, refs)
        b, z = lax.axis_index("batch"), lax.axis_index("seq")
        chip, core = lax.div(b, 2), lax.rem(b, 2)
        sibling = chip * 2 + (1 - core)
        sent = {}

        def group_at(step):
            return lax.rem(b + step, groups)

        def block_at(step):
            return lax.rem(z + step, blocks)

        def span(at, size):
            return pl.ds(pl.multiple_of(at * size, size), size)

        def remote(src, dst, send_sem, recv_sem, **where):
            return pltpu.make_async_remote_copy(
                src_ref=src, dst_ref=dst, send_sem=send_sem, recv_sem=recv_sem,
                device_id=where, device_id_type=MESH,
            )

        def send(key, copy):
            copy.start()
            sent.setdefault(key, []).append(copy)

        def drain(key):
            for copy in sent.pop(key):
                copy.wait_send()

        def tiles(size, total, body):
            def step(i, carry):
                body(pl.multiple_of(i * size, size))
                return carry

            lax.fori_loop(0, total // size, step, 0)

        def load(sem, src, dst):
            copy = pltpu.make_async_copy(src, dst, sem)
            copy.start()
            return copy

        def load_win(block):
            return load(r.win_sem.at[block], r.w_in.at[:, pl.ds(block * width, width)], r.win.at[block])

        load_tok = load(r.load_sem.at[0], r.tokens, r.tok)
        win_loads = [(block, load_win(block)) for block in (1, 2, 0)]
        load_cot = load(r.load_sem.at[5], r.cot, r.cotv)
        load_w3 = load(r.load_sem.at[1], r.filt_w3.at[:, span(z, own)], r.w3)
        load_fade = load(r.load_sem.at[2], r.decay.at[:, span(z, own)], r.fade)
        load_cs = load(r.load_sem.at[3], r.cosine, r.cs)
        load_sn = load(r.load_sem.at[4], r.sine, r.sn)
        load_wout = load(r.load_sem.at[6], r.w_out, r.wout)

        barrier = pltpu.get_barrier_semaphore()
        for step in range(1, groups):
            pl.semaphore_signal(barrier, inc=1, device_id={"batch": group_at(step)}, device_id_type=MESH)
        for step in range(1, blocks):
            pl.semaphore_signal(barrier, inc=1, device_id={"seq": block_at(step)}, device_id_type=MESH)
        pl.semaphore_wait(barrier, peers + zpeers)

        slots = [
            lambda at: r.cot_land.at[lax.div(at, chips), span(lax.rem(at, chips), tokens)],
            lambda at: r.n1_land.at[at],
            lambda at: r.n2_land.at[at],
        ]

        def gather_copy(k, at, src, slot, to):
            return remote(src, slot, r.ag_s.at[k, at], r.ag_r.at[k, at], batch=to)

        def gather_local(k, src):
            return pltpu.make_async_copy(src, slots[k](b), r.local_sem.at[k])

        def gather_start(k, src):
            for step in range(1, chips):
                to = lax.rem(chip + step, chips) * 2 + core
                send(("ag", k), gather_copy(k, step - 1, src, slots[k](b), to))
            send(("ag", k), gather_copy(k, chips - 1, src, slots[k](b), sibling))
            gather_local(k, src).start()

        def stage(k, step):
            if k == 0:
                return r.gproj.at[:, (step - 1) * width : step * width]
            return r.stage.at[step - 1]

        def gather_forward(k):
            if k >= 2:
                drain(("forward", k - 1))
            staged = []
            for step in range(1, chips):
                slot = slots[k](lax.rem(chip + chips - step, chips) * 2 + core)
                gather_copy(k, step - 1, slot, slot, sibling).wait_recv()
                staged.append((slot, load(r.stage_sem.at[step - 1], slot, stage(k, step))))
            for step, (slot, copy) in enumerate(staged, 1):
                copy.wait()
                source = stage(k, step)
                send(("forward", k), gather_copy(k, chips - 1 + step, source, slot, sibling))

        def gather_finish(k):
            for step in range(chips):
                slot = slots[k](lax.rem(chip + chips - step, chips) * 2 + 1 - core)
                gather_copy(k, chips - 1 + step, slot, slot, sibling).wait_recv()

        def turned(value_ref, out_ref):
            def body(at):
                tile = value_ref[:, pl.ds(at, share)].T
                group = lax.div(at, share)
                for block in range(blocks):
                    first = pl.multiple_of(block * own + group * rows_out, rows_out)
                    out_ref[pl.ds(first, rows_out), :] = tile[block * rows_out : (block + 1) * rows_out]

            tiles(share, width, body)

        def turned_by_core(value_ref, out_ref):
            def body(at):
                group = lax.div(at, share)
                out_ref[span(lax.rem(group, 2) * chips + lax.div(group, 2), share), :] = value_ref[
                    :, pl.ds(at, share)
                ].T

            tiles(share, width, body)

        load_cot.wait()
        gather_start(0, r.cotv)

        load_tok.wait()

        def norm1(at):
            rows = pl.ds(at, 32)
            x = r.tok[rows, :].astype(F32)
            xhat, inverse = norm_parts(x)
            r.mean1[rows, :] = jnp.broadcast_to(jnp.mean(x, axis=-1, keepdims=True), (32, 128))
            r.inv1[rows, :] = jnp.broadcast_to(inverse, (32, 128))
            r.n1[rows, :] = (xhat * r.gain1[...]).astype(BF16)

        tiles(32, tokens, norm1)
        for block, copy in win_loads:
            copy.wait()
            cols = slice(block * width, (block + 1) * width)
            proj = mm(r.n1[...], r.win[block], out=BF16)
            r.ext[16:, cols] = proj
            r.halo_out[:, cols] = proj[tokens - 16 :]
        halo = remote(r.halo_out, r.halo_in, r.halo_s.at[0], r.halo_r.at[0], seq=block_at(1))
        send("halo", halo)
        turned(r.n1, r.turn)
        gather_start(1, r.turn)

        def ffn_weights(at, slot):
            group = lax.rem(b + 1 + at, groups)
            where = span(slot, ffc)
            return (
                pltpu.make_async_copy(
                    r.w_up.at[:, span(group, ffc)], r.win.at[0, :, where], r.ffn_sem.at[slot, 0]
                ),
                pltpu.make_async_copy(
                    r.w_down.at[span(group, ffc)], r.win.at[1, where], r.ffn_sem.at[slot, 1]
                ),
            )

        for at in range(2):
            for copy in ffn_weights(at, at):
                copy.start()

        halo.wait_recv()
        r.ext[0:16, :] = (r.halo_in[...].astype(F32) * jnp.where(z > 0, 1.0, 0.0)).astype(BF16)

        def lags_at(cols):
            wide = r.ext[:, cols].astype(F32)
            return [wide[16 - lag : 16 - lag + tokens] for lag in range(3)]

        def mix(cols):
            lags = lags_at(cols)
            short = r.short[:, cols].astype(F32)
            return lags, short[0:1] * lags[0] + short[1:2] * lags[1] + short[2:3] * lags[2]

        def chan_copy(k, src, dst, step, to):
            return remote(src, dst, r.za_s.at[k, step - 1], r.za_r.at[k, step - 1], seq=to)

        def to_channels(k, value_ref, make_cols):
            for step in list(range(1, blocks)) + [0]:
                block = block_at(step)
                make_cols(block)
                if step:
                    src, dst = value_ref.at[:, span(block, own)], r.chan.at[span(z, tokens)]
                    send(("za", k), chan_copy(k, src, dst, step, block))
                else:
                    r.chan[span(z, tokens), :] = value_ref[:, span(block, own)]

        def wait_channels(k):
            for step in range(1, blocks):
                source = block_at(blocks - step)
                dst = r.chan.at[span(source, tokens)]
                chan_copy(k, dst, dst, step, source).wait_recv()

        def signal_block(block):
            def body(at):
                base = block * own + at
                cols = pl.ds(pl.multiple_of(base, 128), 128)
                gate_in = mix(pl.ds(pl.multiple_of(width + base, 128), 128))[1]
                values = mix(pl.ds(pl.multiple_of(2 * width + base, 128), 128))[1]
                r.sig[:, cols] = (values * gate_in).astype(BF16)

            tiles(128, own, body)

        to_channels(0, r.sig, signal_block)

        def gate_cols(at):
            cols = pl.ds(at, 128)
            r.gate_out[:, cols] = mix(cols)[1]

        tiles(128, width, gate_cols)

        load_w3.wait()
        load_fade.wait()

        def fading(at):
            lag = (lax.broadcasted_iota(jnp.int32, (tokens, own), 0) + at).astype(F32)
            return jnp.exp(-r.fade[...] * lag)

        def taps_rows(at):
            rows = pl.ds(at, tokens)
            h1, r.s1[:, rows] = sin_cos(mm_tn(r.filt_w1[...], r.features_t[:, rows], precision=HIGHEST))
            h2, r.s2[:, rows] = sin_cos(mm_tn(r.filt_w2[...], h1, precision=HIGHEST))
            r.h1[:, rows] = h1
            r.h2[:, rows] = h2
            taps = mm_tn(h2, r.w3[...], precision=HIGHEST) * fading(at)
            r.qre[rows, :] = taps.astype(BF16)

        tiles(tokens, length, taps_rows)
        load_cs.wait()
        load_sn.wait()
        scale = 1.0 / length

        def taps_spec(at):
            rows = pl.ds(at, tokens)
            real = mm(r.cs[rows, :], r.qre[...]) * scale
            imag = mm(r.sn[rows, :], r.qre[...]) * -scale
            turn_re, turn_im = r.phase[rows, 0:1], r.phase[rows, 1:2]
            r.hre[rows, :] = real * turn_re - imag * turn_im
            r.him[rows, :] = real * turn_im + imag * turn_re

        tiles(tokens, length, taps_spec)
        gather_forward(0)

        wait_channels(0)

        def conv_spec(at):
            rows = pl.ds(at, tokens)
            real = mm(r.cs[rows, :], r.chan[...])
            imag = -mm(r.sn[rows, :], r.chan[...])
            r.xre[rows, :] = real
            r.xim[rows, :] = imag
            hre, him = r.hre[rows, :], r.him[rows, :]
            r.yre[rows, :] = (hre * real - him * imag).astype(BF16)
            r.yim[rows, :] = (-(hre * imag + him * real)).astype(BF16)

        tiles(tokens, length, conv_spec)

        def to_tokens(k):
            for step in list(range(1, blocks)) + [0]:
                block = block_at(step)
                rows = span(block, tokens)
                tile = (mm(r.cs[rows, :], r.yre[...]) + mm(r.sn[rows, :], r.yim[...])).astype(BF16)
                if step:
                    r.conv_out[rows, :] = tile
                    src, dst = r.conv_out.at[rows], r.conv_in.at[z]
                    send(("za", k), chan_copy(k, src, dst, step, block))
                else:
                    r.conv_in[z] = tile

        def wait_tokens(k):
            for step in range(1, blocks):
                source = block_at(blocks - step)
                dst = r.conv_in.at[source]
                chan_copy(k, dst, dst, step, source).wait_recv()

        to_tokens(1)
        gather_forward(1)
        load_wout.wait()
        wait_tokens(1)

        def conv_cols(at):
            return r.conv_in[
                lax.div(at, own), :, pl.ds(pl.multiple_of(lax.rem(at, own), 128), 128)
            ].astype(F32)

        def long_cols(at):
            cols = pl.ds(at, 128)
            long = conv_cols(at) + r.bias[:, cols] * r.sig[:, cols].astype(F32)
            r.long[:, cols] = long
            r.half[:, cols] = (long * r.gate_out[:, cols]).astype(BF16)

        tiles(128, width, long_cols)
        r.res[...] = mm(r.half[...], r.wout[...])
        turned_by_core(r.half, r.gated_turn)
        mine = span(core, tokens)
        pair_rows = chips * share

        def pair_copy(k, src, dst):
            return remote(src, dst, r.cx_s.at[k], r.cx_r.at[k], batch=sibling)

        gated_copy = pair_copy(
            0, r.gated_turn.at[span(1 - core, pair_rows)], r.gated_pair.at[:, mine]
        )
        send("pair", gated_copy)
        r.gated_pair[:, mine] = r.gated_turn[span(core, pair_rows), :]

        def norm2(at):
            rows = pl.ds(at, 32)
            residual = r.res[rows, :] + r.tok[rows, :].astype(F32)
            r.res[rows, :] = residual
            xhat, inverse = norm_parts(residual)
            r.xhat2[rows, :] = xhat
            r.inv2[rows, :] = jnp.broadcast_to(inverse, (32, 128))
            r.half[rows, :] = (xhat * r.gain2[...]).astype(BF16)

        tiles(32, tokens, norm2)
        drain(("ag", 1))
        gather_local(1, r.turn).wait()
        turned(r.half, r.turn)
        gather_start(2, r.turn)
        r.gn2[...] = jnp.zeros((tokens, width), F32)

        def plane_copy(k, src, dst, at, to):
            return remote(src, dst, r.pa_s.at[k, at], r.pa_r.at[k, at], batch=to)

        def chunk_copies(at, to):
            return (
                plane_copy(0, r.hid_send.at[at], r.hid_own.at[:, span(b, tokens)], at, to),
                plane_copy(1, r.pre_send.at[at], r.pre_own.at[span(b, tokens)], at, to),
            )

        def chunk(at, carry):
            slot = lax.rem(at, 2)
            where = span(slot, ffc)
            for copy in ffn_weights(at, slot):
                copy.wait()
            r.gmix[0:tokens, 0:ffc] = mm(r.half[...], r.win[0, :, where])
            r.gmix[0:tokens, ffc : 2 * ffc] = mm_nt(r.cotv[...], r.win[1, where, :])

            def act(row):
                rows = pl.ds(row, 64)
                pre = r.gmix[rows, 0:ffc]
                square = pre * pre
                bent = jnp.tanh(pre * (GELU_SCALE + GELU_SCALE * GELU_CUBIC * square))
                upper = 0.5 + 0.5 * bent
                slope = upper + pre * (0.5 - 0.5 * bent * bent) * (
                    GELU_SCALE + 3.0 * GELU_SCALE * GELU_CUBIC * square
                )
                r.hid_buf[rows, :] = (pre * upper).astype(BF16)
                r.pre_send[at, rows, :] = (r.gmix[rows, ffc : 2 * ffc] * slope).astype(BF16)

            tiles(64, tokens, act)
            r.hid_send[at] = r.hid_buf[...].T

            @pl.when(at < groups - 1)
            def _():
                for copy in chunk_copies(at, lax.rem(b + 1 + at, groups)):
                    copy.start()

            r.res[...] += mm(r.hid_buf[...], r.win[1, where, :])
            r.gn2[...] += mm_nt(r.pre_send[at], r.win[0, :, where])

            @pl.when(at < groups - 2)
            def _():
                for copy in ffn_weights(at + 2, slot):
                    copy.start()

            return carry

        lax.fori_loop(0, groups, chunk, 0)
        for at in range(peers):
            sent.setdefault("ffn", []).extend(chunk_copies(at, group_at(1 + at)))

        def pool_cot():
            return [load(r.win_sem.at[half], r.cot_land.at[half], r.win.at[half]) for half in range(2)]

        def pool_turned(land):
            return [
                load(
                    r.pool_sem.at[at],
                    land.at[at],
                    r.win.at[at // chips, :, pl.ds(at % chips * tokens, tokens)],
                )
                for at in range(groups)
            ]

        gather_local(0, r.cotv).wait()
        gather_finish(0)
        pool = pool_cot()
        r.hid_own[:, span(b, tokens)] = r.hid_send[groups - 1]
        r.pre_own[span(b, tokens), :] = r.pre_send[groups - 1]

        def norm2_back(at, total):
            rows = pl.ds(pl.multiple_of(at * 32, 32), 32)
            r.half[rows, :] = r.res[rows, :].astype(BF16)
            grad, xhat = r.gn2[rows, :], r.xhat2[rows, :]
            back = r.cotv[rows, :].astype(F32) + norm_back(grad, r.gain2[...], xhat, r.inv2[rows, 0:1])
            r.gres[rows, :] = back
            r.gbr_pair[pl.ds(pl.multiple_of(core * tokens + at * 32, 32), 32), :] = back.astype(BF16)
            return total + jnp.sum((grad * xhat).reshape(4, 8, width), axis=0)

        total = lax.fori_loop(0, tokens // 32, norm2_back, jnp.zeros((8, width), F32))
        r.sum_gain2[...] = jnp.sum(total, axis=0, keepdims=True)
        store_layer = load(r.local_sem.at[8], r.half, r.layer_out)
        branch_copy = pair_copy(1, r.gbr_pair.at[mine], r.gbr_pair.at[mine])
        send("pair", branch_copy)

        def gated_back(block):
            cols = span(block, own)
            grad = mm_nt(r.gbr_pair[mine, :], r.wout[span(block, own), :])
            glong = (grad * r.gate_out[:, cols]).astype(BF16)
            r.glong[:, cols] = glong
            r.gmix[0:tokens, cols] = grad * r.long[:, cols]
            r.sum_bias[:, cols] = jnp.sum(
                glong.astype(F32) * r.sig[:, cols].astype(F32), axis=0, keepdims=True
            )

        to_channels(2, r.glong, gated_back)

        branch_copy.wait_recv()
        gated_copy.wait_recv()
        for step in list(range(1, chips)) + [0]:
            to = lax.rem(chip + step, chips)
            part = mm(r.gated_pair[span(to, share), :], r.gbr_pair[...])
            if step:
                at = step - 1
                r.out_send[at] = part.astype(BF16)
                sems = r.wo_s.at[0, at], r.wo_r.at[0, at]
                send("out", remote(r.out_send.at[at], r.out_land.at[at], *sems, batch=to * 2 + core))
            else:
                r.out_own[...] = part
        gather_forward(2)

        near = z + 1 - 2 * lax.rem(z, 2)
        far = block_at(2)

        def reduce_first(k, refs):
            return remote(refs[0], refs[1], r.rs_s.at[k, 0], r.rs_r.at[k, 0], seq=near)

        def reduce_second(k, refs):
            return remote(refs[2], refs[3], r.rs_s.at[k, 1], r.rs_r.at[k, 1], seq=far)

        def reduce_send(k, refs, part_of):
            send_ref, _, next_ref, _, own_ref = refs
            send_ref[0] = part_of(near).astype(BF16)
            send_ref[1] = part_of(lax.rem(near + 2, blocks)).astype(BF16)
            send("rs", reduce_first(k, refs))
            next_ref[...] = part_of(far).astype(BF16)
            own_ref[...] = part_of(z)

        def reduce_next(k, refs):
            _, land_ref, next_ref, _, own_ref = refs
            reduce_first(k, refs).wait_recv()
            next_ref[...] = (next_ref[...].astype(F32) + land_ref[1].astype(F32)).astype(BF16)
            send("rs", reduce_second(k, refs))
            own_ref[...] += land_ref[0].astype(F32)

        def reduce_finish(k, refs):
            reduce_second(k, refs).wait_recv()
            refs[4][...] += refs[3][...].astype(F32)

        down_refs = (r.down_send, r.down_land, r.down_next, r.down_last, r.down_own)
        up_refs = (r.up_send, r.up_land, r.up_next, r.up_last, r.up_own)
        in_refs = (r.in_send, r.in_land, r.in_next, r.in_last, r.in_own)

        def wait_plane(k, dst_of):
            for at in range(peers):
                source = group_at(groups - 1 - at)
                dst = dst_of(source)
                plane_copy(k, dst, dst, at, source).wait_recv()

        deep = groups // 2 * tokens

        def down_part(block):
            rows = span(block, ffc // blocks)
            return mm(r.hid_own[rows, :deep], r.win[0]) + mm(r.hid_own[rows, deep:], r.win[1])

        def turned_part(right_ref):
            def part(block):
                rows = span(block, own)
                return mm(r.win[0, rows, :], right_ref[:deep]) + mm(r.win[1, rows, :], right_ref[deep:])

            return part


        wait_channels(2)

        def grad_spec(at):
            rows = pl.ds(at, tokens)
            real = mm(r.cs[rows, :], r.chan[...])
            imag = -mm(r.sn[rows, :], r.chan[...])
            hre, him = r.hre[rows, :], r.him[rows, :]
            r.yre[rows, :] = (hre * real + him * imag).astype(BF16)
            r.yim[rows, :] = (him * real - hre * imag).astype(BF16)
            xre, xim = r.xre[rows, :], r.xim[rows, :]
            both_re = xre * real + xim * imag
            both_im = xre * imag - xim * real
            turn_re, turn_im = r.phase[rows, 0:1], r.phase[rows, 1:2]
            r.qre[rows, :] = ((both_re * turn_re + both_im * turn_im) * scale).astype(BF16)
            r.qim[rows, :] = ((both_re * turn_im - both_im * turn_re) * scale).astype(BF16)

        tiles(tokens, length, grad_spec)
        drain(("za", 1))
        to_tokens(3)
        r.w12[...] = jnp.zeros((net_rows, 128), F32)
        r.sum_w3[...] = jnp.zeros((filt, own), F32)
        for at in range(0, length, tokens):
            rows = slice(at, at + tokens)
            grad_taps = mm(r.cs[rows, :], r.qre[...]) + mm(r.sn[rows, :], r.qim[...])
            grad_filt = grad_taps * fading(at)
            r.sum_w3[...] += mm(r.h2[:, rows], grad_filt, precision=HIGHEST)
            grad_angle2 = mm_nt(r.w3[...], grad_filt, precision=HIGHEST) * r.s2[:, rows]
            r.w12[net_at:, :filt] += mm_nt(r.h1[:, rows], grad_angle2, precision=HIGHEST)
            grad_angle1 = mm(r.filt_w2[...], grad_angle2, precision=HIGHEST) * r.s1[:, rows]
            r.w12[:emb, :filt] += mm_nt(r.features_t[:, rows], grad_angle1, precision=HIGHEST)

        def small_copy(k, src, dst, at, to):
            return remote(src, dst, r.sm_s.at[k, at], r.sm_r.at[k, at], batch=to)

        def small_z_copy(k, src, dst, step, to):
            return remote(src, dst, r.sz_s.at[k, step - 1], r.sz_r.at[k, step - 1], seq=to)

        def small_z_send(k, src, dst_of):
            for step in range(1, blocks):
                send("small", small_z_copy(k, src, dst_of(step), step, block_at(step)))

        def small_z_wait(k, dst_of):
            for step in range(1, blocks):
                dst = dst_of(step)
                small_z_copy(k, dst, dst, step, block_at(blocks - step)).wait_recv()

        def small_send(k, src_of, dst_of):
            for at in range(peers):
                to = group_at(1 + at)
                send("small", small_copy(k, src_of(to), dst_of(at), at, to))

        def small_wait(k, dst_of):
            for at in range(peers):
                dst = dst_of(at)
                small_copy(k, dst, dst, at, group_at(groups - 1 - at)).wait_recv()

        w3_rows = filt // groups
        small_z_send(0, r.w12, lambda step: r.w12_z.at[step - 1])
        small_send(0, lambda to: r.sum_w3.at[span(to, w3_rows)], lambda at: r.w3_land.at[at])

        def outz_copy(step, to):
            sems = r.wo_s.at[1, step - 1], r.wo_r.at[1, step - 1]
            return remote(r.outz_send.at[span(to, rows_out)], r.outz_land.at[step - 1], *sems, seq=to)

        for step in range(1, chips):
            land = r.out_land.at[step - 1]
            sems = r.wo_s.at[0, step - 1], r.wo_r.at[0, step - 1]
            source = lax.rem(chip + chips - step, chips) * 2 + core
            remote(land, land, *sems, batch=source).wait_recv()
        total = r.out_own[...]
        for step in range(chips - 1):
            total = total + r.out_land[step].astype(F32)
        r.out_own[...] = total
        r.outz_send[...] = total.astype(BF16)
        for step in range(1, blocks):
            send("outz", outz_copy(step, block_at(step)))
        r.outz_own[...] = r.out_own[span(z, rows_out), :]

        wait_tokens(3)

        def short_sums(cols, grad, lags):
            for lag in range(3):
                r.sum_short[lag : lag + 1, cols] = jnp.sum(grad * lags[lag], axis=0, keepdims=True)

        def mixed_cols(at):
            cols = pl.ds(at, 128)
            grad_signal = conv_cols(at) + r.bias[:, cols] * r.glong[:, cols].astype(F32)
            gate_cols = pl.ds(pl.multiple_of(width + at, 128), 128)
            value_cols = pl.ds(pl.multiple_of(2 * width + at, 128), 128)
            gate_lags, gate_in = mix(gate_cols)
            value_lags, values = mix(value_cols)
            grad_gate = grad_signal * values
            r.gmix[0:tokens, gate_cols] = grad_gate
            short_sums(gate_cols, grad_gate, gate_lags)
            grad_value = grad_signal * gate_in
            r.gmix[0:tokens, value_cols] = grad_value
            short_sums(value_cols, grad_value, value_lags)

        tiles(128, width, mixed_cols)
        halo = remote(
            r.gmix.at[0:8], r.gmix.at[tokens : tokens + 8],
            r.halo_s.at[1], r.halo_r.at[1], seq=block_at(blocks - 1),
        )
        send("halo", halo)

        def gate_short(at):
            cols = pl.ds(at, 128)
            short_sums(cols, r.gmix[0:tokens, cols], lags_at(cols))

        tiles(128, width, gate_short)
        small_z_wait(0, lambda step: r.w12_z.at[step - 1])
        net = r.w12[...]
        for step in range(zpeers):
            net = net + r.w12_z[step]
        r.w12_sum[...] = net
        small_send(1, lambda to: r.w12_sum, lambda at: r.w12_plane.at[at])
        small_wait(0, lambda at: r.w3_land.at[at])
        part = r.sum_w3[span(b, w3_rows), :]
        for at in range(peers):
            part = part + r.w3_land[at]
        r.w3_part[...] = part
        r.w3_all[z, span(b, w3_rows), :] = part
        small_send(2, lambda to: r.w3_part, lambda at: r.w3_all.at[z, span(b, w3_rows)])
        halo.wait_recv()
        r.gmix[tokens:, :] = r.gmix[tokens:, :] * jnp.where(z < blocks - 1, 1.0, 0.0)

        drain(("forward", 0))
        for step in list(range(1, groups)) + [0]:
            group = group_at(step)

            def proj_cols(at, group=group):
                cols = pl.ds(pl.multiple_of(group * inc + at, 128), 128)
                short = r.short[:, cols].astype(F32)
                grads = [r.gmix[lag : lag + tokens, cols] for lag in range(3)]
                total = short[0:1] * grads[0] + short[1:2] * grads[1] + short[2:3] * grads[2]
                r.gproj[:, cols] = total.astype(BF16)

            tiles(128, inc, proj_cols)
            mine = r.gproj_own.at[span(b, tokens)]
            if step:
                send("gproj", plane_copy(2, r.gproj.at[:, span(group, inc)], mine, step - 1, group))
            else:
                r.gproj_own[span(b, tokens), :] = r.gproj[:, span(group, inc)]

        def spread(k, own_ref, out_ref, size):
            for at in range(peers):
                to = group_at(1 + at)
                src, dst = own_ref.at[span(to, rows_out)], out_ref.at[:, span(b, size)]
                send("spread", remote(src, dst, r.tr_s.at[k, at], r.tr_r.at[k, at], batch=to))
            return load(r.local_sem.at[14 + k], own_ref.at[span(b, rows_out)], out_ref.at[:, span(b, size)])

        def spread_finish(k, copy, out_ref, size):
            for at in range(peers):
                source = group_at(groups - 1 - at)
                dst = out_ref.at[:, span(source, size)]
                remote(dst, dst, r.tr_s.at[k, at], r.tr_r.at[k, at], batch=source).wait_recv()
            copy.wait()

        for copy in pool:
            copy.wait()
        wait_plane(0, lambda at: r.hid_own.at[:, span(at, tokens)])
        reduce_send(0, down_refs, down_part)
        gather_local(2, r.turn).wait()
        gather_finish(2)
        pool = pool_turned(r.n2_land)
        small_wait(1, lambda at: r.w12_plane.at[at])
        net = r.w12_sum[...]
        for at in range(peers):
            net = net + r.w12_plane[at]
        r.grad_w1[...] = net[:emb, :filt]
        r.grad_w2[...] = net[net_at:, :filt]
        for at in range(peers):
            dst = r.w3_all.at[z, span(group_at(groups - 1 - at), w3_rows)]
            small_copy(2, dst, dst, at, group_at(groups - 1 - at)).wait_recv()
        small_z_send(1, r.w3_all.at[z], lambda step: r.w3_all.at[z])
        for copy in pool:
            copy.wait()
        wait_plane(1, lambda at: r.pre_own.at[span(at, tokens)])
        reduce_next(0, down_refs)
        reduce_send(1, up_refs, turned_part(r.pre_own))
        win_loads = [(block, load_win(block)) for block in range(2)]
        for step in range(1, blocks):
            outz_copy(step, block_at(blocks - step)).wait_recv()
        total = r.outz_own[...]
        for step in range(zpeers):
            total = total + r.outz_land[step].astype(F32)
        r.outz_own[...] = total
        store_out = load(r.local_sem.at[11], r.outz_own, r.grad_w_out)
        reduce_finish(0, down_refs)
        store_down = load(r.local_sem.at[9], r.down_own, r.grad_w_down)
        for _, copy in win_loads:
            copy.wait()
        r.gn2[...] = mm_nt(r.gproj[:, :width], r.win[0])
        r.gn2[...] += mm_nt(r.gproj[:, width : 2 * width], r.win[1])
        reduce_next(1, up_refs)
        gather_finish(1)
        pool = pool_turned(r.n1_land)
        r.gn2[...] += mm_nt(r.gproj[:, 2 * width :], r.win[2])

        def norm1_back(at, total):
            rows = pl.ds(pl.multiple_of(at * 32, 32), 32)
            grad, inverse = r.gn2[rows, :], r.inv1[rows, 0:1]
            xhat = (r.tok[rows, :].astype(F32) - r.mean1[rows, 0:1]) * inverse
            r.res[rows, :] = r.gres[rows, :] + norm_back(grad, r.gain1[...], xhat, inverse)
            return total + jnp.sum((grad * xhat).reshape(4, 8, width), axis=0)

        total = lax.fori_loop(0, tokens // 32, norm1_back, jnp.zeros((8, width), F32))
        r.sum_gain1[...] = jnp.sum(total, axis=0, keepdims=True)
        r.small_send[...] = jnp.zeros((groups, 16, share), F32)
        for group in range(groups):
            cols = slice(group * share, (group + 1) * share)
            r.small_send[group, 0:1, :] = r.sum_gain1[:, cols]
            r.small_send[group, 1:2, :] = r.sum_gain2[:, cols]
            r.small_send[group, 2:3, :] = r.sum_bias[:, cols]
            for lag in range(3):
                for third in range(3):
                    at = group * inc + third * share
                    row = 3 + 3 * lag + third
                    r.small_send[group, row : row + 1, :] = r.sum_short[lag : lag + 1, at : at + share]
        small_send(3, lambda to: r.small_send.at[to], lambda at: r.small_land.at[b])
        r.small_land[b] = r.small_send[b]
        store_tokens = load(r.local_sem.at[13], r.res, r.tokens_grad)
        for copy in pool:
            copy.wait()
        wait_plane(2, lambda at: r.gproj_own.at[span(at, tokens)])
        reduce_send(2, in_refs, turned_part(r.gproj_own))
        reduce_finish(1, up_refs)
        spread_up = spread(0, r.up_own, r.grad_w_up, ffc)
        for at in range(peers):
            source = group_at(groups - 1 - at)
            dst = r.small_land.at[source]
            small_copy(3, dst, dst, at, source).wait_recv()
        small = r.small_land[0]
        for group in range(1, groups):
            small = small + r.small_land[group]
        r.small_sum[...] = small
        small_z_send(2, r.small_sum, lambda step: r.small_z.at[step - 1])
        reduce_next(2, in_refs)
        reduce_finish(2, in_refs)
        spread_in = spread(1, r.in_own, r.grad_w_in, inc)

        def chosen(value, size):
            picked = value[:, :size]
            for block in range(1, blocks):
                picked = jnp.where(z == block, value[:, block * size : (block + 1) * size], picked)
            return picked

        for step in range(1, blocks):
            source = block_at(blocks - step)
            dst = r.w3_all.at[source]
            small_z_copy(1, dst, dst, step, source).wait_recv()
        third = r.w3_all[lax.div(b * share, own)]
        halves = own // share
        picked = third[:, :share]
        for half in range(1, halves):
            here = lax.rem(b, halves) == half
            picked = jnp.where(here, third[:, half * share : (half + 1) * share], picked)
        r.grad_w3[...] = chosen(picked, rows_out)
        small_z_wait(2, lambda step: r.small_z.at[step - 1])
        small = r.small_sum[...]
        for step in range(zpeers):
            small = small + r.small_z[step]
        r.grad_gain1[...] = chosen(small[0:1], rows_out)
        r.grad_gain2[...] = chosen(small[1:2], rows_out)
        r.grad_bias[...] = chosen(small[2:3], rows_out)
        for lag in range(3):
            for third in range(3):
                row = 3 + 3 * lag + third
                r.short_all[lag : lag + 1, third * share : (third + 1) * share] = small[row : row + 1]
        r.grad_short[...] = chosen(r.short_all[0:3, :], 3 * rows_out)
        spread_finish(0, spread_up, r.grad_w_up, ffc)
        spread_finish(1, spread_in, r.grad_w_in, inc)
        store_layer.wait()
        store_down.wait()
        store_out.wait()
        store_tokens.wait()
        for key in list(sent):
            drain(key)

    def call(args):
        result = pl.pallas_call(
            kernel,
            out_shape=[jax.ShapeDtypeStruct(shape, dtype) for shape, dtype, _ in outputs.values()],
            in_specs=[pl.BlockSpec(memory_space=space) for space in inputs.values()],
            out_specs=[pl.BlockSpec(memory_space=space) for *_, space in outputs.values()],
            scratch_shapes=list(scratch.values()),
            compiler_params=pltpu.CompilerParams(
                collective_id=0, has_side_effects=True, vmem_limit_bytes=KERNEL_VMEM
            ),
        )(*[args[name] for name in inputs])
        return settled(result[:13])

    return call


def settled(values):
    count = len(values)

    def copy_all(*refs):
        for source, target in zip(refs[:count], refs[count:]):
            target[...] = source[...].reshape(target.shape)

    return pl.pallas_call(
        copy_all,
        out_shape=[
            jax.ShapeDtypeStruct(value.shape[1:] if value.shape[0] == 1 else value.shape, value.dtype)
            for value in values
        ],
        in_specs=[pl.BlockSpec(memory_space=pltpu.VMEM)] * count,
        out_specs=[pl.BlockSpec(memory_space=pltpu.VMEM)] * count,
    )(*values)


def small_sums(gain1, bias, gain2, short, w1, w2, w3_own):
    blocks, position = lax.axis_size("seq"), lax.axis_index("seq")
    dests = lax.axis_size("batch") * blocks
    width, (filt_dim, own), emb = gain1.shape[0], w3_own.shape, w1.shape[0]
    w3_all = lax.dynamic_update_slice_in_dim(
        jnp.zeros((filt_dim, width), F32), w3_own, position * own, 1
    )
    share = width // dests
    small = jnp.concatenate(
        [
            gain1.reshape(dests, share),
            bias.reshape(dests, share),
            gain2.reshape(dests, share),
            short.reshape(3, dests, 3 * share).transpose(1, 0, 2).reshape(dests, 9 * share),
            w3_all.reshape(filt_dim, dests, share).transpose(1, 0, 2).reshape(dests, filt_dim * share),
        ],
        axis=1,
    )
    small = scatter_sum(small, wire=F32)[0]
    filters = all_sum(jnp.concatenate([w1, w2], axis=0))
    return (
        small[:share],
        small[3 * share : 12 * share].reshape(3, 3 * share),
        filters[:emb],
        filters[emb:],
        small[12 * share :].reshape(filt_dim, share),
        small[share : 2 * share],
        small[2 * share : 3 * share],
    )


def kernel_layer(
    tokens,
    norm_gain1,
    w_in,
    short_kernel,
    filt_w1,
    filt_w2,
    filt_w3,
    decay_rate,
    conv_bias,
    w_out,
    norm_gain2,
    w_up,
    w_down,
    cotangent,
):
    _, block_len, width = tokens.shape
    groups, blocks = lax.axis_size("batch"), lax.axis_size("seq")
    emb, filt = filt_w1.shape
    (cosine, sine), phase = symmetric_tables(block_len * blocks)
    features = lag_features(emb, block_len * blocks)
    call = kernel_plan(groups, blocks, block_len, width, w_up.shape[1], filt, emb)
    out = call(
        dict(
            tokens=tokens[0],
            cot=cotangent[0],
            w_in=w_in,
            w_out=w_out,
            w_up=w_up,
            w_down=w_down,
            cosine=jnp.asarray(cosine),
            sine=jnp.asarray(sine),
            filt_w3=filt_w3,
            decay=decay_rate[None],
            gain1=norm_gain1[None],
            gain2=norm_gain2[None],
            bias=conv_bias[None],
            short=short_kernel,
            filt_w1=filt_w1,
            filt_w2=filt_w2,
            features_t=jnp.asarray(features.T),
            phase=jnp.asarray(phase),
        )
    )
    layer_out, tokens_grad, w_in, w_out, w_up, w_down, gain1, gain2, bias, short, w1, w2, w3 = out
    return layer_out[None], tokens_grad[None], (gain1, short, w1, w2, w3, bias, gain2), (w_in, w_out, w_up, w_down)


def on_device(*args):
    tokens = args[0]
    fits = lax.axis_size("batch") == 8 and lax.axis_size("seq") == 4 and tokens.shape[1] * lax.axis_size("seq") <= 1024
    layer = kernel_layer if fits else plain_layer
    layer_out, tokens_grad, small, large = layer(*args)
    gain1, short, w1, w2, w3, bias, gain2 = small
    grad_w_in, grad_w_out, grad_w_up, grad_w_down = large
    return (
        layer_out, tokens_grad, gain1, grad_w_in, short, w1, w2, w3, bias, grad_w_out, gain2,
        grad_w_up, grad_w_down,
    )


def solution(mesh):
    split = P("batch", "seq", None)
    both = ("batch", "seq")
    return jax.shard_map(
        on_device,
        mesh=mesh,
        in_specs=(split,) + (P(),) * 12 + (split,),
        out_specs=(
            split,
            split,
            P(both),
            P(both, None),
            P(None, both),
            P(),
            P(),
            P(None, both),
            P(both),
            P(both, None),
            P(both),
            P(both, None),
            P(both, None),
        ),
        check_vma=False,
    )
```

```python
import math

import jax
import jax.numpy as jnp
import ml_dtypes
import numpy as np
from jax import lax
from jax.experimental import pallas as pl
from jax.experimental.pallas import tpu as pltpu
from jax.sharding import PartitionSpec as P

F32 = jnp.float32
BF16 = jnp.bfloat16
HIGHEST = lax.Precision.HIGHEST
GELU_SCALE = math.sqrt(2.0 / math.pi)
GELU_CUBIC = 0.044715


def dot(left, right, contract, out=F32, precision=None):
    return lax.dot_general(
        left, right, (contract, ((), ())), precision=precision, preferred_element_type=F32
    ).astype(out)


def mm(left, right, **kw):
    return dot(left, right, ((1,), (0,)), **kw)


def mm_nt(left, right, **kw):
    return dot(left, right, ((1,), (1,)), **kw)


def mm_tn(left, right, **kw):
    return dot(left, right, ((0,), (0,)), **kw)


def shifted(value, axis, steps):
    count = lax.axis_size(axis)
    first, last = (max(0, -steps), min(count, count - steps))
    return lax.ppermute(value, axis, [(source, source + steps) for source in range(first, last)])


def exchange(value, axis, bit):
    count = lax.axis_size(axis)
    return lax.ppermute(value, axis, [(at, at ^ (1 << bit)) for at in range(count)])


def bits_of(axis):
    return lax.axis_size(axis).bit_length() - 1


def stage_order(swap):
    batch_bits, seq_bits = bits_of("batch"), bits_of("seq")
    rest = list(range(1, batch_bits))
    half = len(rest) // 2
    if swap:
        rest = rest[half:] + rest[:half]
    return [("batch", bit) for bit in [0] + rest] + [("seq", bit) for bit in range(seq_bits)]


def scatter_sum(partial, swap=False, wire=BF16):
    batch_bits, seq_bits = bits_of("batch"), bits_of("seq")
    dims = [("batch", bit) for bit in reversed(range(batch_bits))]
    dims += [("seq", bit) for bit in reversed(range(seq_bits))]
    rows = partial.shape[0] >> len(dims)
    value = partial.reshape((2,) * len(dims) + (rows,) + partial.shape[1:]).astype(wire)
    for axis, bit in stage_order(swap):
        at = dims.index((axis, bit))
        mine = (lax.axis_index(axis) >> bit) & 1
        keep = lax.dynamic_index_in_dim(value, mine, at, keepdims=False)
        send = lax.dynamic_index_in_dim(value, 1 - mine, at, keepdims=False)
        got = exchange(send, axis, bit)
        value = keep.astype(F32) + got.astype(F32)
        dims.pop(at)
        if dims:
            value = value.astype(wire)
    return value


def gather_batch(value):
    return lax.all_gather(value, "batch", axis=0, tiled=True)


def columns_batch(value):
    return lax.all_to_all(value, "batch", 1, 0, tiled=True)


def rows_sum(left_own, right_all):
    blocks = lax.axis_size("seq")
    part = mm_tn(left_own, right_all, out=BF16)
    got = lax.all_to_all(part.reshape(blocks, -1, part.shape[1]), "seq", 0, 0, tiled=True)
    return jnp.sum(got.astype(F32), axis=0)


def columns_sum(left_all, right_own):
    blocks, groups = lax.axis_size("seq"), lax.axis_size("batch")
    part = mm_tn(left_all, right_own, out=BF16)
    part = part.reshape(groups * blocks, -1, part.shape[1])
    got = lax.all_to_all(part, ("batch", "seq"), 0, 0, tiled=True)
    got = jnp.sum(got.reshape(groups, blocks, -1, part.shape[2]).astype(F32), axis=1)
    return got.transpose(1, 0, 2).reshape(got.shape[1], -1)


def all_sum(value):
    for axis, bit in stage_order(False):
        value = value + exchange(value, axis, bit)
    return value


def norm_parts(values):
    centered = values - jnp.mean(values, axis=-1, keepdims=True)
    inverse = lax.rsqrt(jnp.mean(centered * centered, axis=-1, keepdims=True) + 1e-05)
    return centered * inverse, inverse


def norm_back(grad, gain, xhat, inverse):
    scaled = grad * gain
    return (
        scaled
        - jnp.mean(scaled, axis=-1, keepdims=True)
        - xhat * jnp.mean(scaled * xhat, axis=-1, keepdims=True)
    ) * inverse


def transform_table(length):
    count = np.arange(length, dtype=np.int64)
    turns = (2 * count[:, None] + 1) * count[None, :] % (4 * length)
    angles = turns.astype(np.float64) * (2.0 * np.pi / (4 * length))
    table = np.concatenate([np.cos(angles), -np.sin(angles)], axis=0)
    return table.astype(np.float32).astype(ml_dtypes.bfloat16)


def lag_features(emb, length):
    bands = (emb - 1) // 2
    lag = np.arange(length, dtype=np.float64)
    freq = 1e-4 + np.arange(bands, dtype=np.float64) * ((bands - 1 - 1e-4) / (bands - 1))
    phases = (lag * (2.0 * np.pi / length))[:, None] * freq[None, :]
    return np.concatenate(
        [(lag / (length - 1))[:, None], np.cos(phases), -np.sin(phases)], axis=1
    ).astype(np.float32)


def to_channels(value):
    return lax.all_to_all(value, "seq", 1, 0, tiled=True)


def to_tokens(value):
    return lax.all_to_all(value, "seq", 0, 1, tiled=True)


def plain_layer(
    tokens,
    norm_gain1,
    w_in,
    short_kernel,
    filt_w1,
    filt_w2,
    filt_w3,
    decay_rate,
    conv_bias,
    w_out,
    norm_gain2,
    w_up,
    w_down,
    cotangent,
):
    num_seqs, block_len, width = tokens.shape
    assert num_seqs == 1
    blocks = lax.axis_size("seq")
    position = lax.axis_index("seq")
    seq_len = block_len * blocks
    own = width // blocks
    table = jnp.asarray(transform_table(seq_len))
    features = jnp.asarray(lag_features(filt_w1.shape[0], seq_len))
    cot = cotangent[0]
    cot_all = gather_batch(cot)
    inputs = tokens[0].astype(F32)

    xhat1, inverse1 = norm_parts(inputs)
    normed1 = (xhat1 * norm_gain1).astype(BF16)
    normed1_all = gather_batch(normed1)
    projected = mm(normed1, w_in, out=BF16)
    earlier = shifted(projected[block_len - 2 :], "seq", 1)
    extended = jnp.concatenate([earlier, projected], axis=0).astype(F32)
    taps3 = short_kernel.astype(F32)
    lags = [extended[2 - lag : 2 - lag + block_len] for lag in range(3)]
    mixed = taps3[0] * lags[0] + taps3[1] * lags[1] + taps3[2] * lags[2]
    gate_out = mixed[:, :width]
    gate_in = mixed[:, width : 2 * width]
    values = mixed[:, 2 * width :]
    signal = (values * gate_in).astype(BF16)

    w3_own = lax.dynamic_slice_in_dim(filt_w3, position * own, own, 1)
    decay_own = lax.dynamic_slice_in_dim(decay_rate, position * own, own, 0)
    angle1 = mm(features, filt_w1, precision=HIGHEST)
    hidden1, slope1 = jnp.sin(angle1), jnp.cos(angle1)
    angle2 = mm(hidden1, filt_w2, precision=HIGHEST)
    hidden2, slope2 = jnp.sin(angle2), jnp.cos(angle2)
    lag_index = jnp.arange(seq_len).astype(F32)
    fading = jnp.exp(-decay_own[None, :] * lag_index[:, None])
    taps = (mm(hidden2, w3_own, precision=HIGHEST) * fading).astype(BF16)
    taps_spec = mm(table, taps)
    taps_re, taps_im = taps_spec[:seq_len], taps_spec[seq_len:]

    signal_spec = mm(table, to_channels(signal))
    signal_re, signal_im = signal_spec[:seq_len], signal_spec[seq_len:]
    scale = 1.0 / seq_len

    def inverse_of(real, imag):
        both = (jnp.concatenate([real, imag], axis=0) * scale).astype(BF16)
        return mm_tn(table, both)

    conv = inverse_of(
        taps_re * signal_re - taps_im * signal_im, taps_re * signal_im + taps_im * signal_re
    )
    long_out = to_tokens(conv.astype(BF16)).astype(F32) + conv_bias * signal.astype(F32)
    gated = (long_out * gate_out).astype(BF16)
    gated_all = gather_batch(gated)
    residual1 = inputs + mm(gated, w_out)
    xhat2, inverse2 = norm_parts(residual1)
    normed2 = (xhat2 * norm_gain2).astype(BF16)
    normed2_all = gather_batch(normed2)
    pre = mm(normed2, w_up)
    bent = jnp.tanh(GELU_SCALE * (pre + GELU_CUBIC * pre * pre * pre))
    hidden = (0.5 * pre * (1.0 + bent)).astype(BF16)
    layer_out = (residual1 + mm(hidden, w_down)).astype(BF16)

    slope = 0.5 * (1.0 + bent) + 0.5 * pre * (1.0 - bent * bent) * GELU_SCALE * (
        1.0 + 3.0 * GELU_CUBIC * pre * pre
    )
    grad_pre = (mm_nt(cot, w_down) * slope).astype(BF16)
    grad_w_down = rows_sum(columns_batch(hidden), cot_all)
    grad_w_up = columns_sum(normed2_all, columns_batch(grad_pre))
    grad_norm2 = mm_nt(grad_pre, w_up)
    grad_gain2 = jnp.sum(grad_norm2 * xhat2, axis=0)
    grad_res = cot.astype(F32) + norm_back(grad_norm2, norm_gain2, xhat2, inverse2)
    grad_branch = grad_res.astype(BF16)
    grad_w_out = columns_sum(gated_all, columns_batch(grad_branch))
    grad_gated = mm_nt(grad_branch, w_out)
    grad_long = (grad_gated * gate_out).astype(BF16)
    grad_gate_out = grad_gated * long_out
    grad_bias = jnp.sum(grad_long.astype(F32) * signal.astype(F32), axis=0)

    grad_spec = mm(table, to_channels(grad_long))
    grad_re, grad_im = grad_spec[:seq_len], grad_spec[seq_len:]
    grad_conv = inverse_of(
        taps_re * grad_re + taps_im * grad_im, taps_re * grad_im - taps_im * grad_re
    )
    grad_signal = to_tokens(grad_conv.astype(BF16)).astype(F32) + conv_bias * grad_long.astype(F32)
    grad_taps = inverse_of(
        signal_re * grad_re + signal_im * grad_im, signal_re * grad_im - signal_im * grad_re
    )
    grad_filt = grad_taps * fading
    grad_w3_own = mm_tn(hidden2, grad_filt)
    grad_angle2 = mm_nt(grad_filt, w3_own) * slope2
    grad_w2 = mm_tn(hidden1, grad_angle2)
    grad_angle1 = mm_nt(grad_angle2, filt_w2) * slope1
    grad_w1 = mm_tn(features, grad_angle1)

    grad_mixed = jnp.concatenate(
        [grad_gate_out, grad_signal * values, grad_signal * gate_in], axis=1
    )
    later = shifted(grad_mixed[:2], "seq", -1)
    grad_ext = jnp.concatenate([grad_mixed, later], axis=0)
    grad_proj = (
        taps3[0] * grad_ext[:block_len]
        + taps3[1] * grad_ext[1 : block_len + 1]
        + taps3[2] * grad_ext[2:]
    ).astype(BF16)
    grad_short = jnp.stack([jnp.sum(grad_mixed * lag, axis=0) for lag in lags])
    grad_w_in = columns_sum(normed1_all, columns_batch(grad_proj))
    grad_norm1 = mm_nt(grad_proj, w_in)
    grad_gain1 = jnp.sum(grad_norm1 * xhat1, axis=0)
    tokens_grad = grad_res + norm_back(grad_norm1, norm_gain1, xhat1, inverse1)

    return layer_out[None], tokens_grad[None], small_sums(
        grad_gain1, grad_bias, grad_gain2, grad_short, grad_w1, grad_w2, grad_w3_own
    ), (grad_w_in, grad_w_out, grad_w_up, grad_w_down)


MESH = pl.DeviceIdType.MESH
KERNEL_VMEM = 63 * 1024 * 1024


def symmetric_tables(length):
    odd = 2 * np.arange(length, dtype=np.int64) + 1
    angles = (odd[:, None] * odd[None, :] % (8 * length)).astype(np.float64) * (
        np.pi / (4 * length)
    )
    phase = odd.astype(np.float64) * (np.pi / (4 * length))
    tables = [np.cos(angles), np.sin(angles)]
    tables = [t.astype(np.float32).astype(ml_dtypes.bfloat16) for t in tables]
    return tables, np.stack([np.cos(phase), np.sin(phase)], axis=1).astype(np.float32)


def sin_cos(x):
    turns = jnp.floor(x * (2.0 / np.pi) + 0.5)
    rest = ((x - turns * 1.5703125) - turns * 4.837512969970703e-4) - turns * 7.54978995489188e-8
    square = rest * rest
    sine = rest + rest * square * (
        -1.6666654611e-1 + square * (8.3321608736e-3 - square * 1.9515295891e-4)
    )
    cosine = (1.0 - 0.5 * square) + square * square * (
        4.166664568298827e-2 + square * (-1.388731625493765e-3 + square * 2.443315711809948e-5)
    )
    quarter = turns - 4.0 * jnp.floor(turns * 0.25)
    odd = (quarter == 1.0) | (quarter == 3.0)
    sin_sign = jnp.where(quarter >= 2.0, -1.0, 1.0)
    cos_sign = jnp.where((quarter == 1.0) | (quarter == 2.0), -1.0, 1.0)
    return sin_sign * jnp.where(odd, cosine, sine), cos_sign * jnp.where(odd, sine, cosine)


class Named:
    def __init__(self, names, refs):
        assert len(names) == len(refs)
        for name, ref in zip(names, refs):
            setattr(self, name, ref)


def kernel_plan(groups, blocks, tokens, width, hidden, filt, emb):
    length = tokens * blocks
    own = width // blocks
    ffc = hidden // groups
    share = width // groups
    rows_out = share // blocks
    inc = 3 * share
    spare = 16
    chips = groups // 2
    down_rows = ffc // blocks
    net_at = -(-emb // 8) * 8
    net_rows = net_at + filt
    peers, zpeers = groups - 1, blocks - 1
    vm, hbm = pltpu.VMEM, pl.ANY
    inputs = dict(
        tokens=hbm, cot=hbm, w_in=hbm, w_out=hbm, w_up=hbm, w_down=hbm,
        cosine=hbm, sine=hbm, filt_w3=hbm, decay=hbm,
        gain1=vm, gain2=vm, bias=vm, short=vm, filt_w1=vm, filt_w2=vm,
        features_t=vm, phase=vm,
    )
    outputs = dict(
        layer_out=((tokens, width), BF16, hbm),
        tokens_grad=((tokens, width), F32, hbm),
        grad_w_in=((rows_out, 3 * width), F32, hbm),
        grad_w_out=((rows_out, width), F32, hbm),
        grad_w_up=((rows_out, hidden), F32, hbm),
        grad_w_down=((ffc // blocks, width), F32, hbm),
        grad_gain1=((1, rows_out), F32, vm),
        grad_gain2=((1, rows_out), F32, vm),
        grad_bias=((1, rows_out), F32, vm),
        grad_short=((3, 3 * rows_out), F32, vm),
        grad_w1=((emb, filt), F32, vm),
        grad_w2=((filt, filt), F32, vm),
        grad_w3=((filt, rows_out), F32, vm),
        cot_land=((2, groups // 2 * tokens, width), BF16, hbm),
        n2_land=((groups, width, tokens), BF16, hbm),
    )
    dma = pltpu.SemaphoreType.DMA
    scratch = dict(
        tok=vm((tokens, width), BF16), cotv=vm((tokens, width), BF16),
        mean1=vm((tokens, 128), F32), inv1=vm((tokens, 128), F32),
        n1_all=vm((length, width), BF16), turn=vm((width, tokens), BF16),
        gated_turn=vm((width, tokens), BF16), gated_pair=vm((width // 2, 2 * tokens), BF16),
        hid_buf=vm((tokens, ffc), BF16),
        ghalo=vm((8, 3 * width), F32), ghalo_in=vm((8, 3 * width), F32), tail=vm((16, 3 * width), F32),
        ext_c=vm((length + 32, 3 * own), BF16), gproj_c=vm((length, 3 * own), BF16),
        gconv_c=vm((length + 16, own), BF16), glong_c=vm((length + 16, own), BF16),
        ggb=vm((tokens, width), BF16),
        win=vm((3, width, width), BF16), wout=vm((width, width), BF16),
        cs=vm((length, length), BF16), sn=vm((length, length), BF16),
        ext=vm((tokens + 16, 3 * width), BF16),
        halo_out=vm((16, 3 * width), BF16), halo_in=vm((16, 3 * width), BF16),
        gate_out=vm((tokens, width), F32),
        sig=vm((tokens, width), BF16), chan=vm((length + 16, own), BF16),
        w3=vm((filt, own), F32), fade=vm((1, own), F32),
        h1=vm((filt, length), F32), s1=vm((filt, length), F32),
        h2=vm((filt, length), F32), s2=vm((filt, length), F32),
        sum_gain1=vm((1, width), F32), sum_gain2=vm((1, width), F32),
        sum_bias=vm((1, width), F32), sum_short=vm((3, 3 * width), F32),
        small_send=vm((groups, 16, share), F32), small_land=vm((groups, 16, share), F32),
        small_sum=vm((16, share), F32), small_z=vm((zpeers, 16, share), F32),
        short_all=vm((8, inc), F32),
        w12=vm((net_rows, 128), F32), w12_z=vm((zpeers, net_rows, 128), F32),
        w12_sum=vm((net_rows, 128), F32), w12_plane=vm((peers, net_rows, 128), F32),
        sum_w3=vm((filt, own), F32), w3_land=vm((peers, filt // groups, own), F32),
        w3_part=vm((filt // groups, own), F32), w3_all=vm((blocks, filt, own), F32),
        hre=vm((length, own), F32), him=vm((length, own), F32),
        xre=vm((length, own), F32), xim=vm((length, own), F32),
        yre=vm((length, own), BF16), yim=vm((length, own), BF16),
        qre=vm((length, own), BF16), qim=vm((length, own), BF16),
        conv_out=vm((length + 16, own), BF16), conv_in=vm((blocks, tokens, own), BF16),
        long=vm((tokens, width), F32), half=vm((tokens, width), BF16),
        res=vm((tokens, width), F32), xhat2=vm((tokens, width), F32),
        inv2=vm((tokens, 128), F32), gn2=vm((tokens, width), F32),
        gres=vm((tokens, width), F32),
        hid_send=vm((groups, ffc, tokens), BF16), hid_own=vm((ffc, groups * tokens), BF16),
        pre_send=vm((groups, tokens, ffc), BF16), pre_own=vm((groups * tokens, ffc), BF16),
        gbr_pair=vm((2 * tokens, width), BF16),
        glong=vm((tokens, width), BF16),
        gproj=vm((tokens, 3 * width), BF16),
        down_send=vm((2, down_rows, width), BF16), down_land=vm((2, down_rows, width), BF16),
        down_next=vm((down_rows, width), BF16), down_last=vm((down_rows, width), BF16),
        up_send=vm((2, own, ffc), BF16), up_land=vm((2, own, ffc), BF16),
        up_next=vm((own, ffc), BF16), up_last=vm((own, ffc), BF16),
        in_send=vm((chips, share, 3 * own), BF16), in_pair=vm((chips, share, 3 * own), BF16),
        in_land=vm((chips - 1, share, 3 * own), BF16), in_own=vm((share, 3 * own), F32),
        out_send=vm((chips - 1, share, width), BF16), out_land=vm((chips - 1, share, width), BF16),
        outz_send=vm((share, width), BF16), outz_land=vm((zpeers, rows_out, width), BF16),
        outz_own=vm((rows_out, width), F32),
        load_sem=dma((16,)),
        pool_sem=dma((groups,)),
        win_sem=dma((3,)),
        ffn_sem=dma((2, 2)),
        local_sem=dma((16,)),
        stage_sem=dma((chips - 1,)),
        ag_s=dma((2, groups - 1)), ag_r=dma((2, groups - 1)),
        halo_s=dma((2,)), halo_r=dma((2,)),
        za_s=dma((4, zpeers)), za_r=dma((4, zpeers)),
        pa_s=dma((2, peers)), pa_r=dma((2, peers)),
        cx_s=dma((3,)), cx_r=dma((3,)), zg_s=dma((zpeers,)), zg_r=dma((zpeers,)),
        wi_s=dma((chips - 1,)), wi_r=dma((chips - 1,)), ti_s=dma((zpeers, 3)), ti_r=dma((zpeers, 3)), wo_s=dma((2, chips - 1)), wo_r=dma((2, chips - 1)),
        rs_s=dma((2, 2)), rs_r=dma((2, 2)),
        sm_s=dma((4, peers)), sm_r=dma((4, peers)),
        sz_s=dma((3, zpeers)), sz_r=dma((3, zpeers)),
        tr_s=dma((1, peers)), tr_r=dma((1, peers)),
    )
    names = [*inputs, *outputs, *scratch]

    def kernel(*refs):
        r = Named(names, refs)
        b, z = lax.axis_index("batch"), lax.axis_index("seq")
        chip, core = lax.div(b, 2), lax.rem(b, 2)
        sibling = chip * 2 + (1 - core)
        sent = {}

        def group_at(step):
            return lax.rem(b + step, groups)

        def block_at(step):
            return lax.rem(z + step, blocks)

        def span(at, size):
            return pl.ds(pl.multiple_of(at * size, size), size)

        def remote(src, dst, send_sem, recv_sem, **where):
            return pltpu.make_async_remote_copy(
                src_ref=src, dst_ref=dst, send_sem=send_sem, recv_sem=recv_sem,
                device_id=where, device_id_type=MESH,
            )

        def send(key, copy):
            copy.start()
            sent.setdefault(key, []).append(copy)

        def drain(key):
            for copy in sent.pop(key):
                copy.wait_send()

        def tiles(size, total, body):
            def step(i, carry):
                body(pl.multiple_of(i * size, size))
                return carry

            lax.fori_loop(0, total // size, step, 0)

        def load(sem, src, dst):
            copy = pltpu.make_async_copy(src, dst, sem)
            copy.start()
            return copy

        def load_win(block):
            return load(r.win_sem.at[block], r.w_in.at[:, pl.ds(block * width, width)], r.win.at[block])

        load_tok = load(r.load_sem.at[0], r.tokens, r.tok)
        win_loads = [(block, load_win(block)) for block in (1, 2, 0)]
        load_cot = load(r.load_sem.at[5], r.cot, r.cotv)
        load_w3 = load(r.load_sem.at[1], r.filt_w3.at[:, span(z, own)], r.w3)
        load_fade = load(r.load_sem.at[2], r.decay.at[:, span(z, own)], r.fade)
        load_cs = load(r.load_sem.at[3], r.cosine, r.cs)
        load_sn = load(r.load_sem.at[4], r.sine, r.sn)
        load_wout = load(r.load_sem.at[6], r.w_out, r.wout)

        barrier = pltpu.get_barrier_semaphore()
        for step in range(1, groups):
            pl.semaphore_signal(barrier, inc=1, device_id={"batch": group_at(step)}, device_id_type=MESH)
        for step in range(1, blocks):
            pl.semaphore_signal(barrier, inc=1, device_id={"seq": block_at(step)}, device_id_type=MESH)

        slots = [
            lambda at: r.cot_land.at[lax.div(at, chips), span(lax.rem(at, chips), tokens)],
            lambda at: r.n2_land.at[at],
        ]

        def gather_copy(k, at, src, slot, to):
            return remote(src, slot, r.ag_s.at[k, at], r.ag_r.at[k, at], batch=to)

        def gather_local(k, src):
            return pltpu.make_async_copy(src, slots[k](b), r.local_sem.at[k])

        def gather_start(k, src):
            for step in range(1, chips):
                to = lax.rem(chip + step, chips) * 2 + core
                send(("ag", k), gather_copy(k, step - 1, src, slots[k](b), to))
            send(("ag", k), gather_copy(k, chips - 1, src, slots[k](b), sibling))
            gather_local(k, src).start()

        def stage(k, step):
            if k == 0:
                return r.gproj.at[:, (step - 1) * width : step * width]
            return r.win.at[0, :, (step - 1) * tokens : step * tokens]

        def gather_forward(k):
            staged = []
            for step in range(1, chips):
                slot = slots[k](lax.rem(chip + chips - step, chips) * 2 + core)
                gather_copy(k, step - 1, slot, slot, sibling).wait_recv()
                staged.append((slot, load(r.stage_sem.at[step - 1], slot, stage(k, step))))
            for step, (slot, copy) in enumerate(staged, 1):
                copy.wait()
                source = stage(k, step)
                send(("forward", k), gather_copy(k, chips - 1 + step, source, slot, sibling))

        def gather_finish(k):
            for step in range(chips):
                slot = slots[k](lax.rem(chip + chips - step, chips) * 2 + 1 - core)
                gather_copy(k, chips - 1 + step, slot, slot, sibling).wait_recv()

        def turned(value_ref, out_ref):
            def body(at):
                tile = value_ref[:, pl.ds(at, share)].T
                group = lax.div(at, share)
                for block in range(blocks):
                    first = pl.multiple_of(block * own + group * rows_out, rows_out)
                    out_ref[pl.ds(first, rows_out), :] = tile[block * rows_out : (block + 1) * rows_out]

            tiles(share, width, body)

        def turned_by_core(value_ref, out_ref):
            def body(at):
                group = lax.div(at, share)
                out_ref[span(lax.rem(group, 2) * chips + lax.div(group, 2), share), :] = value_ref[
                    :, pl.ds(at, share)
                ].T

            tiles(share, width, body)

        load_tok.wait()

        def norm1(at):
            rows = pl.ds(at, 32)
            x = r.tok[rows, :].astype(F32)
            xhat, inverse = norm_parts(x)
            r.mean1[rows, :] = jnp.broadcast_to(jnp.mean(x, axis=-1, keepdims=True), (32, 128))
            r.inv1[rows, :] = jnp.broadcast_to(inverse, (32, 128))
            r.n1_all[pl.ds(pl.multiple_of(z * tokens + at, 32), 32), :] = (xhat * r.gain1[...]).astype(BF16)

        tiles(32, tokens, norm1)
        for block, copy in win_loads:
            copy.wait()
            cols = slice(block * width, (block + 1) * width)
            proj = mm(r.n1_all[span(z, tokens), :], r.win[block], out=BF16)
            r.ext[16:, cols] = proj
            r.halo_out[:, cols] = proj[tokens - 16 :]
        pl.semaphore_wait(barrier, peers + zpeers)
        halo = remote(r.halo_out, r.halo_in, r.halo_s.at[0], r.halo_r.at[0], seq=block_at(1))
        send("halo", halo)
        own_loads = [
            load(
                r.load_sem.at[7 + part],
                r.w_in.at[:, pl.ds(pl.multiple_of(part * width + z * own, own), own)],
                r.win.at[2, :, part * own : (part + 1) * own],
            )
            for part in range(3)
        ]
        for padded in (r.chan, r.conv_out, r.gconv_c, r.glong_c):
            padded[length:, :] = jnp.zeros((spare, own), BF16)
        r.ext_c[0:spare, :] = jnp.zeros((spare, 3 * own), BF16)
        r.ext_c[length + spare :, :] = jnp.zeros((spare, 3 * own), BF16)

        def up_weights(at, slot):
            group = lax.rem(b + 1 + at, groups)
            return pltpu.make_async_copy(
                r.w_up.at[:, span(group, ffc)], r.win.at[0, :, span(slot, ffc)], r.ffn_sem.at[slot, 0]
            )

        def down_weights(at, slot):
            group = lax.rem(b + 1 + at, groups)
            return pltpu.make_async_copy(
                r.w_down.at[span(group, ffc)], r.win.at[1, span(slot, ffc)], r.ffn_sem.at[slot, 1]
            )

        for at in range(2):
            down_weights(at, at).start()
            up_weights(at, at).start()

        halo.wait_recv()
        r.ext[0:16, :] = (r.halo_in[...].astype(F32) * jnp.where(z > 0, 1.0, 0.0)).astype(BF16)

        def lags_at(cols):
            wide = r.ext[:, cols].astype(F32)
            return [wide[16 - lag : 16 - lag + tokens] for lag in range(3)]

        def mix(cols):
            lags = lags_at(cols)
            short = r.short[:, cols].astype(F32)
            return lags, short[0:1] * lags[0] + short[1:2] * lags[1] + short[2:3] * lags[2]

        def chan_copy(k, src, dst, step, to):
            return remote(src, dst, r.za_s.at[k, step - 1], r.za_r.at[k, step - 1], seq=to)

        def to_channels(k, value_ref, make_cols):
            for step in list(range(1, blocks)) + [0]:
                block = block_at(step)
                make_cols(block)
                if step:
                    src, dst = value_ref.at[:, span(block, own)], r.chan.at[span(z, tokens)]
                    send(("za", k), chan_copy(k, src, dst, step, block))
                else:
                    r.chan[span(z, tokens), :] = value_ref[:, span(block, own)]

        def wait_channels(k):
            for step in range(1, blocks):
                source = block_at(blocks - step)
                dst = r.chan.at[span(source, tokens)]
                chan_copy(k, dst, dst, step, source).wait_recv()

        def signal_block(block):
            def body(at):
                base = block * own + at
                cols = pl.ds(pl.multiple_of(base, 128), 128)
                gate_in = mix(pl.ds(pl.multiple_of(width + base, 128), 128))[1]
                values = mix(pl.ds(pl.multiple_of(2 * width + base, 128), 128))[1]
                r.sig[:, cols] = (values * gate_in).astype(BF16)

            tiles(128, own, body)

        to_channels(0, r.sig, signal_block)

        load_w3.wait()
        load_fade.wait()

        def fading(at):
            lag = (lax.broadcasted_iota(jnp.int32, (tokens, own), 0) + at).astype(F32)
            return jnp.exp(-r.fade[...] * lag)

        def taps_rows(at):
            rows = pl.ds(at, tokens)
            h1, r.s1[:, rows] = sin_cos(mm_tn(r.filt_w1[...], r.features_t[:, rows], precision=HIGHEST))
            h2, r.s2[:, rows] = sin_cos(mm_tn(r.filt_w2[...], h1, precision=HIGHEST))
            r.h1[:, rows] = h1
            r.h2[:, rows] = h2
            taps = mm_tn(h2, r.w3[...], precision=HIGHEST) * fading(at)
            r.qre[rows, :] = taps.astype(BF16)

        tiles(tokens, length, taps_rows)
        load_cs.wait()
        load_sn.wait()
        scale = 1.0 / length

        def taps_spec(at):
            rows = pl.ds(at, tokens)
            real = mm(r.cs[rows, :], r.qre[...]) * scale
            imag = mm(r.sn[rows, :], r.qre[...]) * -scale
            turn_re, turn_im = r.phase[rows, 0:1], r.phase[rows, 1:2]
            r.hre[rows, :] = real * turn_re - imag * turn_im
            r.him[rows, :] = real * turn_im + imag * turn_re

        tiles(tokens, length, taps_spec)

        wait_channels(0)

        def conv_spec(at):
            rows = pl.ds(at, tokens)
            real = mm(r.cs[rows, :], r.chan[0:length, :])
            imag = -mm(r.sn[rows, :], r.chan[0:length, :])
            r.xre[rows, :] = real
            r.xim[rows, :] = imag
            hre, him = r.hre[rows, :], r.him[rows, :]
            r.yre[rows, :] = (hre * real - him * imag).astype(BF16)
            r.yim[rows, :] = (-(hre * imag + him * real)).astype(BF16)

        tiles(tokens, length, conv_spec)

        def to_tokens(k, out_ref):
            for step in list(range(1, blocks)) + [0]:
                block = block_at(step)
                rows = span(block, tokens)
                tile = (mm(r.cs[rows, :], r.yre[...]) + mm(r.sn[rows, :], r.yim[...])).astype(BF16)
                out_ref[rows, :] = tile
                if step:
                    src, dst = out_ref.at[rows], r.conv_in.at[z]
                    send(("za", k), chan_copy(k, src, dst, step, block))
                else:
                    r.conv_in[z] = tile

        def wait_tokens(k):
            for step in range(1, blocks):
                source = block_at(blocks - step)
                dst = r.conv_in.at[source]
                chan_copy(k, dst, dst, step, source).wait_recv()

        to_tokens(1, r.conv_out)
        load_cot.wait()
        gather_start(0, r.cotv)
        load_wout.wait()
        def gate_cols(at):
            cols = pl.ds(at, 128)
            r.gate_out[:, cols] = mix(cols)[1]

        tiles(128, width, gate_cols)

        def grad_hidden(at, carry):
            slot = lax.rem(at, 2)
            down_weights(at, slot).wait()
            r.pre_send[at] = mm_nt(r.cotv[...], r.win[1, span(slot, ffc), :], out=BF16)
            down_weights(lax.rem(at + 2, groups), slot).start()
            return carry

        lax.fori_loop(0, groups, grad_hidden, 0)
        wait_tokens(1)

        def seq_gather(step, source, to):
            rows = r.n1_all.at[span(source, tokens)]
            return remote(rows, rows, r.zg_s.at[step - 1], r.zg_r.at[step - 1], seq=to)

        for step in range(1, blocks):
            send("n1", seq_gather(step, z, block_at(step)))

        def conv_cols(at):
            return r.conv_in[
                lax.div(at, own), :, pl.ds(pl.multiple_of(lax.rem(at, own), 128), 128)
            ].astype(F32)

        def long_cols(at):
            cols = pl.ds(at, 128)
            long = conv_cols(at) + r.bias[:, cols] * r.sig[:, cols].astype(F32)
            r.long[:, cols] = long
            r.half[:, cols] = (long * r.gate_out[:, cols]).astype(BF16)

        tiles(128, width, long_cols)
        r.res[...] = mm(r.half[...], r.wout[...])
        turned_by_core(r.half, r.gated_turn)
        mine = span(core, tokens)
        pair_rows = chips * share

        def pair_copy(k, src, dst):
            return remote(src, dst, r.cx_s.at[k], r.cx_r.at[k], batch=sibling)

        gated_copy = pair_copy(
            0, r.gated_turn.at[span(1 - core, pair_rows)], r.gated_pair.at[:, mine]
        )
        send("pair", gated_copy)
        r.gated_pair[:, mine] = r.gated_turn[span(core, pair_rows), :]

        def norm2(at):
            rows = pl.ds(at, 32)
            residual = r.res[rows, :] + r.tok[rows, :].astype(F32)
            r.res[rows, :] = residual
            xhat, inverse = norm_parts(residual)
            r.xhat2[rows, :] = xhat
            r.inv2[rows, :] = jnp.broadcast_to(inverse, (32, 128))
            r.half[rows, :] = (xhat * r.gain2[...]).astype(BF16)

        tiles(32, tokens, norm2)
        turned(r.half, r.turn)
        r.gn2[...] = jnp.zeros((tokens, width), F32)

        def plane_copy(k, src, dst, at, to):
            return remote(src, dst, r.pa_s.at[k, at], r.pa_r.at[k, at], batch=to)

        def hidden_copy(at, to):
            return plane_copy(0, r.hid_send.at[at], r.hid_own.at[:, span(b, tokens)], at, to)

        def pre_copy(at, to):
            return plane_copy(1, r.pre_send.at[at], r.pre_own.at[span(b, tokens)], at, to)

        def chunk(at, carry):
            slot = lax.rem(at, 2)
            where = span(slot, ffc)
            up_weights(at, slot).wait()
            r.gres[:, 0:ffc] = mm(r.half[...], r.win[0, :, where])

            def act(row):
                rows = pl.ds(row, 32)
                pre = r.gres[rows, 0:ffc]
                square = pre * pre
                bent = jnp.tanh(pre * (GELU_SCALE + GELU_SCALE * GELU_CUBIC * square))
                upper = 0.5 + 0.5 * bent
                slope = upper + pre * (0.5 - 0.5 * bent * bent) * (
                    GELU_SCALE + 3.0 * GELU_SCALE * GELU_CUBIC * square
                )
                r.hid_buf[rows, :] = (pre * upper).astype(BF16)
                r.pre_send[at, rows, :] = (r.pre_send[at, rows, :].astype(F32) * slope).astype(BF16)

            tiles(32, tokens, act)
            r.hid_send[at] = r.hid_buf[...].T

            @pl.when(at < groups - 1)
            def _():
                hidden_copy(at, lax.rem(b + 1 + at, groups)).start()

            down_weights(at, slot).wait()
            r.res[...] += mm(r.hid_buf[...], r.win[1, where, :])
            r.gn2[...] += mm_nt(r.pre_send[at], r.win[0, :, where])

            @pl.when(at < groups - 2)
            def _():
                up_weights(at + 2, slot).start()
                down_weights(at + 2, slot).start()

            return carry

        lax.fori_loop(0, groups, chunk, 0)
        for at in range(peers):
            sent.setdefault("ffn", []).append(hidden_copy(at, group_at(1 + at)))

        def pool_cot():
            return [load(r.win_sem.at[half], r.cot_land.at[half], r.win.at[half]) for half in range(2)]

        def pool_turned(land):
            return [
                load(
                    r.pool_sem.at[at],
                    land.at[at],
                    r.win.at[at // chips, :, pl.ds(at % chips * tokens, tokens)],
                )
                for at in range(groups)
            ]

        gather_forward(0)
        r.hid_own[:, span(b, tokens)] = r.hid_send[groups - 1]
        r.pre_own[span(b, tokens), :] = r.pre_send[groups - 1]

        def norm2_back(at, total):
            rows = pl.ds(pl.multiple_of(at * 32, 32), 32)
            r.half[rows, :] = r.res[rows, :].astype(BF16)
            grad, xhat = r.gn2[rows, :], r.xhat2[rows, :]
            back = r.cotv[rows, :].astype(F32) + norm_back(grad, r.gain2[...], xhat, r.inv2[rows, 0:1])
            r.gres[rows, :] = back
            r.gbr_pair[pl.ds(pl.multiple_of(core * tokens + at * 32, 32), 32), :] = back.astype(BF16)
            return total + jnp.sum((grad * xhat).reshape(4, 8, width), axis=0)

        total = lax.fori_loop(0, tokens // 32, norm2_back, jnp.zeros((8, width), F32))
        r.sum_gain2[...] = jnp.sum(total, axis=0, keepdims=True)
        store_layer = load(r.local_sem.at[8], r.half, r.layer_out)
        branch_copy = pair_copy(1, r.gbr_pair.at[mine], r.gbr_pair.at[mine])
        send("pair", branch_copy)

        def gated_back(block):
            cols = span(block, own)
            grad = mm_nt(r.gbr_pair[mine, :], r.wout[span(block, own), :])
            glong = (grad * r.gate_out[:, cols]).astype(BF16)
            r.glong[:, cols] = glong
            r.ggb[:, cols] = grad.astype(BF16)
            r.long[:, cols] = grad * r.long[:, cols]
            r.sum_bias[:, cols] = jnp.sum(
                glong.astype(F32) * r.sig[:, cols].astype(F32), axis=0, keepdims=True
            )

        to_channels(2, r.ggb, gated_back)

        gather_start(1, r.turn)

        branch_copy.wait_recv()
        gated_copy.wait_recv()

        def out_copy(step, to):
            sems = r.wo_s.at[0, step - 1], r.wo_r.at[0, step - 1]
            return remote(r.out_send.at[step - 1], r.out_land.at[step - 1], *sems, batch=to * 2 + core)

        for step in range(chips):
            part = mm(r.gated_pair[span(lax.rem(chip + step, chips), share), :], r.gbr_pair[...])
            if step:
                r.out_send[step - 1] = part.astype(BF16)
            else:
                r.xhat2[share : 2 * share, :] = part

        near = z + 1 - 2 * lax.rem(z, 2)
        far = block_at(2)

        def reduce_first(k, refs):
            return remote(refs[0], refs[1], r.rs_s.at[k, 0], r.rs_r.at[k, 0], seq=near)

        def reduce_second(k, refs):
            return remote(refs[2], refs[3], r.rs_s.at[k, 1], r.rs_r.at[k, 1], seq=far)

        def reduce_send(k, refs, part_of):
            send_ref, _, next_ref, _, own_ref = refs
            send_ref[0] = part_of(near).astype(BF16)
            send_ref[1] = part_of(lax.rem(near + 2, blocks)).astype(BF16)
            send("rs", reduce_first(k, refs))
            next_ref[...] = part_of(far).astype(BF16)
            own_ref[...] = part_of(z)

        def reduce_next(k, refs):
            _, land_ref, next_ref, _, own_ref = refs
            reduce_first(k, refs).wait_recv()
            next_ref[...] = (next_ref[...].astype(F32) + land_ref[1].astype(F32)).astype(BF16)
            send("rs", reduce_second(k, refs))
            own_ref[...] += land_ref[0].astype(F32)

        def reduce_finish(k, refs):
            reduce_second(k, refs).wait_recv()
            refs[4][...] += refs[3][...].astype(F32)

        down_refs = (r.down_send, r.down_land, r.down_next, r.down_last, r.xhat2.at[0:down_rows])
        up_refs = (r.up_send, r.up_land, r.up_next, r.up_last, r.gate_out.at[:, 0:ffc])

        def wait_plane(k, dst_of):
            for at in range(peers):
                source = group_at(groups - 1 - at)
                dst = dst_of(source)
                plane_copy(k, dst, dst, at, source).wait_recv()

        deep = groups // 2 * tokens

        def down_part(block):
            rows = span(block, ffc // blocks)
            return mm(r.hid_own[rows, :deep], r.win[0]) + mm(r.hid_own[rows, deep:], r.win[1])

        def turned_part(right_ref):
            def part(block):
                rows = span(block, own)
                return mm(r.win[0, rows, :], right_ref[:deep]) + mm(r.win[1, rows, :], right_ref[deep:])

            return part


        gather_local(0, r.cotv).wait()
        gather_finish(0)
        pool = pool_cot()

        for step in range(1, blocks):
            source = block_at(blocks - step)
            seq_gather(step, source, source).wait_recv()
        for copy in own_loads:
            copy.wait()

        def proj_rows(at):
            r.ext_c[pl.ds(pl.multiple_of(at + spare, spare), tokens), :] = mm(
                r.n1_all[pl.ds(at, tokens), :], r.win[2, :, 0 : 3 * own], out=BF16
            )

        tiles(tokens, length, proj_rows)

        def own_cols(part, at):
            return pl.ds(pl.multiple_of(part * width + z * own + at, 128), 128)

        def mix_own(part, at, first, rows):
            wide = r.ext_c[pl.ds(first, rows + spare), part * own + at : part * own + at + 128].astype(F32)
            short = r.short[:, own_cols(part, at)].astype(F32)
            lags = [wide[spare - lag : spare - lag + rows] for lag in range(3)]
            return short[0:1] * lags[0] + short[1:2] * lags[1] + short[2:3] * lags[2]

        wait_channels(2)

        def long_rows(first):
            rows = pl.ds(first, tokens)
            for at in range(0, own, 128):
                cols = slice(at, at + 128)
                gate = mix_own(0, at, first, tokens)
                r.glong_c[rows, cols] = (r.chan[rows, cols].astype(F32) * gate).astype(BF16)

        tiles(tokens, length, long_rows)

        def grad_spec(at):
            rows = pl.ds(at, tokens)
            real = mm(r.cs[rows, :], r.glong_c[0:length, :])
            imag = -mm(r.sn[rows, :], r.glong_c[0:length, :])
            hre, him = r.hre[rows, :], r.him[rows, :]
            r.yre[rows, :] = (hre * real + him * imag).astype(BF16)
            r.yim[rows, :] = (him * real - hre * imag).astype(BF16)
            xre, xim = r.xre[rows, :], r.xim[rows, :]
            both_re = xre * real + xim * imag
            both_im = xre * imag - xim * real
            turn_re, turn_im = r.phase[rows, 0:1], r.phase[rows, 1:2]
            r.qre[rows, :] = ((both_re * turn_re + both_im * turn_im) * scale).astype(BF16)
            r.qim[rows, :] = ((both_re * turn_im - both_im * turn_re) * scale).astype(BF16)

        tiles(tokens, length, grad_spec)
        to_tokens(3, r.gconv_c)
        for at in range(peers):
            send("ffn", pre_copy(at, group_at(1 + at)))

        def proj_back(first):
            rows = pl.ds(first, tokens + spare)
            for at in range(0, own, 128):
                cols = slice(at, at + 128)
                gate_in = mix_own(1, at, first, tokens + spare)
                values = mix_own(2, at, first, tokens + spare)
                bias = r.bias[:, own_cols(0, at)]
                signal = (values * gate_in).astype(BF16).astype(F32)
                long = r.conv_out[rows, cols].astype(F32) + bias * signal
                grad_signal = r.gconv_c[rows, cols].astype(F32) + bias * r.glong_c[rows, cols].astype(F32)
                parts = (r.chan[rows, cols].astype(F32) * long, grad_signal * values, grad_signal * gate_in)
                for part, grad in enumerate(parts):
                    short = r.short[:, own_cols(part, at)].astype(F32)
                    total = (
                        short[0:1] * grad[0:tokens]
                        + short[1:2] * grad[1 : tokens + 1]
                        + short[2:3] * grad[2 : tokens + 2]
                    )
                    r.gproj_c[pl.ds(first, tokens), part * own + at : part * own + at + 128] = total.astype(BF16)

        tiles(tokens, length, proj_back)

        def in_part(group):
            return mm_tn(r.n1_all[:, span(group, share)], r.gproj_c[...])

        for at in range(chips):
            r.in_send[at] = in_part(at * 2 + 1 - core).astype(BF16)
        in_pair = pair_copy(2, r.in_send, r.in_pair)
        send("in_pair", in_pair)
        for copy in pool:
            copy.wait()
        wait_plane(0, lambda at: r.hid_own.at[:, span(at, tokens)])
        reduce_send(0, down_refs, down_part)
        in_pair.wait_recv()
        drain("in_pair")

        def in_copy(step, to):
            sems = r.wi_s.at[step - 1], r.wi_r.at[step - 1]
            return remote(r.in_send.at[step - 1], r.in_land.at[step - 1], *sems, batch=to * 2 + core)

        for step in list(range(1, chips)) + [0]:
            to = lax.rem(chip + step, chips)
            part = in_part(to * 2 + core) + r.in_pair[to].astype(F32)
            if step:
                r.in_send[step - 1] = part.astype(BF16)
                send("in", in_copy(step, to))
            else:
                r.in_own[...] = part

        r.w12[...] = jnp.zeros((net_rows, 128), F32)
        r.sum_w3[...] = jnp.zeros((filt, own), F32)
        for at in range(0, length, tokens):
            rows = slice(at, at + tokens)
            grad_taps = mm(r.cs[rows, :], r.qre[...]) + mm(r.sn[rows, :], r.qim[...])
            grad_filt = grad_taps * fading(at)
            r.sum_w3[...] += mm(r.h2[:, rows], grad_filt, precision=HIGHEST)
            grad_angle2 = mm_nt(r.w3[...], grad_filt, precision=HIGHEST) * r.s2[:, rows]
            r.w12[net_at:, :filt] += mm_nt(r.h1[:, rows], grad_angle2, precision=HIGHEST)
            grad_angle1 = mm(r.filt_w2[...], grad_angle2, precision=HIGHEST) * r.s1[:, rows]
            r.w12[:emb, :filt] += mm_nt(r.features_t[:, rows], grad_angle1, precision=HIGHEST)

        def small_copy(k, src, dst, at, to):
            return remote(src, dst, r.sm_s.at[k, at], r.sm_r.at[k, at], batch=to)

        def small_z_copy(k, src, dst, step, to):
            return remote(src, dst, r.sz_s.at[k, step - 1], r.sz_r.at[k, step - 1], seq=to)

        def small_z_send(k, src, dst_of):
            for step in range(1, blocks):
                send("small", small_z_copy(k, src, dst_of(step), step, block_at(step)))

        def small_z_wait(k, dst_of):
            for step in range(1, blocks):
                dst = dst_of(step)
                small_z_copy(k, dst, dst, step, block_at(blocks - step)).wait_recv()

        def small_send(k, src_of, dst_of):
            for at in range(peers):
                to = group_at(1 + at)
                send("small", small_copy(k, src_of(to), dst_of(at), at, to))

        def small_wait(k, dst_of):
            for at in range(peers):
                dst = dst_of(at)
                small_copy(k, dst, dst, at, group_at(groups - 1 - at)).wait_recv()

        w3_rows = filt // groups
        small_z_send(0, r.w12, lambda step: r.w12_z.at[step - 1])
        small_send(0, lambda to: r.sum_w3.at[span(to, w3_rows)], lambda at: r.w3_land.at[at])

        def outz_copy(step, to):
            sems = r.wo_s.at[1, step - 1], r.wo_r.at[1, step - 1]
            return remote(r.outz_send.at[span(to, rows_out)], r.outz_land.at[step - 1], *sems, seq=to)


        def short_sums(cols, grad, lags):
            for lag in range(3):
                r.sum_short[lag : lag + 1, cols] = jnp.sum(grad * lags[lag], axis=0, keepdims=True)

        def back_cols(cols, grad, lags):
            short_sums(cols, grad, lags)
            r.ghalo[:, cols] = grad[0:8]
            short = r.short[:, cols].astype(F32)
            longer = jnp.concatenate([grad, jnp.zeros((8, 128), F32)], axis=0)
            total = (
                short[0:1] * grad
                + short[1:2] * longer[1 : tokens + 1]
                + short[2:3] * longer[2 : tokens + 2]
            )
            r.gproj[:, cols] = total.astype(BF16)
            r.tail[:, cols] = total[tokens - 16 :]

        def mixed_cols(at):
            cols = pl.ds(at, 128)
            grad_signal = conv_cols(at) + r.bias[:, cols] * r.glong[:, cols].astype(F32)
            gate_cols = pl.ds(pl.multiple_of(width + at, 128), 128)
            value_cols = pl.ds(pl.multiple_of(2 * width + at, 128), 128)
            gate_lags, gate_in = mix(gate_cols)
            value_lags, values = mix(value_cols)
            back_cols(gate_cols, grad_signal * values, gate_lags)
            back_cols(value_cols, grad_signal * gate_in, value_lags)

        def gate_back(at):
            cols = pl.ds(at, 128)
            back_cols(cols, r.long[:, cols], lags_at(cols))

        drain(("forward", 0))
        tiles(128, width, gate_back)
        wait_tokens(3)
        tiles(128, width, mixed_cols)
        halo = remote(r.ghalo, r.ghalo_in, r.halo_s.at[1], r.halo_r.at[1], seq=block_at(blocks - 1))
        send("halo", halo)
        gather_forward(1)
        halo.wait_recv()
        later = r.ghalo_in[...] * jnp.where(z < blocks - 1, 1.0, 0.0)

        def tail_cols(at):
            cols = slice(at, at + width)
            short = r.short[:, cols].astype(F32)
            row = lax.broadcasted_iota(jnp.int32, (16, width), 0)
            last = short[1:2] * later[0:1, cols] + short[2:3] * later[1:2, cols]
            total = r.tail[:, cols] + jnp.where(row == 15, last, 0.0)
            total = total + jnp.where(row == 14, short[2:3] * later[0:1, cols], 0.0)
            r.gproj[tokens - 16 :, cols] = total.astype(BF16)

        for part in range(3):
            tail_cols(part * width)

        def spread(k, own_ref, out_ref, size):
            for at in range(peers):
                to = group_at(1 + at)
                src, dst = own_ref.at[span(to, rows_out)], out_ref.at[:, span(b, size)]
                send("spread", remote(src, dst, r.tr_s.at[k, at], r.tr_r.at[k, at], batch=to))
            return load(r.local_sem.at[14 + k], own_ref.at[span(b, rows_out)], out_ref.at[:, span(b, size)])

        def spread_finish(k, copy, out_ref, size):
            for at in range(peers):
                source = group_at(groups - 1 - at)
                dst = out_ref.at[:, span(source, size)]
                remote(dst, dst, r.tr_s.at[k, at], r.tr_r.at[k, at], batch=source).wait_recv()
            copy.wait()

        for step in range(1, chips):
            send("out", out_copy(step, lax.rem(chip + step, chips)))
        small_z_wait(0, lambda step: r.w12_z.at[step - 1])
        net = r.w12[...]
        for step in range(zpeers):
            net = net + r.w12_z[step]
        r.w12_sum[...] = net
        small_send(1, lambda to: r.w12_sum, lambda at: r.w12_plane.at[at])
        small_wait(0, lambda at: r.w3_land.at[at])
        part = r.sum_w3[span(b, w3_rows), :]
        for at in range(peers):
            part = part + r.w3_land[at]
        r.w3_part[...] = part
        r.w3_all[z, span(b, w3_rows), :] = part
        small_send(2, lambda to: r.w3_part, lambda at: r.w3_all.at[z, span(b, w3_rows)])
        reduce_next(0, down_refs)
        gather_local(1, r.turn).wait()
        gather_finish(1)
        drain(("forward", 1))
        pool = pool_turned(r.n2_land)
        small_wait(1, lambda at: r.w12_plane.at[at])
        net = r.w12_sum[...]
        for at in range(peers):
            net = net + r.w12_plane[at]
        r.grad_w1[...] = net[:emb, :filt]
        r.grad_w2[...] = net[net_at:, :filt]
        for at in range(peers):
            dst = r.w3_all.at[z, span(group_at(groups - 1 - at), w3_rows)]
            small_copy(2, dst, dst, at, group_at(groups - 1 - at)).wait_recv()
        small_z_send(1, r.w3_all.at[z], lambda step: r.w3_all.at[z])
        for copy in pool:
            copy.wait()
        wait_plane(1, lambda at: r.pre_own.at[span(at, tokens)])
        reduce_send(1, up_refs, turned_part(r.pre_own))
        win_loads = [(block, load_win(block)) for block in range(3)]
        for step in range(1, chips):
            in_copy(step, lax.rem(chip + step, chips)).wait_recv()
        total = r.in_own[...]
        for step in range(chips - 1):
            total = total + r.in_land[step].astype(F32)
        r.in_own[...] = total

        def in_spread(step, part, block, to):
            src = r.in_own.at[span(to, rows_out), part * own : (part + 1) * own]
            dst = r.grad_w_in.at[:, pl.ds(pl.multiple_of(part * width + block * own, own), own)]
            if step == 0:
                return pltpu.make_async_copy(src, dst, r.load_sem.at[10 + part])
            return remote(src, dst, r.ti_s.at[step - 1, part], r.ti_r.at[step - 1, part], seq=to)

        for part in range(3):
            for step in range(1, blocks):
                send("in_spread", in_spread(step, part, z, block_at(step)))
            in_spread(0, part, z, z).start()
        for _, copy in win_loads:
            copy.wait()
        r.gn2[...] = mm_nt(r.gproj[:, :width], r.win[0])
        r.gn2[...] += mm_nt(r.gproj[:, width : 2 * width], r.win[1])
        r.gn2[...] += mm_nt(r.gproj[:, 2 * width :], r.win[2])

        reduce_next(1, up_refs)
        def norm1_back(at, total):
            rows = pl.ds(pl.multiple_of(at * 32, 32), 32)
            grad, inverse = r.gn2[rows, :], r.inv1[rows, 0:1]
            xhat = (r.tok[rows, :].astype(F32) - r.mean1[rows, 0:1]) * inverse
            r.res[rows, :] = r.gres[rows, :] + norm_back(grad, r.gain1[...], xhat, inverse)
            return total + jnp.sum((grad * xhat).reshape(4, 8, width), axis=0)

        total = lax.fori_loop(0, tokens // 32, norm1_back, jnp.zeros((8, width), F32))
        r.sum_gain1[...] = jnp.sum(total, axis=0, keepdims=True)
        r.small_send[...] = jnp.zeros((groups, 16, share), F32)
        for group in range(groups):
            cols = slice(group * share, (group + 1) * share)
            r.small_send[group, 0:1, :] = r.sum_gain1[:, cols]
            r.small_send[group, 1:2, :] = r.sum_gain2[:, cols]
            r.small_send[group, 2:3, :] = r.sum_bias[:, cols]
            for lag in range(3):
                for third in range(3):
                    at = group * inc + third * share
                    row = 3 + 3 * lag + third
                    r.small_send[group, row : row + 1, :] = r.sum_short[lag : lag + 1, at : at + share]
        small_send(3, lambda to: r.small_send.at[to], lambda at: r.small_land.at[b])
        r.small_land[b] = r.small_send[b]
        store_tokens = load(r.local_sem.at[13], r.res, r.tokens_grad)
        reduce_finish(0, down_refs)
        store_down = load(r.local_sem.at[9], down_refs[4], r.grad_w_down)
        for step in range(1, chips):
            out_copy(step, lax.rem(chip + step, chips)).wait_recv()
        total = r.xhat2[share : 2 * share, :]
        for step in range(chips - 1):
            total = total + r.out_land[step].astype(F32)
        r.xhat2[share : 2 * share, :] = total
        r.outz_send[...] = total.astype(BF16)
        for step in range(1, blocks):
            send("outz", outz_copy(step, block_at(step)))
        r.outz_own[...] = r.xhat2[pl.ds(pl.multiple_of(share + z * rows_out, rows_out), rows_out), :]

        for at in range(peers):
            source = group_at(groups - 1 - at)
            dst = r.small_land.at[source]
            small_copy(3, dst, dst, at, source).wait_recv()
        small = r.small_land[0]
        for group in range(1, groups):
            small = small + r.small_land[group]
        r.small_sum[...] = small
        small_z_send(2, r.small_sum, lambda step: r.small_z.at[step - 1])
        reduce_finish(1, up_refs)
        spread_up = spread(0, up_refs[4], r.grad_w_up, ffc)
        for step in range(1, blocks):
            outz_copy(step, block_at(blocks - step)).wait_recv()
        total = r.outz_own[...]
        for step in range(zpeers):
            total = total + r.outz_land[step].astype(F32)
        r.outz_own[...] = total
        store_out = load(r.local_sem.at[11], r.outz_own, r.grad_w_out)
        def chosen(value, size):
            picked = value[:, :size]
            for block in range(1, blocks):
                picked = jnp.where(z == block, value[:, block * size : (block + 1) * size], picked)
            return picked

        for step in range(1, blocks):
            source = block_at(blocks - step)
            dst = r.w3_all.at[source]
            small_z_copy(1, dst, dst, step, source).wait_recv()
        third = r.w3_all[lax.div(b * share, own)]
        halves = own // share
        picked = third[:, :share]
        for half in range(1, halves):
            here = lax.rem(b, halves) == half
            picked = jnp.where(here, third[:, half * share : (half + 1) * share], picked)
        r.grad_w3[...] = chosen(picked, rows_out)
        small_z_wait(2, lambda step: r.small_z.at[step - 1])
        small = r.small_sum[...]
        for step in range(zpeers):
            small = small + r.small_z[step]
        r.grad_gain1[...] = chosen(small[0:1], rows_out)
        r.grad_gain2[...] = chosen(small[1:2], rows_out)
        r.grad_bias[...] = chosen(small[2:3], rows_out)
        for lag in range(3):
            for third in range(3):
                row = 3 + 3 * lag + third
                r.short_all[lag : lag + 1, third * share : (third + 1) * share] = small[row : row + 1]
        r.grad_short[...] = chosen(r.short_all[0:3, :], 3 * rows_out)
        spread_finish(0, spread_up, r.grad_w_up, ffc)
        for part in range(3):
            for step in range(1, blocks):
                source = block_at(blocks - step)
                in_spread(step, part, source, source).wait_recv()
            in_spread(0, part, z, z).wait()
        store_layer.wait()
        store_down.wait()
        store_out.wait()
        store_tokens.wait()
        for key in list(sent):
            drain(key)

    def call(args):
        result = pl.pallas_call(
            kernel,
            out_shape=[jax.ShapeDtypeStruct(shape, dtype) for shape, dtype, _ in outputs.values()],
            in_specs=[pl.BlockSpec(memory_space=space) for space in inputs.values()],
            out_specs=[pl.BlockSpec(memory_space=space) for *_, space in outputs.values()],
            scratch_shapes=list(scratch.values()),
            compiler_params=pltpu.CompilerParams(
                collective_id=0, has_side_effects=True, vmem_limit_bytes=KERNEL_VMEM
            ),
        )(*[args[name] for name in inputs])
        return settled(result[:13])

    return call


def settled(values):
    count = len(values)
    large = [at for at, value in enumerate(values) if value.size >= 1 << 15]

    def copy_all(*refs):
        sources, targets, held = refs[:count], refs[count : 2 * count], refs[2 * count : -1]
        sems = refs[-1]
        copies = [
            pltpu.make_async_copy(sources[at], held[k], sems.at[0, k]) for k, at in enumerate(large)
        ]
        for copy in copies:
            copy.start()
        for at in range(count):
            if at not in large:
                if at == count - 1:
                    targets[at][...] = sources[at][...].T
                else:
                    targets[at][...] = sources[at][...].reshape(targets[at].shape)
        stores = []
        for k, at in enumerate(large):
            copies[k].wait()
            stores.append(pltpu.make_async_copy(held[k], targets[at], sems.at[1, k]))
            stores[-1].start()
        for copy in stores:
            copy.wait()

    specs = [
        pl.BlockSpec(memory_space=pl.ANY if at in large else pltpu.VMEM) for at in range(count)
    ]
    return pl.pallas_call(
        copy_all,
        out_shape=[
            jax.ShapeDtypeStruct(value.shape[1:] if value.shape[0] == 1 else value.shape, value.dtype)
            for value in values[:-1]
        ]
        + [jax.ShapeDtypeStruct(values[-1].shape[::-1], values[-1].dtype)        ],
        in_specs=specs,
        out_specs=specs,
        scratch_shapes=[pltpu.VMEM(values[at].shape, values[at].dtype) for at in large]
        + [pltpu.SemaphoreType.DMA((2, len(large)))],
    )(*values)


def small_sums(gain1, bias, gain2, short, w1, w2, w3_own):
    blocks, position = lax.axis_size("seq"), lax.axis_index("seq")
    dests = lax.axis_size("batch") * blocks
    width, (filt_dim, own), emb = gain1.shape[0], w3_own.shape, w1.shape[0]
    w3_all = lax.dynamic_update_slice_in_dim(
        jnp.zeros((filt_dim, width), F32), w3_own, position * own, 1
    )
    share = width // dests
    small = jnp.concatenate(
        [
            gain1.reshape(dests, share),
            bias.reshape(dests, share),
            gain2.reshape(dests, share),
            short.reshape(3, dests, 3 * share).transpose(1, 0, 2).reshape(dests, 9 * share),
            w3_all.reshape(filt_dim, dests, share).transpose(1, 0, 2).reshape(dests, filt_dim * share),
        ],
        axis=1,
    )
    small = scatter_sum(small, wire=F32)[0]
    filters = all_sum(jnp.concatenate([w1, w2], axis=0))
    return (
        small[:share],
        small[3 * share : 12 * share].reshape(3, 3 * share),
        filters[:emb],
        filters[emb:],
        small[12 * share :].reshape(filt_dim, share),
        small[share : 2 * share],
        small[2 * share : 3 * share],
    )


def kernel_layer(
    tokens,
    norm_gain1,
    w_in,
    short_kernel,
    filt_w1,
    filt_w2,
    filt_w3,
    decay_rate,
    conv_bias,
    w_out,
    norm_gain2,
    w_up,
    w_down,
    cotangent,
):
    _, block_len, width = tokens.shape
    groups, blocks = lax.axis_size("batch"), lax.axis_size("seq")
    emb, filt = filt_w1.shape
    (cosine, sine), phase = symmetric_tables(block_len * blocks)
    features = lag_features(emb, block_len * blocks)
    call = kernel_plan(groups, blocks, block_len, width, w_up.shape[1], filt, emb)
    out = call(
        dict(
            tokens=tokens[0],
            cot=cotangent[0],
            w_in=w_in,
            w_out=w_out,
            w_up=w_up,
            w_down=w_down,
            cosine=jnp.asarray(cosine),
            sine=jnp.asarray(sine),
            filt_w3=filt_w3,
            decay=decay_rate[None],
            gain1=norm_gain1[None],
            gain2=norm_gain2[None],
            bias=conv_bias[None],
            short=short_kernel,
            filt_w1=filt_w1,
            filt_w2=filt_w2,
            features_t=jnp.asarray(features.T),
            phase=jnp.asarray(phase),
        )
    )
    layer_out, tokens_grad, w_in, w_out, w_up, w_down, gain1, gain2, bias, short, w1, w2, w3 = out
    return layer_out[None], tokens_grad[None], (gain1, short, w1, w2, w3.T, bias, gain2), (w_in, w_out, w_up, w_down)


def on_device(*args):
    tokens = args[0]
    fits = lax.axis_size("batch") == 8 and lax.axis_size("seq") == 4 and tokens.shape[1] * lax.axis_size("seq") <= 1024
    layer = kernel_layer if fits else plain_layer
    layer_out, tokens_grad, small, large = layer(*args)
    gain1, short, w1, w2, w3, bias, gain2 = small
    grad_w_in, grad_w_out, grad_w_up, grad_w_down = large
    return (
        layer_out, tokens_grad, gain1, grad_w_in, short, w1, w2, w3, bias, grad_w_out, gain2,
        grad_w_up, grad_w_down,
    )


def solution(mesh):
    split = P("batch", "seq", None)
    both = ("batch", "seq")
    return jax.shard_map(
        on_device,
        mesh=mesh,
        in_specs=(split,) + (P(),) * 12 + (split,),
        out_specs=(
            split,
            split,
            P(both),
            P(both, None),
            P(None, both),
            P(),
            P(),
            P(None, both),
            P(both),
            P(both, None),
            P(both),
            P(both, None),
            P(both, None),
        ),
        check_vma=False,
    )
```

```python
import math

import jax
import jax.numpy as jnp
import ml_dtypes
import numpy as np
from jax import lax
from jax.experimental import pallas as pl
from jax.experimental.pallas import tpu as pltpu
from jax.sharding import PartitionSpec as P

F32 = jnp.float32
BF16 = jnp.bfloat16
HIGHEST = lax.Precision.HIGHEST
GELU_SCALE = math.sqrt(2.0 / math.pi)
GELU_CUBIC = 0.044715


def dot(left, right, contract, out=F32, precision=None):
    return lax.dot_general(
        left, right, (contract, ((), ())), precision=precision, preferred_element_type=F32
    ).astype(out)


def mm(left, right, **kw):
    return dot(left, right, ((1,), (0,)), **kw)


def mm_nt(left, right, **kw):
    return dot(left, right, ((1,), (1,)), **kw)


def mm_tn(left, right, **kw):
    return dot(left, right, ((0,), (0,)), **kw)


def shifted(value, axis, steps):
    count = lax.axis_size(axis)
    first, last = (max(0, -steps), min(count, count - steps))
    return lax.ppermute(value, axis, [(source, source + steps) for source in range(first, last)])


def exchange(value, axis, bit):
    count = lax.axis_size(axis)
    return lax.ppermute(value, axis, [(at, at ^ (1 << bit)) for at in range(count)])


def bits_of(axis):
    return lax.axis_size(axis).bit_length() - 1


def stage_order(swap):
    batch_bits, seq_bits = bits_of("batch"), bits_of("seq")
    rest = list(range(1, batch_bits))
    half = len(rest) // 2
    if swap:
        rest = rest[half:] + rest[:half]
    return [("batch", bit) for bit in [0] + rest] + [("seq", bit) for bit in range(seq_bits)]


def scatter_sum(partial, swap=False, wire=BF16):
    batch_bits, seq_bits = bits_of("batch"), bits_of("seq")
    dims = [("batch", bit) for bit in reversed(range(batch_bits))]
    dims += [("seq", bit) for bit in reversed(range(seq_bits))]
    rows = partial.shape[0] >> len(dims)
    value = partial.reshape((2,) * len(dims) + (rows,) + partial.shape[1:]).astype(wire)
    for axis, bit in stage_order(swap):
        at = dims.index((axis, bit))
        mine = (lax.axis_index(axis) >> bit) & 1
        keep = lax.dynamic_index_in_dim(value, mine, at, keepdims=False)
        send = lax.dynamic_index_in_dim(value, 1 - mine, at, keepdims=False)
        got = exchange(send, axis, bit)
        value = keep.astype(F32) + got.astype(F32)
        dims.pop(at)
        if dims:
            value = value.astype(wire)
    return value


def gather_batch(value):
    return lax.all_gather(value, "batch", axis=0, tiled=True)


def columns_batch(value):
    return lax.all_to_all(value, "batch", 1, 0, tiled=True)


def rows_sum(left_own, right_all):
    blocks = lax.axis_size("seq")
    part = mm_tn(left_own, right_all, out=BF16)
    got = lax.all_to_all(part.reshape(blocks, -1, part.shape[1]), "seq", 0, 0, tiled=True)
    return jnp.sum(got.astype(F32), axis=0)


def columns_sum(left_all, right_own):
    blocks, groups = lax.axis_size("seq"), lax.axis_size("batch")
    part = mm_tn(left_all, right_own, out=BF16)
    part = part.reshape(groups * blocks, -1, part.shape[1])
    got = lax.all_to_all(part, ("batch", "seq"), 0, 0, tiled=True)
    got = jnp.sum(got.reshape(groups, blocks, -1, part.shape[2]).astype(F32), axis=1)
    return got.transpose(1, 0, 2).reshape(got.shape[1], -1)


def all_sum(value):
    for axis, bit in stage_order(False):
        value = value + exchange(value, axis, bit)
    return value


def norm_parts(values):
    centered = values - jnp.mean(values, axis=-1, keepdims=True)
    inverse = lax.rsqrt(jnp.mean(centered * centered, axis=-1, keepdims=True) + 1e-05)
    return centered * inverse, inverse


def norm_back(grad, gain, xhat, inverse):
    scaled = grad * gain
    return (
        scaled
        - jnp.mean(scaled, axis=-1, keepdims=True)
        - xhat * jnp.mean(scaled * xhat, axis=-1, keepdims=True)
    ) * inverse


def transform_table(length):
    count = np.arange(length, dtype=np.int64)
    turns = (2 * count[:, None] + 1) * count[None, :] % (4 * length)
    angles = turns.astype(np.float64) * (2.0 * np.pi / (4 * length))
    table = np.concatenate([np.cos(angles), -np.sin(angles)], axis=0)
    return table.astype(np.float32).astype(ml_dtypes.bfloat16)


def lag_features(emb, length):
    bands = (emb - 1) // 2
    lag = np.arange(length, dtype=np.float64)
    freq = 1e-4 + np.arange(bands, dtype=np.float64) * ((bands - 1 - 1e-4) / (bands - 1))
    phases = (lag * (2.0 * np.pi / length))[:, None] * freq[None, :]
    return np.concatenate(
        [(lag / (length - 1))[:, None], np.cos(phases), -np.sin(phases)], axis=1
    ).astype(np.float32)


def to_channels(value):
    return lax.all_to_all(value, "seq", 1, 0, tiled=True)


def to_tokens(value):
    return lax.all_to_all(value, "seq", 0, 1, tiled=True)


def plain_layer(
    tokens,
    norm_gain1,
    w_in,
    short_kernel,
    filt_w1,
    filt_w2,
    filt_w3,
    decay_rate,
    conv_bias,
    w_out,
    norm_gain2,
    w_up,
    w_down,
    cotangent,
):
    num_seqs, block_len, width = tokens.shape
    assert num_seqs == 1
    blocks = lax.axis_size("seq")
    position = lax.axis_index("seq")
    seq_len = block_len * blocks
    own = width // blocks
    table = jnp.asarray(transform_table(seq_len))
    features = jnp.asarray(lag_features(filt_w1.shape[0], seq_len))
    cot = cotangent[0]
    cot_all = gather_batch(cot)
    inputs = tokens[0].astype(F32)

    xhat1, inverse1 = norm_parts(inputs)
    normed1 = (xhat1 * norm_gain1).astype(BF16)
    normed1_all = gather_batch(normed1)
    projected = mm(normed1, w_in, out=BF16)
    earlier = shifted(projected[block_len - 2 :], "seq", 1)
    extended = jnp.concatenate([earlier, projected], axis=0).astype(F32)
    taps3 = short_kernel.astype(F32)
    lags = [extended[2 - lag : 2 - lag + block_len] for lag in range(3)]
    mixed = taps3[0] * lags[0] + taps3[1] * lags[1] + taps3[2] * lags[2]
    gate_out = mixed[:, :width]
    gate_in = mixed[:, width : 2 * width]
    values = mixed[:, 2 * width :]
    signal = (values * gate_in).astype(BF16)

    w3_own = lax.dynamic_slice_in_dim(filt_w3, position * own, own, 1)
    decay_own = lax.dynamic_slice_in_dim(decay_rate, position * own, own, 0)
    angle1 = mm(features, filt_w1, precision=HIGHEST)
    hidden1, slope1 = jnp.sin(angle1), jnp.cos(angle1)
    angle2 = mm(hidden1, filt_w2, precision=HIGHEST)
    hidden2, slope2 = jnp.sin(angle2), jnp.cos(angle2)
    lag_index = jnp.arange(seq_len).astype(F32)
    fading = jnp.exp(-decay_own[None, :] * lag_index[:, None])
    taps = (mm(hidden2, w3_own, precision=HIGHEST) * fading).astype(BF16)
    taps_spec = mm(table, taps)
    taps_re, taps_im = taps_spec[:seq_len], taps_spec[seq_len:]

    signal_spec = mm(table, to_channels(signal))
    signal_re, signal_im = signal_spec[:seq_len], signal_spec[seq_len:]
    scale = 1.0 / seq_len

    def inverse_of(real, imag):
        both = (jnp.concatenate([real, imag], axis=0) * scale).astype(BF16)
        return mm_tn(table, both)

    conv = inverse_of(
        taps_re * signal_re - taps_im * signal_im, taps_re * signal_im + taps_im * signal_re
    )
    long_out = to_tokens(conv.astype(BF16)).astype(F32) + conv_bias * signal.astype(F32)
    gated = (long_out * gate_out).astype(BF16)
    gated_all = gather_batch(gated)
    residual1 = inputs + mm(gated, w_out)
    xhat2, inverse2 = norm_parts(residual1)
    normed2 = (xhat2 * norm_gain2).astype(BF16)
    normed2_all = gather_batch(normed2)
    pre = mm(normed2, w_up)
    bent = jnp.tanh(GELU_SCALE * (pre + GELU_CUBIC * pre * pre * pre))
    hidden = (0.5 * pre * (1.0 + bent)).astype(BF16)
    layer_out = (residual1 + mm(hidden, w_down)).astype(BF16)

    slope = 0.5 * (1.0 + bent) + 0.5 * pre * (1.0 - bent * bent) * GELU_SCALE * (
        1.0 + 3.0 * GELU_CUBIC * pre * pre
    )
    grad_pre = (mm_nt(cot, w_down) * slope).astype(BF16)
    grad_w_down = rows_sum(columns_batch(hidden), cot_all)
    grad_w_up = columns_sum(normed2_all, columns_batch(grad_pre))
    grad_norm2 = mm_nt(grad_pre, w_up)
    grad_gain2 = jnp.sum(grad_norm2 * xhat2, axis=0)
    grad_res = cot.astype(F32) + norm_back(grad_norm2, norm_gain2, xhat2, inverse2)
    grad_branch = grad_res.astype(BF16)
    grad_w_out = columns_sum(gated_all, columns_batch(grad_branch))
    grad_gated = mm_nt(grad_branch, w_out)
    grad_long = (grad_gated * gate_out).astype(BF16)
    grad_gate_out = grad_gated * long_out
    grad_bias = jnp.sum(grad_long.astype(F32) * signal.astype(F32), axis=0)

    grad_spec = mm(table, to_channels(grad_long))
    grad_re, grad_im = grad_spec[:seq_len], grad_spec[seq_len:]
    grad_conv = inverse_of(
        taps_re * grad_re + taps_im * grad_im, taps_re * grad_im - taps_im * grad_re
    )
    grad_signal = to_tokens(grad_conv.astype(BF16)).astype(F32) + conv_bias * grad_long.astype(F32)
    grad_taps = inverse_of(
        signal_re * grad_re + signal_im * grad_im, signal_re * grad_im - signal_im * grad_re
    )
    grad_filt = grad_taps * fading
    grad_w3_own = mm_tn(hidden2, grad_filt)
    grad_angle2 = mm_nt(grad_filt, w3_own) * slope2
    grad_w2 = mm_tn(hidden1, grad_angle2)
    grad_angle1 = mm_nt(grad_angle2, filt_w2) * slope1
    grad_w1 = mm_tn(features, grad_angle1)

    grad_mixed = jnp.concatenate(
        [grad_gate_out, grad_signal * values, grad_signal * gate_in], axis=1
    )
    later = shifted(grad_mixed[:2], "seq", -1)
    grad_ext = jnp.concatenate([grad_mixed, later], axis=0)
    grad_proj = (
        taps3[0] * grad_ext[:block_len]
        + taps3[1] * grad_ext[1 : block_len + 1]
        + taps3[2] * grad_ext[2:]
    ).astype(BF16)
    grad_short = jnp.stack([jnp.sum(grad_mixed * lag, axis=0) for lag in lags])
    grad_w_in = columns_sum(normed1_all, columns_batch(grad_proj))
    grad_norm1 = mm_nt(grad_proj, w_in)
    grad_gain1 = jnp.sum(grad_norm1 * xhat1, axis=0)
    tokens_grad = grad_res + norm_back(grad_norm1, norm_gain1, xhat1, inverse1)

    return layer_out[None], tokens_grad[None], small_sums(
        grad_gain1, grad_bias, grad_gain2, grad_short, grad_w1, grad_w2, grad_w3_own
    ), (grad_w_in, grad_w_out, grad_w_up, grad_w_down)


MESH = pl.DeviceIdType.MESH
KERNEL_VMEM = 63 * 1024 * 1024


def symmetric_tables(length):
    odd = 2 * np.arange(length, dtype=np.int64) + 1
    angles = (odd[:, None] * odd[None, :] % (8 * length)).astype(np.float64) * (
        np.pi / (4 * length)
    )
    phase = odd.astype(np.float64) * (np.pi / (4 * length))
    tables = [np.cos(angles), np.sin(angles)]
    tables = [t.astype(np.float32).astype(ml_dtypes.bfloat16) for t in tables]
    return tables, np.stack([np.cos(phase), np.sin(phase)], axis=1).astype(np.float32)


def sin_cos(x):
    turns = jnp.floor(x * (2.0 / np.pi) + 0.5)
    rest = ((x - turns * 1.5703125) - turns * 4.837512969970703e-4) - turns * 7.54978995489188e-8
    square = rest * rest
    sine = rest + rest * square * (
        -1.6666654611e-1 + square * (8.3321608736e-3 - square * 1.9515295891e-4)
    )
    cosine = (1.0 - 0.5 * square) + square * square * (
        4.166664568298827e-2 + square * (-1.388731625493765e-3 + square * 2.443315711809948e-5)
    )
    quarter = turns - 4.0 * jnp.floor(turns * 0.25)
    odd = (quarter == 1.0) | (quarter == 3.0)
    sin_sign = jnp.where(quarter >= 2.0, -1.0, 1.0)
    cos_sign = jnp.where((quarter == 1.0) | (quarter == 2.0), -1.0, 1.0)
    return sin_sign * jnp.where(odd, cosine, sine), cos_sign * jnp.where(odd, sine, cosine)


class Named:
    def __init__(self, names, refs):
        assert len(names) == len(refs)
        for name, ref in zip(names, refs):
            setattr(self, name, ref)


def kernel_plan(groups, blocks, tokens, width, hidden, filt, emb):
    length = tokens * blocks
    own = width // blocks
    ffc = hidden // groups
    share = width // groups
    rows_out = share // blocks
    inc = 3 * share
    spare = 16
    chips = groups // 2
    down_rows = ffc // blocks
    net_at = -(-emb // 8) * 8
    net_rows = net_at + filt
    peers, zpeers = groups - 1, blocks - 1
    vm, hbm = pltpu.VMEM, pl.ANY
    inputs = dict(
        tokens=hbm, cot=hbm, w_in=hbm, w_out=hbm, w_up=hbm, w_down=hbm,
        cosine=hbm, sine=hbm, filt_w3=hbm, decay=hbm,
        gain1=vm, gain2=vm, bias=vm, short=vm, filt_w1=vm, filt_w2=vm,
        features_t=vm, phase=vm,
    )
    outputs = dict(
        layer_out=((tokens, width), BF16, hbm),
        tokens_grad=((tokens, width), F32, hbm),
        grad_w_in=((rows_out, 3 * width), F32, hbm),
        grad_w_out=((rows_out, width), F32, hbm),
        grad_w_up=((rows_out, hidden), F32, hbm),
        grad_w_down=((ffc // blocks, width), F32, hbm),
        grad_gain1=((1, rows_out), F32, vm),
        grad_gain2=((1, rows_out), F32, vm),
        grad_bias=((1, rows_out), F32, vm),
        grad_short=((3, 3 * rows_out), F32, vm),
        grad_w1=((emb, filt), F32, vm),
        grad_w2=((filt, filt), F32, vm),
        grad_w3=((filt, rows_out), F32, vm),
        cot_land=((2, groups // 2 * tokens, width), BF16, hbm),
        n2_land=((groups, width, tokens), BF16, hbm),
    )
    dma = pltpu.SemaphoreType.DMA
    scratch = dict(
        tok=vm((tokens, width), BF16), cotv=vm((tokens, width), BF16),
        mean1=vm((tokens, 128), F32), inv1=vm((tokens, 128), F32),
        n1_all=vm((length, width), BF16), turn=vm((width, tokens), BF16),
        gated_turn=vm((width, tokens), BF16), gated_pair=vm((width // 2, 2 * tokens), BF16),
        hid_buf=vm((tokens, ffc), BF16),
        ghalo=vm((8, 3 * width), F32), ghalo_in=vm((8, 3 * width), F32), tail=vm((16, 3 * width), F32),
        ext_c=vm((length + 32, 3 * own), BF16), gproj_c=vm((length, 3 * own), BF16),
        gconv_c=vm((length + 16, own), BF16), glong_c=vm((length + 16, own), BF16),
        ggb=vm((tokens, width), BF16),
        win=vm((3, width, width), BF16), wout=vm((width, width), BF16),
        cs=vm((length, length), BF16), sn=vm((length, length), BF16),
        ext=vm((tokens + 16, 3 * width), BF16),
        halo_out=vm((16, 3 * width), BF16), halo_in=vm((16, 3 * width), BF16),
        gate_out=vm((tokens, width), F32),
        sig=vm((tokens, width), BF16), chan=vm((length + 16, own), BF16),
        w3=vm((filt, own), F32), fade=vm((1, own), F32),
        h1=vm((filt, length), F32), s1=vm((filt, length), F32),
        h2=vm((filt, length), F32), s2=vm((filt, length), F32),
        sum_gain1=vm((1, width), F32), sum_gain2=vm((1, width), F32),
        sum_bias=vm((1, width), F32), sum_short=vm((3, 3 * width), F32),
        small_send=vm((groups, 16, share), F32), small_land=vm((groups, 16, share), F32),
        small_sum=vm((16, share), F32), small_z=vm((zpeers, 16, share), F32),
        short_all=vm((8, inc), F32),
        w12=vm((net_rows, 128), F32), w12_z=vm((zpeers, net_rows, 128), F32),
        w12_sum=vm((net_rows, 128), F32), w12_plane=vm((peers, net_rows, 128), F32),
        sum_w3=vm((filt, own), F32), w3_land=vm((peers, filt // groups, own), F32),
        w3_part=vm((filt // groups, own), F32), w3_all=vm((blocks, filt, own), F32),
        hre=vm((length, own), F32), him=vm((length, own), F32),
        xre=vm((length, own), F32), xim=vm((length, own), F32),
        yre=vm((length, own), BF16), yim=vm((length, own), BF16),
        qre=vm((length, own), BF16), qim=vm((length, own), BF16),
        conv_out=vm((length + 16, own), BF16), conv_in=vm((blocks, tokens, own), BF16),
        long=vm((tokens, width), F32), half=vm((tokens, width), BF16),
        res=vm((tokens, width), F32), xhat2=vm((tokens, width), F32),
        inv2=vm((tokens, 128), F32), gn2=vm((tokens, width), F32),
        gres=vm((tokens, width), F32),
        hid_send=vm((groups, ffc, tokens), BF16), hid_own=vm((ffc, groups * tokens), BF16),
        pre_send=vm((groups, tokens, ffc), BF16), pre_own=vm((groups * tokens, ffc), BF16),
        gbr_pair=vm((2 * tokens, width), BF16),
        glong=vm((tokens, width), BF16),
        gproj=vm((tokens, 3 * width), BF16),
        down_send=vm((2, down_rows, width), BF16), down_land=vm((2, down_rows, width), BF16),
        down_next=vm((down_rows, width), BF16), down_last=vm((down_rows, width), BF16),
        up_send=vm((2, own, ffc), BF16), up_land=vm((2, own, ffc), BF16),
        up_next=vm((own, ffc), BF16), up_last=vm((own, ffc), BF16),
        in_send=vm((chips, share, 3 * own), BF16), in_pair=vm((chips, share, 3 * own), BF16),
        in_land=vm((chips - 1, share, 3 * own), BF16), in_own=vm((share, 3 * own), F32),
        out_send=vm((chips - 1, share, width), BF16), out_land=vm((chips - 1, share, width), BF16),
        outz_send=vm((share, width), BF16), outz_land=vm((zpeers, rows_out, width), BF16),
        outz_own=vm((rows_out, width), F32),
        load_sem=dma((16,)),
        pool_sem=dma((groups,)),
        win_sem=dma((3,)),
        ffn_sem=dma((2, 2)),
        local_sem=dma((16,)),
        stage_sem=dma((chips - 1,)),
        ag_s=dma((2, groups - 1)), ag_r=dma((2, groups - 1)),
        halo_s=dma((2,)), halo_r=dma((2,)),
        za_s=dma((4, zpeers)), za_r=dma((4, zpeers)),
        pa_s=dma((2, peers)), pa_r=dma((2, peers)),
        cx_s=dma((3,)), cx_r=dma((3,)), zg_s=dma((zpeers,)), zg_r=dma((zpeers,)),
        wi_s=dma((chips - 1,)), wi_r=dma((chips - 1,)), ti_s=dma((zpeers, 3)), ti_r=dma((zpeers, 3)), wo_s=dma((2, chips - 1)), wo_r=dma((2, chips - 1)),
        rs_s=dma((2, 2)), rs_r=dma((2, 2)),
        sm_s=dma((4, peers)), sm_r=dma((4, peers)),
        sz_s=dma((3, zpeers)), sz_r=dma((3, zpeers)),
        tr_s=dma((1, peers)), tr_r=dma((1, peers)),
    )
    names = [*inputs, *outputs, *scratch]

    def kernel(*refs):
        r = Named(names, refs)
        b, z = lax.axis_index("batch"), lax.axis_index("seq")
        chip, core = lax.div(b, 2), lax.rem(b, 2)
        sibling = chip * 2 + (1 - core)
        sent = {}

        chip_x, chip_y = lax.rem(chip, 2), lax.div(chip, 2)

        def flipped(turn_x, turn_y):
            x = chip_x + turn_x - 2 * chip_x * turn_x
            y = chip_y + turn_y - 2 * chip_y * turn_y
            return y * 2 + x

        def partner(way):
            return flipped(1 - way % 2, (way + 1) // 2)

        def way_of(step):
            return 2 if step == 2 else step + core - 2 * step * core

        def partner_at(way):
            return flipped(1 - lax.rem(way, 2), lax.div(way + 1, 2))

        def peer(at):
            at = jnp.int32(at)
            late, last = lax.div(at, 4), lax.div(at, 6)
            way = (1 - late) * lax.rem(at + core, 2) + late * 2
            to_core = (1 - late) * lax.div(at, 2) + late * (at - 4)
            to_chip = flipped((1 - last) * (1 - lax.rem(way, 2)), (1 - last) * lax.div(way + 1, 2))
            own_chip = (7 - at) * (1 - core) + (at - 6) * core
            group = to_chip * 2 + (1 - last) * to_core + last * own_chip
            return group, (1 - last) * (way * 2 + to_core) + last * 6, (1 - last) * (way * 2 + core) + last * 6

        def group_at(step):
            return lax.rem(b + step, groups)

        def block_at(step):
            return lax.rem(z + step, blocks)

        def span(at, size):
            return pl.ds(pl.multiple_of(at * size, size), size)

        def remote(src, dst, send_sem, recv_sem, **where):
            return pltpu.make_async_remote_copy(
                src_ref=src, dst_ref=dst, send_sem=send_sem, recv_sem=recv_sem,
                device_id=where, device_id_type=MESH,
            )

        def send(key, copy):
            copy.start()
            sent.setdefault(key, []).append(copy)

        def drain(key):
            for copy in sent.pop(key):
                copy.wait_send()

        def tiles(size, total, body):
            def step(i, carry):
                body(pl.multiple_of(i * size, size))
                return carry

            lax.fori_loop(0, total // size, step, 0)

        def load(sem, src, dst):
            copy = pltpu.make_async_copy(src, dst, sem)
            copy.start(priority=1)
            return copy

        def load_win(block):
            return load(r.win_sem.at[block], r.w_in.at[:, pl.ds(block * width, width)], r.win.at[block])

        load_tok = load(r.load_sem.at[0], r.tokens, r.tok)
        win_loads = [(block, load_win(block)) for block in (1, 2, 0)]
        load_cot = load(r.load_sem.at[5], r.cot, r.cotv)
        load_w3 = load(r.load_sem.at[1], r.filt_w3.at[:, span(z, own)], r.w3)
        load_fade = load(r.load_sem.at[2], r.decay.at[:, span(z, own)], r.fade)
        load_cs = load(r.load_sem.at[3], r.cosine, r.cs)
        load_sn = load(r.load_sem.at[4], r.sine, r.sn)
        load_wout = load(r.load_sem.at[6], r.w_out, r.wout)

        barrier = pltpu.get_barrier_semaphore()
        for step in range(1, groups):
            pl.semaphore_signal(barrier, inc=1, device_id={"batch": group_at(step)}, device_id_type=MESH)
        for step in range(1, blocks):
            pl.semaphore_signal(barrier, inc=1, device_id={"seq": block_at(step)}, device_id_type=MESH)

        slots = [
            lambda at: r.cot_land.at[lax.div(at, chips), span(lax.rem(at, chips), tokens)],
            lambda at: r.n2_land.at[at],
        ]

        def gather_copy(k, at, src, slot, to):
            return remote(src, slot, r.ag_s.at[k, at], r.ag_r.at[k, at], batch=to)

        def gather_local(k, src):
            return pltpu.make_async_copy(src, slots[k](b), r.local_sem.at[k])

        def gather_start(k, src):
            for step in range(chips - 1):
                way = way_of(step)
                to = partner_at(jnp.int32(way)) * 2 + core
                send(("ag", k), gather_copy(k, way, src, slots[k](b), to))
            send(("ag", k), gather_copy(k, chips - 1, src, slots[k](b), sibling))
            gather_local(k, src).start(priority=1)

        def stage(k, step):
            if k == 0:
                return r.gproj.at[:, (step - 1) * width : step * width]
            return r.win.at[0, :, (step - 1) * tokens : step * tokens]

        def gather_forward(k):
            staged = []
            for step in range(1, chips):
                slot = slots[k](partner(step - 1) * 2 + core)
                gather_copy(k, step - 1, slot, slot, sibling).wait_recv()
                staged.append((slot, load(r.stage_sem.at[step - 1], slot, stage(k, step))))
            for step, (slot, copy) in enumerate(staged, 1):
                copy.wait()
                source = stage(k, step)
                send(("forward", k), gather_copy(k, chips - 1 + step, source, slot, sibling))

        def gather_finish(k):
            for step in range(chips):
                slot = slots[k]((partner(step - 1) if step else chip) * 2 + 1 - core)
                gather_copy(k, chips - 1 + step, slot, slot, sibling).wait_recv()

        def turned(value_ref, out_ref):
            def body(at):
                tile = value_ref[:, pl.ds(at, share)].T
                group = lax.div(at, share)
                for block in range(blocks):
                    first = pl.multiple_of(block * own + group * rows_out, rows_out)
                    out_ref[pl.ds(first, rows_out), :] = tile[block * rows_out : (block + 1) * rows_out]

            tiles(share, width, body)

        def turned_by_core(value_ref, out_ref):
            def body(at):
                group = lax.div(at, share)
                out_ref[span(lax.rem(group, 2) * chips + lax.div(group, 2), share), :] = value_ref[
                    :, pl.ds(at, share)
                ].T

            tiles(share, width, body)

        load_tok.wait()

        def norm1(at):
            rows = pl.ds(at, 32)
            x = r.tok[rows, :].astype(F32)
            xhat, inverse = norm_parts(x)
            r.mean1[rows, :] = jnp.broadcast_to(jnp.mean(x, axis=-1, keepdims=True), (32, 128))
            r.inv1[rows, :] = jnp.broadcast_to(inverse, (32, 128))
            r.n1_all[pl.ds(pl.multiple_of(z * tokens + at, 32), 32), :] = (xhat * r.gain1[...]).astype(BF16)

        tiles(32, tokens, norm1)
        for block, copy in win_loads:
            copy.wait()
            cols = slice(block * width, (block + 1) * width)
            proj = mm(r.n1_all[span(z, tokens), :], r.win[block], out=BF16)
            r.ext[16:, cols] = proj
            r.halo_out[:, cols] = proj[tokens - 16 :]
        pl.semaphore_wait(barrier, peers + zpeers)
        halo = remote(r.halo_out, r.halo_in, r.halo_s.at[0], r.halo_r.at[0], seq=block_at(1))
        send("halo", halo)
        own_loads = [
            load(
                r.load_sem.at[7 + part],
                r.w_in.at[:, pl.ds(pl.multiple_of(part * width + z * own, own), own)],
                r.win.at[2, :, part * own : (part + 1) * own],
            )
            for part in range(3)
        ]
        for padded in (r.chan, r.conv_out, r.gconv_c, r.glong_c):
            padded[length:, :] = jnp.zeros((spare, own), BF16)
        r.ext_c[0:spare, :] = jnp.zeros((spare, 3 * own), BF16)
        r.ext_c[length + spare :, :] = jnp.zeros((spare, 3 * own), BF16)

        def up_weights(at, slot):
            group = peer(at)[0]
            return pltpu.make_async_copy(
                r.w_up.at[:, span(group, ffc)], r.win.at[0, :, span(slot, ffc)], r.ffn_sem.at[slot, 0]
            )

        def down_weights(at, slot):
            group = peer(at)[0]
            return pltpu.make_async_copy(
                r.w_down.at[span(group, ffc)], r.win.at[1, span(slot, ffc)], r.ffn_sem.at[slot, 1]
            )

        for at in range(2):
            down_weights(at, at).start(priority=1)
            up_weights(at, at).start(priority=1)

        halo.wait_recv()
        r.ext[0:16, :] = (r.halo_in[...].astype(F32) * jnp.where(z > 0, 1.0, 0.0)).astype(BF16)

        def lags_at(cols):
            wide = r.ext[:, cols].astype(F32)
            return [wide[16 - lag : 16 - lag + tokens] for lag in range(3)]

        def mix(cols):
            lags = lags_at(cols)
            short = r.short[:, cols].astype(F32)
            return lags, short[0:1] * lags[0] + short[1:2] * lags[1] + short[2:3] * lags[2]

        def chan_copy(k, src, dst, step, to):
            return remote(src, dst, r.za_s.at[k, step - 1], r.za_r.at[k, step - 1], seq=to)

        def to_channels(k, value_ref, make_cols):
            for step in list(range(1, blocks)) + [0]:
                block = block_at(step)
                make_cols(block)
                if step:
                    src, dst = value_ref.at[:, span(block, own)], r.chan.at[span(z, tokens)]
                    send(("za", k), chan_copy(k, src, dst, step, block))
                else:
                    r.chan[span(z, tokens), :] = value_ref[:, span(block, own)]

        def wait_channels(k):
            for step in range(1, blocks):
                source = block_at(blocks - step)
                dst = r.chan.at[span(source, tokens)]
                chan_copy(k, dst, dst, step, source).wait_recv()

        def signal_block(block):
            def body(at):
                base = block * own + at
                cols = pl.ds(pl.multiple_of(base, 128), 128)
                gate_in = mix(pl.ds(pl.multiple_of(width + base, 128), 128))[1]
                values = mix(pl.ds(pl.multiple_of(2 * width + base, 128), 128))[1]
                r.sig[:, cols] = (values * gate_in).astype(BF16)

            tiles(128, own, body)

        to_channels(0, r.sig, signal_block)
        load_cot.wait()
        gather_start(0, r.cotv)

        load_w3.wait()
        load_fade.wait()

        def fading(at):
            lag = (lax.broadcasted_iota(jnp.int32, (tokens, own), 0) + at).astype(F32)
            return jnp.exp(-r.fade[...] * lag)

        def taps_rows(at):
            rows = pl.ds(at, tokens)
            h1, r.s1[:, rows] = sin_cos(mm_tn(r.filt_w1[...], r.features_t[:, rows], precision=HIGHEST))
            h2, r.s2[:, rows] = sin_cos(mm_tn(r.filt_w2[...], h1, precision=HIGHEST))
            r.h1[:, rows] = h1
            r.h2[:, rows] = h2
            taps = mm_tn(h2, r.w3[...], precision=HIGHEST) * fading(at)
            r.qre[rows, :] = taps.astype(BF16)

        tiles(tokens, length, taps_rows)
        load_cs.wait()
        load_sn.wait()
        scale = 1.0 / length

        def taps_spec(at):
            rows = pl.ds(at, tokens)
            real = mm(r.cs[rows, :], r.qre[...]) * scale
            imag = mm(r.sn[rows, :], r.qre[...]) * -scale
            turn_re, turn_im = r.phase[rows, 0:1], r.phase[rows, 1:2]
            r.hre[rows, :] = real * turn_re - imag * turn_im
            r.him[rows, :] = real * turn_im + imag * turn_re

        tiles(tokens, length, taps_spec)

        wait_channels(0)

        def conv_spec(at):
            rows = pl.ds(at, tokens)
            real = mm(r.cs[rows, :], r.chan[0:length, :])
            imag = -mm(r.sn[rows, :], r.chan[0:length, :])
            r.xre[rows, :] = real
            r.xim[rows, :] = imag
            hre, him = r.hre[rows, :], r.him[rows, :]
            r.yre[rows, :] = (hre * real - him * imag).astype(BF16)
            r.yim[rows, :] = (-(hre * imag + him * real)).astype(BF16)

        tiles(tokens, length, conv_spec)

        def to_tokens(k, out_ref):
            for step in list(range(1, blocks)) + [0]:
                block = block_at(step)
                rows = span(block, tokens)
                tile = (mm(r.cs[rows, :], r.yre[...]) + mm(r.sn[rows, :], r.yim[...])).astype(BF16)
                out_ref[rows, :] = tile
                if step:
                    src, dst = out_ref.at[rows], r.conv_in.at[z]
                    send(("za", k), chan_copy(k, src, dst, step, block))
                else:
                    r.conv_in[z] = tile

        def wait_tokens(k):
            for step in range(1, blocks):
                source = block_at(blocks - step)
                dst = r.conv_in.at[source]
                chan_copy(k, dst, dst, step, source).wait_recv()

        to_tokens(1, r.conv_out)

        def seq_gather(step, source, to):
            rows = r.n1_all.at[span(source, tokens)]
            return remote(rows, rows, r.zg_s.at[step - 1], r.zg_r.at[step - 1], seq=to)

        for step in range(1, blocks):
            send("n1", seq_gather(step, z, block_at(step)))

        load_wout.wait()
        def gate_cols(at):
            cols = pl.ds(at, 128)
            r.gate_out[:, cols] = mix(cols)[1]

        tiles(128, width, gate_cols)

        def grad_hidden(at, carry):
            slot = lax.rem(at, 2)
            down_weights(at, slot).wait()
            r.pre_send[at] = mm_nt(r.cotv[...], r.win[1, span(slot, ffc), :], out=BF16)
            down_weights(lax.rem(at + 2, groups), slot).start(priority=1)
            return carry

        lax.fori_loop(0, groups, grad_hidden, 0)
        wait_tokens(1)

        def conv_cols(at):
            return r.conv_in[
                lax.div(at, own), :, pl.ds(pl.multiple_of(lax.rem(at, own), 128), 128)
            ].astype(F32)

        def long_cols(at):
            cols = pl.ds(at, 128)
            long = conv_cols(at) + r.bias[:, cols] * r.sig[:, cols].astype(F32)
            r.long[:, cols] = long
            r.half[:, cols] = (long * r.gate_out[:, cols]).astype(BF16)

        tiles(128, width, long_cols)
        r.res[...] = mm(r.half[...], r.wout[...])
        turned_by_core(r.half, r.gated_turn)
        mine = span(core, tokens)
        pair_rows = chips * share

        def pair_copy(k, src, dst):
            return remote(src, dst, r.cx_s.at[k], r.cx_r.at[k], batch=sibling)

        gated_copy = pair_copy(
            0, r.gated_turn.at[span(1 - core, pair_rows)], r.gated_pair.at[:, mine]
        )
        send("pair", gated_copy)
        r.gated_pair[:, mine] = r.gated_turn[span(core, pair_rows), :]

        def norm2(at):
            rows = pl.ds(at, 32)
            residual = r.res[rows, :] + r.tok[rows, :].astype(F32)
            r.res[rows, :] = residual
            xhat, inverse = norm_parts(residual)
            r.xhat2[rows, :] = xhat
            r.inv2[rows, :] = jnp.broadcast_to(inverse, (32, 128))
            r.half[rows, :] = (xhat * r.gain2[...]).astype(BF16)

        tiles(32, tokens, norm2)
        turned(r.half, r.turn)
        r.gn2[...] = jnp.zeros((tokens, width), F32)

        def plane_copy(k, src, dst, at):
            to, send_at, recv_at = peer(at)
            return remote(src, dst, r.pa_s.at[k, send_at], r.pa_r.at[k, recv_at], batch=to)

        def hidden_copy(at):
            return plane_copy(0, r.hid_send.at[at], r.hid_own.at[:, span(b, tokens)], at)

        def pre_copy(at):
            return plane_copy(1, r.pre_send.at[at], r.pre_own.at[span(b, tokens)], at)

        def chunk(at, carry):
            slot = lax.rem(at, 2)
            where = span(slot, ffc)
            up_weights(at, slot).wait()
            r.gres[:, 0:ffc] = mm(r.half[...], r.win[0, :, where])

            def act(row):
                rows = pl.ds(row, 32)
                pre = r.gres[rows, 0:ffc]
                square = pre * pre
                bent = jnp.tanh(pre * (GELU_SCALE + GELU_SCALE * GELU_CUBIC * square))
                upper = 0.5 + 0.5 * bent
                slope = upper + pre * (0.5 - 0.5 * bent * bent) * (
                    GELU_SCALE + 3.0 * GELU_SCALE * GELU_CUBIC * square
                )
                r.hid_buf[rows, :] = (pre * upper).astype(BF16)
                r.pre_send[at, rows, :] = (r.pre_send[at, rows, :].astype(F32) * slope).astype(BF16)

            tiles(32, tokens, act)
            r.hid_send[at] = r.hid_buf[...].T

            @pl.when(at < groups - 1)
            def _():
                hidden_copy(at).start()

            down_weights(at, slot).wait()
            r.res[...] += mm(r.hid_buf[...], r.win[1, where, :])
            r.gn2[...] += mm_nt(r.pre_send[at], r.win[0, :, where])

            @pl.when(at < groups - 2)
            def _():
                up_weights(at + 2, slot).start(priority=1)
                down_weights(at + 2, slot).start(priority=1)

            return carry

        lax.fori_loop(0, groups, chunk, 0)
        for at in range(peers):
            sent.setdefault("ffn", []).append(hidden_copy(at))

        def pool_cot():
            return [load(r.win_sem.at[half], r.cot_land.at[half], r.win.at[half]) for half in range(2)]

        def pool_turned(land):
            return [
                load(
                    r.pool_sem.at[at],
                    land.at[at],
                    r.win.at[at // chips, :, pl.ds(at % chips * tokens, tokens)],
                )
                for at in range(groups)
            ]

        gather_forward(0)
        r.hid_own[:, span(b, tokens)] = r.hid_send[groups - 1]
        r.pre_own[span(b, tokens), :] = r.pre_send[groups - 1]

        def norm2_back(at, total):
            rows = pl.ds(pl.multiple_of(at * 32, 32), 32)
            r.half[rows, :] = r.res[rows, :].astype(BF16)
            grad, xhat = r.gn2[rows, :], r.xhat2[rows, :]
            back = r.cotv[rows, :].astype(F32) + norm_back(grad, r.gain2[...], xhat, r.inv2[rows, 0:1])
            r.gres[rows, :] = back
            r.gbr_pair[pl.ds(pl.multiple_of(core * tokens + at * 32, 32), 32), :] = back.astype(BF16)
            return total + jnp.sum((grad * xhat).reshape(4, 8, width), axis=0)

        total = lax.fori_loop(0, tokens // 32, norm2_back, jnp.zeros((8, width), F32))
        r.sum_gain2[...] = jnp.sum(total, axis=0, keepdims=True)
        store_layer = load(r.local_sem.at[8], r.half, r.layer_out)
        branch_copy = pair_copy(1, r.gbr_pair.at[mine], r.gbr_pair.at[mine])
        send("pair", branch_copy)

        def gated_back(block):
            cols = span(block, own)
            grad = mm_nt(r.gbr_pair[mine, :], r.wout[span(block, own), :])
            glong = (grad * r.gate_out[:, cols]).astype(BF16)
            r.glong[:, cols] = glong
            r.ggb[:, cols] = grad.astype(BF16)
            r.long[:, cols] = grad * r.long[:, cols]
            r.sum_bias[:, cols] = jnp.sum(
                glong.astype(F32) * r.sig[:, cols].astype(F32), axis=0, keepdims=True
            )

        to_channels(2, r.ggb, gated_back)

        gather_start(1, r.turn)

        branch_copy.wait_recv()
        gated_copy.wait_recv()

        def out_copy(way):
            sems = r.wo_s.at[0, way], r.wo_r.at[0, way]
            to = partner_at(jnp.int32(way)) * 2 + core
            return remote(r.out_send.at[way], r.out_land.at[way], *sems, batch=to)

        for step in range(chips):
            to = partner(step - 1) if step else chip
            part = mm(r.gated_pair[span(to, share), :], r.gbr_pair[...])
            if step:
                r.out_send[step - 1] = part.astype(BF16)
            else:
                r.xhat2[share : 2 * share, :] = part

        near = z + 1 - 2 * lax.rem(z, 2)
        far = block_at(2)

        def reduce_first(k, refs):
            return remote(refs[0], refs[1], r.rs_s.at[k, 0], r.rs_r.at[k, 0], seq=near)

        def reduce_second(k, refs):
            return remote(refs[2], refs[3], r.rs_s.at[k, 1], r.rs_r.at[k, 1], seq=far)

        def reduce_send(k, refs, part_of):
            send_ref, _, next_ref, _, own_ref = refs
            send_ref[0] = part_of(near).astype(BF16)
            send_ref[1] = part_of(lax.rem(near + 2, blocks)).astype(BF16)
            send("rs", reduce_first(k, refs))
            next_ref[...] = part_of(far).astype(BF16)
            own_ref[...] = part_of(z)

        def reduce_next(k, refs):
            _, land_ref, next_ref, _, own_ref = refs
            reduce_first(k, refs).wait_recv()
            next_ref[...] = (next_ref[...].astype(F32) + land_ref[1].astype(F32)).astype(BF16)
            send("rs", reduce_second(k, refs))
            own_ref[...] += land_ref[0].astype(F32)

        def reduce_finish(k, refs):
            reduce_second(k, refs).wait_recv()
            refs[4][...] += refs[3][...].astype(F32)

        down_refs = (r.down_send, r.down_land, r.down_next, r.down_last, r.xhat2.at[0:down_rows])
        up_refs = (r.up_send, r.up_land, r.up_next, r.up_last, r.gate_out.at[:, 0:ffc])

        def wait_plane(k, dst_of):
            for at in range(peers):
                source = sibling if at == 6 else partner(at // 2) * 2 + at % 2
                dst = dst_of(source)
                remote(dst, dst, r.pa_s.at[k, at], r.pa_r.at[k, at], batch=source).wait_recv()

        deep = groups // 2 * tokens

        def down_part(block):
            rows = span(block, ffc // blocks)
            return mm(r.hid_own[rows, :deep], r.win[0]) + mm(r.hid_own[rows, deep:], r.win[1])

        def turned_part(right_ref):
            def part(block):
                rows = span(block, own)
                return mm(r.win[0, rows, :], right_ref[:deep]) + mm(r.win[1, rows, :], right_ref[deep:])

            return part


        gather_local(0, r.cotv).wait()
        gather_finish(0)
        pool = pool_cot()

        for step in range(1, blocks):
            source = block_at(blocks - step)
            seq_gather(step, source, source).wait_recv()
        for copy in own_loads:
            copy.wait()

        def proj_rows(at):
            r.ext_c[pl.ds(pl.multiple_of(at + spare, spare), tokens), :] = mm(
                r.n1_all[pl.ds(at, tokens), :], r.win[2, :, 0 : 3 * own], out=BF16
            )

        tiles(tokens, length, proj_rows)

        def own_cols(part, at):
            return pl.ds(pl.multiple_of(part * width + z * own + at, 128), 128)

        def mix_own(part, at, first, rows):
            wide = r.ext_c[pl.ds(first, rows + spare), part * own + at : part * own + at + 128].astype(F32)
            short = r.short[:, own_cols(part, at)].astype(F32)
            lags = [wide[spare - lag : spare - lag + rows] for lag in range(3)]
            return short[0:1] * lags[0] + short[1:2] * lags[1] + short[2:3] * lags[2]

        wait_channels(2)

        def long_rows(first):
            rows = pl.ds(first, tokens)
            for at in range(0, own, 128):
                cols = slice(at, at + 128)
                gate = mix_own(0, at, first, tokens)
                r.glong_c[rows, cols] = (r.chan[rows, cols].astype(F32) * gate).astype(BF16)

        tiles(tokens, length, long_rows)

        def grad_spec(at):
            rows = pl.ds(at, tokens)
            real = mm(r.cs[rows, :], r.glong_c[0:length, :])
            imag = -mm(r.sn[rows, :], r.glong_c[0:length, :])
            hre, him = r.hre[rows, :], r.him[rows, :]
            r.yre[rows, :] = (hre * real + him * imag).astype(BF16)
            r.yim[rows, :] = (him * real - hre * imag).astype(BF16)
            xre, xim = r.xre[rows, :], r.xim[rows, :]
            both_re = xre * real + xim * imag
            both_im = xre * imag - xim * real
            turn_re, turn_im = r.phase[rows, 0:1], r.phase[rows, 1:2]
            r.qre[rows, :] = ((both_re * turn_re + both_im * turn_im) * scale).astype(BF16)
            r.qim[rows, :] = ((both_re * turn_im - both_im * turn_re) * scale).astype(BF16)

        tiles(tokens, length, grad_spec)
        to_tokens(3, r.gconv_c)
        for at in range(peers):
            send("ffn", pre_copy(at))

        def proj_back(first):
            rows = pl.ds(first, tokens + spare)
            for at in range(0, own, 128):
                cols = slice(at, at + 128)
                gate_in = mix_own(1, at, first, tokens + spare)
                values = mix_own(2, at, first, tokens + spare)
                bias = r.bias[:, own_cols(0, at)]
                signal = (values * gate_in).astype(BF16).astype(F32)
                long = r.conv_out[rows, cols].astype(F32) + bias * signal
                grad_signal = r.gconv_c[rows, cols].astype(F32) + bias * r.glong_c[rows, cols].astype(F32)
                parts = (r.chan[rows, cols].astype(F32) * long, grad_signal * values, grad_signal * gate_in)
                for part, grad in enumerate(parts):
                    short = r.short[:, own_cols(part, at)].astype(F32)
                    total = (
                        short[0:1] * grad[0:tokens]
                        + short[1:2] * grad[1 : tokens + 1]
                        + short[2:3] * grad[2 : tokens + 2]
                    )
                    r.gproj_c[pl.ds(first, tokens), part * own + at : part * own + at + 128] = total.astype(BF16)

        tiles(tokens, length, proj_back)

        def in_part(group):
            return mm_tn(r.n1_all[:, span(group, share)], r.gproj_c[...])

        for at in range(chips):
            r.in_send[at] = in_part(at * 2 + 1 - core).astype(BF16)
        in_pair = pair_copy(2, r.in_send, r.in_pair)
        send("in_pair", in_pair)
        for copy in pool:
            copy.wait()
        wait_plane(0, lambda at: r.hid_own.at[:, span(at, tokens)])
        reduce_send(0, down_refs, down_part)
        in_pair.wait_recv()
        drain("in_pair")

        def in_copy(way):
            sems = r.wi_s.at[way], r.wi_r.at[way]
            to = partner_at(jnp.int32(way)) * 2 + core
            return remote(r.in_send.at[way], r.in_land.at[way], *sems, batch=to)

        for step in range(chips):
            way = way_of(step) if step < chips - 1 else None
            to = chip if way is None else partner_at(jnp.int32(way))
            part = in_part(to * 2 + core) + r.in_pair[to].astype(F32)
            if way is None:
                r.in_own[...] = part
            else:
                r.in_send[way] = part.astype(BF16)
                send("in", in_copy(way))

        r.w12[...] = jnp.zeros((net_rows, 128), F32)
        r.sum_w3[...] = jnp.zeros((filt, own), F32)
        for at in range(0, length, tokens):
            rows = slice(at, at + tokens)
            grad_taps = mm(r.cs[rows, :], r.qre[...]) + mm(r.sn[rows, :], r.qim[...])
            grad_filt = grad_taps * fading(at)
            r.sum_w3[...] += mm(r.h2[:, rows], grad_filt, precision=HIGHEST)
            grad_angle2 = mm_nt(r.w3[...], grad_filt, precision=HIGHEST) * r.s2[:, rows]
            r.w12[net_at:, :filt] += mm_nt(r.h1[:, rows], grad_angle2, precision=HIGHEST)
            grad_angle1 = mm(r.filt_w2[...], grad_angle2, precision=HIGHEST) * r.s1[:, rows]
            r.w12[:emb, :filt] += mm_nt(r.features_t[:, rows], grad_angle1, precision=HIGHEST)

        def small_copy(k, src, dst, at, to):
            return remote(src, dst, r.sm_s.at[k, at], r.sm_r.at[k, at], batch=to)

        def small_z_copy(k, src, dst, step, to):
            return remote(src, dst, r.sz_s.at[k, step - 1], r.sz_r.at[k, step - 1], seq=to)

        def small_z_send(k, src, dst_of):
            for step in range(1, blocks):
                send("small", small_z_copy(k, src, dst_of(step), step, block_at(step)))

        def small_z_wait(k, dst_of):
            for step in range(1, blocks):
                dst = dst_of(step)
                small_z_copy(k, dst, dst, step, block_at(blocks - step)).wait_recv()

        def small_send(k, src_of, dst_of):
            for at in range(peers):
                to = group_at(1 + at)
                send("small", small_copy(k, src_of(to), dst_of(at), at, to))

        def small_wait(k, dst_of):
            for at in range(peers):
                dst = dst_of(at)
                small_copy(k, dst, dst, at, group_at(groups - 1 - at)).wait_recv()

        w3_rows = filt // groups
        small_z_send(0, r.w12, lambda step: r.w12_z.at[step - 1])
        small_send(0, lambda to: r.sum_w3.at[span(to, w3_rows)], lambda at: r.w3_land.at[at])

        def outz_copy(step, to):
            sems = r.wo_s.at[1, step - 1], r.wo_r.at[1, step - 1]
            return remote(r.outz_send.at[span(to, rows_out)], r.outz_land.at[step - 1], *sems, seq=to)


        def short_sums(cols, grad, lags):
            for lag in range(3):
                r.sum_short[lag : lag + 1, cols] = jnp.sum(grad * lags[lag], axis=0, keepdims=True)

        def back_cols(cols, grad, lags):
            short_sums(cols, grad, lags)
            r.ghalo[:, cols] = grad[0:8]
            short = r.short[:, cols].astype(F32)
            longer = jnp.concatenate([grad, jnp.zeros((8, 128), F32)], axis=0)
            total = (
                short[0:1] * grad
                + short[1:2] * longer[1 : tokens + 1]
                + short[2:3] * longer[2 : tokens + 2]
            )
            r.gproj[:, cols] = total.astype(BF16)
            r.tail[:, cols] = total[tokens - 16 :]

        def mixed_cols(at):
            cols = pl.ds(at, 128)
            grad_signal = conv_cols(at) + r.bias[:, cols] * r.glong[:, cols].astype(F32)
            gate_cols = pl.ds(pl.multiple_of(width + at, 128), 128)
            value_cols = pl.ds(pl.multiple_of(2 * width + at, 128), 128)
            gate_lags, gate_in = mix(gate_cols)
            value_lags, values = mix(value_cols)
            back_cols(gate_cols, grad_signal * values, gate_lags)
            back_cols(value_cols, grad_signal * gate_in, value_lags)

        def gate_back(at):
            cols = pl.ds(at, 128)
            back_cols(cols, r.long[:, cols], lags_at(cols))

        drain(("forward", 0))
        tiles(128, width, gate_back)
        wait_tokens(3)
        tiles(128, width, mixed_cols)
        halo = remote(r.ghalo, r.ghalo_in, r.halo_s.at[1], r.halo_r.at[1], seq=block_at(blocks - 1))
        send("halo", halo)
        gather_forward(1)
        halo.wait_recv()
        later = r.ghalo_in[...] * jnp.where(z < blocks - 1, 1.0, 0.0)

        def tail_cols(at):
            cols = slice(at, at + width)
            short = r.short[:, cols].astype(F32)
            row = lax.broadcasted_iota(jnp.int32, (16, width), 0)
            last = short[1:2] * later[0:1, cols] + short[2:3] * later[1:2, cols]
            total = r.tail[:, cols] + jnp.where(row == 15, last, 0.0)
            total = total + jnp.where(row == 14, short[2:3] * later[0:1, cols], 0.0)
            r.gproj[tokens - 16 :, cols] = total.astype(BF16)

        for part in range(3):
            tail_cols(part * width)

        def spread(k, own_ref, out_ref, size):
            for at in range(peers):
                to = group_at(1 + at)
                src, dst = own_ref.at[span(to, rows_out)], out_ref.at[:, span(b, size)]
                send("spread", remote(src, dst, r.tr_s.at[k, at], r.tr_r.at[k, at], batch=to))
            return load(r.local_sem.at[14 + k], own_ref.at[span(b, rows_out)], out_ref.at[:, span(b, size)])

        def spread_finish(k, copy, out_ref, size):
            for at in range(peers):
                source = group_at(groups - 1 - at)
                dst = out_ref.at[:, span(source, size)]
                remote(dst, dst, r.tr_s.at[k, at], r.tr_r.at[k, at], batch=source).wait_recv()
            copy.wait()

        for step in range(chips - 1):
            send("out", out_copy(way_of(step)))
        small_z_wait(0, lambda step: r.w12_z.at[step - 1])
        net = r.w12[...]
        for step in range(zpeers):
            net = net + r.w12_z[step]
        r.w12_sum[...] = net
        small_send(1, lambda to: r.w12_sum, lambda at: r.w12_plane.at[at])
        small_wait(0, lambda at: r.w3_land.at[at])
        part = r.sum_w3[span(b, w3_rows), :]
        for at in range(peers):
            part = part + r.w3_land[at]
        r.w3_part[...] = part
        r.w3_all[z, span(b, w3_rows), :] = part
        small_send(2, lambda to: r.w3_part, lambda at: r.w3_all.at[z, span(b, w3_rows)])
        reduce_next(0, down_refs)
        gather_local(1, r.turn).wait()
        gather_finish(1)
        drain(("forward", 1))
        pool = pool_turned(r.n2_land)
        small_wait(1, lambda at: r.w12_plane.at[at])
        net = r.w12_sum[...]
        for at in range(peers):
            net = net + r.w12_plane[at]
        r.grad_w1[...] = net[:emb, :filt]
        r.grad_w2[...] = net[net_at:, :filt]
        for at in range(peers):
            dst = r.w3_all.at[z, span(group_at(groups - 1 - at), w3_rows)]
            small_copy(2, dst, dst, at, group_at(groups - 1 - at)).wait_recv()
        small_z_send(1, r.w3_all.at[z], lambda step: r.w3_all.at[z])
        for copy in pool:
            copy.wait()
        wait_plane(1, lambda at: r.pre_own.at[span(at, tokens)])
        reduce_send(1, up_refs, turned_part(r.pre_own))
        win_loads = [(block, load_win(block)) for block in range(3)]
        for way in range(chips - 1):
            in_copy(way).wait_recv()
        total = r.in_own[...]
        for step in range(chips - 1):
            total = total + r.in_land[step].astype(F32)
        r.in_own[...] = total

        def in_spread(step, part, block, to):
            src = r.in_own.at[span(to, rows_out), part * own : (part + 1) * own]
            dst = r.grad_w_in.at[:, pl.ds(pl.multiple_of(part * width + block * own, own), own)]
            if step == 0:
                return pltpu.make_async_copy(src, dst, r.load_sem.at[10 + part])
            return remote(src, dst, r.ti_s.at[step - 1, part], r.ti_r.at[step - 1, part], seq=to)

        for part in range(3):
            for step in range(1, blocks):
                send("in_spread", in_spread(step, part, z, block_at(step)))
            in_spread(0, part, z, z).start()
        for _, copy in win_loads:
            copy.wait()
        r.gn2[...] = mm_nt(r.gproj[:, :width], r.win[0])
        r.gn2[...] += mm_nt(r.gproj[:, width : 2 * width], r.win[1])
        r.gn2[...] += mm_nt(r.gproj[:, 2 * width :], r.win[2])

        reduce_next(1, up_refs)
        def norm1_back(at, total):
            rows = pl.ds(pl.multiple_of(at * 32, 32), 32)
            grad, inverse = r.gn2[rows, :], r.inv1[rows, 0:1]
            xhat = (r.tok[rows, :].astype(F32) - r.mean1[rows, 0:1]) * inverse
            r.res[rows, :] = r.gres[rows, :] + norm_back(grad, r.gain1[...], xhat, inverse)
            return total + jnp.sum((grad * xhat).reshape(4, 8, width), axis=0)

        total = lax.fori_loop(0, tokens // 32, norm1_back, jnp.zeros((8, width), F32))
        r.sum_gain1[...] = jnp.sum(total, axis=0, keepdims=True)
        r.small_send[...] = jnp.zeros((groups, 16, share), F32)
        for group in range(groups):
            cols = slice(group * share, (group + 1) * share)
            r.small_send[group, 0:1, :] = r.sum_gain1[:, cols]
            r.small_send[group, 1:2, :] = r.sum_gain2[:, cols]
            r.small_send[group, 2:3, :] = r.sum_bias[:, cols]
            for lag in range(3):
                for third in range(3):
                    at = group * inc + third * share
                    row = 3 + 3 * lag + third
                    r.small_send[group, row : row + 1, :] = r.sum_short[lag : lag + 1, at : at + share]
        small_send(3, lambda to: r.small_send.at[to], lambda at: r.small_land.at[b])
        r.small_land[b] = r.small_send[b]
        store_tokens = load(r.local_sem.at[13], r.res, r.tokens_grad)
        reduce_finish(0, down_refs)
        store_down = load(r.local_sem.at[9], down_refs[4], r.grad_w_down)
        for way in range(chips - 1):
            out_copy(way).wait_recv()
        total = r.xhat2[share : 2 * share, :]
        for step in range(chips - 1):
            total = total + r.out_land[step].astype(F32)
        r.xhat2[share : 2 * share, :] = total
        r.outz_send[...] = total.astype(BF16)
        for step in range(1, blocks):
            send("outz", outz_copy(step, block_at(step)))
        r.outz_own[...] = r.xhat2[pl.ds(pl.multiple_of(share + z * rows_out, rows_out), rows_out), :]

        for at in range(peers):
            source = group_at(groups - 1 - at)
            dst = r.small_land.at[source]
            small_copy(3, dst, dst, at, source).wait_recv()
        small = r.small_land[0]
        for group in range(1, groups):
            small = small + r.small_land[group]
        r.small_sum[...] = small
        small_z_send(2, r.small_sum, lambda step: r.small_z.at[step - 1])
        reduce_finish(1, up_refs)
        spread_up = spread(0, up_refs[4], r.grad_w_up, ffc)
        for step in range(1, blocks):
            outz_copy(step, block_at(blocks - step)).wait_recv()
        total = r.outz_own[...]
        for step in range(zpeers):
            total = total + r.outz_land[step].astype(F32)
        r.outz_own[...] = total
        store_out = load(r.local_sem.at[11], r.outz_own, r.grad_w_out)
        def chosen(value, size):
            picked = value[:, :size]
            for block in range(1, blocks):
                picked = jnp.where(z == block, value[:, block * size : (block + 1) * size], picked)
            return picked

        for step in range(1, blocks):
            source = block_at(blocks - step)
            dst = r.w3_all.at[source]
            small_z_copy(1, dst, dst, step, source).wait_recv()
        third = r.w3_all[lax.div(b * share, own)]
        halves = own // share
        picked = third[:, :share]
        for half in range(1, halves):
            here = lax.rem(b, halves) == half
            picked = jnp.where(here, third[:, half * share : (half + 1) * share], picked)
        r.grad_w3[...] = chosen(picked, rows_out)
        small_z_wait(2, lambda step: r.small_z.at[step - 1])
        small = r.small_sum[...]
        for step in range(zpeers):
            small = small + r.small_z[step]
        r.grad_gain1[...] = chosen(small[0:1], rows_out)
        r.grad_gain2[...] = chosen(small[1:2], rows_out)
        r.grad_bias[...] = chosen(small[2:3], rows_out)
        for lag in range(3):
            for third in range(3):
                row = 3 + 3 * lag + third
                r.short_all[lag : lag + 1, third * share : (third + 1) * share] = small[row : row + 1]
        r.grad_short[...] = chosen(r.short_all[0:3, :], 3 * rows_out)
        spread_finish(0, spread_up, r.grad_w_up, ffc)
        for part in range(3):
            for step in range(1, blocks):
                source = block_at(blocks - step)
                in_spread(step, part, source, source).wait_recv()
            in_spread(0, part, z, z).wait()
        store_layer.wait()
        store_down.wait()
        store_out.wait()
        store_tokens.wait()
        for key in list(sent):
            drain(key)

    def call(args):
        result = pl.pallas_call(
            kernel,
            out_shape=[jax.ShapeDtypeStruct(shape, dtype) for shape, dtype, _ in outputs.values()],
            in_specs=[pl.BlockSpec(memory_space=space) for space in inputs.values()],
            out_specs=[pl.BlockSpec(memory_space=space) for *_, space in outputs.values()],
            scratch_shapes=list(scratch.values()),
            compiler_params=pltpu.CompilerParams(
                collective_id=0, has_side_effects=True, vmem_limit_bytes=KERNEL_VMEM
            ),
        )(*[args[name] for name in inputs])
        return settled(result[:13])

    return call


def settled(values):
    count = len(values)
    large = [at for at, value in enumerate(values) if value.size >= 1 << 15]

    def copy_all(*refs):
        sources, targets, held = refs[:count], refs[count : 2 * count], refs[2 * count : -1]
        sems = refs[-1]
        copies = [
            pltpu.make_async_copy(sources[at], held[k], sems.at[0, k]) for k, at in enumerate(large)
        ]
        for copy in copies:
            copy.start()
        for at in range(count):
            if at not in large:
                if at == count - 1:
                    targets[at][...] = sources[at][...].T
                else:
                    targets[at][...] = sources[at][...].reshape(targets[at].shape)
        stores = []
        for k, at in enumerate(large):
            copies[k].wait()
            stores.append(pltpu.make_async_copy(held[k], targets[at], sems.at[1, k]))
            stores[-1].start()
        for copy in stores:
            copy.wait()

    specs = [
        pl.BlockSpec(memory_space=pl.ANY if at in large else pltpu.VMEM) for at in range(count)
    ]
    return pl.pallas_call(
        copy_all,
        out_shape=[
            jax.ShapeDtypeStruct(value.shape[1:] if value.shape[0] == 1 else value.shape, value.dtype)
            for value in values[:-1]
        ]
        + [jax.ShapeDtypeStruct(values[-1].shape[::-1], values[-1].dtype)        ],
        in_specs=specs,
        out_specs=specs,
        scratch_shapes=[pltpu.VMEM(values[at].shape, values[at].dtype) for at in large]
        + [pltpu.SemaphoreType.DMA((2, len(large)))],
    )(*values)


def small_sums(gain1, bias, gain2, short, w1, w2, w3_own):
    blocks, position = lax.axis_size("seq"), lax.axis_index("seq")
    dests = lax.axis_size("batch") * blocks
    width, (filt_dim, own), emb = gain1.shape[0], w3_own.shape, w1.shape[0]
    w3_all = lax.dynamic_update_slice_in_dim(
        jnp.zeros((filt_dim, width), F32), w3_own, position * own, 1
    )
    share = width // dests
    small = jnp.concatenate(
        [
            gain1.reshape(dests, share),
            bias.reshape(dests, share),
            gain2.reshape(dests, share),
            short.reshape(3, dests, 3 * share).transpose(1, 0, 2).reshape(dests, 9 * share),
            w3_all.reshape(filt_dim, dests, share).transpose(1, 0, 2).reshape(dests, filt_dim * share),
        ],
        axis=1,
    )
    small = scatter_sum(small, wire=F32)[0]
    filters = all_sum(jnp.concatenate([w1, w2], axis=0))
    return (
        small[:share],
        small[3 * share : 12 * share].reshape(3, 3 * share),
        filters[:emb],
        filters[emb:],
        small[12 * share :].reshape(filt_dim, share),
        small[share : 2 * share],
        small[2 * share : 3 * share],
    )


def kernel_layer(
    tokens,
    norm_gain1,
    w_in,
    short_kernel,
    filt_w1,
    filt_w2,
    filt_w3,
    decay_rate,
    conv_bias,
    w_out,
    norm_gain2,
    w_up,
    w_down,
    cotangent,
):
    _, block_len, width = tokens.shape
    groups, blocks = lax.axis_size("batch"), lax.axis_size("seq")
    emb, filt = filt_w1.shape
    (cosine, sine), phase = symmetric_tables(block_len * blocks)
    features = lag_features(emb, block_len * blocks)
    call = kernel_plan(groups, blocks, block_len, width, w_up.shape[1], filt, emb)
    out = call(
        dict(
            tokens=tokens[0],
            cot=cotangent[0],
            w_in=w_in,
            w_out=w_out,
            w_up=w_up,
            w_down=w_down,
            cosine=jnp.asarray(cosine),
            sine=jnp.asarray(sine),
            filt_w3=filt_w3,
            decay=decay_rate[None],
            gain1=norm_gain1[None],
            gain2=norm_gain2[None],
            bias=conv_bias[None],
            short=short_kernel,
            filt_w1=filt_w1,
            filt_w2=filt_w2,
            features_t=jnp.asarray(features.T),
            phase=jnp.asarray(phase),
        )
    )
    layer_out, tokens_grad, w_in, w_out, w_up, w_down, gain1, gain2, bias, short, w1, w2, w3 = out
    return layer_out[None], tokens_grad[None], (gain1, short, w1, w2, w3.T, bias, gain2), (w_in, w_out, w_up, w_down)


def on_device(*args):
    tokens = args[0]
    fits = lax.axis_size("batch") == 8 and lax.axis_size("seq") == 4 and tokens.shape[1] * lax.axis_size("seq") <= 1024
    layer = kernel_layer if fits else plain_layer
    layer_out, tokens_grad, small, large = layer(*args)
    gain1, short, w1, w2, w3, bias, gain2 = small
    grad_w_in, grad_w_out, grad_w_up, grad_w_down = large
    return (
        layer_out, tokens_grad, gain1, grad_w_in, short, w1, w2, w3, bias, grad_w_out, gain2,
        grad_w_up, grad_w_down,
    )


def solution(mesh):
    split = P("batch", "seq", None)
    both = ("batch", "seq")
    return jax.shard_map(
        on_device,
        mesh=mesh,
        in_specs=(split,) + (P(),) * 12 + (split,),
        out_specs=(
            split,
            split,
            P(both),
            P(both, None),
            P(None, both),
            P(),
            P(),
            P(None, both),
            P(both),
            P(both, None),
            P(both),
            P(both, None),
            P(both, None),
        ),
        check_vma=False,
    )
```

```python
import math

import jax
import jax.numpy as jnp
import ml_dtypes
import numpy as np
from jax import lax
from jax.experimental import pallas as pl
from jax.experimental.pallas import tpu as pltpu
from jax.sharding import PartitionSpec as P

F32 = jnp.float32
BF16 = jnp.bfloat16
HIGHEST = lax.Precision.HIGHEST
GELU_SCALE = math.sqrt(2.0 / math.pi)
GELU_CUBIC = 0.044715


def dot(left, right, contract, out=F32, precision=None):
    return lax.dot_general(
        left, right, (contract, ((), ())), precision=precision, preferred_element_type=F32
    ).astype(out)


def mm(left, right, **kw):
    return dot(left, right, ((1,), (0,)), **kw)


def mm_nt(left, right, **kw):
    return dot(left, right, ((1,), (1,)), **kw)


def mm_tn(left, right, **kw):
    return dot(left, right, ((0,), (0,)), **kw)


def shifted(value, axis, steps):
    count = lax.axis_size(axis)
    first, last = (max(0, -steps), min(count, count - steps))
    return lax.ppermute(value, axis, [(source, source + steps) for source in range(first, last)])


def exchange(value, axis, bit):
    count = lax.axis_size(axis)
    return lax.ppermute(value, axis, [(at, at ^ (1 << bit)) for at in range(count)])


def bits_of(axis):
    return lax.axis_size(axis).bit_length() - 1


def stage_order(swap):
    batch_bits, seq_bits = bits_of("batch"), bits_of("seq")
    rest = list(range(1, batch_bits))
    half = len(rest) // 2
    if swap:
        rest = rest[half:] + rest[:half]
    return [("batch", bit) for bit in [0] + rest] + [("seq", bit) for bit in range(seq_bits)]


def scatter_sum(partial, swap=False, wire=BF16):
    batch_bits, seq_bits = bits_of("batch"), bits_of("seq")
    dims = [("batch", bit) for bit in reversed(range(batch_bits))]
    dims += [("seq", bit) for bit in reversed(range(seq_bits))]
    rows = partial.shape[0] >> len(dims)
    value = partial.reshape((2,) * len(dims) + (rows,) + partial.shape[1:]).astype(wire)
    for axis, bit in stage_order(swap):
        at = dims.index((axis, bit))
        mine = (lax.axis_index(axis) >> bit) & 1
        keep = lax.dynamic_index_in_dim(value, mine, at, keepdims=False)
        send = lax.dynamic_index_in_dim(value, 1 - mine, at, keepdims=False)
        got = exchange(send, axis, bit)
        value = keep.astype(F32) + got.astype(F32)
        dims.pop(at)
        if dims:
            value = value.astype(wire)
    return value


def gather_batch(value):
    return lax.all_gather(value, "batch", axis=0, tiled=True)


def columns_batch(value):
    return lax.all_to_all(value, "batch", 1, 0, tiled=True)


def rows_sum(left_own, right_all):
    blocks = lax.axis_size("seq")
    part = mm_tn(left_own, right_all, out=BF16)
    got = lax.all_to_all(part.reshape(blocks, -1, part.shape[1]), "seq", 0, 0, tiled=True)
    return jnp.sum(got.astype(F32), axis=0)


def columns_sum(left_all, right_own):
    blocks, groups = lax.axis_size("seq"), lax.axis_size("batch")
    part = mm_tn(left_all, right_own, out=BF16)
    part = part.reshape(groups * blocks, -1, part.shape[1])
    got = lax.all_to_all(part, ("batch", "seq"), 0, 0, tiled=True)
    got = jnp.sum(got.reshape(groups, blocks, -1, part.shape[2]).astype(F32), axis=1)
    return got.transpose(1, 0, 2).reshape(got.shape[1], -1)


def all_sum(value):
    for axis, bit in stage_order(False):
        value = value + exchange(value, axis, bit)
    return value


def norm_parts(values):
    centered = values - jnp.mean(values, axis=-1, keepdims=True)
    inverse = lax.rsqrt(jnp.mean(centered * centered, axis=-1, keepdims=True) + 1e-05)
    return centered * inverse, inverse


def norm_back(grad, gain, xhat, inverse):
    scaled = grad * gain
    return (
        scaled
        - jnp.mean(scaled, axis=-1, keepdims=True)
        - xhat * jnp.mean(scaled * xhat, axis=-1, keepdims=True)
    ) * inverse


def transform_table(length):
    count = np.arange(length, dtype=np.int64)
    turns = (2 * count[:, None] + 1) * count[None, :] % (4 * length)
    angles = turns.astype(np.float64) * (2.0 * np.pi / (4 * length))
    table = np.concatenate([np.cos(angles), -np.sin(angles)], axis=0)
    return table.astype(np.float32).astype(ml_dtypes.bfloat16)


def lag_features(emb, length):
    bands = (emb - 1) // 2
    lag = np.arange(length, dtype=np.float64)
    freq = 1e-4 + np.arange(bands, dtype=np.float64) * ((bands - 1 - 1e-4) / (bands - 1))
    phases = (lag * (2.0 * np.pi / length))[:, None] * freq[None, :]
    return np.concatenate(
        [(lag / (length - 1))[:, None], np.cos(phases), -np.sin(phases)], axis=1
    ).astype(np.float32)


def to_channels(value):
    return lax.all_to_all(value, "seq", 1, 0, tiled=True)


def to_tokens(value):
    return lax.all_to_all(value, "seq", 0, 1, tiled=True)


def plain_layer(
    tokens,
    norm_gain1,
    w_in,
    short_kernel,
    filt_w1,
    filt_w2,
    filt_w3,
    decay_rate,
    conv_bias,
    w_out,
    norm_gain2,
    w_up,
    w_down,
    cotangent,
):
    num_seqs, block_len, width = tokens.shape
    assert num_seqs == 1
    blocks = lax.axis_size("seq")
    position = lax.axis_index("seq")
    seq_len = block_len * blocks
    own = width // blocks
    table = jnp.asarray(transform_table(seq_len))
    features = jnp.asarray(lag_features(filt_w1.shape[0], seq_len))
    cot = cotangent[0]
    cot_all = gather_batch(cot)
    inputs = tokens[0].astype(F32)

    xhat1, inverse1 = norm_parts(inputs)
    normed1 = (xhat1 * norm_gain1).astype(BF16)
    normed1_all = gather_batch(normed1)
    projected = mm(normed1, w_in, out=BF16)
    earlier = shifted(projected[block_len - 2 :], "seq", 1)
    extended = jnp.concatenate([earlier, projected], axis=0).astype(F32)
    taps3 = short_kernel.astype(F32)
    lags = [extended[2 - lag : 2 - lag + block_len] for lag in range(3)]
    mixed = taps3[0] * lags[0] + taps3[1] * lags[1] + taps3[2] * lags[2]
    gate_out = mixed[:, :width]
    gate_in = mixed[:, width : 2 * width]
    values = mixed[:, 2 * width :]
    signal = (values * gate_in).astype(BF16)

    w3_own = lax.dynamic_slice_in_dim(filt_w3, position * own, own, 1)
    decay_own = lax.dynamic_slice_in_dim(decay_rate, position * own, own, 0)
    angle1 = mm(features, filt_w1, precision=HIGHEST)
    hidden1, slope1 = jnp.sin(angle1), jnp.cos(angle1)
    angle2 = mm(hidden1, filt_w2, precision=HIGHEST)
    hidden2, slope2 = jnp.sin(angle2), jnp.cos(angle2)
    lag_index = jnp.arange(seq_len).astype(F32)
    fading = jnp.exp(-decay_own[None, :] * lag_index[:, None])
    taps = (mm(hidden2, w3_own, precision=HIGHEST) * fading).astype(BF16)
    taps_spec = mm(table, taps)
    taps_re, taps_im = taps_spec[:seq_len], taps_spec[seq_len:]

    signal_spec = mm(table, to_channels(signal))
    signal_re, signal_im = signal_spec[:seq_len], signal_spec[seq_len:]
    scale = 1.0 / seq_len

    def inverse_of(real, imag):
        both = (jnp.concatenate([real, imag], axis=0) * scale).astype(BF16)
        return mm_tn(table, both)

    conv = inverse_of(
        taps_re * signal_re - taps_im * signal_im, taps_re * signal_im + taps_im * signal_re
    )
    long_out = to_tokens(conv.astype(BF16)).astype(F32) + conv_bias * signal.astype(F32)
    gated = (long_out * gate_out).astype(BF16)
    gated_all = gather_batch(gated)
    residual1 = inputs + mm(gated, w_out)
    xhat2, inverse2 = norm_parts(residual1)
    normed2 = (xhat2 * norm_gain2).astype(BF16)
    normed2_all = gather_batch(normed2)
    pre = mm(normed2, w_up)
    bent = jnp.tanh(GELU_SCALE * (pre + GELU_CUBIC * pre * pre * pre))
    hidden = (0.5 * pre * (1.0 + bent)).astype(BF16)
    layer_out = (residual1 + mm(hidden, w_down)).astype(BF16)

    slope = 0.5 * (1.0 + bent) + 0.5 * pre * (1.0 - bent * bent) * GELU_SCALE * (
        1.0 + 3.0 * GELU_CUBIC * pre * pre
    )
    grad_pre = (mm_nt(cot, w_down) * slope).astype(BF16)
    grad_w_down = rows_sum(columns_batch(hidden), cot_all)
    grad_w_up = columns_sum(normed2_all, columns_batch(grad_pre))
    grad_norm2 = mm_nt(grad_pre, w_up)
    grad_gain2 = jnp.sum(grad_norm2 * xhat2, axis=0)
    grad_res = cot.astype(F32) + norm_back(grad_norm2, norm_gain2, xhat2, inverse2)
    grad_branch = grad_res.astype(BF16)
    grad_w_out = columns_sum(gated_all, columns_batch(grad_branch))
    grad_gated = mm_nt(grad_branch, w_out)
    grad_long = (grad_gated * gate_out).astype(BF16)
    grad_gate_out = grad_gated * long_out
    grad_bias = jnp.sum(grad_long.astype(F32) * signal.astype(F32), axis=0)

    grad_spec = mm(table, to_channels(grad_long))
    grad_re, grad_im = grad_spec[:seq_len], grad_spec[seq_len:]
    grad_conv = inverse_of(
        taps_re * grad_re + taps_im * grad_im, taps_re * grad_im - taps_im * grad_re
    )
    grad_signal = to_tokens(grad_conv.astype(BF16)).astype(F32) + conv_bias * grad_long.astype(F32)
    grad_taps = inverse_of(
        signal_re * grad_re + signal_im * grad_im, signal_re * grad_im - signal_im * grad_re
    )
    grad_filt = grad_taps * fading
    grad_w3_own = mm_tn(hidden2, grad_filt)
    grad_angle2 = mm_nt(grad_filt, w3_own) * slope2
    grad_w2 = mm_tn(hidden1, grad_angle2)
    grad_angle1 = mm_nt(grad_angle2, filt_w2) * slope1
    grad_w1 = mm_tn(features, grad_angle1)

    grad_mixed = jnp.concatenate(
        [grad_gate_out, grad_signal * values, grad_signal * gate_in], axis=1
    )
    later = shifted(grad_mixed[:2], "seq", -1)
    grad_ext = jnp.concatenate([grad_mixed, later], axis=0)
    grad_proj = (
        taps3[0] * grad_ext[:block_len]
        + taps3[1] * grad_ext[1 : block_len + 1]
        + taps3[2] * grad_ext[2:]
    ).astype(BF16)
    grad_short = jnp.stack([jnp.sum(grad_mixed * lag, axis=0) for lag in lags])
    grad_w_in = columns_sum(normed1_all, columns_batch(grad_proj))
    grad_norm1 = mm_nt(grad_proj, w_in)
    grad_gain1 = jnp.sum(grad_norm1 * xhat1, axis=0)
    tokens_grad = grad_res + norm_back(grad_norm1, norm_gain1, xhat1, inverse1)

    return layer_out[None], tokens_grad[None], small_sums(
        grad_gain1, grad_bias, grad_gain2, grad_short, grad_w1, grad_w2, grad_w3_own
    ), (grad_w_in, grad_w_out, grad_w_up, grad_w_down)


MESH = pl.DeviceIdType.MESH
KERNEL_VMEM = 63 * 1024 * 1024
PART_BYTES = 96 * 1024


def symmetric_tables(length):
    odd = 2 * np.arange(length, dtype=np.int64) + 1
    angles = (odd[:, None] * odd[None, :] % (8 * length)).astype(np.float64) * (
        np.pi / (4 * length)
    )
    phase = odd.astype(np.float64) * (np.pi / (4 * length))
    tables = [np.cos(angles), np.sin(angles)]
    tables = [t.astype(np.float32).astype(ml_dtypes.bfloat16) for t in tables]
    return tables, np.stack([np.cos(phase), np.sin(phase)], axis=1).astype(np.float32)


def sin_cos(x):
    turns = jnp.floor(x * (2.0 / np.pi) + 0.5)
    rest = ((x - turns * 1.5703125) - turns * 4.837512969970703e-4) - turns * 7.54978995489188e-8
    square = rest * rest
    sine = rest + rest * square * (
        -1.6666654611e-1 + square * (8.3321608736e-3 - square * 1.9515295891e-4)
    )
    cosine = (1.0 - 0.5 * square) + square * square * (
        4.166664568298827e-2 + square * (-1.388731625493765e-3 + square * 2.443315711809948e-5)
    )
    quarter = turns - 4.0 * jnp.floor(turns * 0.25)
    odd = (quarter == 1.0) | (quarter == 3.0)
    sin_sign = jnp.where(quarter >= 2.0, -1.0, 1.0)
    cos_sign = jnp.where((quarter == 1.0) | (quarter == 2.0), -1.0, 1.0)
    return sin_sign * jnp.where(odd, cosine, sine), cos_sign * jnp.where(odd, sine, cosine)


class InParts:
    def __init__(self, src, dst, send_sem, recv_sem, where):
        self.refs, self.sems, self.where = (src, dst), (send_sem, recv_sem), where

    def whole(self):
        return self.part(*self.refs)

    def part(self, src, dst):
        return pltpu.make_async_remote_copy(
            src_ref=src,
            dst_ref=dst,
            send_sem=self.sems[0],
            recv_sem=self.sems[1],
            device_id=self.where,
            device_id_type=MESH,
        )

    def start(self):
        src, dst = self.refs
        shape, size = src.shape, math.prod(src.shape) * jnp.dtype(src.dtype).itemsize
        want = max(1, min(8, size // PART_BYTES))
        lead = shape[0] if len(shape) == 3 else 1
        outer = max(count for count in range(1, lead + 1) if lead % count == 0 and count <= want)
        inner = 1
        while outer * inner * 2 <= want and shape[-2] % (inner * 2 * 16) == 0:
            inner *= 2
        rows = shape[-2] // inner
        for first in range(outer):
            for second in range(inner):
                at = (pl.ds(second * rows, rows),)
                if len(shape) == 3:
                    at = (pl.ds(first * (lead // outer), lead // outer), *at)
                self.part(src.at[at], dst.at[at]).start()

    def wait_send(self):
        self.whole().wait_send()

    def wait_recv(self):
        self.whole().wait_recv()


class Named:
    def __init__(self, names, refs):
        assert len(names) == len(refs)
        for name, ref in zip(names, refs):
            setattr(self, name, ref)


def kernel_plan(groups, blocks, tokens, width, hidden, filt, emb):
    length = tokens * blocks
    own = width // blocks
    ffc = hidden // groups
    share = width // groups
    rows_out = share // blocks
    inc = 3 * share
    spare = 16
    chips = groups // 2
    down_rows = ffc // blocks
    net_at = -(-emb // 8) * 8
    net_rows = net_at + filt
    peers, zpeers = groups - 1, blocks - 1
    vm, hbm = pltpu.VMEM, pl.ANY
    inputs = dict(
        tokens=hbm, cot=hbm, w_in=hbm, w_out=hbm, w_up=hbm, w_down=hbm,
        cosine=hbm, sine=hbm, filt_w3=hbm, decay=hbm,
        gain1=vm, gain2=vm, bias=vm, short=vm, filt_w1=vm, filt_w2=vm,
        features_t=vm, phase=vm,
    )
    outputs = dict(
        layer_out=((tokens, width), BF16, hbm),
        tokens_grad=((tokens, width), F32, hbm),
        grad_w_in=((rows_out, 3 * width), F32, hbm),
        grad_w_out=((rows_out, width), F32, hbm),
        grad_w_up=((rows_out, hidden), F32, hbm),
        grad_w_down=((ffc // blocks, width), F32, hbm),
        grad_gain1=((1, rows_out), F32, vm),
        grad_gain2=((1, rows_out), F32, vm),
        grad_bias=((1, rows_out), F32, vm),
        grad_short=((3, 3 * rows_out), F32, vm),
        grad_w1=((emb, filt), F32, vm),
        grad_w2=((filt, filt), F32, vm),
        grad_w3=((filt, rows_out), F32, vm),
        cot_land=((2, groups // 2 * tokens, width), BF16, hbm),
        n2_land=((groups, width, tokens), BF16, hbm),
    )
    dma = pltpu.SemaphoreType.DMA
    scratch = dict(
        tok=vm((tokens, width), BF16), cotv=vm((tokens, width), BF16),
        mean1=vm((tokens, 128), F32), inv1=vm((tokens, 128), F32),
        n1_all=vm((length, width), BF16), turn=vm((width, tokens), BF16),
        gated_turn=vm((width, tokens), BF16), gated_pair=vm((width // 2, 2 * tokens), BF16),
        hid_buf=vm((tokens, ffc), BF16),
        ghalo=vm((8, 3 * width), F32), ghalo_in=vm((8, 3 * width), F32), tail=vm((16, 3 * width), F32),
        ext_c=vm((length + 32, 3 * own), BF16), gproj_c=vm((length, 3 * own), BF16),
        gconv_c=vm((length + 16, own), BF16), glong_c=vm((length + 16, own), BF16),
        ggb=vm((tokens, width), BF16),
        win=vm((3, width, width), BF16), wout=vm((width, width), BF16),
        cs=vm((length, length), BF16), sn=vm((length, length), BF16),
        ext=vm((tokens + 16, 3 * width), BF16),
        halo_out=vm((16, 3 * width), BF16), halo_in=vm((16, 3 * width), BF16),
        gate_out=vm((tokens, width), F32),
        sig=vm((tokens, width), BF16), chan=vm((length + 16, own), BF16),
        w3=vm((filt, own), F32), fade=vm((1, own), F32),
        h1=vm((filt, length), F32), s1=vm((filt, length), F32),
        h2=vm((filt, length), F32), s2=vm((filt, length), F32),
        sum_gain1=vm((1, width), F32), sum_gain2=vm((1, width), F32),
        sum_bias=vm((1, width), F32), sum_short=vm((3, 3 * width), F32),
        small_send=vm((groups, 16, share), F32), small_land=vm((groups, 16, share), F32),
        small_sum=vm((16, share), F32), small_z=vm((zpeers, 16, share), F32),
        short_all=vm((8, inc), F32),
        w12=vm((net_rows, 128), F32), w12_z=vm((zpeers, net_rows, 128), F32),
        w12_sum=vm((net_rows, 128), F32), w12_plane=vm((peers, net_rows, 128), F32),
        sum_w3=vm((filt, own), F32), w3_land=vm((peers, filt // groups, own), F32),
        w3_part=vm((filt // groups, own), F32), w3_all=vm((blocks, filt, own), F32),
        hre=vm((length, own), F32), him=vm((length, own), F32),
        xre=vm((length, own), F32), xim=vm((length, own), F32),
        yre=vm((length, own), BF16), yim=vm((length, own), BF16),
        qre=vm((length, own), BF16), qim=vm((length, own), BF16),
        conv_out=vm((length + 16, own), BF16), conv_in=vm((blocks, tokens, own), BF16),
        long=vm((tokens, width), F32), half=vm((tokens, width), BF16),
        res=vm((tokens, width), F32), xhat2=vm((tokens, width), F32),
        inv2=vm((tokens, 128), F32), gn2=vm((tokens, width), F32),
        gres=vm((tokens, width), F32),
        hid_send=vm((groups, ffc, tokens), BF16), hid_own=vm((ffc, groups * tokens), BF16),
        pre_send=vm((groups, tokens, ffc), BF16), pre_own=vm((groups * tokens, ffc), BF16),
        gbr_pair=vm((2 * tokens, width), BF16),
        glong=vm((tokens, width), BF16),
        gproj=vm((tokens, 3 * width), BF16),
        down_send=vm((2, down_rows, width), BF16), down_land=vm((2, down_rows, width), BF16),
        down_next=vm((down_rows, width), BF16), down_last=vm((down_rows, width), BF16),
        up_send=vm((2, own, ffc), BF16), up_land=vm((2, own, ffc), BF16),
        up_next=vm((own, ffc), BF16), up_last=vm((own, ffc), BF16),
        in_send=vm((chips, share, 3 * own), BF16), in_pair=vm((chips, share, 3 * own), BF16),
        in_land=vm((chips - 1, share, 3 * own), BF16), in_own=vm((share, 3 * own), F32),
        out_send=vm((chips - 1, share, width), BF16), out_land=vm((chips - 1, share, width), BF16),
        outz_send=vm((share, width), BF16), outz_land=vm((zpeers, rows_out, width), BF16),
        outz_own=vm((rows_out, width), F32),
        load_sem=dma((16,)),
        pool_sem=dma((groups,)),
        win_sem=dma((3,)),
        ffn_sem=dma((2, 2)),
        local_sem=dma((16,)),
        stage_sem=dma((chips - 1,)),
        ag_s=dma((2, groups - 1)), ag_r=dma((2, groups - 1)),
        halo_s=dma((2,)), halo_r=dma((2,)),
        za_s=dma((4, zpeers)), za_r=dma((4, zpeers)),
        pa_s=dma((2, peers)), pa_r=dma((2, peers)),
        cx_s=dma((3,)), cx_r=dma((3,)), zg_s=dma((zpeers,)), zg_r=dma((zpeers,)),
        wi_s=dma((chips - 1,)), wi_r=dma((chips - 1,)), ti_s=dma((zpeers, 3)), ti_r=dma((zpeers, 3)), wo_s=dma((2, chips - 1)), wo_r=dma((2, chips - 1)),
        rs_s=dma((2, 2)), rs_r=dma((2, 2)),
        sm_s=dma((4, peers)), sm_r=dma((4, peers)),
        sz_s=dma((3, zpeers)), sz_r=dma((3, zpeers)),
        tr_s=dma((1, peers)), tr_r=dma((1, peers)),
    )
    names = [*inputs, *outputs, *scratch]

    def kernel(*refs):
        r = Named(names, refs)
        b, z = lax.axis_index("batch"), lax.axis_index("seq")
        chip, core = lax.div(b, 2), lax.rem(b, 2)
        sibling = chip * 2 + (1 - core)
        sent = {}

        chip_x, chip_y = lax.rem(chip, 2), lax.div(chip, 2)

        def flipped(turn_x, turn_y):
            x = chip_x + turn_x - 2 * chip_x * turn_x
            y = chip_y + turn_y - 2 * chip_y * turn_y
            return y * 2 + x

        def partner(way):
            return flipped(1 - way % 2, (way + 1) // 2)

        def way_of(step):
            return 2 if step == 2 else step + core - 2 * step * core

        def partner_at(way):
            return flipped(1 - lax.rem(way, 2), lax.div(way + 1, 2))

        def peer(at):
            at = jnp.int32(at)
            late, last = lax.div(at, 4), lax.div(at, 6)
            way = (1 - late) * lax.rem(at + core, 2) + late * 2
            to_core = (1 - late) * lax.div(at, 2) + late * (at - 4)
            to_chip = flipped((1 - last) * (1 - lax.rem(way, 2)), (1 - last) * lax.div(way + 1, 2))
            own_chip = (7 - at) * (1 - core) + (at - 6) * core
            group = to_chip * 2 + (1 - last) * to_core + last * own_chip
            return group, (1 - last) * (way * 2 + to_core) + last * 6, (1 - last) * (way * 2 + core) + last * 6

        def group_at(step):
            return lax.rem(b + step, groups)

        def block_at(step):
            return lax.rem(z + step, blocks)

        def span(at, size):
            return pl.ds(pl.multiple_of(at * size, size), size)

        def remote(src, dst, send_sem, recv_sem, **where):
            return InParts(src, dst, send_sem, recv_sem, where)

        def send(key, copy):
            copy.start()
            sent.setdefault(key, []).append(copy)

        def drain(key):
            for copy in sent.pop(key):
                copy.wait_send()

        def tiles(size, total, body):
            def step(i, carry):
                body(pl.multiple_of(i * size, size))
                return carry

            lax.fori_loop(0, total // size, step, 0)

        def load(sem, src, dst):
            copy = pltpu.make_async_copy(src, dst, sem)
            copy.start(priority=1)
            return copy

        def load_win(block):
            return load(r.win_sem.at[block], r.w_in.at[:, pl.ds(block * width, width)], r.win.at[block])

        load_tok = load(r.load_sem.at[0], r.tokens, r.tok)
        win_loads = [(block, load_win(block)) for block in (1, 2, 0)]
        load_cot = load(r.load_sem.at[5], r.cot, r.cotv)
        load_w3 = load(r.load_sem.at[1], r.filt_w3.at[:, span(z, own)], r.w3)
        load_fade = load(r.load_sem.at[2], r.decay.at[:, span(z, own)], r.fade)
        load_cs = load(r.load_sem.at[3], r.cosine, r.cs)
        load_sn = load(r.load_sem.at[4], r.sine, r.sn)
        load_wout = load(r.load_sem.at[6], r.w_out, r.wout)

        barrier = pltpu.get_barrier_semaphore()
        for step in range(1, groups):
            pl.semaphore_signal(barrier, inc=1, device_id={"batch": group_at(step)}, device_id_type=MESH)
        for step in range(1, blocks):
            pl.semaphore_signal(barrier, inc=1, device_id={"seq": block_at(step)}, device_id_type=MESH)

        slots = [
            lambda at: r.cot_land.at[lax.div(at, chips), span(lax.rem(at, chips), tokens)],
            lambda at: r.n2_land.at[at],
        ]

        def gather_copy(k, at, src, slot, to):
            return remote(src, slot, r.ag_s.at[k, at], r.ag_r.at[k, at], batch=to)

        def gather_local(k, src):
            return pltpu.make_async_copy(src, slots[k](b), r.local_sem.at[k])

        def gather_start(k, src):
            for step in range(chips - 1):
                way = way_of(step)
                to = partner_at(jnp.int32(way)) * 2 + core
                send(("ag", k), gather_copy(k, way, src, slots[k](b), to))
            send(("ag", k), gather_copy(k, chips - 1, src, slots[k](b), sibling))
            gather_local(k, src).start(priority=1)

        def stage(k, step):
            if k == 0:
                return r.gproj.at[:, (step - 1) * width : step * width]
            return r.win.at[0, :, (step - 1) * tokens : step * tokens]

        def gather_forward(k):
            staged = []
            for step in range(1, chips):
                slot = slots[k](partner(step - 1) * 2 + core)
                gather_copy(k, step - 1, slot, slot, sibling).wait_recv()
                staged.append((slot, load(r.stage_sem.at[step - 1], slot, stage(k, step))))
            for step, (slot, copy) in enumerate(staged, 1):
                copy.wait()
                source = stage(k, step)
                send(("forward", k), gather_copy(k, chips - 1 + step, source, slot, sibling))

        def gather_finish(k):
            for step in range(chips):
                slot = slots[k]((partner(step - 1) if step else chip) * 2 + 1 - core)
                gather_copy(k, chips - 1 + step, slot, slot, sibling).wait_recv()

        def turned(value_ref, out_ref):
            def body(at):
                tile = value_ref[:, pl.ds(at, share)].T
                group = lax.div(at, share)
                for block in range(blocks):
                    first = pl.multiple_of(block * own + group * rows_out, rows_out)
                    out_ref[pl.ds(first, rows_out), :] = tile[block * rows_out : (block + 1) * rows_out]

            tiles(share, width, body)

        def turned_by_core(value_ref, out_ref):
            def body(at):
                group = lax.div(at, share)
                out_ref[span(lax.rem(group, 2) * chips + lax.div(group, 2), share), :] = value_ref[
                    :, pl.ds(at, share)
                ].T

            tiles(share, width, body)

        load_tok.wait()

        def norm1(at):
            rows = pl.ds(at, 32)
            x = r.tok[rows, :].astype(F32)
            xhat, inverse = norm_parts(x)
            r.mean1[rows, :] = jnp.broadcast_to(jnp.mean(x, axis=-1, keepdims=True), (32, 128))
            r.inv1[rows, :] = jnp.broadcast_to(inverse, (32, 128))
            r.n1_all[pl.ds(pl.multiple_of(z * tokens + at, 32), 32), :] = (xhat * r.gain1[...]).astype(BF16)

        tiles(32, tokens, norm1)
        for block, copy in win_loads:
            copy.wait()
            cols = slice(block * width, (block + 1) * width)
            proj = mm(r.n1_all[span(z, tokens), :], r.win[block], out=BF16)
            r.ext[16:, cols] = proj
            r.halo_out[:, cols] = proj[tokens - 16 :]
        pl.semaphore_wait(barrier, peers + zpeers)
        halo = remote(r.halo_out, r.halo_in, r.halo_s.at[0], r.halo_r.at[0], seq=block_at(1))
        send("halo", halo)
        own_loads = [
            load(
                r.load_sem.at[7 + part],
                r.w_in.at[:, pl.ds(pl.multiple_of(part * width + z * own, own), own)],
                r.win.at[2, :, part * own : (part + 1) * own],
            )
            for part in range(3)
        ]
        for padded in (r.chan, r.conv_out, r.gconv_c, r.glong_c):
            padded[length:, :] = jnp.zeros((spare, own), BF16)
        r.ext_c[0:spare, :] = jnp.zeros((spare, 3 * own), BF16)
        r.ext_c[length + spare :, :] = jnp.zeros((spare, 3 * own), BF16)

        def up_weights(at, slot):
            group = peer(at)[0]
            return pltpu.make_async_copy(
                r.w_up.at[:, span(group, ffc)], r.win.at[0, :, span(slot, ffc)], r.ffn_sem.at[slot, 0]
            )

        def down_weights(at, slot):
            group = peer(at)[0]
            return pltpu.make_async_copy(
                r.w_down.at[span(group, ffc)], r.win.at[1, span(slot, ffc)], r.ffn_sem.at[slot, 1]
            )

        for at in range(2):
            down_weights(at, at).start(priority=1)
            up_weights(at, at).start(priority=1)

        halo.wait_recv()
        r.ext[0:16, :] = (r.halo_in[...].astype(F32) * jnp.where(z > 0, 1.0, 0.0)).astype(BF16)

        def lags_at(cols):
            wide = r.ext[:, cols].astype(F32)
            return [wide[16 - lag : 16 - lag + tokens] for lag in range(3)]

        def mix(cols):
            lags = lags_at(cols)
            short = r.short[:, cols].astype(F32)
            return lags, short[0:1] * lags[0] + short[1:2] * lags[1] + short[2:3] * lags[2]

        def chan_copy(k, src, dst, step, to):
            return remote(src, dst, r.za_s.at[k, step - 1], r.za_r.at[k, step - 1], seq=to)

        def to_channels(k, value_ref, make_cols):
            for step in list(range(1, blocks)) + [0]:
                block = block_at(step)
                make_cols(block)
                if step:
                    src, dst = value_ref.at[:, span(block, own)], r.chan.at[span(z, tokens)]
                    send(("za", k), chan_copy(k, src, dst, step, block))
                else:
                    r.chan[span(z, tokens), :] = value_ref[:, span(block, own)]

        def wait_channels(k):
            for step in range(1, blocks):
                source = block_at(blocks - step)
                dst = r.chan.at[span(source, tokens)]
                chan_copy(k, dst, dst, step, source).wait_recv()

        def signal_block(block):
            def body(at):
                base = block * own + at
                cols = pl.ds(pl.multiple_of(base, 128), 128)
                gate_in = mix(pl.ds(pl.multiple_of(width + base, 128), 128))[1]
                values = mix(pl.ds(pl.multiple_of(2 * width + base, 128), 128))[1]
                r.sig[:, cols] = (values * gate_in).astype(BF16)

            tiles(128, own, body)

        to_channels(0, r.sig, signal_block)
        load_cot.wait()
        gather_start(0, r.cotv)

        load_w3.wait()
        load_fade.wait()

        def fading(at):
            lag = (lax.broadcasted_iota(jnp.int32, (tokens, own), 0) + at).astype(F32)
            return jnp.exp(-r.fade[...] * lag)

        def taps_rows(at):
            rows = pl.ds(at, tokens)
            h1, r.s1[:, rows] = sin_cos(mm_tn(r.filt_w1[...], r.features_t[:, rows], precision=HIGHEST))
            h2, r.s2[:, rows] = sin_cos(mm_tn(r.filt_w2[...], h1, precision=HIGHEST))
            r.h1[:, rows] = h1
            r.h2[:, rows] = h2
            taps = mm_tn(h2, r.w3[...], precision=HIGHEST) * fading(at)
            r.qre[rows, :] = taps.astype(BF16)

        tiles(tokens, length, taps_rows)
        load_cs.wait()
        load_sn.wait()
        scale = 1.0 / length

        def taps_spec(at):
            rows = pl.ds(at, tokens)
            real = mm(r.cs[rows, :], r.qre[...]) * scale
            imag = mm(r.sn[rows, :], r.qre[...]) * -scale
            turn_re, turn_im = r.phase[rows, 0:1], r.phase[rows, 1:2]
            r.hre[rows, :] = real * turn_re - imag * turn_im
            r.him[rows, :] = real * turn_im + imag * turn_re

        tiles(tokens, length, taps_spec)

        wait_channels(0)

        def conv_spec(at):
            rows = pl.ds(at, tokens)
            real = mm(r.cs[rows, :], r.chan[0:length, :])
            imag = -mm(r.sn[rows, :], r.chan[0:length, :])
            r.xre[rows, :] = real
            r.xim[rows, :] = imag
            hre, him = r.hre[rows, :], r.him[rows, :]
            r.yre[rows, :] = (hre * real - him * imag).astype(BF16)
            r.yim[rows, :] = (-(hre * imag + him * real)).astype(BF16)

        tiles(tokens, length, conv_spec)

        def to_tokens(k, out_ref):
            for step in list(range(1, blocks)) + [0]:
                block = block_at(step)
                rows = span(block, tokens)
                tile = (mm(r.cs[rows, :], r.yre[...]) + mm(r.sn[rows, :], r.yim[...])).astype(BF16)
                out_ref[rows, :] = tile
                if step:
                    src, dst = out_ref.at[rows], r.conv_in.at[z]
                    send(("za", k), chan_copy(k, src, dst, step, block))
                else:
                    r.conv_in[z] = tile

        def wait_tokens(k):
            for step in range(1, blocks):
                source = block_at(blocks - step)
                dst = r.conv_in.at[source]
                chan_copy(k, dst, dst, step, source).wait_recv()

        to_tokens(1, r.conv_out)

        def seq_gather(step, source, to):
            rows = r.n1_all.at[span(source, tokens)]
            return remote(rows, rows, r.zg_s.at[step - 1], r.zg_r.at[step - 1], seq=to)

        for step in range(1, blocks):
            send("n1", seq_gather(step, z, block_at(step)))

        load_wout.wait()
        def gate_cols(at):
            cols = pl.ds(at, 128)
            r.gate_out[:, cols] = mix(cols)[1]

        tiles(128, width, gate_cols)

        def grad_hidden(at, carry):
            slot = lax.rem(at, 2)
            down_weights(at, slot).wait()
            r.pre_send[at] = mm_nt(r.cotv[...], r.win[1, span(slot, ffc), :], out=BF16)
            down_weights(lax.rem(at + 2, groups), slot).start(priority=1)
            return carry

        lax.fori_loop(0, groups, grad_hidden, 0)
        wait_tokens(1)

        def conv_cols(at):
            return r.conv_in[
                lax.div(at, own), :, pl.ds(pl.multiple_of(lax.rem(at, own), 128), 128)
            ].astype(F32)

        def long_cols(at):
            cols = pl.ds(at, 128)
            long = conv_cols(at) + r.bias[:, cols] * r.sig[:, cols].astype(F32)
            r.long[:, cols] = long
            r.half[:, cols] = (long * r.gate_out[:, cols]).astype(BF16)

        tiles(128, width, long_cols)
        r.res[...] = mm(r.half[...], r.wout[...])
        turned_by_core(r.half, r.gated_turn)
        mine = span(core, tokens)
        pair_rows = chips * share

        def pair_copy(k, src, dst):
            return remote(src, dst, r.cx_s.at[k], r.cx_r.at[k], batch=sibling)

        gated_copy = pair_copy(
            0, r.gated_turn.at[span(1 - core, pair_rows)], r.gated_pair.at[:, mine]
        )
        send("pair", gated_copy)
        r.gated_pair[:, mine] = r.gated_turn[span(core, pair_rows), :]

        def norm2(at):
            rows = pl.ds(at, 32)
            residual = r.res[rows, :] + r.tok[rows, :].astype(F32)
            r.res[rows, :] = residual
            xhat, inverse = norm_parts(residual)
            r.xhat2[rows, :] = xhat
            r.inv2[rows, :] = jnp.broadcast_to(inverse, (32, 128))
            r.half[rows, :] = (xhat * r.gain2[...]).astype(BF16)

        tiles(32, tokens, norm2)
        turned(r.half, r.turn)
        r.gn2[...] = jnp.zeros((tokens, width), F32)

        def plane_copy(k, src, dst, at):
            to, send_at, recv_at = peer(at)
            return remote(src, dst, r.pa_s.at[k, send_at], r.pa_r.at[k, recv_at], batch=to)

        def hidden_copy(at):
            return plane_copy(0, r.hid_send.at[at], r.hid_own.at[:, span(b, tokens)], at)

        def pre_copy(at):
            return plane_copy(1, r.pre_send.at[at], r.pre_own.at[span(b, tokens)], at)

        def chunk(at, carry):
            slot = lax.rem(at, 2)
            where = span(slot, ffc)
            up_weights(at, slot).wait()
            r.gres[:, 0:ffc] = mm(r.half[...], r.win[0, :, where])

            def act(row):
                rows = pl.ds(row, 32)
                pre = r.gres[rows, 0:ffc]
                square = pre * pre
                bent = jnp.tanh(pre * (GELU_SCALE + GELU_SCALE * GELU_CUBIC * square))
                upper = 0.5 + 0.5 * bent
                slope = upper + pre * (0.5 - 0.5 * bent * bent) * (
                    GELU_SCALE + 3.0 * GELU_SCALE * GELU_CUBIC * square
                )
                r.hid_buf[rows, :] = (pre * upper).astype(BF16)
                r.pre_send[at, rows, :] = (r.pre_send[at, rows, :].astype(F32) * slope).astype(BF16)

            tiles(32, tokens, act)
            r.hid_send[at] = r.hid_buf[...].T

            @pl.when(at < groups - 1)
            def _():
                hidden_copy(at).start()

            down_weights(at, slot).wait()
            r.res[...] += mm(r.hid_buf[...], r.win[1, where, :])
            r.gn2[...] += mm_nt(r.pre_send[at], r.win[0, :, where])

            @pl.when(at < groups - 2)
            def _():
                up_weights(at + 2, slot).start(priority=1)
                down_weights(at + 2, slot).start(priority=1)

            return carry

        lax.fori_loop(0, groups, chunk, 0)
        for at in range(peers):
            sent.setdefault("ffn", []).append(hidden_copy(at))

        def pool_cot():
            return [load(r.win_sem.at[half], r.cot_land.at[half], r.win.at[half]) for half in range(2)]

        def pool_turned(land):
            return [
                load(
                    r.pool_sem.at[at],
                    land.at[at],
                    r.win.at[at // chips, :, pl.ds(at % chips * tokens, tokens)],
                )
                for at in range(groups)
            ]

        gather_forward(0)
        r.hid_own[:, span(b, tokens)] = r.hid_send[groups - 1]
        r.pre_own[span(b, tokens), :] = r.pre_send[groups - 1]

        def norm2_back(at, total):
            rows = pl.ds(pl.multiple_of(at * 32, 32), 32)
            r.half[rows, :] = r.res[rows, :].astype(BF16)
            grad, xhat = r.gn2[rows, :], r.xhat2[rows, :]
            back = r.cotv[rows, :].astype(F32) + norm_back(grad, r.gain2[...], xhat, r.inv2[rows, 0:1])
            r.gres[rows, :] = back
            r.gbr_pair[pl.ds(pl.multiple_of(core * tokens + at * 32, 32), 32), :] = back.astype(BF16)
            return total + jnp.sum((grad * xhat).reshape(4, 8, width), axis=0)

        total = lax.fori_loop(0, tokens // 32, norm2_back, jnp.zeros((8, width), F32))
        r.sum_gain2[...] = jnp.sum(total, axis=0, keepdims=True)
        store_layer = load(r.local_sem.at[8], r.half, r.layer_out)
        branch_copy = pair_copy(1, r.gbr_pair.at[mine], r.gbr_pair.at[mine])
        send("pair", branch_copy)

        def gated_back(block):
            cols = span(block, own)
            grad = mm_nt(r.gbr_pair[mine, :], r.wout[span(block, own), :])
            glong = (grad * r.gate_out[:, cols]).astype(BF16)
            r.glong[:, cols] = glong
            r.ggb[:, cols] = grad.astype(BF16)
            r.long[:, cols] = grad * r.long[:, cols]
            r.sum_bias[:, cols] = jnp.sum(
                glong.astype(F32) * r.sig[:, cols].astype(F32), axis=0, keepdims=True
            )

        to_channels(2, r.ggb, gated_back)

        gather_start(1, r.turn)

        branch_copy.wait_recv()
        gated_copy.wait_recv()

        def out_copy(way):
            sems = r.wo_s.at[0, way], r.wo_r.at[0, way]
            to = partner_at(jnp.int32(way)) * 2 + core
            return remote(r.out_send.at[way], r.out_land.at[way], *sems, batch=to)

        for step in range(chips):
            to = partner(step - 1) if step else chip
            part = mm(r.gated_pair[span(to, share), :], r.gbr_pair[...])
            if step:
                r.out_send[step - 1] = part.astype(BF16)
            else:
                r.xhat2[share : 2 * share, :] = part

        near = z + 1 - 2 * lax.rem(z, 2)
        far = block_at(2)

        def reduce_first(k, refs):
            return remote(refs[0], refs[1], r.rs_s.at[k, 0], r.rs_r.at[k, 0], seq=near)

        def reduce_second(k, refs):
            return remote(refs[2], refs[3], r.rs_s.at[k, 1], r.rs_r.at[k, 1], seq=far)

        def reduce_send(k, refs, part_of):
            send_ref, _, next_ref, _, own_ref = refs
            send_ref[0] = part_of(near).astype(BF16)
            send_ref[1] = part_of(lax.rem(near + 2, blocks)).astype(BF16)
            send("rs", reduce_first(k, refs))
            next_ref[...] = part_of(far).astype(BF16)
            own_ref[...] = part_of(z)

        def reduce_next(k, refs):
            _, land_ref, next_ref, _, own_ref = refs
            reduce_first(k, refs).wait_recv()
            next_ref[...] = (next_ref[...].astype(F32) + land_ref[1].astype(F32)).astype(BF16)
            send("rs", reduce_second(k, refs))
            own_ref[...] += land_ref[0].astype(F32)

        def reduce_finish(k, refs):
            reduce_second(k, refs).wait_recv()
            refs[4][...] += refs[3][...].astype(F32)

        down_refs = (r.down_send, r.down_land, r.down_next, r.down_last, r.xhat2.at[0:down_rows])
        up_refs = (r.up_send, r.up_land, r.up_next, r.up_last, r.gate_out.at[:, 0:ffc])

        def wait_plane(k, dst_of):
            for at in range(peers):
                source = sibling if at == 6 else partner(at // 2) * 2 + at % 2
                dst = dst_of(source)
                remote(dst, dst, r.pa_s.at[k, at], r.pa_r.at[k, at], batch=source).wait_recv()

        deep = groups // 2 * tokens

        def down_part(block):
            rows = span(block, ffc // blocks)
            return mm(r.hid_own[rows, :deep], r.win[0]) + mm(r.hid_own[rows, deep:], r.win[1])

        def turned_part(right_ref):
            def part(block):
                rows = span(block, own)
                return mm(r.win[0, rows, :], right_ref[:deep]) + mm(r.win[1, rows, :], right_ref[deep:])

            return part


        gather_local(0, r.cotv).wait()
        gather_finish(0)
        pool = pool_cot()

        for step in range(1, blocks):
            source = block_at(blocks - step)
            seq_gather(step, source, source).wait_recv()
        for copy in own_loads:
            copy.wait()

        def proj_rows(at):
            r.ext_c[pl.ds(pl.multiple_of(at + spare, spare), tokens), :] = mm(
                r.n1_all[pl.ds(at, tokens), :], r.win[2, :, 0 : 3 * own], out=BF16
            )

        tiles(tokens, length, proj_rows)

        def own_cols(part, at):
            return pl.ds(pl.multiple_of(part * width + z * own + at, 128), 128)

        def mix_own(part, at, first, rows):
            wide = r.ext_c[pl.ds(first, rows + spare), part * own + at : part * own + at + 128].astype(F32)
            short = r.short[:, own_cols(part, at)].astype(F32)
            lags = [wide[spare - lag : spare - lag + rows] for lag in range(3)]
            return short[0:1] * lags[0] + short[1:2] * lags[1] + short[2:3] * lags[2]

        wait_channels(2)

        def long_rows(first):
            rows = pl.ds(first, tokens)
            for at in range(0, own, 128):
                cols = slice(at, at + 128)
                gate = mix_own(0, at, first, tokens)
                r.glong_c[rows, cols] = (r.chan[rows, cols].astype(F32) * gate).astype(BF16)

        tiles(tokens, length, long_rows)

        def grad_spec(at):
            rows = pl.ds(at, tokens)
            real = mm(r.cs[rows, :], r.glong_c[0:length, :])
            imag = -mm(r.sn[rows, :], r.glong_c[0:length, :])
            hre, him = r.hre[rows, :], r.him[rows, :]
            r.yre[rows, :] = (hre * real + him * imag).astype(BF16)
            r.yim[rows, :] = (him * real - hre * imag).astype(BF16)
            xre, xim = r.xre[rows, :], r.xim[rows, :]
            both_re = xre * real + xim * imag
            both_im = xre * imag - xim * real
            turn_re, turn_im = r.phase[rows, 0:1], r.phase[rows, 1:2]
            r.qre[rows, :] = ((both_re * turn_re + both_im * turn_im) * scale).astype(BF16)
            r.qim[rows, :] = ((both_re * turn_im - both_im * turn_re) * scale).astype(BF16)

        tiles(tokens, length, grad_spec)
        to_tokens(3, r.gconv_c)
        for at in range(peers):
            send("ffn", pre_copy(at))

        def proj_back(first):
            rows = pl.ds(first, tokens + spare)
            for at in range(0, own, 128):
                cols = slice(at, at + 128)
                gate_in = mix_own(1, at, first, tokens + spare)
                values = mix_own(2, at, first, tokens + spare)
                bias = r.bias[:, own_cols(0, at)]
                signal = (values * gate_in).astype(BF16).astype(F32)
                long = r.conv_out[rows, cols].astype(F32) + bias * signal
                grad_signal = r.gconv_c[rows, cols].astype(F32) + bias * r.glong_c[rows, cols].astype(F32)
                parts = (r.chan[rows, cols].astype(F32) * long, grad_signal * values, grad_signal * gate_in)
                for part, grad in enumerate(parts):
                    short = r.short[:, own_cols(part, at)].astype(F32)
                    total = (
                        short[0:1] * grad[0:tokens]
                        + short[1:2] * grad[1 : tokens + 1]
                        + short[2:3] * grad[2 : tokens + 2]
                    )
                    r.gproj_c[pl.ds(first, tokens), part * own + at : part * own + at + 128] = total.astype(BF16)

        tiles(tokens, length, proj_back)

        def in_part(group):
            return mm_tn(r.n1_all[:, span(group, share)], r.gproj_c[...])

        for at in range(chips):
            r.in_send[at] = in_part(at * 2 + 1 - core).astype(BF16)
        in_pair = pair_copy(2, r.in_send, r.in_pair)
        send("in_pair", in_pair)
        for copy in pool:
            copy.wait()
        wait_plane(0, lambda at: r.hid_own.at[:, span(at, tokens)])
        reduce_send(0, down_refs, down_part)
        in_pair.wait_recv()
        drain("in_pair")

        def in_copy(way):
            sems = r.wi_s.at[way], r.wi_r.at[way]
            to = partner_at(jnp.int32(way)) * 2 + core
            return remote(r.in_send.at[way], r.in_land.at[way], *sems, batch=to)

        for step in range(chips):
            way = way_of(step) if step < chips - 1 else None
            to = chip if way is None else partner_at(jnp.int32(way))
            part = in_part(to * 2 + core) + r.in_pair[to].astype(F32)
            if way is None:
                r.in_own[...] = part
            else:
                r.in_send[way] = part.astype(BF16)
                send("in", in_copy(way))

        r.w12[...] = jnp.zeros((net_rows, 128), F32)
        r.sum_w3[...] = jnp.zeros((filt, own), F32)
        for at in range(0, length, tokens):
            rows = slice(at, at + tokens)
            grad_taps = mm(r.cs[rows, :], r.qre[...]) + mm(r.sn[rows, :], r.qim[...])
            grad_filt = grad_taps * fading(at)
            r.sum_w3[...] += mm(r.h2[:, rows], grad_filt, precision=HIGHEST)
            grad_angle2 = mm_nt(r.w3[...], grad_filt, precision=HIGHEST) * r.s2[:, rows]
            r.w12[net_at:, :filt] += mm_nt(r.h1[:, rows], grad_angle2, precision=HIGHEST)
            grad_angle1 = mm(r.filt_w2[...], grad_angle2, precision=HIGHEST) * r.s1[:, rows]
            r.w12[:emb, :filt] += mm_nt(r.features_t[:, rows], grad_angle1, precision=HIGHEST)

        def small_copy(k, src, dst, at, to):
            return remote(src, dst, r.sm_s.at[k, at], r.sm_r.at[k, at], batch=to)

        def small_z_copy(k, src, dst, step, to):
            return remote(src, dst, r.sz_s.at[k, step - 1], r.sz_r.at[k, step - 1], seq=to)

        def small_z_send(k, src, dst_of):
            for step in range(1, blocks):
                send("small", small_z_copy(k, src, dst_of(step), step, block_at(step)))

        def small_z_wait(k, dst_of):
            for step in range(1, blocks):
                dst = dst_of(step)
                small_z_copy(k, dst, dst, step, block_at(blocks - step)).wait_recv()

        def small_send(k, src_of, dst_of):
            for at in range(peers):
                to = group_at(1 + at)
                send("small", small_copy(k, src_of(to), dst_of(at), at, to))

        def small_wait(k, dst_of):
            for at in range(peers):
                dst = dst_of(at)
                small_copy(k, dst, dst, at, group_at(groups - 1 - at)).wait_recv()

        w3_rows = filt // groups
        small_z_send(0, r.w12, lambda step: r.w12_z.at[step - 1])
        small_send(0, lambda to: r.sum_w3.at[span(to, w3_rows)], lambda at: r.w3_land.at[at])

        def outz_copy(step, to):
            sems = r.wo_s.at[1, step - 1], r.wo_r.at[1, step - 1]
            return remote(r.outz_send.at[span(to, rows_out)], r.outz_land.at[step - 1], *sems, seq=to)


        def short_sums(cols, grad, lags):
            for lag in range(3):
                r.sum_short[lag : lag + 1, cols] = jnp.sum(grad * lags[lag], axis=0, keepdims=True)

        def back_cols(cols, grad, lags):
            short_sums(cols, grad, lags)
            r.ghalo[:, cols] = grad[0:8]
            short = r.short[:, cols].astype(F32)
            longer = jnp.concatenate([grad, jnp.zeros((8, 128), F32)], axis=0)
            total = (
                short[0:1] * grad
                + short[1:2] * longer[1 : tokens + 1]
                + short[2:3] * longer[2 : tokens + 2]
            )
            r.gproj[:, cols] = total.astype(BF16)
            r.tail[:, cols] = total[tokens - 16 :]

        def mixed_cols(at):
            cols = pl.ds(at, 128)
            grad_signal = conv_cols(at) + r.bias[:, cols] * r.glong[:, cols].astype(F32)
            gate_cols = pl.ds(pl.multiple_of(width + at, 128), 128)
            value_cols = pl.ds(pl.multiple_of(2 * width + at, 128), 128)
            gate_lags, gate_in = mix(gate_cols)
            value_lags, values = mix(value_cols)
            back_cols(gate_cols, grad_signal * values, gate_lags)
            back_cols(value_cols, grad_signal * gate_in, value_lags)

        def gate_back(at):
            cols = pl.ds(at, 128)
            back_cols(cols, r.long[:, cols], lags_at(cols))

        drain(("forward", 0))
        tiles(128, width, gate_back)
        wait_tokens(3)
        tiles(128, width, mixed_cols)
        halo = remote(r.ghalo, r.ghalo_in, r.halo_s.at[1], r.halo_r.at[1], seq=block_at(blocks - 1))
        send("halo", halo)
        gather_forward(1)
        halo.wait_recv()
        later = r.ghalo_in[...] * jnp.where(z < blocks - 1, 1.0, 0.0)

        def tail_cols(at):
            cols = slice(at, at + width)
            short = r.short[:, cols].astype(F32)
            row = lax.broadcasted_iota(jnp.int32, (16, width), 0)
            last = short[1:2] * later[0:1, cols] + short[2:3] * later[1:2, cols]
            total = r.tail[:, cols] + jnp.where(row == 15, last, 0.0)
            total = total + jnp.where(row == 14, short[2:3] * later[0:1, cols], 0.0)
            r.gproj[tokens - 16 :, cols] = total.astype(BF16)

        for part in range(3):
            tail_cols(part * width)

        def spread(k, own_ref, out_ref, size):
            for at in range(peers):
                to = group_at(1 + at)
                src, dst = own_ref.at[span(to, rows_out)], out_ref.at[:, span(b, size)]
                send("spread", remote(src, dst, r.tr_s.at[k, at], r.tr_r.at[k, at], batch=to))
            return load(r.local_sem.at[14 + k], own_ref.at[span(b, rows_out)], out_ref.at[:, span(b, size)])

        def spread_finish(k, copy, out_ref, size):
            for at in range(peers):
                source = group_at(groups - 1 - at)
                dst = out_ref.at[:, span(source, size)]
                remote(dst, dst, r.tr_s.at[k, at], r.tr_r.at[k, at], batch=source).wait_recv()
            copy.wait()

        for step in range(chips - 1):
            send("out", out_copy(way_of(step)))
        small_z_wait(0, lambda step: r.w12_z.at[step - 1])
        net = r.w12[...]
        for step in range(zpeers):
            net = net + r.w12_z[step]
        r.w12_sum[...] = net
        small_send(1, lambda to: r.w12_sum, lambda at: r.w12_plane.at[at])
        small_wait(0, lambda at: r.w3_land.at[at])
        part = r.sum_w3[span(b, w3_rows), :]
        for at in range(peers):
            part = part + r.w3_land[at]
        r.w3_part[...] = part
        r.w3_all[z, span(b, w3_rows), :] = part
        small_send(2, lambda to: r.w3_part, lambda at: r.w3_all.at[z, span(b, w3_rows)])
        reduce_next(0, down_refs)
        gather_local(1, r.turn).wait()
        gather_finish(1)
        drain(("forward", 1))
        pool = pool_turned(r.n2_land)
        small_wait(1, lambda at: r.w12_plane.at[at])
        net = r.w12_sum[...]
        for at in range(peers):
            net = net + r.w12_plane[at]
        r.grad_w1[...] = net[:emb, :filt]
        r.grad_w2[...] = net[net_at:, :filt]
        for at in range(peers):
            dst = r.w3_all.at[z, span(group_at(groups - 1 - at), w3_rows)]
            small_copy(2, dst, dst, at, group_at(groups - 1 - at)).wait_recv()
        small_z_send(1, r.w3_all.at[z], lambda step: r.w3_all.at[z])
        for copy in pool:
            copy.wait()
        wait_plane(1, lambda at: r.pre_own.at[span(at, tokens)])
        reduce_send(1, up_refs, turned_part(r.pre_own))
        win_loads = [(block, load_win(block)) for block in range(3)]
        for way in range(chips - 1):
            in_copy(way).wait_recv()
        total = r.in_own[...]
        for step in range(chips - 1):
            total = total + r.in_land[step].astype(F32)
        r.in_own[...] = total

        def in_spread(step, part, block, to):
            src = r.in_own.at[span(to, rows_out), part * own : (part + 1) * own]
            dst = r.grad_w_in.at[:, pl.ds(pl.multiple_of(part * width + block * own, own), own)]
            if step == 0:
                return pltpu.make_async_copy(src, dst, r.load_sem.at[10 + part])
            return remote(src, dst, r.ti_s.at[step - 1, part], r.ti_r.at[step - 1, part], seq=to)

        for part in range(3):
            for step in range(1, blocks):
                send("in_spread", in_spread(step, part, z, block_at(step)))
            in_spread(0, part, z, z).start()
        for _, copy in win_loads:
            copy.wait()
        r.gn2[...] = mm_nt(r.gproj[:, :width], r.win[0])
        r.gn2[...] += mm_nt(r.gproj[:, width : 2 * width], r.win[1])
        r.gn2[...] += mm_nt(r.gproj[:, 2 * width :], r.win[2])

        reduce_next(1, up_refs)
        def norm1_back(at, total):
            rows = pl.ds(pl.multiple_of(at * 32, 32), 32)
            grad, inverse = r.gn2[rows, :], r.inv1[rows, 0:1]
            xhat = (r.tok[rows, :].astype(F32) - r.mean1[rows, 0:1]) * inverse
            r.res[rows, :] = r.gres[rows, :] + norm_back(grad, r.gain1[...], xhat, inverse)
            return total + jnp.sum((grad * xhat).reshape(4, 8, width), axis=0)

        total = lax.fori_loop(0, tokens // 32, norm1_back, jnp.zeros((8, width), F32))
        r.sum_gain1[...] = jnp.sum(total, axis=0, keepdims=True)
        r.small_send[...] = jnp.zeros((groups, 16, share), F32)
        for group in range(groups):
            cols = slice(group * share, (group + 1) * share)
            r.small_send[group, 0:1, :] = r.sum_gain1[:, cols]
            r.small_send[group, 1:2, :] = r.sum_gain2[:, cols]
            r.small_send[group, 2:3, :] = r.sum_bias[:, cols]
            for lag in range(3):
                for third in range(3):
                    at = group * inc + third * share
                    row = 3 + 3 * lag + third
                    r.small_send[group, row : row + 1, :] = r.sum_short[lag : lag + 1, at : at + share]
        small_send(3, lambda to: r.small_send.at[to], lambda at: r.small_land.at[b])
        r.small_land[b] = r.small_send[b]
        store_tokens = load(r.local_sem.at[13], r.res, r.tokens_grad)
        reduce_finish(0, down_refs)
        store_down = load(r.local_sem.at[9], down_refs[4], r.grad_w_down)
        for way in range(chips - 1):
            out_copy(way).wait_recv()
        total = r.xhat2[share : 2 * share, :]
        for step in range(chips - 1):
            total = total + r.out_land[step].astype(F32)
        r.xhat2[share : 2 * share, :] = total
        r.outz_send[...] = total.astype(BF16)
        for step in range(1, blocks):
            send("outz", outz_copy(step, block_at(step)))
        r.outz_own[...] = r.xhat2[pl.ds(pl.multiple_of(share + z * rows_out, rows_out), rows_out), :]

        for at in range(peers):
            source = group_at(groups - 1 - at)
            dst = r.small_land.at[source]
            small_copy(3, dst, dst, at, source).wait_recv()
        small = r.small_land[0]
        for group in range(1, groups):
            small = small + r.small_land[group]
        r.small_sum[...] = small
        small_z_send(2, r.small_sum, lambda step: r.small_z.at[step - 1])
        reduce_finish(1, up_refs)
        spread_up = spread(0, up_refs[4], r.grad_w_up, ffc)
        for step in range(1, blocks):
            outz_copy(step, block_at(blocks - step)).wait_recv()
        total = r.outz_own[...]
        for step in range(zpeers):
            total = total + r.outz_land[step].astype(F32)
        r.outz_own[...] = total
        store_out = load(r.local_sem.at[11], r.outz_own, r.grad_w_out)
        def chosen(value, size):
            picked = value[:, :size]
            for block in range(1, blocks):
                picked = jnp.where(z == block, value[:, block * size : (block + 1) * size], picked)
            return picked

        for step in range(1, blocks):
            source = block_at(blocks - step)
            dst = r.w3_all.at[source]
            small_z_copy(1, dst, dst, step, source).wait_recv()
        third = r.w3_all[lax.div(b * share, own)]
        halves = own // share
        picked = third[:, :share]
        for half in range(1, halves):
            here = lax.rem(b, halves) == half
            picked = jnp.where(here, third[:, half * share : (half + 1) * share], picked)
        r.grad_w3[...] = chosen(picked, rows_out)
        small_z_wait(2, lambda step: r.small_z.at[step - 1])
        small = r.small_sum[...]
        for step in range(zpeers):
            small = small + r.small_z[step]
        r.grad_gain1[...] = chosen(small[0:1], rows_out)
        r.grad_gain2[...] = chosen(small[1:2], rows_out)
        r.grad_bias[...] = chosen(small[2:3], rows_out)
        for lag in range(3):
            for third in range(3):
                row = 3 + 3 * lag + third
                r.short_all[lag : lag + 1, third * share : (third + 1) * share] = small[row : row + 1]
        r.grad_short[...] = chosen(r.short_all[0:3, :], 3 * rows_out)
        spread_finish(0, spread_up, r.grad_w_up, ffc)
        for part in range(3):
            for step in range(1, blocks):
                source = block_at(blocks - step)
                in_spread(step, part, source, source).wait_recv()
            in_spread(0, part, z, z).wait()
        store_layer.wait()
        store_down.wait()
        store_out.wait()
        store_tokens.wait()
        for key in list(sent):
            drain(key)

    def call(args):
        result = pl.pallas_call(
            kernel,
            out_shape=[jax.ShapeDtypeStruct(shape, dtype) for shape, dtype, _ in outputs.values()],
            in_specs=[pl.BlockSpec(memory_space=space) for space in inputs.values()],
            out_specs=[pl.BlockSpec(memory_space=space) for *_, space in outputs.values()],
            scratch_shapes=list(scratch.values()),
            compiler_params=pltpu.CompilerParams(
                collective_id=0, has_side_effects=True, vmem_limit_bytes=KERNEL_VMEM
            ),
        )(*[args[name] for name in inputs])
        return settled(result[:13])

    return call


def settled(values):
    count = len(values)
    large = [at for at, value in enumerate(values) if value.size >= 1 << 15]

    def copy_all(*refs):
        sources, targets, held = refs[:count], refs[count : 2 * count], refs[2 * count : -1]
        sems = refs[-1]
        copies = [
            pltpu.make_async_copy(sources[at], held[k], sems.at[0, k]) for k, at in enumerate(large)
        ]
        for copy in copies:
            copy.start()
        for at in range(count):
            if at not in large:
                if at == count - 1:
                    targets[at][...] = sources[at][...].T
                else:
                    targets[at][...] = sources[at][...].reshape(targets[at].shape)
        stores = []
        for k, at in enumerate(large):
            copies[k].wait()
            stores.append(pltpu.make_async_copy(held[k], targets[at], sems.at[1, k]))
            stores[-1].start()
        for copy in stores:
            copy.wait()

    specs = [
        pl.BlockSpec(memory_space=pl.ANY if at in large else pltpu.VMEM) for at in range(count)
    ]
    return pl.pallas_call(
        copy_all,
        out_shape=[
            jax.ShapeDtypeStruct(value.shape[1:] if value.shape[0] == 1 else value.shape, value.dtype)
            for value in values[:-1]
        ]
        + [jax.ShapeDtypeStruct(values[-1].shape[::-1], values[-1].dtype)        ],
        in_specs=specs,
        out_specs=specs,
        scratch_shapes=[pltpu.VMEM(values[at].shape, values[at].dtype) for at in large]
        + [pltpu.SemaphoreType.DMA((2, len(large)))],
    )(*values)


def small_sums(gain1, bias, gain2, short, w1, w2, w3_own):
    blocks, position = lax.axis_size("seq"), lax.axis_index("seq")
    dests = lax.axis_size("batch") * blocks
    width, (filt_dim, own), emb = gain1.shape[0], w3_own.shape, w1.shape[0]
    w3_all = lax.dynamic_update_slice_in_dim(
        jnp.zeros((filt_dim, width), F32), w3_own, position * own, 1
    )
    share = width // dests
    small = jnp.concatenate(
        [
            gain1.reshape(dests, share),
            bias.reshape(dests, share),
            gain2.reshape(dests, share),
            short.reshape(3, dests, 3 * share).transpose(1, 0, 2).reshape(dests, 9 * share),
            w3_all.reshape(filt_dim, dests, share).transpose(1, 0, 2).reshape(dests, filt_dim * share),
        ],
        axis=1,
    )
    small = scatter_sum(small, wire=F32)[0]
    filters = all_sum(jnp.concatenate([w1, w2], axis=0))
    return (
        small[:share],
        small[3 * share : 12 * share].reshape(3, 3 * share),
        filters[:emb],
        filters[emb:],
        small[12 * share :].reshape(filt_dim, share),
        small[share : 2 * share],
        small[2 * share : 3 * share],
    )


def kernel_layer(
    tokens,
    norm_gain1,
    w_in,
    short_kernel,
    filt_w1,
    filt_w2,
    filt_w3,
    decay_rate,
    conv_bias,
    w_out,
    norm_gain2,
    w_up,
    w_down,
    cotangent,
):
    _, block_len, width = tokens.shape
    groups, blocks = lax.axis_size("batch"), lax.axis_size("seq")
    emb, filt = filt_w1.shape
    (cosine, sine), phase = symmetric_tables(block_len * blocks)
    features = lag_features(emb, block_len * blocks)
    call = kernel_plan(groups, blocks, block_len, width, w_up.shape[1], filt, emb)
    out = call(
        dict(
            tokens=tokens[0],
            cot=cotangent[0],
            w_in=w_in,
            w_out=w_out,
            w_up=w_up,
            w_down=w_down,
            cosine=jnp.asarray(cosine),
            sine=jnp.asarray(sine),
            filt_w3=filt_w3,
            decay=decay_rate[None],
            gain1=norm_gain1[None],
            gain2=norm_gain2[None],
            bias=conv_bias[None],
            short=short_kernel,
            filt_w1=filt_w1,
            filt_w2=filt_w2,
            features_t=jnp.asarray(features.T),
            phase=jnp.asarray(phase),
        )
    )
    layer_out, tokens_grad, w_in, w_out, w_up, w_down, gain1, gain2, bias, short, w1, w2, w3 = out
    return layer_out[None], tokens_grad[None], (gain1, short, w1, w2, w3.T, bias, gain2), (w_in, w_out, w_up, w_down)


def on_device(*args):
    tokens = args[0]
    fits = lax.axis_size("batch") == 8 and lax.axis_size("seq") == 4 and tokens.shape[1] * lax.axis_size("seq") <= 1024
    layer = kernel_layer if fits else plain_layer
    layer_out, tokens_grad, small, large = layer(*args)
    gain1, short, w1, w2, w3, bias, gain2 = small
    grad_w_in, grad_w_out, grad_w_up, grad_w_down = large
    return (
        layer_out, tokens_grad, gain1, grad_w_in, short, w1, w2, w3, bias, grad_w_out, gain2,
        grad_w_up, grad_w_down,
    )


def solution(mesh):
    split = P("batch", "seq", None)
    both = ("batch", "seq")
    return jax.shard_map(
        on_device,
        mesh=mesh,
        in_specs=(split,) + (P(),) * 12 + (split,),
        out_specs=(
            split,
            split,
            P(both),
            P(both, None),
            P(None, both),
            P(),
            P(),
            P(None, both),
            P(both),
            P(both, None),
            P(both),
            P(both, None),
            P(both, None),
        ),
        check_vma=False,
    )
```

```python
import math

import jax
import jax.numpy as jnp
import ml_dtypes
import numpy as np
from jax import lax
from jax.experimental import pallas as pl
from jax.experimental.pallas import tpu as pltpu
from jax.sharding import PartitionSpec as P

F32 = jnp.float32
BF16 = jnp.bfloat16
HIGHEST = lax.Precision.HIGHEST
GELU_SCALE = math.sqrt(2.0 / math.pi)
GELU_CUBIC = 0.044715


def dot(left, right, contract, out=F32, precision=None):
    return lax.dot_general(
        left, right, (contract, ((), ())), precision=precision, preferred_element_type=F32
    ).astype(out)


def mm(left, right, **kw):
    return dot(left, right, ((1,), (0,)), **kw)


def mm_nt(left, right, **kw):
    return dot(left, right, ((1,), (1,)), **kw)


def mm_tn(left, right, **kw):
    return dot(left, right, ((0,), (0,)), **kw)


def shifted(value, axis, steps):
    count = lax.axis_size(axis)
    first, last = (max(0, -steps), min(count, count - steps))
    return lax.ppermute(value, axis, [(source, source + steps) for source in range(first, last)])


def exchange(value, axis, bit):
    count = lax.axis_size(axis)
    return lax.ppermute(value, axis, [(at, at ^ (1 << bit)) for at in range(count)])


def bits_of(axis):
    return lax.axis_size(axis).bit_length() - 1


def stage_order(swap):
    batch_bits, seq_bits = bits_of("batch"), bits_of("seq")
    rest = list(range(1, batch_bits))
    half = len(rest) // 2
    if swap:
        rest = rest[half:] + rest[:half]
    return [("batch", bit) for bit in [0] + rest] + [("seq", bit) for bit in range(seq_bits)]


def scatter_sum(partial, swap=False, wire=BF16):
    batch_bits, seq_bits = bits_of("batch"), bits_of("seq")
    dims = [("batch", bit) for bit in reversed(range(batch_bits))]
    dims += [("seq", bit) for bit in reversed(range(seq_bits))]
    rows = partial.shape[0] >> len(dims)
    value = partial.reshape((2,) * len(dims) + (rows,) + partial.shape[1:]).astype(wire)
    for axis, bit in stage_order(swap):
        at = dims.index((axis, bit))
        mine = (lax.axis_index(axis) >> bit) & 1
        keep = lax.dynamic_index_in_dim(value, mine, at, keepdims=False)
        send = lax.dynamic_index_in_dim(value, 1 - mine, at, keepdims=False)
        got = exchange(send, axis, bit)
        value = keep.astype(F32) + got.astype(F32)
        dims.pop(at)
        if dims:
            value = value.astype(wire)
    return value


def gather_batch(value):
    return lax.all_gather(value, "batch", axis=0, tiled=True)


def columns_batch(value):
    return lax.all_to_all(value, "batch", 1, 0, tiled=True)


def rows_sum(left_own, right_all):
    blocks = lax.axis_size("seq")
    part = mm_tn(left_own, right_all, out=BF16)
    got = lax.all_to_all(part.reshape(blocks, -1, part.shape[1]), "seq", 0, 0, tiled=True)
    return jnp.sum(got.astype(F32), axis=0)


def columns_sum(left_all, right_own):
    blocks, groups = lax.axis_size("seq"), lax.axis_size("batch")
    part = mm_tn(left_all, right_own, out=BF16)
    part = part.reshape(groups * blocks, -1, part.shape[1])
    got = lax.all_to_all(part, ("batch", "seq"), 0, 0, tiled=True)
    got = jnp.sum(got.reshape(groups, blocks, -1, part.shape[2]).astype(F32), axis=1)
    return got.transpose(1, 0, 2).reshape(got.shape[1], -1)


def all_sum(value):
    for axis, bit in stage_order(False):
        value = value + exchange(value, axis, bit)
    return value


def norm_parts(values):
    centered = values - jnp.mean(values, axis=-1, keepdims=True)
    inverse = lax.rsqrt(jnp.mean(centered * centered, axis=-1, keepdims=True) + 1e-05)
    return centered * inverse, inverse


def norm_back(grad, gain, xhat, inverse):
    scaled = grad * gain
    return (
        scaled
        - jnp.mean(scaled, axis=-1, keepdims=True)
        - xhat * jnp.mean(scaled * xhat, axis=-1, keepdims=True)
    ) * inverse


def transform_table(length):
    count = np.arange(length, dtype=np.int64)
    turns = (2 * count[:, None] + 1) * count[None, :] % (4 * length)
    angles = turns.astype(np.float64) * (2.0 * np.pi / (4 * length))
    table = np.concatenate([np.cos(angles), -np.sin(angles)], axis=0)
    return table.astype(np.float32).astype(ml_dtypes.bfloat16)


def lag_features(emb, length):
    bands = (emb - 1) // 2
    lag = np.arange(length, dtype=np.float64)
    freq = 1e-4 + np.arange(bands, dtype=np.float64) * ((bands - 1 - 1e-4) / (bands - 1))
    phases = (lag * (2.0 * np.pi / length))[:, None] * freq[None, :]
    return np.concatenate(
        [(lag / (length - 1))[:, None], np.cos(phases), -np.sin(phases)], axis=1
    ).astype(np.float32)


def to_channels(value):
    return lax.all_to_all(value, "seq", 1, 0, tiled=True)


def to_tokens(value):
    return lax.all_to_all(value, "seq", 0, 1, tiled=True)


def plain_layer(
    tokens,
    norm_gain1,
    w_in,
    short_kernel,
    filt_w1,
    filt_w2,
    filt_w3,
    decay_rate,
    conv_bias,
    w_out,
    norm_gain2,
    w_up,
    w_down,
    cotangent,
):
    num_seqs, block_len, width = tokens.shape
    assert num_seqs == 1
    blocks = lax.axis_size("seq")
    position = lax.axis_index("seq")
    seq_len = block_len * blocks
    own = width // blocks
    table = jnp.asarray(transform_table(seq_len))
    features = jnp.asarray(lag_features(filt_w1.shape[0], seq_len))
    cot = cotangent[0]
    cot_all = gather_batch(cot)
    inputs = tokens[0].astype(F32)

    xhat1, inverse1 = norm_parts(inputs)
    normed1 = (xhat1 * norm_gain1).astype(BF16)
    normed1_all = gather_batch(normed1)
    projected = mm(normed1, w_in, out=BF16)
    earlier = shifted(projected[block_len - 2 :], "seq", 1)
    extended = jnp.concatenate([earlier, projected], axis=0).astype(F32)
    taps3 = short_kernel.astype(F32)
    lags = [extended[2 - lag : 2 - lag + block_len] for lag in range(3)]
    mixed = taps3[0] * lags[0] + taps3[1] * lags[1] + taps3[2] * lags[2]
    gate_out = mixed[:, :width]
    gate_in = mixed[:, width : 2 * width]
    values = mixed[:, 2 * width :]
    signal = (values * gate_in).astype(BF16)

    w3_own = lax.dynamic_slice_in_dim(filt_w3, position * own, own, 1)
    decay_own = lax.dynamic_slice_in_dim(decay_rate, position * own, own, 0)
    angle1 = mm(features, filt_w1, precision=HIGHEST)
    hidden1, slope1 = jnp.sin(angle1), jnp.cos(angle1)
    angle2 = mm(hidden1, filt_w2, precision=HIGHEST)
    hidden2, slope2 = jnp.sin(angle2), jnp.cos(angle2)
    lag_index = jnp.arange(seq_len).astype(F32)
    fading = jnp.exp(-decay_own[None, :] * lag_index[:, None])
    taps = (mm(hidden2, w3_own, precision=HIGHEST) * fading).astype(BF16)
    taps_spec = mm(table, taps)
    taps_re, taps_im = taps_spec[:seq_len], taps_spec[seq_len:]

    signal_spec = mm(table, to_channels(signal))
    signal_re, signal_im = signal_spec[:seq_len], signal_spec[seq_len:]
    scale = 1.0 / seq_len

    def inverse_of(real, imag):
        both = (jnp.concatenate([real, imag], axis=0) * scale).astype(BF16)
        return mm_tn(table, both)

    conv = inverse_of(
        taps_re * signal_re - taps_im * signal_im, taps_re * signal_im + taps_im * signal_re
    )
    long_out = to_tokens(conv.astype(BF16)).astype(F32) + conv_bias * signal.astype(F32)
    gated = (long_out * gate_out).astype(BF16)
    gated_all = gather_batch(gated)
    residual1 = inputs + mm(gated, w_out)
    xhat2, inverse2 = norm_parts(residual1)
    normed2 = (xhat2 * norm_gain2).astype(BF16)
    normed2_all = gather_batch(normed2)
    pre = mm(normed2, w_up)
    bent = jnp.tanh(GELU_SCALE * (pre + GELU_CUBIC * pre * pre * pre))
    hidden = (0.5 * pre * (1.0 + bent)).astype(BF16)
    layer_out = (residual1 + mm(hidden, w_down)).astype(BF16)

    slope = 0.5 * (1.0 + bent) + 0.5 * pre * (1.0 - bent * bent) * GELU_SCALE * (
        1.0 + 3.0 * GELU_CUBIC * pre * pre
    )
    grad_pre = (mm_nt(cot, w_down) * slope).astype(BF16)
    grad_w_down = rows_sum(columns_batch(hidden), cot_all)
    grad_w_up = columns_sum(normed2_all, columns_batch(grad_pre))
    grad_norm2 = mm_nt(grad_pre, w_up)
    grad_gain2 = jnp.sum(grad_norm2 * xhat2, axis=0)
    grad_res = cot.astype(F32) + norm_back(grad_norm2, norm_gain2, xhat2, inverse2)
    grad_branch = grad_res.astype(BF16)
    grad_w_out = columns_sum(gated_all, columns_batch(grad_branch))
    grad_gated = mm_nt(grad_branch, w_out)
    grad_long = (grad_gated * gate_out).astype(BF16)
    grad_gate_out = grad_gated * long_out
    grad_bias = jnp.sum(grad_long.astype(F32) * signal.astype(F32), axis=0)

    grad_spec = mm(table, to_channels(grad_long))
    grad_re, grad_im = grad_spec[:seq_len], grad_spec[seq_len:]
    grad_conv = inverse_of(
        taps_re * grad_re + taps_im * grad_im, taps_re * grad_im - taps_im * grad_re
    )
    grad_signal = to_tokens(grad_conv.astype(BF16)).astype(F32) + conv_bias * grad_long.astype(F32)
    grad_taps = inverse_of(
        signal_re * grad_re + signal_im * grad_im, signal_re * grad_im - signal_im * grad_re
    )
    grad_filt = grad_taps * fading
    grad_w3_own = mm_tn(hidden2, grad_filt)
    grad_angle2 = mm_nt(grad_filt, w3_own) * slope2
    grad_w2 = mm_tn(hidden1, grad_angle2)
    grad_angle1 = mm_nt(grad_angle2, filt_w2) * slope1
    grad_w1 = mm_tn(features, grad_angle1)

    grad_mixed = jnp.concatenate(
        [grad_gate_out, grad_signal * values, grad_signal * gate_in], axis=1
    )
    later = shifted(grad_mixed[:2], "seq", -1)
    grad_ext = jnp.concatenate([grad_mixed, later], axis=0)
    grad_proj = (
        taps3[0] * grad_ext[:block_len]
        + taps3[1] * grad_ext[1 : block_len + 1]
        + taps3[2] * grad_ext[2:]
    ).astype(BF16)
    grad_short = jnp.stack([jnp.sum(grad_mixed * lag, axis=0) for lag in lags])
    grad_w_in = columns_sum(normed1_all, columns_batch(grad_proj))
    grad_norm1 = mm_nt(grad_proj, w_in)
    grad_gain1 = jnp.sum(grad_norm1 * xhat1, axis=0)
    tokens_grad = grad_res + norm_back(grad_norm1, norm_gain1, xhat1, inverse1)

    return layer_out[None], tokens_grad[None], small_sums(
        grad_gain1, grad_bias, grad_gain2, grad_short, grad_w1, grad_w2, grad_w3_own
    ), (grad_w_in, grad_w_out, grad_w_up, grad_w_down)


MESH = pl.DeviceIdType.MESH
KERNEL_VMEM = 63 * 1024 * 1024


def symmetric_tables(length):
    odd = 2 * np.arange(length, dtype=np.int64) + 1
    angles = (odd[:, None] * odd[None, :] % (8 * length)).astype(np.float64) * (
        np.pi / (4 * length)
    )
    phase = odd.astype(np.float64) * (np.pi / (4 * length))
    tables = [np.cos(angles), np.sin(angles)]
    tables = [t.astype(np.float32).astype(ml_dtypes.bfloat16) for t in tables]
    return tables, np.stack([np.cos(phase), np.sin(phase)], axis=1).astype(np.float32)


def sin_cos(x):
    turns = jnp.floor(x * (2.0 / np.pi) + 0.5)
    rest = ((x - turns * 1.5703125) - turns * 4.837512969970703e-4) - turns * 7.54978995489188e-8
    square = rest * rest
    sine = rest + rest * square * (
        -1.6666654611e-1 + square * (8.3321608736e-3 - square * 1.9515295891e-4)
    )
    cosine = (1.0 - 0.5 * square) + square * square * (
        4.166664568298827e-2 + square * (-1.388731625493765e-3 + square * 2.443315711809948e-5)
    )
    quarter = turns - 4.0 * jnp.floor(turns * 0.25)
    odd = (quarter == 1.0) | (quarter == 3.0)
    sin_sign = jnp.where(quarter >= 2.0, -1.0, 1.0)
    cos_sign = jnp.where((quarter == 1.0) | (quarter == 2.0), -1.0, 1.0)
    return sin_sign * jnp.where(odd, cosine, sine), cos_sign * jnp.where(odd, sine, cosine)


class Named:
    def __init__(self, names, refs):
        assert len(names) == len(refs)
        for name, ref in zip(names, refs):
            setattr(self, name, ref)


def kernel_plan(groups, blocks, tokens, width, hidden, filt, emb):
    length = tokens * blocks
    own = width // blocks
    ffc = hidden // groups
    share = width // groups
    rows_out = share // blocks
    inc = 3 * share
    spare = 16
    chips = groups // 2
    down_rows = ffc // blocks
    net_rows = filt
    peers, zpeers = groups - 1, blocks - 1
    vm, hbm = pltpu.VMEM, pl.ANY
    inputs = dict(
        tokens=hbm, cot=hbm, w_in=hbm, w_out=hbm, w_up=hbm, w_down=hbm,
        cosine=hbm, sine=hbm, filt_w3=hbm, decay=hbm,
        gain1=vm, gain2=vm, bias=vm, short=vm, filt_w1=vm, filt_w2=vm,
        features_t=vm, phase=vm,
    )
    outputs = dict(
        layer_out=((tokens, width), BF16, hbm),
        tokens_grad=((tokens, width), F32, hbm),
        grad_w_in=((rows_out, 3 * width), F32, hbm),
        grad_w_out=((rows_out, width), F32, hbm),
        grad_w_up=((rows_out, hidden), F32, hbm),
        grad_w_down=((ffc // blocks, width), F32, hbm),
        grad_gain1=((1, rows_out), F32, vm),
        grad_gain2=((1, rows_out), F32, vm),
        grad_bias=((1, rows_out), F32, vm),
        grad_short=((3, 3 * rows_out), F32, vm),
        grad_w1=((emb, filt), F32, vm),
        grad_w2=((filt, filt), F32, vm),
        grad_w3=((filt, rows_out), F32, vm),
        cot_land=((4 * tokens, width), BF16, hbm),
        n2_land=((4, width, tokens), BF16, hbm),
    )
    dma = pltpu.SemaphoreType.DMA
    scratch = dict(
        tok=vm((tokens, width), BF16), cotv=vm((tokens, width), BF16),
        mean1=vm((tokens, 128), F32), inv1=vm((tokens, 128), F32),
        n1_all=vm((length, width), BF16), turn=vm((width, tokens), BF16),
        gated_turn=vm((width, tokens), BF16), gated_pair=vm((width // 2, 2 * tokens), BF16),
        hid_buf=vm((tokens, ffc), BF16),
        ghalo=vm((8, 3 * width), F32), ghalo_in=vm((8, 3 * width), F32), tail=vm((16, 3 * width), F32),
        ext_c=vm((length + 32, 3 * own), BF16), gproj_c=vm((length, 3 * own), BF16),
        gconv_c=vm((length + 16, own), BF16), glong_c=vm((length + 16, own), BF16),

        win=vm((3, width, width), BF16), wout=vm((width, width), BF16),
        cs=vm((length, length), BF16), sn=vm((length, length), BF16),
        ext=vm((tokens + 16, 3 * width), BF16),
        halo_out=vm((16, 3 * width), BF16), halo_in=vm((16, 3 * width), BF16),
        gate_out=vm((tokens, width), F32),
        sig=vm((tokens, width), BF16), chan=vm((length + 16, own), BF16),
        w3=vm((filt, own), F32), fade=vm((1, own), F32),
        h1=vm((filt, length), F32), s1=vm((filt, length), F32),
        h2=vm((filt, length), F32), s2=vm((filt, length), F32),
        sum_gain1=vm((1, width), F32), sum_gain2=vm((1, width), F32),
        sum_bias=vm((1, width), F32), sum_short=vm((3, 3 * width), F32),
        small_send=vm((groups, 16, share), F32), small_land=vm((groups, 16, share), F32),
        small_sum=vm((16, share), F32), small_z=vm((zpeers, 16, share), F32),
        short_all=vm((8, inc), F32),
        w12=vm((net_rows, 128), F32), w12_z=vm((zpeers, net_rows, 128), F32),
        w12_sum=vm((net_rows, 128), F32), w12_plane=vm((peers, net_rows, 128), F32),
        sum_w3=vm((filt, own), F32), w3_land=vm((peers, filt // groups, own), F32),
        w3_part=vm((filt // groups, own), F32), w3_all=vm((blocks, filt, own), F32),
        hre=vm((length, own), BF16), him=vm((length, own), BF16),
        xre=vm((length, own), BF16), xim=vm((length, own), BF16),
        yre=vm((length, own), BF16), yim=vm((length, own), BF16),
        qre=vm((length, own), BF16), qim=vm((length, own), BF16),
        conv_out=vm((length + 16, own), BF16), conv_in=vm((blocks, tokens, own), BF16),
        long=vm((tokens, width), F32), half=vm((tokens, width), BF16),
        res=vm((tokens, width), F32), xhat2=vm((tokens, width), F32),
        inv2=vm((tokens, 128), F32), gn2=vm((tokens, width), F32),
        gres=vm((tokens, width), F32),
        hid_send=vm((groups, ffc, tokens), BF16), hid_own=vm((2, ffc, 4 * tokens), BF16),
        pre_send=vm((groups, tokens, ffc), BF16), pre_own=vm((2, 4 * tokens, ffc), BF16),
        gbr_pair=vm((2 * tokens, width), BF16),
        glong=vm((tokens, width), BF16),
        gproj=vm((tokens, 3 * width), BF16),
        down_send=vm((4, down_rows, width), BF16), down_first=vm((4, down_rows, width), BF16),
        down_land=vm((2, down_rows, width), BF16), down_last=vm((down_rows, width), BF16),
        up_send=vm((4, own, ffc), BF16), up_first=vm((4, own, ffc), BF16),
        up_land=vm((2, own, ffc), BF16), up_last=vm((own, ffc), BF16),
        in_send=vm((chips, share, 3 * own), BF16), in_pair=vm((chips, share, 3 * own), BF16),
        in_land=vm((chips - 1, share, 3 * own), BF16), in_own=vm((share, 3 * own), F32),
        out_send=vm((chips - 1, share, width), BF16), out_land=vm((chips - 1, share, width), BF16),
        outz_send=vm((share, width), BF16), outz_land=vm((zpeers, rows_out, width), BF16),
        outz_own=vm((rows_out, width), F32),
        load_sem=dma((16,)),
        pool_sem=dma((groups,)),
        win_sem=dma((3,)),
        ffn_sem=dma((2, 2)),
        local_sem=dma((16,)),
        stage_sem=dma((2,)),
        ag_s=dma((2, 3)), ag_r=dma((2, 3)), fs_s=dma((2,)), fs_r=dma((2,)),
        halo_s=dma((2,)), halo_r=dma((2,)),
        za_s=dma((4, zpeers)), za_r=dma((4, zpeers)),
        pa_s=dma((2, 6)), pa_r=dma((2, 6)),
        cx_s=dma((3,)), cx_r=dma((3,)), zg_s=dma((zpeers,)), zg_r=dma((zpeers,)),
        wi_s=dma((chips - 1,)), wi_r=dma((chips - 1,)), ti_s=dma((zpeers, 3)), ti_r=dma((zpeers, 3)), wo_s=dma((2, chips - 1)), wo_r=dma((2, chips - 1)),
        rs_s=dma((2, 2)), rs_r=dma((2, 2)),
        sm_s=dma((4, peers)), sm_r=dma((4, peers)),
        sz_s=dma((3, zpeers)), sz_r=dma((3, zpeers)),
        tr_s=dma((1, peers)), tr_r=dma((1, peers)),
    )
    names = [*inputs, *outputs, *scratch]

    def kernel(*refs):
        r = Named(names, refs)
        b, z = lax.axis_index("batch"), lax.axis_index("seq")
        chip, core = lax.div(b, 2), lax.rem(b, 2)
        sibling = chip * 2 + (1 - core)
        sent = {}

        chip_x, chip_y = lax.rem(chip, 2), lax.div(chip, 2)

        def flipped(turn_x, turn_y):
            x = chip_x + turn_x - 2 * chip_x * turn_x
            y = chip_y + turn_y - 2 * chip_y * turn_y
            return y * 2 + x

        def partner(way):
            return flipped(1 - way % 2, (way + 1) // 2)

        def way_of(step):
            return 2 if step == 2 else step + core - 2 * step * core

        def partner_at(way):
            return flipped(1 - lax.rem(way, 2), lax.div(way + 1, 2))

        def flip(value, turn):
            return value + turn - 2 * value * turn

        def turns(at):
            rest = 7 - at
            return lax.rem(rest, 2), lax.rem(lax.div(rest, 2), 2), lax.div(rest, 4)

        def chunk_group(at):
            turn_core, turn_x, turn_y = turns(jnp.int32(at))
            return (flip(chip_y, turn_y) * 2 + flip(chip_x, turn_x)) * 2 + flip(core, turn_core)

        def group_at(step):
            return lax.rem(b + step, groups)

        def block_at(step):
            return lax.rem(z + step, blocks)

        def span(at, size):
            return pl.ds(pl.multiple_of(at * size, size), size)

        def remote(src, dst, send_sem, recv_sem, **where):
            return pltpu.make_async_remote_copy(
                src_ref=src, dst_ref=dst, send_sem=send_sem, recv_sem=recv_sem,
                device_id=where, device_id_type=MESH,
            )

        def send(key, copy):
            copy.start()
            sent.setdefault(key, []).append(copy)

        def drain(key):
            for copy in sent.pop(key):
                copy.wait_send()

        def tiles(size, total, body):
            def step(i, carry):
                body(pl.multiple_of(i * size, size))
                return carry

            lax.fori_loop(0, total // size, step, 0)

        def load(sem, src, dst):
            copy = pltpu.make_async_copy(src, dst, sem)
            copy.start(priority=1)
            return copy

        def load_win(block):
            return load(r.win_sem.at[block], r.w_in.at[:, pl.ds(block * width, width)], r.win.at[block])

        load_tok = load(r.load_sem.at[0], r.tokens, r.tok)
        win_loads = [(block, load_win(block)) for block in (1, 2, 0)]
        load_cot = load(r.load_sem.at[5], r.cot, r.cotv)
        load_w3 = load(r.load_sem.at[1], r.filt_w3.at[:, span(z, own)], r.w3)
        load_fade = load(r.load_sem.at[2], r.decay.at[:, span(z, own)], r.fade)
        load_cs = load(r.load_sem.at[3], r.cosine, r.cs)
        load_sn = load(r.load_sem.at[4], r.sine, r.sn)
        load_wout = load(r.load_sem.at[6], r.w_out, r.wout)

        barrier = pltpu.get_barrier_semaphore()
        for step in range(1, groups):
            pl.semaphore_signal(barrier, inc=1, device_id={"batch": group_at(step)}, device_id_type=MESH)
        for step in range(1, blocks):
            pl.semaphore_signal(barrier, inc=1, device_id={"seq": block_at(step)}, device_id_type=MESH)

        def member(k, turn_side, turn_core):
            side = chip_y if k else chip_x
            return flip(side, turn_side) * 2 + flip(core, turn_core)

        def slot(k, at):
            return r.n2_land.at[at] if k else r.cot_land.at[span(at, tokens)]

        def gather_copy(k, at, src, dst, to):
            return remote(src, dst, r.ag_s.at[k, at], r.ag_r.at[k, at], batch=to)

        def gather_local(k, src):
            return pltpu.make_async_copy(src, slot(k, member(k, 0, 0)), r.local_sem.at[k])

        def gather_start(k, src):
            dst = slot(k, member(k, 0, 0))
            send(("ag", k), gather_copy(k, 0, src, dst, partner(k) * 2 + core))
            send(("ag", k), gather_copy(k, 1, src, dst, sibling))
            gather_local(k, src).start(priority=1)

        def gather_forward(k):
            dst = slot(k, member(k, 1, 0))
            gather_copy(k, 0, dst, dst, sibling).wait_recv()
            staged = r.win.at[2, :, 3 * own : 3 * own + tokens] if k else r.gproj.at[:, 0:width]
            load(r.stage_sem.at[k], dst, staged).wait()
            send(("forward", k), gather_copy(k, 2, staged, dst, sibling))

        def gather_finish(k, src):
            gather_local(k, src).wait()
            for at in range(2):
                dst = slot(k, member(k, at, 1))
                gather_copy(k, 1 + at, dst, dst, sibling).wait_recv()

        def turned(value_ref, out_ref):
            def body(at):
                tile = value_ref[:, pl.ds(at, share)].T
                group = lax.div(at, share)
                for block in range(blocks):
                    first = pl.multiple_of(block * own + group * rows_out, rows_out)
                    out_ref[pl.ds(first, rows_out), :] = tile[block * rows_out : (block + 1) * rows_out]

            tiles(share, width, body)

        def turned_by_core(value_ref, out_ref):
            def body(at):
                group = lax.div(at, share)
                out_ref[span(lax.rem(group, 2) * chips + lax.div(group, 2), share), :] = value_ref[
                    :, pl.ds(at, share)
                ].T

            tiles(share, width, body)

        load_tok.wait()

        def norm1(at):
            rows = pl.ds(at, 32)
            x = r.tok[rows, :].astype(F32)
            xhat, inverse = norm_parts(x)
            r.mean1[rows, :] = jnp.broadcast_to(jnp.mean(x, axis=-1, keepdims=True), (32, 128))
            r.inv1[rows, :] = jnp.broadcast_to(inverse, (32, 128))
            r.n1_all[pl.ds(pl.multiple_of(z * tokens + at, 32), 32), :] = (xhat * r.gain1[...]).astype(BF16)

        tiles(32, tokens, norm1)
        for block, copy in win_loads:
            copy.wait()
            cols = slice(block * width, (block + 1) * width)
            proj = mm(r.n1_all[span(z, tokens), :], r.win[block], out=BF16)
            r.ext[16:, cols] = proj
            r.halo_out[:, cols] = proj[tokens - 16 :]
        pl.semaphore_wait(barrier, peers + zpeers)
        halo = remote(r.halo_out, r.halo_in, r.halo_s.at[0], r.halo_r.at[0], seq=block_at(1))
        send("halo", halo)
        own_loads = [
            load(
                r.load_sem.at[7 + part],
                r.w_in.at[:, pl.ds(pl.multiple_of(part * width + z * own, own), own)],
                r.win.at[2, :, part * own : (part + 1) * own],
            )
            for part in range(3)
        ]
        for padded in (r.chan, r.conv_out, r.gconv_c, r.glong_c):
            padded[length:, :] = jnp.zeros((spare, own), BF16)
        r.ext_c[0:spare, :] = jnp.zeros((spare, 3 * own), BF16)
        r.ext_c[length + spare :, :] = jnp.zeros((spare, 3 * own), BF16)

        def up_weights(at, slot):
            group = chunk_group(at)
            return pltpu.make_async_copy(
                r.w_up.at[:, span(group, ffc)], r.win.at[0, :, span(slot, ffc)], r.ffn_sem.at[slot, 0]
            )

        def down_weights(at, slot):
            group = chunk_group(at)
            return pltpu.make_async_copy(
                r.w_down.at[span(group, ffc)], r.win.at[1, span(slot, ffc)], r.ffn_sem.at[slot, 1]
            )

        for at in range(2):
            down_weights(at, at).start(priority=1)
            up_weights(at, at).start(priority=1)

        halo.wait_recv()
        r.ext[0:16, :] = (r.halo_in[...].astype(F32) * jnp.where(z > 0, 1.0, 0.0)).astype(BF16)

        def lags_at(cols):
            wide = r.ext[:, cols].astype(F32)
            return [wide[16 - lag : 16 - lag + tokens] for lag in range(3)]

        def mix(cols):
            lags = lags_at(cols)
            short = r.short[:, cols].astype(F32)
            return lags, short[0:1] * lags[0] + short[1:2] * lags[1] + short[2:3] * lags[2]

        def chan_copy(k, src, dst, step, to):
            return remote(src, dst, r.za_s.at[k, step - 1], r.za_r.at[k, step - 1], seq=to)

        def to_channels(k, value_ref, make_cols):
            for step in list(range(1, blocks)) + [0]:
                block = block_at(step)
                make_cols(block)
                if step:
                    src, dst = value_ref.at[:, span(block, own)], r.chan.at[span(z, tokens)]
                    send(("za", k), chan_copy(k, src, dst, step, block))
                else:
                    r.chan[span(z, tokens), :] = value_ref[:, span(block, own)]

        def wait_channels(k):
            for step in range(1, blocks):
                source = block_at(blocks - step)
                dst = r.chan.at[span(source, tokens)]
                chan_copy(k, dst, dst, step, source).wait_recv()

        def signal_block(block):
            def body(at):
                base = block * own + at
                cols = pl.ds(pl.multiple_of(base, 128), 128)
                gate_in = mix(pl.ds(pl.multiple_of(width + base, 128), 128))[1]
                values = mix(pl.ds(pl.multiple_of(2 * width + base, 128), 128))[1]
                r.sig[:, cols] = (values * gate_in).astype(BF16)

            tiles(128, own, body)

        to_channels(0, r.sig, signal_block)
        load_cot.wait()
        gather_start(0, r.cotv)

        load_w3.wait()
        load_fade.wait()

        def fading(at):
            lag = (lax.broadcasted_iota(jnp.int32, (tokens, own), 0) + at).astype(F32)
            return jnp.exp(-r.fade[...] * lag)

        def taps_rows(at):
            rows = pl.ds(at, tokens)
            h1, r.s1[:, rows] = sin_cos(mm_tn(r.filt_w1[...], r.features_t[:, rows], precision=HIGHEST))
            h2, r.s2[:, rows] = sin_cos(mm_tn(r.filt_w2[...], h1, precision=HIGHEST))
            r.h1[:, rows] = h1
            r.h2[:, rows] = h2
            taps = mm_tn(h2, r.w3[...], precision=HIGHEST) * fading(at)
            r.qre[rows, :] = taps.astype(BF16)

        tiles(tokens, length, taps_rows)
        load_cs.wait()
        load_sn.wait()
        scale = 1.0 / length

        def taps_spec(at):
            rows = pl.ds(at, tokens)
            real = mm(r.cs[rows, :], r.qre[...]) * scale
            imag = mm(r.sn[rows, :], r.qre[...]) * -scale
            turn_re, turn_im = r.phase[rows, 0:1], r.phase[rows, 1:2]
            r.hre[rows, :] = (real * turn_re - imag * turn_im).astype(BF16)
            r.him[rows, :] = (real * turn_im + imag * turn_re).astype(BF16)

        tiles(tokens, length, taps_spec)

        wait_channels(0)

        def conv_spec(at):
            rows = pl.ds(at, tokens)
            real = mm(r.cs[rows, :], r.chan[0:length, :])
            imag = -mm(r.sn[rows, :], r.chan[0:length, :])
            r.xre[rows, :] = real.astype(BF16)
            r.xim[rows, :] = imag.astype(BF16)
            hre, him = r.hre[rows, :].astype(F32), r.him[rows, :].astype(F32)
            r.yre[rows, :] = (hre * real - him * imag).astype(BF16)
            r.yim[rows, :] = (-(hre * imag + him * real)).astype(BF16)

        tiles(tokens, length, conv_spec)

        def to_tokens(k, out_ref):
            for step in list(range(1, blocks)) + [0]:
                block = block_at(step)
                rows = span(block, tokens)
                tile = (mm(r.cs[rows, :], r.yre[...]) + mm(r.sn[rows, :], r.yim[...])).astype(BF16)
                out_ref[rows, :] = tile
                if step:
                    src, dst = out_ref.at[rows], r.conv_in.at[z]
                    send(("za", k), chan_copy(k, src, dst, step, block))
                else:
                    r.conv_in[z] = tile

        def wait_tokens(k):
            for step in range(1, blocks):
                source = block_at(blocks - step)
                dst = r.conv_in.at[source]
                chan_copy(k, dst, dst, step, source).wait_recv()

        to_tokens(1, r.conv_out)

        def seq_gather(step, source, to):
            rows = r.n1_all.at[span(source, tokens)]
            return remote(rows, rows, r.zg_s.at[step - 1], r.zg_r.at[step - 1], seq=to)

        for step in range(1, blocks):
            send("n1", seq_gather(step, z, block_at(step)))

        load_wout.wait()
        def gate_cols(at):
            cols = pl.ds(at, 128)
            r.gate_out[:, cols] = mix(cols)[1]

        tiles(128, width, gate_cols)

        def grad_hidden(at, carry):
            slot = lax.rem(at, 2)
            down_weights(at, slot).wait()
            r.pre_send[at] = mm_nt(r.cotv[...], r.win[1, span(slot, ffc), :], out=BF16)
            down_weights(lax.rem(at + 2, groups), slot).start(priority=1)
            return carry

        lax.fori_loop(0, groups, grad_hidden, 0)
        wait_tokens(1)

        def conv_cols(at):
            return r.conv_in[
                lax.div(at, own), :, pl.ds(pl.multiple_of(lax.rem(at, own), 128), 128)
            ].astype(F32)

        def long_cols(at):
            cols = pl.ds(at, 128)
            long = conv_cols(at) + r.bias[:, cols] * r.sig[:, cols].astype(F32)
            r.long[:, cols] = long
            r.half[:, cols] = (long * r.gate_out[:, cols]).astype(BF16)

        tiles(128, width, long_cols)
        r.res[...] = mm(r.half[...], r.wout[...])
        turned_by_core(r.half, r.gated_turn)
        mine = span(core, tokens)
        pair_rows = chips * share

        def pair_copy(k, src, dst):
            return remote(src, dst, r.cx_s.at[k], r.cx_r.at[k], batch=sibling)

        gated_copy = pair_copy(
            0, r.gated_turn.at[span(1 - core, pair_rows)], r.gated_pair.at[:, mine]
        )
        send("pair", gated_copy)
        r.gated_pair[:, mine] = r.gated_turn[span(core, pair_rows), :]

        def norm2(at):
            rows = pl.ds(at, 32)
            residual = r.res[rows, :] + r.tok[rows, :].astype(F32)
            r.res[rows, :] = residual
            xhat, inverse = norm_parts(residual)
            r.xhat2[rows, :] = xhat
            r.inv2[rows, :] = jnp.broadcast_to(inverse, (32, 128))
            r.half[rows, :] = (xhat * r.gain2[...]).astype(BF16)

        tiles(32, tokens, norm2)
        turned(r.half, r.turn)
        gather_start(1, r.turn)
        r.gn2[...] = jnp.zeros((tokens, width), F32)

        def plane_copy(k, at):
            turn_core, turn_x, turn_y = turns(jnp.int32(at))
            turn_side, turn_far = (turn_y, turn_x) if k else (turn_x, turn_y)
            index = turn_far * 3 + turn_side * 2 + turn_core - 1
            if k:
                to = (flip(chip_y, turn_y) * 2 + chip_x) * 2 + flip(core, turn_core)
                src, dst = r.pre_send.at[at], r.pre_own.at[flip(chip_x, turn_x), span(member(1, 0, 0), tokens)]
            else:
                to = (chip_y * 2 + flip(chip_x, turn_x)) * 2 + flip(core, turn_core)
                src = r.hid_send.at[at]
                dst = r.hid_own.at[flip(chip_y, turn_y), :, span(member(0, 0, 0), tokens)]
            return remote(src, dst, r.pa_s.at[k, index], r.pa_r.at[k, index], batch=to)

        hidden_remote = [0, 1, 2, 4, 5, 6]
        pre_remote = [0, 1, 2, 3, 4, 6]

        def chunk(at, carry):
            slot = lax.rem(at, 2)
            where = span(slot, ffc)
            up_weights(at, slot).wait()
            r.gres[:, 0:ffc] = mm(r.half[...], r.win[0, :, where])

            def act(row):
                rows = pl.ds(row, 32)
                pre = r.gres[rows, 0:ffc]
                square = pre * pre
                bent = jnp.tanh(pre * (GELU_SCALE + GELU_SCALE * GELU_CUBIC * square))
                upper = 0.5 + 0.5 * bent
                slope = upper + pre * (0.5 - 0.5 * bent * bent) * (
                    GELU_SCALE + 3.0 * GELU_SCALE * GELU_CUBIC * square
                )
                r.hid_buf[rows, :] = (pre * upper).astype(BF16)
                r.pre_send[at, rows, :] = (r.pre_send[at, rows, :].astype(F32) * slope).astype(BF16)

            tiles(32, tokens, act)
            r.hid_send[at] = r.hid_buf[...].T

            @pl.when(lax.rem(at, 4) < 3)
            def _():
                plane_copy(0, at).start()

            @pl.when((at < 5) | (at == 6))
            def _():
                plane_copy(1, at).start()

            down_weights(at, slot).wait()
            r.res[...] += mm(r.hid_buf[...], r.win[1, where, :])
            r.gn2[...] += mm_nt(r.pre_send[at], r.win[0, :, where])

            @pl.when(at < groups - 2)
            def _():
                up_weights(at + 2, slot).start(priority=1)
                down_weights(at + 2, slot).start(priority=1)

            return carry

        lax.fori_loop(0, groups, chunk, 0)
        for at in hidden_remote:
            sent.setdefault("ffn", []).append(plane_copy(0, at))
        for at in pre_remote:
            sent.setdefault("ffn", []).append(plane_copy(1, at))

        for turn, at in ((0, 7), (1, 3)):
            r.hid_own[flip(chip_y, turn), :, span(member(0, 0, 0), tokens)] = r.hid_send[at]
        for turn, at in ((0, 7), (1, 5)):
            r.pre_own[flip(chip_x, turn), span(member(1, 0, 0), tokens), :] = r.pre_send[at]

        def norm2_back(at, total):
            rows = pl.ds(pl.multiple_of(at * 32, 32), 32)
            r.half[rows, :] = r.res[rows, :].astype(BF16)
            grad, xhat = r.gn2[rows, :], r.xhat2[rows, :]
            back = r.cotv[rows, :].astype(F32) + norm_back(grad, r.gain2[...], xhat, r.inv2[rows, 0:1])
            r.gres[rows, :] = back
            r.gbr_pair[pl.ds(pl.multiple_of(core * tokens + at * 32, 32), 32), :] = back.astype(BF16)
            return total + jnp.sum((grad * xhat).reshape(4, 8, width), axis=0)

        total = lax.fori_loop(0, tokens // 32, norm2_back, jnp.zeros((8, width), F32))
        r.sum_gain2[...] = jnp.sum(total, axis=0, keepdims=True)
        store_layer = load(r.local_sem.at[8], r.half, r.layer_out)
        branch_copy = pair_copy(1, r.gbr_pair.at[mine], r.gbr_pair.at[mine])
        send("pair", branch_copy)

        def gated_back(block):
            cols = span(block, own)
            grad = mm_nt(r.gbr_pair[mine, :], r.wout[span(block, own), :])
            glong = (grad * r.gate_out[:, cols]).astype(BF16)
            r.glong[:, cols] = glong
            r.tok[:, cols] = grad.astype(BF16)
            r.long[:, cols] = grad * r.long[:, cols]
            r.sum_bias[:, cols] = jnp.sum(
                glong.astype(F32) * r.sig[:, cols].astype(F32), axis=0, keepdims=True
            )

        to_channels(2, r.tok, gated_back)
        gather_forward(0)
        gather_forward(1)


        branch_copy.wait_recv()
        gated_copy.wait_recv()

        def out_copy(way):
            sems = r.wo_s.at[0, way], r.wo_r.at[0, way]
            to = partner_at(jnp.int32(way)) * 2 + core
            return remote(r.out_send.at[way], r.out_land.at[way], *sems, batch=to)

        for step in range(chips):
            to = partner(step - 1) if step else chip
            part = mm(r.gated_pair[span(to, share), :], r.gbr_pair[...])
            if step:
                r.out_send[step - 1] = part.astype(BF16)
            else:
                r.xhat2[share : 2 * share, :] = part

        near = z + 1 - 2 * lax.rem(z, 2)
        far = block_at(2)

        def reduce_zero_copy(k, refs):
            to = partner(0 if k else 1) * 2 + core
            return remote(refs[0], refs[1], r.fs_s.at[k], r.fs_r.at[k], batch=to)

        def reduce_first(k, refs):
            return remote(refs[0].at[0:2], refs[2], r.rs_s.at[k, 0], r.rs_r.at[k, 0], seq=near)

        def reduce_second(k, refs):
            return remote(refs[0].at[2], refs[3], r.rs_s.at[k, 1], r.rs_r.at[k, 1], seq=far)

        def reduce_zero(k, refs, part_of):
            other = 1 - (chip_x if k else chip_y)
            for block in range(blocks):
                refs[0][block] = part_of(other, block).astype(BF16)
            send(("zero", k), reduce_zero_copy(k, refs))

        def reduce_send(k, refs, part_of):
            reduce_zero_copy(k, refs).wait_recv()
            drain(("zero", k))
            mine_too = chip_x if k else chip_y

            def total(block):
                return part_of(mine_too, block) + refs[1][block].astype(F32)

            refs[0][0] = total(near).astype(BF16)
            refs[0][1] = total(lax.rem(near + 2, blocks)).astype(BF16)
            send("rs", reduce_first(k, refs))
            refs[0][2] = total(far).astype(BF16)
            refs[4][...] = total(z)

        def reduce_next(k, refs):
            reduce_first(k, refs).wait_recv()
            refs[0][2] = (refs[0][2].astype(F32) + refs[2][1].astype(F32)).astype(BF16)
            send("rs", reduce_second(k, refs))
            refs[4][...] += refs[2][0].astype(F32)

        def reduce_finish(k, refs):
            reduce_second(k, refs).wait_recv()
            refs[4][...] += refs[3][...].astype(F32)

        down_refs = (r.down_send, r.down_first, r.down_land, r.down_last, r.xhat2.at[0:down_rows])
        up_refs = (r.up_send, r.up_first, r.up_land, r.up_last, r.gate_out.at[:, 0:ffc])

        def wait_plane(k):
            for at in pre_remote if k else hidden_remote:
                plane_copy(k, at).wait_recv()

        def down_part(group, block):
            return mm(r.hid_own[group, span(block, down_rows), :], r.win[0])

        def up_part(group, block):
            return mm(r.win[1, span(block, own), :], r.pre_own[group])

        gather_finish(0, r.cotv)
        cot_pool = load(r.pool_sem.at[4], r.cot_land, r.win.at[0])
        gather_finish(1, r.turn)
        pool = [
            load(r.pool_sem.at[at], r.n2_land.at[at], r.win.at[1, :, pl.ds(at * tokens, tokens)])
            for at in range(4)
        ]
        cot_pool.wait()
        wait_plane(0)
        reduce_zero(0, down_refs, down_part)
        for copy in pool:
            copy.wait()
        wait_plane(1)
        reduce_zero(1, up_refs, up_part)

        for step in range(1, blocks):
            source = block_at(blocks - step)
            seq_gather(step, source, source).wait_recv()
        for copy in own_loads:
            copy.wait()

        def proj_rows(at):
            r.ext_c[pl.ds(pl.multiple_of(at + spare, spare), tokens), :] = mm(
                r.n1_all[pl.ds(at, tokens), :], r.win[2, :, 0 : 3 * own], out=BF16
            )

        tiles(tokens, length, proj_rows)

        def own_cols(part, at):
            return pl.ds(pl.multiple_of(part * width + z * own + at, 128), 128)

        def mix_own(part, at, first, rows):
            wide = r.ext_c[pl.ds(first, rows + spare), part * own + at : part * own + at + 128].astype(F32)
            short = r.short[:, own_cols(part, at)].astype(F32)
            lags = [wide[spare - lag : spare - lag + rows] for lag in range(3)]
            return short[0:1] * lags[0] + short[1:2] * lags[1] + short[2:3] * lags[2]

        wait_channels(2)

        def long_rows(first):
            rows = pl.ds(first, tokens)
            for at in range(0, own, 128):
                cols = slice(at, at + 128)
                gate = mix_own(0, at, first, tokens)
                r.glong_c[rows, cols] = (r.chan[rows, cols].astype(F32) * gate).astype(BF16)

        tiles(tokens, length, long_rows)

        def grad_spec(at):
            rows = pl.ds(at, tokens)
            real = mm(r.cs[rows, :], r.glong_c[0:length, :])
            imag = -mm(r.sn[rows, :], r.glong_c[0:length, :])
            hre, him = r.hre[rows, :].astype(F32), r.him[rows, :].astype(F32)
            r.yre[rows, :] = (hre * real + him * imag).astype(BF16)
            r.yim[rows, :] = (him * real - hre * imag).astype(BF16)
            xre, xim = r.xre[rows, :].astype(F32), r.xim[rows, :].astype(F32)
            both_re = xre * real + xim * imag
            both_im = xre * imag - xim * real
            turn_re, turn_im = r.phase[rows, 0:1], r.phase[rows, 1:2]
            r.qre[rows, :] = ((both_re * turn_re + both_im * turn_im) * scale).astype(BF16)
            r.qim[rows, :] = ((both_re * turn_im - both_im * turn_re) * scale).astype(BF16)

        tiles(tokens, length, grad_spec)
        to_tokens(3, r.gconv_c)

        def proj_back(first):
            rows = pl.ds(first, tokens + spare)
            for at in range(0, own, 128):
                cols = slice(at, at + 128)
                gate_in = mix_own(1, at, first, tokens + spare)
                values = mix_own(2, at, first, tokens + spare)
                bias = r.bias[:, own_cols(0, at)]
                signal = (values * gate_in).astype(BF16).astype(F32)
                long = r.conv_out[rows, cols].astype(F32) + bias * signal
                grad_signal = r.gconv_c[rows, cols].astype(F32) + bias * r.glong_c[rows, cols].astype(F32)
                parts = (r.chan[rows, cols].astype(F32) * long, grad_signal * values, grad_signal * gate_in)
                for part, grad in enumerate(parts):
                    short = r.short[:, own_cols(part, at)].astype(F32)
                    total = (
                        short[0:1] * grad[0:tokens]
                        + short[1:2] * grad[1 : tokens + 1]
                        + short[2:3] * grad[2 : tokens + 2]
                    )
                    r.gproj_c[pl.ds(first, tokens), part * own + at : part * own + at + 128] = total.astype(BF16)

        tiles(tokens, length, proj_back)

        def in_part(group):
            return mm_tn(r.n1_all[:, span(group, share)], r.gproj_c[...])

        for at in range(chips):
            r.in_send[at] = in_part(at * 2 + 1 - core).astype(BF16)
        in_pair = pair_copy(2, r.in_send, r.in_pair)
        send("in_pair", in_pair)
        in_pair.wait_recv()
        drain("in_pair")

        def in_copy(way):
            sems = r.wi_s.at[way], r.wi_r.at[way]
            to = partner_at(jnp.int32(way)) * 2 + core
            return remote(r.in_send.at[way], r.in_land.at[way], *sems, batch=to)

        for step in range(chips):
            way = way_of(step) if step < chips - 1 else None
            to = chip if way is None else partner_at(jnp.int32(way))
            part = in_part(to * 2 + core) + r.in_pair[to].astype(F32)
            if way is None:
                r.in_own[...] = part
            else:
                r.in_send[way] = part.astype(BF16)
                send("in", in_copy(way))

        r.w12[...] = jnp.zeros((net_rows, 128), F32)
        r.sum_w3[...] = jnp.zeros((filt, own), F32)
        for at in range(0, length, tokens):
            rows = slice(at, at + tokens)
            grad_taps = mm(r.cs[rows, :], r.qre[...]) + mm(r.sn[rows, :], r.qim[...])
            grad_filt = grad_taps * fading(at)
            r.sum_w3[...] += mm(r.h2[:, rows], grad_filt, precision=HIGHEST)
            grad_angle2 = mm_nt(r.w3[...], grad_filt, precision=HIGHEST) * r.s2[:, rows]
            r.w12[:, :filt] += mm_nt(r.h1[:, rows], grad_angle2, precision=HIGHEST)
            grad_angle1 = mm(r.filt_w2[...], grad_angle2, precision=HIGHEST) * r.s1[:, rows]
            r.w12[:emb, filt : 2 * filt] += mm_nt(r.features_t[:, rows], grad_angle1, precision=HIGHEST)

        def small_copy(k, src, dst, at, to):
            return remote(src, dst, r.sm_s.at[k, at], r.sm_r.at[k, at], batch=to)

        def small_z_copy(k, src, dst, step, to):
            return remote(src, dst, r.sz_s.at[k, step - 1], r.sz_r.at[k, step - 1], seq=to)

        def small_z_send(k, src, dst_of):
            for step in range(1, blocks):
                send("small", small_z_copy(k, src, dst_of(step), step, block_at(step)))

        def small_z_wait(k, dst_of):
            for step in range(1, blocks):
                dst = dst_of(step)
                small_z_copy(k, dst, dst, step, block_at(blocks - step)).wait_recv()

        def small_send(k, src_of, dst_of):
            for at in range(peers):
                to = group_at(1 + at)
                send("small", small_copy(k, src_of(to), dst_of(at), at, to))

        def small_wait(k, dst_of):
            for at in range(peers):
                dst = dst_of(at)
                small_copy(k, dst, dst, at, group_at(groups - 1 - at)).wait_recv()

        w3_rows = filt // groups
        small_z_send(0, r.w12, lambda step: r.w12_z.at[step - 1])
        small_send(0, lambda to: r.sum_w3.at[span(to, w3_rows)], lambda at: r.w3_land.at[at])

        reduce_send(0, down_refs, down_part)
        reduce_send(1, up_refs, up_part)
        drain(("forward", 1))
        win_loads = [(block, load_win(block)) for block in range(3)]

        def outz_copy(step, to):
            sems = r.wo_s.at[1, step - 1], r.wo_r.at[1, step - 1]
            return remote(r.outz_send.at[span(to, rows_out)], r.outz_land.at[step - 1], *sems, seq=to)


        def short_sums(cols, grad, lags):
            for lag in range(3):
                r.sum_short[lag : lag + 1, cols] = jnp.sum(grad * lags[lag], axis=0, keepdims=True)

        def back_cols(cols, grad, lags):
            short_sums(cols, grad, lags)
            r.ghalo[:, cols] = grad[0:8]
            short = r.short[:, cols].astype(F32)
            longer = jnp.concatenate([grad, jnp.zeros((8, 128), F32)], axis=0)
            total = (
                short[0:1] * grad
                + short[1:2] * longer[1 : tokens + 1]
                + short[2:3] * longer[2 : tokens + 2]
            )
            r.gproj[:, cols] = total.astype(BF16)
            r.tail[:, cols] = total[tokens - 16 :]

        def mixed_cols(at):
            cols = pl.ds(at, 128)
            grad_signal = conv_cols(at) + r.bias[:, cols] * r.glong[:, cols].astype(F32)
            gate_cols = pl.ds(pl.multiple_of(width + at, 128), 128)
            value_cols = pl.ds(pl.multiple_of(2 * width + at, 128), 128)
            gate_lags, gate_in = mix(gate_cols)
            value_lags, values = mix(value_cols)
            back_cols(gate_cols, grad_signal * values, gate_lags)
            back_cols(value_cols, grad_signal * gate_in, value_lags)

        def gate_back(at):
            cols = pl.ds(at, 128)
            back_cols(cols, r.long[:, cols], lags_at(cols))

        drain(("forward", 0))
        tiles(128, width, gate_back)
        wait_tokens(3)
        tiles(128, width, mixed_cols)
        halo = remote(r.ghalo, r.ghalo_in, r.halo_s.at[1], r.halo_r.at[1], seq=block_at(blocks - 1))
        send("halo", halo)
        halo.wait_recv()
        later = r.ghalo_in[...] * jnp.where(z < blocks - 1, 1.0, 0.0)

        def tail_cols(at):
            cols = slice(at, at + width)
            short = r.short[:, cols].astype(F32)
            row = lax.broadcasted_iota(jnp.int32, (16, width), 0)
            last = short[1:2] * later[0:1, cols] + short[2:3] * later[1:2, cols]
            total = r.tail[:, cols] + jnp.where(row == 15, last, 0.0)
            total = total + jnp.where(row == 14, short[2:3] * later[0:1, cols], 0.0)
            r.gproj[tokens - 16 :, cols] = total.astype(BF16)

        for part in range(3):
            tail_cols(part * width)

        def spread(k, own_ref, out_ref, size):
            for at in range(peers):
                to = group_at(1 + at)
                src, dst = own_ref.at[span(to, rows_out)], out_ref.at[:, span(b, size)]
                send("spread", remote(src, dst, r.tr_s.at[k, at], r.tr_r.at[k, at], batch=to))
            return load(r.local_sem.at[14 + k], own_ref.at[span(b, rows_out)], out_ref.at[:, span(b, size)])

        def spread_finish(k, copy, out_ref, size):
            for at in range(peers):
                source = group_at(groups - 1 - at)
                dst = out_ref.at[:, span(source, size)]
                remote(dst, dst, r.tr_s.at[k, at], r.tr_r.at[k, at], batch=source).wait_recv()
            copy.wait()

        for step in range(chips - 1):
            send("out", out_copy(way_of(step)))
        small_z_wait(0, lambda step: r.w12_z.at[step - 1])
        net = r.w12[...]
        for step in range(zpeers):
            net = net + r.w12_z[step]
        r.w12_sum[...] = net
        small_send(1, lambda to: r.w12_sum, lambda at: r.w12_plane.at[at])
        small_wait(0, lambda at: r.w3_land.at[at])
        part = r.sum_w3[span(b, w3_rows), :]
        for at in range(peers):
            part = part + r.w3_land[at]
        r.w3_part[...] = part
        r.w3_all[z, span(b, w3_rows), :] = part
        small_send(2, lambda to: r.w3_part, lambda at: r.w3_all.at[z, span(b, w3_rows)])
        reduce_next(0, down_refs)
        small_wait(1, lambda at: r.w12_plane.at[at])
        net = r.w12_sum[...]
        for at in range(peers):
            net = net + r.w12_plane[at]
        r.grad_w1[...] = net[:emb, filt : 2 * filt]
        r.grad_w2[...] = net[:, :filt]
        for at in range(peers):
            dst = r.w3_all.at[z, span(group_at(groups - 1 - at), w3_rows)]
            small_copy(2, dst, dst, at, group_at(groups - 1 - at)).wait_recv()
        small_z_send(1, r.w3_all.at[z], lambda step: r.w3_all.at[z])
        for way in range(chips - 1):
            in_copy(way).wait_recv()
        total = r.in_own[...]
        for step in range(chips - 1):
            total = total + r.in_land[step].astype(F32)
        r.in_own[...] = total

        def in_spread(step, part, block, to):
            src = r.in_own.at[span(to, rows_out), part * own : (part + 1) * own]
            dst = r.grad_w_in.at[:, pl.ds(pl.multiple_of(part * width + block * own, own), own)]
            if step == 0:
                return pltpu.make_async_copy(src, dst, r.load_sem.at[10 + part])
            return remote(src, dst, r.ti_s.at[step - 1, part], r.ti_r.at[step - 1, part], seq=to)

        for part in range(3):
            for step in range(1, blocks):
                send("in_spread", in_spread(step, part, z, block_at(step)))
            in_spread(0, part, z, z).start()
        for _, copy in win_loads:
            copy.wait()
        r.gn2[...] = mm_nt(r.gproj[:, :width], r.win[0])
        r.gn2[...] += mm_nt(r.gproj[:, width : 2 * width], r.win[1])
        r.gn2[...] += mm_nt(r.gproj[:, 2 * width :], r.win[2])

        reduce_next(1, up_refs)
        drain(("za", 2))
        load(r.load_sem.at[0], r.tokens, r.tok).wait()

        def norm1_back(at, total):
            rows = pl.ds(pl.multiple_of(at * 32, 32), 32)
            grad, inverse = r.gn2[rows, :], r.inv1[rows, 0:1]
            xhat = (r.tok[rows, :].astype(F32) - r.mean1[rows, 0:1]) * inverse
            r.res[rows, :] = r.gres[rows, :] + norm_back(grad, r.gain1[...], xhat, inverse)
            return total + jnp.sum((grad * xhat).reshape(4, 8, width), axis=0)

        total = lax.fori_loop(0, tokens // 32, norm1_back, jnp.zeros((8, width), F32))
        r.sum_gain1[...] = jnp.sum(total, axis=0, keepdims=True)
        r.small_send[...] = jnp.zeros((groups, 16, share), F32)
        for group in range(groups):
            cols = slice(group * share, (group + 1) * share)
            r.small_send[group, 0:1, :] = r.sum_gain1[:, cols]
            r.small_send[group, 1:2, :] = r.sum_gain2[:, cols]
            r.small_send[group, 2:3, :] = r.sum_bias[:, cols]
            for lag in range(3):
                for third in range(3):
                    at = group * inc + third * share
                    row = 3 + 3 * lag + third
                    r.small_send[group, row : row + 1, :] = r.sum_short[lag : lag + 1, at : at + share]
        small_send(3, lambda to: r.small_send.at[to], lambda at: r.small_land.at[b])
        r.small_land[b] = r.small_send[b]
        store_tokens = load(r.local_sem.at[13], r.res, r.tokens_grad)
        reduce_finish(0, down_refs)
        store_down = load(r.local_sem.at[9], down_refs[4], r.grad_w_down)
        for way in range(chips - 1):
            out_copy(way).wait_recv()
        total = r.xhat2[share : 2 * share, :]
        for step in range(chips - 1):
            total = total + r.out_land[step].astype(F32)
        r.xhat2[share : 2 * share, :] = total
        r.outz_send[...] = total.astype(BF16)
        for step in range(1, blocks):
            send("outz", outz_copy(step, block_at(step)))
        r.outz_own[...] = r.xhat2[pl.ds(pl.multiple_of(share + z * rows_out, rows_out), rows_out), :]

        for at in range(peers):
            source = group_at(groups - 1 - at)
            dst = r.small_land.at[source]
            small_copy(3, dst, dst, at, source).wait_recv()
        small = r.small_land[0]
        for group in range(1, groups):
            small = small + r.small_land[group]
        r.small_sum[...] = small
        small_z_send(2, r.small_sum, lambda step: r.small_z.at[step - 1])
        reduce_finish(1, up_refs)
        spread_up = spread(0, up_refs[4], r.grad_w_up, ffc)
        for step in range(1, blocks):
            outz_copy(step, block_at(blocks - step)).wait_recv()
        total = r.outz_own[...]
        for step in range(zpeers):
            total = total + r.outz_land[step].astype(F32)
        r.outz_own[...] = total
        store_out = load(r.local_sem.at[11], r.outz_own, r.grad_w_out)
        def chosen(value, size):
            picked = value[:, :size]
            for block in range(1, blocks):
                picked = jnp.where(z == block, value[:, block * size : (block + 1) * size], picked)
            return picked

        for step in range(1, blocks):
            source = block_at(blocks - step)
            dst = r.w3_all.at[source]
            small_z_copy(1, dst, dst, step, source).wait_recv()
        third = r.w3_all[lax.div(b * share, own)]
        halves = own // share
        picked = third[:, :share]
        for half in range(1, halves):
            here = lax.rem(b, halves) == half
            picked = jnp.where(here, third[:, half * share : (half + 1) * share], picked)
        r.grad_w3[...] = chosen(picked, rows_out)
        small_z_wait(2, lambda step: r.small_z.at[step - 1])
        small = r.small_sum[...]
        for step in range(zpeers):
            small = small + r.small_z[step]
        r.grad_gain1[...] = chosen(small[0:1], rows_out)
        r.grad_gain2[...] = chosen(small[1:2], rows_out)
        r.grad_bias[...] = chosen(small[2:3], rows_out)
        for lag in range(3):
            for third in range(3):
                row = 3 + 3 * lag + third
                r.short_all[lag : lag + 1, third * share : (third + 1) * share] = small[row : row + 1]
        r.grad_short[...] = chosen(r.short_all[0:3, :], 3 * rows_out)
        spread_finish(0, spread_up, r.grad_w_up, ffc)
        for part in range(3):
            for step in range(1, blocks):
                source = block_at(blocks - step)
                in_spread(step, part, source, source).wait_recv()
            in_spread(0, part, z, z).wait()
        store_layer.wait()
        store_down.wait()
        store_out.wait()
        store_tokens.wait()
        for key in list(sent):
            drain(key)

    def call(args):
        result = pl.pallas_call(
            kernel,
            out_shape=[jax.ShapeDtypeStruct(shape, dtype) for shape, dtype, _ in outputs.values()],
            in_specs=[pl.BlockSpec(memory_space=space) for space in inputs.values()],
            out_specs=[pl.BlockSpec(memory_space=space) for *_, space in outputs.values()],
            scratch_shapes=list(scratch.values()),
            compiler_params=pltpu.CompilerParams(
                collective_id=0, has_side_effects=True, vmem_limit_bytes=KERNEL_VMEM
            ),
        )(*[args[name] for name in inputs])
        return settled(result[:13])

    return call


def settled(values):
    count = len(values)
    large = [at for at, value in enumerate(values) if value.size >= 1 << 15]

    def copy_all(*refs):
        sources, targets, held = refs[:count], refs[count : 2 * count], refs[2 * count : -1]
        sems = refs[-1]
        copies = [
            pltpu.make_async_copy(sources[at], held[k], sems.at[0, k]) for k, at in enumerate(large)
        ]
        for copy in copies:
            copy.start()
        for at in range(count):
            if at not in large:
                if at == count - 1:
                    targets[at][...] = sources[at][...].T
                else:
                    targets[at][...] = sources[at][...].reshape(targets[at].shape)
        stores = []
        for k, at in enumerate(large):
            copies[k].wait()
            stores.append(pltpu.make_async_copy(held[k], targets[at], sems.at[1, k]))
            stores[-1].start()
        for copy in stores:
            copy.wait()

    specs = [
        pl.BlockSpec(memory_space=pl.ANY if at in large else pltpu.VMEM) for at in range(count)
    ]
    return pl.pallas_call(
        copy_all,
        out_shape=[
            jax.ShapeDtypeStruct(value.shape[1:] if value.shape[0] == 1 else value.shape, value.dtype)
            for value in values[:-1]
        ]
        + [jax.ShapeDtypeStruct(values[-1].shape[::-1], values[-1].dtype)        ],
        in_specs=specs,
        out_specs=specs,
        scratch_shapes=[pltpu.VMEM(values[at].shape, values[at].dtype) for at in large]
        + [pltpu.SemaphoreType.DMA((2, len(large)))],
    )(*values)


def small_sums(gain1, bias, gain2, short, w1, w2, w3_own):
    blocks, position = lax.axis_size("seq"), lax.axis_index("seq")
    dests = lax.axis_size("batch") * blocks
    width, (filt_dim, own), emb = gain1.shape[0], w3_own.shape, w1.shape[0]
    w3_all = lax.dynamic_update_slice_in_dim(
        jnp.zeros((filt_dim, width), F32), w3_own, position * own, 1
    )
    share = width // dests
    small = jnp.concatenate(
        [
            gain1.reshape(dests, share),
            bias.reshape(dests, share),
            gain2.reshape(dests, share),
            short.reshape(3, dests, 3 * share).transpose(1, 0, 2).reshape(dests, 9 * share),
            w3_all.reshape(filt_dim, dests, share).transpose(1, 0, 2).reshape(dests, filt_dim * share),
        ],
        axis=1,
    )
    small = scatter_sum(small, wire=F32)[0]
    filters = all_sum(jnp.concatenate([w1, w2], axis=0))
    return (
        small[:share],
        small[3 * share : 12 * share].reshape(3, 3 * share),
        filters[:emb],
        filters[emb:],
        small[12 * share :].reshape(filt_dim, share),
        small[share : 2 * share],
        small[2 * share : 3 * share],
    )


def kernel_layer(
    tokens,
    norm_gain1,
    w_in,
    short_kernel,
    filt_w1,
    filt_w2,
    filt_w3,
    decay_rate,
    conv_bias,
    w_out,
    norm_gain2,
    w_up,
    w_down,
    cotangent,
):
    _, block_len, width = tokens.shape
    groups, blocks = lax.axis_size("batch"), lax.axis_size("seq")
    emb, filt = filt_w1.shape
    (cosine, sine), phase = symmetric_tables(block_len * blocks)
    features = lag_features(emb, block_len * blocks)
    call = kernel_plan(groups, blocks, block_len, width, w_up.shape[1], filt, emb)
    out = call(
        dict(
            tokens=tokens[0],
            cot=cotangent[0],
            w_in=w_in,
            w_out=w_out,
            w_up=w_up,
            w_down=w_down,
            cosine=jnp.asarray(cosine),
            sine=jnp.asarray(sine),
            filt_w3=filt_w3,
            decay=decay_rate[None],
            gain1=norm_gain1[None],
            gain2=norm_gain2[None],
            bias=conv_bias[None],
            short=short_kernel,
            filt_w1=filt_w1,
            filt_w2=filt_w2,
            features_t=jnp.asarray(features.T),
            phase=jnp.asarray(phase),
        )
    )
    layer_out, tokens_grad, w_in, w_out, w_up, w_down, gain1, gain2, bias, short, w1, w2, w3 = out
    return layer_out[None], tokens_grad[None], (gain1, short, w1, w2, w3.T, bias, gain2), (w_in, w_out, w_up, w_down)


def on_device(*args):
    tokens = args[0]
    fits = lax.axis_size("batch") == 8 and lax.axis_size("seq") == 4 and tokens.shape[1] * lax.axis_size("seq") <= 1024
    layer = kernel_layer if fits else plain_layer
    layer_out, tokens_grad, small, large = layer(*args)
    gain1, short, w1, w2, w3, bias, gain2 = small
    grad_w_in, grad_w_out, grad_w_up, grad_w_down = large
    return (
        layer_out, tokens_grad, gain1, grad_w_in, short, w1, w2, w3, bias, grad_w_out, gain2,
        grad_w_up, grad_w_down,
    )


def solution(mesh):
    split = P("batch", "seq", None)
    both = ("batch", "seq")
    return jax.shard_map(
        on_device,
        mesh=mesh,
        in_specs=(split,) + (P(),) * 12 + (split,),
        out_specs=(
            split,
            split,
            P(both),
            P(both, None),
            P(None, both),
            P(),
            P(),
            P(None, both),
            P(both),
            P(both, None),
            P(both),
            P(both, None),
            P(both, None),
        ),
        check_vma=False,
    )
```

```python
import math

import jax
import jax.numpy as jnp
import ml_dtypes
import numpy as np
from jax import lax
from jax.experimental import pallas as pl
from jax.experimental.pallas import tpu as pltpu
from jax.sharding import PartitionSpec as P

F32 = jnp.float32
BF16 = jnp.bfloat16
HIGHEST = lax.Precision.HIGHEST
GELU_SCALE = math.sqrt(2.0 / math.pi)
GELU_CUBIC = 0.044715


def dot(left, right, contract, out=F32, precision=None):
    return lax.dot_general(
        left, right, (contract, ((), ())), precision=precision, preferred_element_type=F32
    ).astype(out)


def mm(left, right, **kw):
    return dot(left, right, ((1,), (0,)), **kw)


def mm_nt(left, right, **kw):
    return dot(left, right, ((1,), (1,)), **kw)


def mm_tn(left, right, **kw):
    return dot(left, right, ((0,), (0,)), **kw)


def shifted(value, axis, steps):
    count = lax.axis_size(axis)
    first, last = (max(0, -steps), min(count, count - steps))
    return lax.ppermute(value, axis, [(source, source + steps) for source in range(first, last)])


def exchange(value, axis, bit):
    count = lax.axis_size(axis)
    return lax.ppermute(value, axis, [(at, at ^ (1 << bit)) for at in range(count)])


def bits_of(axis):
    return lax.axis_size(axis).bit_length() - 1


def stage_order(swap):
    batch_bits, seq_bits = bits_of("batch"), bits_of("seq")
    rest = list(range(1, batch_bits))
    half = len(rest) // 2
    if swap:
        rest = rest[half:] + rest[:half]
    return [("batch", bit) for bit in [0] + rest] + [("seq", bit) for bit in range(seq_bits)]


def scatter_sum(partial, swap=False, wire=BF16):
    batch_bits, seq_bits = bits_of("batch"), bits_of("seq")
    dims = [("batch", bit) for bit in reversed(range(batch_bits))]
    dims += [("seq", bit) for bit in reversed(range(seq_bits))]
    rows = partial.shape[0] >> len(dims)
    value = partial.reshape((2,) * len(dims) + (rows,) + partial.shape[1:]).astype(wire)
    for axis, bit in stage_order(swap):
        at = dims.index((axis, bit))
        mine = (lax.axis_index(axis) >> bit) & 1
        keep = lax.dynamic_index_in_dim(value, mine, at, keepdims=False)
        send = lax.dynamic_index_in_dim(value, 1 - mine, at, keepdims=False)
        got = exchange(send, axis, bit)
        value = keep.astype(F32) + got.astype(F32)
        dims.pop(at)
        if dims:
            value = value.astype(wire)
    return value


def gather_batch(value):
    return lax.all_gather(value, "batch", axis=0, tiled=True)


def columns_batch(value):
    return lax.all_to_all(value, "batch", 1, 0, tiled=True)


def rows_sum(left_own, right_all):
    blocks = lax.axis_size("seq")
    part = mm_tn(left_own, right_all, out=BF16)
    got = lax.all_to_all(part.reshape(blocks, -1, part.shape[1]), "seq", 0, 0, tiled=True)
    return jnp.sum(got.astype(F32), axis=0)


def columns_sum(left_all, right_own):
    blocks, groups = lax.axis_size("seq"), lax.axis_size("batch")
    part = mm_tn(left_all, right_own, out=BF16)
    part = part.reshape(groups * blocks, -1, part.shape[1])
    got = lax.all_to_all(part, ("batch", "seq"), 0, 0, tiled=True)
    got = jnp.sum(got.reshape(groups, blocks, -1, part.shape[2]).astype(F32), axis=1)
    return got.transpose(1, 0, 2).reshape(got.shape[1], -1)


def all_sum(value):
    for axis, bit in stage_order(False):
        value = value + exchange(value, axis, bit)
    return value


def norm_parts(values):
    centered = values - jnp.mean(values, axis=-1, keepdims=True)
    inverse = lax.rsqrt(jnp.mean(centered * centered, axis=-1, keepdims=True) + 1e-05)
    return centered * inverse, inverse


def norm_back(grad, gain, xhat, inverse):
    scaled = grad * gain
    return (
        scaled
        - jnp.mean(scaled, axis=-1, keepdims=True)
        - xhat * jnp.mean(scaled * xhat, axis=-1, keepdims=True)
    ) * inverse


def transform_table(length):
    count = np.arange(length, dtype=np.int64)
    turns = (2 * count[:, None] + 1) * count[None, :] % (4 * length)
    angles = turns.astype(np.float64) * (2.0 * np.pi / (4 * length))
    table = np.concatenate([np.cos(angles), -np.sin(angles)], axis=0)
    return table.astype(np.float32).astype(ml_dtypes.bfloat16)


def lag_features(emb, length):
    bands = (emb - 1) // 2
    lag = np.arange(length, dtype=np.float64)
    freq = 1e-4 + np.arange(bands, dtype=np.float64) * ((bands - 1 - 1e-4) / (bands - 1))
    phases = (lag * (2.0 * np.pi / length))[:, None] * freq[None, :]
    return np.concatenate(
        [(lag / (length - 1))[:, None], np.cos(phases), -np.sin(phases)], axis=1
    ).astype(np.float32)


def to_channels(value):
    return lax.all_to_all(value, "seq", 1, 0, tiled=True)


def to_tokens(value):
    return lax.all_to_all(value, "seq", 0, 1, tiled=True)


def plain_layer(
    tokens,
    norm_gain1,
    w_in,
    short_kernel,
    filt_w1,
    filt_w2,
    filt_w3,
    decay_rate,
    conv_bias,
    w_out,
    norm_gain2,
    w_up,
    w_down,
    cotangent,
):
    num_seqs, block_len, width = tokens.shape
    assert num_seqs == 1
    blocks = lax.axis_size("seq")
    position = lax.axis_index("seq")
    seq_len = block_len * blocks
    own = width // blocks
    table = jnp.asarray(transform_table(seq_len))
    features = jnp.asarray(lag_features(filt_w1.shape[0], seq_len))
    cot = cotangent[0]
    cot_all = gather_batch(cot)
    inputs = tokens[0].astype(F32)

    xhat1, inverse1 = norm_parts(inputs)
    normed1 = (xhat1 * norm_gain1).astype(BF16)
    normed1_all = gather_batch(normed1)
    projected = mm(normed1, w_in, out=BF16)
    earlier = shifted(projected[block_len - 2 :], "seq", 1)
    extended = jnp.concatenate([earlier, projected], axis=0).astype(F32)
    taps3 = short_kernel.astype(F32)
    lags = [extended[2 - lag : 2 - lag + block_len] for lag in range(3)]
    mixed = taps3[0] * lags[0] + taps3[1] * lags[1] + taps3[2] * lags[2]
    gate_out = mixed[:, :width]
    gate_in = mixed[:, width : 2 * width]
    values = mixed[:, 2 * width :]
    signal = (values * gate_in).astype(BF16)

    w3_own = lax.dynamic_slice_in_dim(filt_w3, position * own, own, 1)
    decay_own = lax.dynamic_slice_in_dim(decay_rate, position * own, own, 0)
    angle1 = mm(features, filt_w1, precision=HIGHEST)
    hidden1, slope1 = jnp.sin(angle1), jnp.cos(angle1)
    angle2 = mm(hidden1, filt_w2, precision=HIGHEST)
    hidden2, slope2 = jnp.sin(angle2), jnp.cos(angle2)
    lag_index = jnp.arange(seq_len).astype(F32)
    fading = jnp.exp(-decay_own[None, :] * lag_index[:, None])
    taps = (mm(hidden2, w3_own, precision=HIGHEST) * fading).astype(BF16)
    taps_spec = mm(table, taps)
    taps_re, taps_im = taps_spec[:seq_len], taps_spec[seq_len:]

    signal_spec = mm(table, to_channels(signal))
    signal_re, signal_im = signal_spec[:seq_len], signal_spec[seq_len:]
    scale = 1.0 / seq_len

    def inverse_of(real, imag):
        both = (jnp.concatenate([real, imag], axis=0) * scale).astype(BF16)
        return mm_tn(table, both)

    conv = inverse_of(
        taps_re * signal_re - taps_im * signal_im, taps_re * signal_im + taps_im * signal_re
    )
    long_out = to_tokens(conv.astype(BF16)).astype(F32) + conv_bias * signal.astype(F32)
    gated = (long_out * gate_out).astype(BF16)
    gated_all = gather_batch(gated)
    residual1 = inputs + mm(gated, w_out)
    xhat2, inverse2 = norm_parts(residual1)
    normed2 = (xhat2 * norm_gain2).astype(BF16)
    normed2_all = gather_batch(normed2)
    pre = mm(normed2, w_up)
    bent = jnp.tanh(GELU_SCALE * (pre + GELU_CUBIC * pre * pre * pre))
    hidden = (0.5 * pre * (1.0 + bent)).astype(BF16)
    layer_out = (residual1 + mm(hidden, w_down)).astype(BF16)

    slope = 0.5 * (1.0 + bent) + 0.5 * pre * (1.0 - bent * bent) * GELU_SCALE * (
        1.0 + 3.0 * GELU_CUBIC * pre * pre
    )
    grad_pre = (mm_nt(cot, w_down) * slope).astype(BF16)
    grad_w_down = rows_sum(columns_batch(hidden), cot_all)
    grad_w_up = columns_sum(normed2_all, columns_batch(grad_pre))
    grad_norm2 = mm_nt(grad_pre, w_up)
    grad_gain2 = jnp.sum(grad_norm2 * xhat2, axis=0)
    grad_res = cot.astype(F32) + norm_back(grad_norm2, norm_gain2, xhat2, inverse2)
    grad_branch = grad_res.astype(BF16)
    grad_w_out = columns_sum(gated_all, columns_batch(grad_branch))
    grad_gated = mm_nt(grad_branch, w_out)
    grad_long = (grad_gated * gate_out).astype(BF16)
    grad_gate_out = grad_gated * long_out
    grad_bias = jnp.sum(grad_long.astype(F32) * signal.astype(F32), axis=0)

    grad_spec = mm(table, to_channels(grad_long))
    grad_re, grad_im = grad_spec[:seq_len], grad_spec[seq_len:]
    grad_conv = inverse_of(
        taps_re * grad_re + taps_im * grad_im, taps_re * grad_im - taps_im * grad_re
    )
    grad_signal = to_tokens(grad_conv.astype(BF16)).astype(F32) + conv_bias * grad_long.astype(F32)
    grad_taps = inverse_of(
        signal_re * grad_re + signal_im * grad_im, signal_re * grad_im - signal_im * grad_re
    )
    grad_filt = grad_taps * fading
    grad_w3_own = mm_tn(hidden2, grad_filt)
    grad_angle2 = mm_nt(grad_filt, w3_own) * slope2
    grad_w2 = mm_tn(hidden1, grad_angle2)
    grad_angle1 = mm_nt(grad_angle2, filt_w2) * slope1
    grad_w1 = mm_tn(features, grad_angle1)

    grad_mixed = jnp.concatenate(
        [grad_gate_out, grad_signal * values, grad_signal * gate_in], axis=1
    )
    later = shifted(grad_mixed[:2], "seq", -1)
    grad_ext = jnp.concatenate([grad_mixed, later], axis=0)
    grad_proj = (
        taps3[0] * grad_ext[:block_len]
        + taps3[1] * grad_ext[1 : block_len + 1]
        + taps3[2] * grad_ext[2:]
    ).astype(BF16)
    grad_short = jnp.stack([jnp.sum(grad_mixed * lag, axis=0) for lag in lags])
    grad_w_in = columns_sum(normed1_all, columns_batch(grad_proj))
    grad_norm1 = mm_nt(grad_proj, w_in)
    grad_gain1 = jnp.sum(grad_norm1 * xhat1, axis=0)
    tokens_grad = grad_res + norm_back(grad_norm1, norm_gain1, xhat1, inverse1)

    return layer_out[None], tokens_grad[None], small_sums(
        grad_gain1, grad_bias, grad_gain2, grad_short, grad_w1, grad_w2, grad_w3_own
    ), (grad_w_in, grad_w_out, grad_w_up, grad_w_down)


MESH = pl.DeviceIdType.MESH
KERNEL_VMEM = 63 * 1024 * 1024


def symmetric_tables(length):
    odd = 2 * np.arange(length, dtype=np.int64) + 1
    angles = (odd[:, None] * odd[None, :] % (8 * length)).astype(np.float64) * (
        np.pi / (4 * length)
    )
    phase = odd.astype(np.float64) * (np.pi / (4 * length))
    tables = [np.cos(angles), np.sin(angles)]
    tables = [t.astype(np.float32).astype(ml_dtypes.bfloat16) for t in tables]
    return tables, np.stack([np.cos(phase), np.sin(phase)], axis=1).astype(np.float32)


def sin_cos(x):
    turns = jnp.floor(x * (2.0 / np.pi) + 0.5)
    rest = ((x - turns * 1.5703125) - turns * 4.837512969970703e-4) - turns * 7.54978995489188e-8
    square = rest * rest
    sine = rest + rest * square * (
        -1.6666654611e-1 + square * (8.3321608736e-3 - square * 1.9515295891e-4)
    )
    cosine = (1.0 - 0.5 * square) + square * square * (
        4.166664568298827e-2 + square * (-1.388731625493765e-3 + square * 2.443315711809948e-5)
    )
    quarter = turns - 4.0 * jnp.floor(turns * 0.25)
    odd = (quarter == 1.0) | (quarter == 3.0)
    sin_sign = jnp.where(quarter >= 2.0, -1.0, 1.0)
    cos_sign = jnp.where((quarter == 1.0) | (quarter == 2.0), -1.0, 1.0)
    return sin_sign * jnp.where(odd, cosine, sine), cos_sign * jnp.where(odd, sine, cosine)


class Named:
    def __init__(self, names, refs):
        assert len(names) == len(refs)
        for name, ref in zip(names, refs):
            setattr(self, name, ref)


def kernel_plan(groups, blocks, tokens, width, hidden, filt, emb):
    length = tokens * blocks
    own = width // blocks
    ffc = hidden // groups
    share = width // groups
    rows_out = share // blocks
    inc = 3 * share
    spare = 16
    chips = groups // 2
    down_rows = ffc // blocks
    net_rows = filt
    peers, zpeers = groups - 1, blocks - 1
    vm, hbm = pltpu.VMEM, pl.ANY
    inputs = dict(
        tokens=hbm, cot=hbm, w_in=hbm, w_out=hbm, w_up=hbm, w_down=hbm,
        cosine=hbm, sine=hbm, filt_w3=hbm, decay=hbm,
        gain1=vm, gain2=vm, bias=vm, short=vm, filt_w1=vm, filt_w2=vm,
        features_t=vm, phase=vm,
    )
    outputs = dict(
        layer_out=((tokens, width), BF16, hbm),
        tokens_grad=((tokens, width), F32, hbm),
        grad_w_in=((rows_out, 3 * width), F32, hbm),
        grad_w_out=((rows_out, width), F32, hbm),
        grad_w_up=((rows_out, hidden), F32, hbm),
        grad_w_down=((ffc // blocks, width), F32, hbm),
        grad_gain1=((1, rows_out), F32, vm),
        grad_gain2=((1, rows_out), F32, vm),
        grad_bias=((1, rows_out), F32, vm),
        grad_short=((3, 3 * rows_out), F32, vm),
        grad_w1=((emb, filt), F32, vm),
        grad_w2=((filt, filt), F32, vm),
        grad_w3=((filt, rows_out), F32, vm),
        cot_land=((4 * tokens, width), BF16, hbm),
        n2_land=((4, width, tokens), BF16, hbm),
    )
    dma = pltpu.SemaphoreType.DMA
    scratch = dict(
        tok=vm((tokens, width), BF16), cotv=vm((tokens, width), BF16),
        mean1=vm((tokens, 128), F32), inv1=vm((tokens, 128), F32),
        n1_all=vm((length, width), BF16), turn=vm((width, tokens), BF16),
        gated_turn=vm((width, tokens), BF16), gated_pair=vm((width // 2, 2 * tokens), BF16),
        hid_buf=vm((tokens, ffc), BF16),
        ghalo=vm((8, 3 * width), F32), ghalo_in=vm((8, 3 * width), F32), tail=vm((16, 3 * width), F32),
        ext_c=vm((length + 32, 3 * own), BF16), gproj_c=vm((length, 3 * own), BF16),
        gconv_c=vm((length + 16, own), BF16), glong_c=vm((length + 16, own), BF16),

        win=vm((3, width, width), BF16), wout=vm((width, width), BF16),
        cs=vm((length, length), BF16), sn=vm((length, length), BF16),
        ext=vm((tokens + 16, 3 * width), BF16),
        halo_out=vm((16, 3 * width), BF16), halo_in=vm((16, 3 * width), BF16),
        gate_out=vm((tokens, width), F32),
        sig=vm((tokens, width), BF16), chan=vm((length + 16, own), BF16),
        w3=vm((filt, own), F32), fade=vm((1, own), F32),
        h1=vm((filt, length), F32), s1=vm((filt, length), F32),
        h2=vm((filt, length), F32), s2=vm((filt, length), F32),
        sum_gain1=vm((1, width), F32), sum_gain2=vm((1, width), F32),
        sum_bias=vm((1, width), F32), sum_short=vm((3, 3 * width), F32),
        small_send=vm((groups, 16, share), F32), small_land=vm((groups, 16, share), F32),
        small_sum=vm((16, share), F32), small_z=vm((zpeers, 16, share), F32),
        short_all=vm((8, inc), F32),
        w12=vm((net_rows, 128), F32), w12_z=vm((zpeers, net_rows, 128), F32),
        w12_sum=vm((net_rows, 128), F32), w12_plane=vm((peers, net_rows, 128), F32),
        sum_w3=vm((filt, own), F32), w3_land=vm((peers, filt // groups, own), F32),
        w3_part=vm((filt // groups, own), F32), w3_all=vm((filt, own), F32), w3_half=vm((filt, share), F32),
        hre=vm((length, own), BF16), him=vm((length, own), BF16),
        xre=vm((length, own), BF16), xim=vm((length, own), BF16),
        yre=vm((length, own), BF16), yim=vm((length, own), BF16),
        qre=vm((length, own), BF16), qim=vm((length, own), BF16),
        conv_out=vm((length + 16, own), BF16), conv_in=vm((blocks, tokens, own), BF16),
        long=vm((tokens, width), F32), half=vm((tokens, width), BF16),
        res=vm((tokens, width), F32), xhat2=vm((tokens, width), F32),
        inv2=vm((tokens, 128), F32), gn2=vm((tokens, width), F32),
        gres=vm((tokens, width), F32),
        hid_send=vm((groups, ffc, tokens), BF16), hid_own=vm((2, ffc, 4 * tokens), BF16),
        pre_send=vm((groups, tokens, ffc), BF16), pre_own=vm((2, 4 * tokens, ffc), BF16),
        gbr_pair=vm((2 * tokens, width), BF16),
        glong=vm((tokens, width), BF16),
        gproj=vm((tokens, 3 * width), BF16),
        down_send=vm((4, down_rows, width), BF16), down_first=vm((4, down_rows, width), BF16),
        down_land=vm((2, down_rows, width), BF16), down_last=vm((down_rows, width), BF16),
        up_send=vm((4, own, ffc), BF16), up_first=vm((4, own, ffc), BF16),
        up_land=vm((2, own, ffc), BF16), up_last=vm((own, ffc), BF16),
        in_send=vm((chips, share, 3 * own), BF16), in_pair=vm((chips, share, 3 * own), BF16),
        in_land=vm((chips - 1, share, 3 * own), BF16), in_own=vm((share, 3 * own), F32),
        out_send=vm((chips - 1, share, width), BF16), out_land=vm((chips - 1, share, width), BF16),
        outz_send=vm((share, width), BF16), outz_land=vm((zpeers, rows_out, width), BF16),
        outz_own=vm((rows_out, width), F32),
        load_sem=dma((16,)),
        pool_sem=dma((groups,)),
        win_sem=dma((3,)),
        ffn_sem=dma((2, 2)),
        local_sem=dma((16,)),
        stage_sem=dma((2,)),
        ag_s=dma((2, 3)), ag_r=dma((2, 3)), fs_s=dma((2,)), fs_r=dma((2,)),
        halo_s=dma((2,)), halo_r=dma((2,)),
        za_s=dma((4, zpeers)), za_r=dma((4, zpeers)),
        pa_s=dma((2, 6)), pa_r=dma((2, 6)),
        cx_s=dma((3,)), cx_r=dma((3,)), zg_s=dma((2, zpeers)), zg_r=dma((2, zpeers)),
        wi_s=dma((chips - 1,)), wi_r=dma((chips - 1,)), ti_s=dma((zpeers, 3)), ti_r=dma((zpeers, 3)), wo_s=dma((2, chips - 1)), wo_r=dma((2, chips - 1)),
        rs_s=dma((2, 2)), rs_r=dma((2, 2)),
        sm_s=dma((4, peers)), sm_r=dma((4, peers)),
        sz_s=dma((3, zpeers)), sz_r=dma((3, zpeers)),
        tr_s=dma((1, peers)), tr_r=dma((1, peers)),
    )
    names = [*inputs, *outputs, *scratch]

    def kernel(*refs):
        r = Named(names, refs)
        b, z = lax.axis_index("batch"), lax.axis_index("seq")
        chip, core = lax.div(b, 2), lax.rem(b, 2)
        sibling = chip * 2 + (1 - core)
        sent = {}

        chip_x, chip_y = lax.rem(chip, 2), lax.div(chip, 2)

        def flipped(turn_x, turn_y):
            x = chip_x + turn_x - 2 * chip_x * turn_x
            y = chip_y + turn_y - 2 * chip_y * turn_y
            return y * 2 + x

        def partner(way):
            return flipped(1 - way % 2, (way + 1) // 2)

        def way_of(step):
            return 2 if step == 2 else step + core - 2 * step * core

        def partner_at(way):
            return flipped(1 - lax.rem(way, 2), lax.div(way + 1, 2))

        def flip(value, turn):
            return value + turn - 2 * value * turn

        def turns(at):
            rest = 7 - at
            return lax.rem(rest, 2), lax.rem(lax.div(rest, 2), 2), lax.div(rest, 4)

        def chunk_group(at):
            turn_core, turn_x, turn_y = turns(jnp.int32(at))
            return (flip(chip_y, turn_y) * 2 + flip(chip_x, turn_x)) * 2 + flip(core, turn_core)

        def group_at(step):
            return lax.rem(b + step, groups)

        def block_at(step):
            return lax.rem(z + step, blocks)

        def span(at, size):
            return pl.ds(pl.multiple_of(at * size, size), size)

        def remote(src, dst, send_sem, recv_sem, **where):
            return pltpu.make_async_remote_copy(
                src_ref=src, dst_ref=dst, send_sem=send_sem, recv_sem=recv_sem,
                device_id=where, device_id_type=MESH,
            )

        def send(key, copy):
            copy.start()
            sent.setdefault(key, []).append(copy)

        def drain(key):
            for copy in sent.pop(key):
                copy.wait_send()

        def tiles(size, total, body):
            def step(i, carry):
                body(pl.multiple_of(i * size, size))
                return carry

            lax.fori_loop(0, total // size, step, 0)

        def load(sem, src, dst):
            copy = pltpu.make_async_copy(src, dst, sem)
            copy.start(priority=1)
            return copy

        def load_win(block):
            return load(r.win_sem.at[block], r.w_in.at[:, pl.ds(block * width, width)], r.win.at[block])

        load_tok = load(r.load_sem.at[0], r.tokens, r.tok)
        win_loads = [(block, load_win(block)) for block in (1, 2, 0)]
        load_cot = load(r.load_sem.at[5], r.cot, r.cotv)
        load_w3 = load(r.load_sem.at[1], r.filt_w3.at[:, span(z, own)], r.w3)
        load_fade = load(r.load_sem.at[2], r.decay.at[:, span(z, own)], r.fade)
        load_cs = load(r.load_sem.at[3], r.cosine, r.cs)
        load_sn = load(r.load_sem.at[4], r.sine, r.sn)
        load_wout = load(r.load_sem.at[6], r.w_out, r.wout)

        barrier = pltpu.get_barrier_semaphore()
        for step in range(1, groups):
            pl.semaphore_signal(barrier, inc=1, device_id={"batch": group_at(step)}, device_id_type=MESH)
        for step in range(1, blocks):
            pl.semaphore_signal(barrier, inc=1, device_id={"seq": block_at(step)}, device_id_type=MESH)

        def member(k, turn_side, turn_core):
            side = chip_y if k else chip_x
            return flip(side, turn_side) * 2 + flip(core, turn_core)

        def slot(k, at):
            return r.n2_land.at[at] if k else r.cot_land.at[span(at, tokens)]

        def gather_copy(k, at, src, dst, to):
            return remote(src, dst, r.ag_s.at[k, at], r.ag_r.at[k, at], batch=to)

        def gather_local(k, src):
            return pltpu.make_async_copy(src, slot(k, member(k, 0, 0)), r.local_sem.at[k])

        def gather_start(k, src):
            dst = slot(k, member(k, 0, 0))
            send(("ag", k), gather_copy(k, 0, src, dst, partner(k) * 2 + core))
            send(("ag", k), gather_copy(k, 1, src, dst, sibling))
            gather_local(k, src).start(priority=1)

        def gather_forward(k):
            dst = slot(k, member(k, 1, 0))
            gather_copy(k, 0, dst, dst, sibling).wait_recv()
            staged = r.win.at[2, :, 3 * own : 3 * own + tokens] if k else r.gproj.at[:, 0:width]
            load(r.stage_sem.at[k], dst, staged).wait()
            send(("forward", k), gather_copy(k, 2, staged, dst, sibling))

        def gather_finish(k, src):
            gather_local(k, src).wait()
            for at in range(2):
                dst = slot(k, member(k, at, 1))
                gather_copy(k, 1 + at, dst, dst, sibling).wait_recv()

        def turned(value_ref, out_ref):
            def body(at):
                tile = value_ref[:, pl.ds(at, share)].T
                group = lax.div(at, share)
                for block in range(blocks):
                    first = pl.multiple_of(block * own + group * rows_out, rows_out)
                    out_ref[pl.ds(first, rows_out), :] = tile[block * rows_out : (block + 1) * rows_out]

            tiles(share, width, body)

        def turned_by_core(value_ref, out_ref):
            def body(at):
                group = lax.div(at, share)
                out_ref[span(lax.rem(group, 2) * chips + lax.div(group, 2), share), :] = value_ref[
                    :, pl.ds(at, share)
                ].T

            tiles(share, width, body)

        load_tok.wait()

        def norm1(at):
            rows = pl.ds(at, 32)
            x = r.tok[rows, :].astype(F32)
            xhat, inverse = norm_parts(x)
            r.mean1[rows, :] = jnp.broadcast_to(jnp.mean(x, axis=-1, keepdims=True), (32, 128))
            r.inv1[rows, :] = jnp.broadcast_to(inverse, (32, 128))
            r.n1_all[pl.ds(pl.multiple_of(z * tokens + at, 32), 32), :] = (xhat * r.gain1[...]).astype(BF16)

        tiles(32, tokens, norm1)
        for block, copy in win_loads:
            copy.wait()
            cols = slice(block * width, (block + 1) * width)
            proj = mm(r.n1_all[span(z, tokens), :], r.win[block], out=BF16)
            r.ext[16:, cols] = proj
            r.halo_out[:, cols] = proj[tokens - 16 :]
        pl.semaphore_wait(barrier, peers + zpeers)
        halo = remote(r.halo_out, r.halo_in, r.halo_s.at[0], r.halo_r.at[0], seq=block_at(1))
        send("halo", halo)
        own_loads = [
            load(
                r.load_sem.at[7 + part],
                r.w_in.at[:, pl.ds(pl.multiple_of(part * width + z * own, own), own)],
                r.win.at[2, :, part * own : (part + 1) * own],
            )
            for part in range(3)
        ]
        for padded in (r.chan, r.conv_out, r.gconv_c, r.glong_c):
            padded[length:, :] = jnp.zeros((spare, own), BF16)
        r.ext_c[0:spare, :] = jnp.zeros((spare, 3 * own), BF16)
        r.ext_c[length + spare :, :] = jnp.zeros((spare, 3 * own), BF16)

        def up_weights(at, slot):
            group = chunk_group(at)
            return pltpu.make_async_copy(
                r.w_up.at[:, span(group, ffc)], r.win.at[0, :, span(slot, ffc)], r.ffn_sem.at[slot, 0]
            )

        def down_weights(at, slot):
            group = chunk_group(at)
            return pltpu.make_async_copy(
                r.w_down.at[span(group, ffc)], r.win.at[1, span(slot, ffc)], r.ffn_sem.at[slot, 1]
            )

        for at in range(2):
            down_weights(at, at).start(priority=1)
            up_weights(at, at).start(priority=1)

        halo.wait_recv()
        r.ext[0:16, :] = (r.halo_in[...].astype(F32) * jnp.where(z > 0, 1.0, 0.0)).astype(BF16)

        def lags_at(cols):
            wide = r.ext[:, cols].astype(F32)
            return [wide[16 - lag : 16 - lag + tokens] for lag in range(3)]

        def mix(cols):
            lags = lags_at(cols)
            short = r.short[:, cols].astype(F32)
            return lags, short[0:1] * lags[0] + short[1:2] * lags[1] + short[2:3] * lags[2]

        def chan_copy(k, src, dst, step, to):
            return remote(src, dst, r.za_s.at[k, step - 1], r.za_r.at[k, step - 1], seq=to)

        def to_channels(k, value_ref, make_cols):
            for step in list(range(1, blocks)) + [0]:
                block = block_at(step)
                make_cols(block)
                if step:
                    src, dst = value_ref.at[:, span(block, own)], r.chan.at[span(z, tokens)]
                    send(("za", k), chan_copy(k, src, dst, step, block))
                else:
                    r.chan[span(z, tokens), :] = value_ref[:, span(block, own)]

        def wait_channels(k):
            for step in range(1, blocks):
                source = block_at(blocks - step)
                dst = r.chan.at[span(source, tokens)]
                chan_copy(k, dst, dst, step, source).wait_recv()

        def signal_block(block):
            def body(at):
                base = block * own + at
                cols = pl.ds(pl.multiple_of(base, 128), 128)
                gate_in = mix(pl.ds(pl.multiple_of(width + base, 128), 128))[1]
                values = mix(pl.ds(pl.multiple_of(2 * width + base, 128), 128))[1]
                r.sig[:, cols] = (values * gate_in).astype(BF16)

            tiles(128, own, body)

        to_channels(0, r.sig, signal_block)
        load_cot.wait()
        gather_start(0, r.cotv)

        load_w3.wait()
        load_fade.wait()

        def fading(at):
            lag = (lax.broadcasted_iota(jnp.int32, (tokens, own), 0) + at).astype(F32)
            return jnp.exp(-r.fade[...] * lag)

        def taps_rows(at):
            rows = pl.ds(at, tokens)
            h1, r.s1[:, rows] = sin_cos(mm_tn(r.filt_w1[...], r.features_t[:, rows], precision=HIGHEST))
            h2, r.s2[:, rows] = sin_cos(mm_tn(r.filt_w2[...], h1, precision=HIGHEST))
            r.h1[:, rows] = h1
            r.h2[:, rows] = h2
            taps = mm_tn(h2, r.w3[...], precision=HIGHEST) * fading(at)
            r.qre[rows, :] = taps.astype(BF16)

        tiles(tokens, length, taps_rows)
        load_cs.wait()
        load_sn.wait()
        scale = 1.0 / length

        def taps_spec(at):
            rows = pl.ds(at, tokens)
            real = mm(r.cs[rows, :], r.qre[...]) * scale
            imag = mm(r.sn[rows, :], r.qre[...]) * -scale
            turn_re, turn_im = r.phase[rows, 0:1], r.phase[rows, 1:2]
            r.hre[rows, :] = (real * turn_re - imag * turn_im).astype(BF16)
            r.him[rows, :] = (real * turn_im + imag * turn_re).astype(BF16)

        tiles(tokens, length, taps_spec)

        wait_channels(0)

        def conv_spec(at):
            rows = pl.ds(at, tokens)
            real = mm(r.cs[rows, :], r.chan[0:length, :])
            imag = -mm(r.sn[rows, :], r.chan[0:length, :])
            r.xre[rows, :] = real.astype(BF16)
            r.xim[rows, :] = imag.astype(BF16)
            hre, him = r.hre[rows, :].astype(F32), r.him[rows, :].astype(F32)
            r.yre[rows, :] = (hre * real - him * imag).astype(BF16)
            r.yim[rows, :] = (-(hre * imag + him * real)).astype(BF16)

        tiles(tokens, length, conv_spec)

        def to_tokens(k, out_ref):
            for step in list(range(1, blocks)) + [0]:
                block = block_at(step)
                rows = span(block, tokens)
                tile = (mm(r.cs[rows, :], r.yre[...]) + mm(r.sn[rows, :], r.yim[...])).astype(BF16)
                out_ref[rows, :] = tile
                if step:
                    src, dst = out_ref.at[rows], r.conv_in.at[z]
                    send(("za", k), chan_copy(k, src, dst, step, block))
                else:
                    r.conv_in[z] = tile

        def wait_tokens(k):
            for step in range(1, blocks):
                source = block_at(blocks - step)
                dst = r.conv_in.at[source]
                chan_copy(k, dst, dst, step, source).wait_recv()

        to_tokens(1, r.conv_out)

        def seq_copy(down, step):
            block = lax.rem(z + step, blocks) if down else lax.rem(z + blocks - step, blocks)
            to = block_at(blocks - 1 if down else 1)
            rows = r.n1_all.at[span(block, tokens)]
            return remote(rows, rows, r.zg_s.at[down, step], r.zg_r.at[down, step], seq=to)

        def seq_sends(down, step):
            return (z > 0) & (z + step < blocks) if down else (z < blocks - 1) & (z >= step)

        def seq_receives(down, step):
            return z + 1 + step < blocks if down else z >= 1 + step

        def seq_step(step):
            for down in range(2):
                if step:

                    @pl.when(seq_receives(down, step - 1))
                    def _():
                        seq_copy(down, step - 1).wait_recv()

                if step < zpeers:

                    @pl.when(seq_sends(down, step))
                    def _():
                        seq_copy(down, step).start()

        def gate_cols(at):
            cols = pl.ds(at, 128)
            r.gate_out[:, cols] = mix(cols)[1]

        tiles(128, width, gate_cols)

        def grad_hidden(at, carry):
            slot = lax.rem(at, 2)
            down_weights(at, slot).wait()
            r.pre_send[at] = mm_nt(r.cotv[...], r.win[1, span(slot, ffc), :], out=BF16)
            down_weights(lax.rem(at + 2, groups), slot).start(priority=1)
            return carry

        lax.fori_loop(0, groups, grad_hidden, 0)
        load_wout.wait()
        wait_tokens(1)
        seq_step(0)

        def conv_cols(at):
            return r.conv_in[
                lax.div(at, own), :, pl.ds(pl.multiple_of(lax.rem(at, own), 128), 128)
            ].astype(F32)

        def long_cols(at):
            cols = pl.ds(at, 128)
            long = conv_cols(at) + r.bias[:, cols] * r.sig[:, cols].astype(F32)
            r.long[:, cols] = long
            r.half[:, cols] = (long * r.gate_out[:, cols]).astype(BF16)

        tiles(128, width, long_cols)
        r.res[...] = mm(r.half[...], r.wout[...])
        turned_by_core(r.half, r.gated_turn)
        mine = span(core, tokens)
        pair_rows = chips * share

        def pair_copy(k, src, dst):
            return remote(src, dst, r.cx_s.at[k], r.cx_r.at[k], batch=sibling)

        gated_copy = pair_copy(
            0, r.gated_turn.at[span(1 - core, pair_rows)], r.gated_pair.at[:, mine]
        )
        send("pair", gated_copy)
        r.gated_pair[:, mine] = r.gated_turn[span(core, pair_rows), :]

        def norm2(at):
            rows = pl.ds(at, 32)
            residual = r.res[rows, :] + r.tok[rows, :].astype(F32)
            r.res[rows, :] = residual
            xhat, inverse = norm_parts(residual)
            r.xhat2[rows, :] = xhat
            r.inv2[rows, :] = jnp.broadcast_to(inverse, (32, 128))
            r.half[rows, :] = (xhat * r.gain2[...]).astype(BF16)

        tiles(32, tokens, norm2)
        turned(r.half, r.turn)
        gather_start(1, r.turn)
        r.gn2[...] = jnp.zeros((tokens, width), F32)

        def plane_copy(k, at):
            turn_core, turn_x, turn_y = turns(jnp.int32(at))
            turn_side, turn_far = (turn_y, turn_x) if k else (turn_x, turn_y)
            index = turn_far * 3 + turn_side * 2 + turn_core - 1
            if k:
                to = (flip(chip_y, turn_y) * 2 + chip_x) * 2 + flip(core, turn_core)
                src, dst = r.pre_send.at[at], r.pre_own.at[flip(chip_x, turn_x), span(member(1, 0, 0), tokens)]
            else:
                to = (chip_y * 2 + flip(chip_x, turn_x)) * 2 + flip(core, turn_core)
                src = r.hid_send.at[at]
                dst = r.hid_own.at[flip(chip_y, turn_y), :, span(member(0, 0, 0), tokens)]
            return remote(src, dst, r.pa_s.at[k, index], r.pa_r.at[k, index], batch=to)

        hidden_remote = [0, 1, 2, 4, 5, 6]
        pre_remote = [0, 1, 2, 3, 4, 6]

        def chunk(at, carry):
            slot = lax.rem(at, 2)
            where = span(slot, ffc)
            up_weights(at, slot).wait()
            r.gres[:, 0:ffc] = mm(r.half[...], r.win[0, :, where])

            def act(row):
                rows = pl.ds(row, 32)
                pre = r.gres[rows, 0:ffc]
                square = pre * pre
                bent = jnp.tanh(pre * (GELU_SCALE + GELU_SCALE * GELU_CUBIC * square))
                upper = 0.5 + 0.5 * bent
                slope = upper + pre * (0.5 - 0.5 * bent * bent) * (
                    GELU_SCALE + 3.0 * GELU_SCALE * GELU_CUBIC * square
                )
                r.hid_buf[rows, :] = (pre * upper).astype(BF16)
                r.pre_send[at, rows, :] = (r.pre_send[at, rows, :].astype(F32) * slope).astype(BF16)

            tiles(32, tokens, act)
            r.hid_send[at] = r.hid_buf[...].T

            @pl.when(lax.rem(at, 4) < 3)
            def _():
                plane_copy(0, at).start()

            @pl.when((at < 5) | (at == 6))
            def _():
                plane_copy(1, at).start()

            down_weights(at, slot).wait()
            r.res[...] += mm(r.hid_buf[...], r.win[1, where, :])
            r.gn2[...] += mm_nt(r.pre_send[at], r.win[0, :, where])

            @pl.when(at < groups - 2)
            def _():
                up_weights(at + 2, slot).start(priority=1)
                down_weights(at + 2, slot).start(priority=1)

            return carry

        lax.fori_loop(0, groups // 2, chunk, 0)
        seq_step(1)
        lax.fori_loop(groups // 2, groups, chunk, 0)
        seq_step(2)
        for at in hidden_remote:
            sent.setdefault("ffn", []).append(plane_copy(0, at))
        for at in pre_remote:
            sent.setdefault("ffn", []).append(plane_copy(1, at))

        for turn, at in ((0, 7), (1, 3)):
            r.hid_own[flip(chip_y, turn), :, span(member(0, 0, 0), tokens)] = r.hid_send[at]
        for turn, at in ((0, 7), (1, 5)):
            r.pre_own[flip(chip_x, turn), span(member(1, 0, 0), tokens), :] = r.pre_send[at]

        def norm2_back(at, total):
            rows = pl.ds(pl.multiple_of(at * 32, 32), 32)
            r.half[rows, :] = r.res[rows, :].astype(BF16)
            grad, xhat = r.gn2[rows, :], r.xhat2[rows, :]
            back = r.cotv[rows, :].astype(F32) + norm_back(grad, r.gain2[...], xhat, r.inv2[rows, 0:1])
            r.gres[rows, :] = back
            r.gbr_pair[pl.ds(pl.multiple_of(core * tokens + at * 32, 32), 32), :] = back.astype(BF16)
            return total + jnp.sum((grad * xhat).reshape(4, 8, width), axis=0)

        total = lax.fori_loop(0, tokens // 32, norm2_back, jnp.zeros((8, width), F32))
        r.sum_gain2[...] = jnp.sum(total, axis=0, keepdims=True)
        store_layer = load(r.local_sem.at[8], r.half, r.layer_out)
        branch_copy = pair_copy(1, r.gbr_pair.at[mine], r.gbr_pair.at[mine])
        send("pair", branch_copy)

        def gated_back(block):
            cols = span(block, own)
            grad = mm_nt(r.gbr_pair[mine, :], r.wout[span(block, own), :])
            glong = (grad * r.gate_out[:, cols]).astype(BF16)
            r.glong[:, cols] = glong
            r.tok[:, cols] = grad.astype(BF16)
            r.long[:, cols] = grad * r.long[:, cols]
            r.sum_bias[:, cols] = jnp.sum(
                glong.astype(F32) * r.sig[:, cols].astype(F32), axis=0, keepdims=True
            )

        to_channels(2, r.tok, gated_back)
        gather_forward(0)
        gather_forward(1)


        branch_copy.wait_recv()
        gated_copy.wait_recv()

        def out_copy(way):
            sems = r.wo_s.at[0, way], r.wo_r.at[0, way]
            to = partner_at(jnp.int32(way)) * 2 + core
            return remote(r.out_send.at[way], r.out_land.at[way], *sems, batch=to)

        for step in range(chips):
            to = partner(step - 1) if step else chip
            part = mm(r.gated_pair[span(to, share), :], r.gbr_pair[...])
            if step:
                r.out_send[step - 1] = part.astype(BF16)
            else:
                r.xhat2[share : 2 * share, :] = part

        near = z + 1 - 2 * lax.rem(z, 2)
        far = block_at(2)

        def reduce_zero_copy(k, refs):
            to = partner(0 if k else 1) * 2 + core
            return remote(refs[0], refs[1], r.fs_s.at[k], r.fs_r.at[k], batch=to)

        def reduce_first(k, refs):
            return remote(refs[0].at[0:2], refs[2], r.rs_s.at[k, 0], r.rs_r.at[k, 0], seq=near)

        def reduce_second(k, refs):
            return remote(refs[0].at[2], refs[3], r.rs_s.at[k, 1], r.rs_r.at[k, 1], seq=far)

        def reduce_zero(k, refs, part_of):
            other = 1 - (chip_x if k else chip_y)
            for block in range(blocks):
                refs[0][block] = part_of(other, block).astype(BF16)
            send(("zero", k), reduce_zero_copy(k, refs))

        def reduce_send(k, refs, part_of):
            reduce_zero_copy(k, refs).wait_recv()
            drain(("zero", k))
            mine_too = chip_x if k else chip_y

            def total(block):
                return part_of(mine_too, block) + refs[1][block].astype(F32)

            refs[0][0] = total(near).astype(BF16)
            refs[0][1] = total(lax.rem(near + 2, blocks)).astype(BF16)
            send("rs", reduce_first(k, refs))
            refs[0][2] = total(far).astype(BF16)
            refs[4][...] = total(z)

        def reduce_next(k, refs):
            reduce_first(k, refs).wait_recv()
            refs[0][2] = (refs[0][2].astype(F32) + refs[2][1].astype(F32)).astype(BF16)
            send("rs", reduce_second(k, refs))
            refs[4][...] += refs[2][0].astype(F32)

        def reduce_finish(k, refs):
            reduce_second(k, refs).wait_recv()
            refs[4][...] += refs[3][...].astype(F32)

        down_refs = (r.down_send, r.down_first, r.down_land, r.down_last, r.xhat2.at[0:down_rows])
        up_refs = (r.up_send, r.up_first, r.up_land, r.up_last, r.gate_out.at[:, 0:ffc])

        def wait_plane(k):
            for at in pre_remote if k else hidden_remote:
                plane_copy(k, at).wait_recv()

        def down_part(group, block):
            return mm(r.hid_own[group, span(block, down_rows), :], r.win[0])

        def up_part(group, block):
            return mm(r.win[1, span(block, own), :], r.pre_own[group])

        gather_finish(0, r.cotv)
        cot_pool = load(r.pool_sem.at[4], r.cot_land, r.win.at[0])
        gather_finish(1, r.turn)
        pool = [
            load(r.pool_sem.at[at], r.n2_land.at[at], r.win.at[1, :, pl.ds(at * tokens, tokens)])
            for at in range(4)
        ]
        cot_pool.wait()
        wait_plane(0)
        reduce_zero(0, down_refs, down_part)
        for copy in pool:
            copy.wait()
        wait_plane(1)
        reduce_zero(1, up_refs, up_part)

        seq_step(3)
        for copy in own_loads:
            copy.wait()

        def proj_rows(at):
            r.ext_c[pl.ds(pl.multiple_of(at + spare, spare), tokens), :] = mm(
                r.n1_all[pl.ds(at, tokens), :], r.win[2, :, 0 : 3 * own], out=BF16
            )

        tiles(tokens, length, proj_rows)

        def own_cols(part, at):
            return pl.ds(pl.multiple_of(part * width + z * own + at, 128), 128)

        def mix_own(part, at, first, rows):
            wide = r.ext_c[pl.ds(first, rows + spare), part * own + at : part * own + at + 128].astype(F32)
            short = r.short[:, own_cols(part, at)].astype(F32)
            lags = [wide[spare - lag : spare - lag + rows] for lag in range(3)]
            return short[0:1] * lags[0] + short[1:2] * lags[1] + short[2:3] * lags[2]

        wait_channels(2)

        def long_rows(first):
            rows = pl.ds(first, tokens)
            for at in range(0, own, 128):
                cols = slice(at, at + 128)
                gate = mix_own(0, at, first, tokens)
                r.glong_c[rows, cols] = (r.chan[rows, cols].astype(F32) * gate).astype(BF16)

        tiles(tokens, length, long_rows)

        def grad_spec(at):
            rows = pl.ds(at, tokens)
            real = mm(r.cs[rows, :], r.glong_c[0:length, :])
            imag = -mm(r.sn[rows, :], r.glong_c[0:length, :])
            hre, him = r.hre[rows, :].astype(F32), r.him[rows, :].astype(F32)
            r.yre[rows, :] = (hre * real + him * imag).astype(BF16)
            r.yim[rows, :] = (him * real - hre * imag).astype(BF16)
            xre, xim = r.xre[rows, :].astype(F32), r.xim[rows, :].astype(F32)
            both_re = xre * real + xim * imag
            both_im = xre * imag - xim * real
            turn_re, turn_im = r.phase[rows, 0:1], r.phase[rows, 1:2]
            r.qre[rows, :] = ((both_re * turn_re + both_im * turn_im) * scale).astype(BF16)
            r.qim[rows, :] = ((both_re * turn_im - both_im * turn_re) * scale).astype(BF16)

        tiles(tokens, length, grad_spec)
        to_tokens(3, r.gconv_c)

        def proj_back(first):
            rows = pl.ds(first, tokens + spare)
            for at in range(0, own, 128):
                cols = slice(at, at + 128)
                gate_in = mix_own(1, at, first, tokens + spare)
                values = mix_own(2, at, first, tokens + spare)
                bias = r.bias[:, own_cols(0, at)]
                signal = (values * gate_in).astype(BF16).astype(F32)
                long = r.conv_out[rows, cols].astype(F32) + bias * signal
                grad_signal = r.gconv_c[rows, cols].astype(F32) + bias * r.glong_c[rows, cols].astype(F32)
                parts = (r.chan[rows, cols].astype(F32) * long, grad_signal * values, grad_signal * gate_in)
                for part, grad in enumerate(parts):
                    short = r.short[:, own_cols(part, at)].astype(F32)
                    total = (
                        short[0:1] * grad[0:tokens]
                        + short[1:2] * grad[1 : tokens + 1]
                        + short[2:3] * grad[2 : tokens + 2]
                    )
                    r.gproj_c[pl.ds(first, tokens), part * own + at : part * own + at + 128] = total.astype(BF16)

        tiles(tokens, length, proj_back)

        def in_part(group):
            return mm_tn(r.n1_all[:, span(group, share)], r.gproj_c[...])

        for at in range(chips):
            r.in_send[at] = in_part(at * 2 + 1 - core).astype(BF16)
        in_pair = pair_copy(2, r.in_send, r.in_pair)
        send("in_pair", in_pair)
        in_pair.wait_recv()
        drain("in_pair")

        def in_copy(way):
            sems = r.wi_s.at[way], r.wi_r.at[way]
            to = partner_at(jnp.int32(way)) * 2 + core
            return remote(r.in_send.at[way], r.in_land.at[way], *sems, batch=to)

        for step in range(chips):
            way = way_of(step) if step < chips - 1 else None
            to = chip if way is None else partner_at(jnp.int32(way))
            part = in_part(to * 2 + core) + r.in_pair[to].astype(F32)
            if way is None:
                r.in_own[...] = part
            else:
                r.in_send[way] = part.astype(BF16)
                send("in", in_copy(way))

        r.w12[...] = jnp.zeros((net_rows, 128), F32)
        r.sum_w3[...] = jnp.zeros((filt, own), F32)
        for at in range(0, length, tokens):
            rows = slice(at, at + tokens)
            grad_taps = mm(r.cs[rows, :], r.qre[...]) + mm(r.sn[rows, :], r.qim[...])
            grad_filt = grad_taps * fading(at)
            r.sum_w3[...] += mm(r.h2[:, rows], grad_filt, precision=HIGHEST)
            grad_angle2 = mm_nt(r.w3[...], grad_filt, precision=HIGHEST) * r.s2[:, rows]
            r.w12[:, :filt] += mm_nt(r.h1[:, rows], grad_angle2, precision=HIGHEST)
            grad_angle1 = mm(r.filt_w2[...], grad_angle2, precision=HIGHEST) * r.s1[:, rows]
            r.w12[:emb, filt : 2 * filt] += mm_nt(r.features_t[:, rows], grad_angle1, precision=HIGHEST)

        def small_copy(k, src, dst, at, to):
            return remote(src, dst, r.sm_s.at[k, at], r.sm_r.at[k, at], batch=to)

        def small_z_copy(k, src, dst, step, to):
            return remote(src, dst, r.sz_s.at[k, step - 1], r.sz_r.at[k, step - 1], seq=to)

        def small_z_send(k, src, dst_of):
            for step in range(1, blocks):
                send("small", small_z_copy(k, src, dst_of(step), step, block_at(step)))

        def small_z_wait(k, dst_of):
            for step in range(1, blocks):
                dst = dst_of(step)
                small_z_copy(k, dst, dst, step, block_at(blocks - step)).wait_recv()

        def small_send(k, src_of, dst_of):
            for at in range(peers):
                to = group_at(1 + at)
                send("small", small_copy(k, src_of(to), dst_of(at), at, to))

        def small_wait(k, dst_of):
            for at in range(peers):
                dst = dst_of(at)
                small_copy(k, dst, dst, at, group_at(groups - 1 - at)).wait_recv()

        w3_rows = filt // groups
        small_z_send(0, r.w12, lambda step: r.w12_z.at[step - 1])
        small_send(0, lambda to: r.sum_w3.at[span(to, w3_rows)], lambda at: r.w3_land.at[at])

        reduce_send(0, down_refs, down_part)
        reduce_send(1, up_refs, up_part)
        drain(("forward", 1))
        win_loads = [(block, load_win(block)) for block in range(3)]

        def outz_copy(step, to):
            sems = r.wo_s.at[1, step - 1], r.wo_r.at[1, step - 1]
            return remote(r.outz_send.at[span(to, rows_out)], r.outz_land.at[step - 1], *sems, seq=to)


        def short_sums(cols, grad, lags):
            for lag in range(3):
                r.sum_short[lag : lag + 1, cols] = jnp.sum(grad * lags[lag], axis=0, keepdims=True)

        def back_cols(cols, grad, lags):
            short_sums(cols, grad, lags)
            r.ghalo[:, cols] = grad[0:8]
            short = r.short[:, cols].astype(F32)
            longer = jnp.concatenate([grad, jnp.zeros((8, 128), F32)], axis=0)
            total = (
                short[0:1] * grad
                + short[1:2] * longer[1 : tokens + 1]
                + short[2:3] * longer[2 : tokens + 2]
            )
            r.gproj[:, cols] = total.astype(BF16)
            r.tail[:, cols] = total[tokens - 16 :]

        def mixed_cols(at):
            cols = pl.ds(at, 128)
            grad_signal = conv_cols(at) + r.bias[:, cols] * r.glong[:, cols].astype(F32)
            gate_cols = pl.ds(pl.multiple_of(width + at, 128), 128)
            value_cols = pl.ds(pl.multiple_of(2 * width + at, 128), 128)
            gate_lags, gate_in = mix(gate_cols)
            value_lags, values = mix(value_cols)
            back_cols(gate_cols, grad_signal * values, gate_lags)
            back_cols(value_cols, grad_signal * gate_in, value_lags)

        def gate_back(at):
            cols = pl.ds(at, 128)
            back_cols(cols, r.long[:, cols], lags_at(cols))

        drain(("forward", 0))
        tiles(128, width, gate_back)
        wait_tokens(3)
        tiles(128, width, mixed_cols)
        halo = remote(r.ghalo, r.ghalo_in, r.halo_s.at[1], r.halo_r.at[1], seq=block_at(blocks - 1))
        send("halo", halo)
        halo.wait_recv()
        later = r.ghalo_in[...] * jnp.where(z < blocks - 1, 1.0, 0.0)

        def tail_cols(at):
            cols = slice(at, at + width)
            short = r.short[:, cols].astype(F32)
            row = lax.broadcasted_iota(jnp.int32, (16, width), 0)
            last = short[1:2] * later[0:1, cols] + short[2:3] * later[1:2, cols]
            total = r.tail[:, cols] + jnp.where(row == 15, last, 0.0)
            total = total + jnp.where(row == 14, short[2:3] * later[0:1, cols], 0.0)
            r.gproj[tokens - 16 :, cols] = total.astype(BF16)

        for part in range(3):
            tail_cols(part * width)

        def spread(k, own_ref, out_ref, size):
            for at in range(peers):
                to = group_at(1 + at)
                src, dst = own_ref.at[span(to, rows_out)], out_ref.at[:, span(b, size)]
                send("spread", remote(src, dst, r.tr_s.at[k, at], r.tr_r.at[k, at], batch=to))
            return load(r.local_sem.at[14 + k], own_ref.at[span(b, rows_out)], out_ref.at[:, span(b, size)])

        def spread_finish(k, copy, out_ref, size):
            for at in range(peers):
                source = group_at(groups - 1 - at)
                dst = out_ref.at[:, span(source, size)]
                remote(dst, dst, r.tr_s.at[k, at], r.tr_r.at[k, at], batch=source).wait_recv()
            copy.wait()

        for step in range(chips - 1):
            send("out", out_copy(way_of(step)))
        small_z_wait(0, lambda step: r.w12_z.at[step - 1])
        net = r.w12[...]
        for step in range(zpeers):
            net = net + r.w12_z[step]
        r.w12_sum[...] = net
        small_send(1, lambda to: r.w12_sum, lambda at: r.w12_plane.at[at])
        small_wait(0, lambda at: r.w3_land.at[at])
        part = r.sum_w3[span(b, w3_rows), :]
        for at in range(peers):
            part = part + r.w3_land[at]
        r.w3_part[...] = part
        r.w3_all[span(b, w3_rows), :] = part
        small_send(2, lambda to: r.w3_part, lambda at: r.w3_all.at[span(b, w3_rows)])
        reduce_next(0, down_refs)
        small_wait(1, lambda at: r.w12_plane.at[at])
        net = r.w12_sum[...]
        for at in range(peers):
            net = net + r.w12_plane[at]
        r.grad_w1[...] = net[:emb, filt : 2 * filt]
        r.grad_w2[...] = net[:, :filt]
        for at in range(peers):
            dst = r.w3_all.at[span(group_at(groups - 1 - at), w3_rows)]
            small_copy(2, dst, dst, at, group_at(groups - 1 - at)).wait_recv()
        holder, halves = lax.div(b * share, own), own // share
        third = r.w3_all[...]
        picked = third[:, :share]
        for half in range(1, halves):
            here = lax.rem(b, halves) == half
            picked = jnp.where(here, third[:, half * share : (half + 1) * share], picked)

        def w3_copy(step, to):
            return small_z_copy(1, r.w3_half, r.w3_half, step, to)

        @pl.when(z == holder)
        def _():
            r.w3_half[...] = picked
            for step in range(1, blocks):
                w3_copy(step, block_at(step)).start()

        for way in range(chips - 1):
            in_copy(way).wait_recv()
        total = r.in_own[...]
        for step in range(chips - 1):
            total = total + r.in_land[step].astype(F32)
        r.in_own[...] = total

        def in_spread(step, part, block, to):
            src = r.in_own.at[span(to, rows_out), part * own : (part + 1) * own]
            dst = r.grad_w_in.at[:, pl.ds(pl.multiple_of(part * width + block * own, own), own)]
            if step == 0:
                return pltpu.make_async_copy(src, dst, r.load_sem.at[10 + part])
            return remote(src, dst, r.ti_s.at[step - 1, part], r.ti_r.at[step - 1, part], seq=to)

        for part in range(3):
            for step in range(1, blocks):
                send("in_spread", in_spread(step, part, z, block_at(step)))
            in_spread(0, part, z, z).start()
        for _, copy in win_loads:
            copy.wait()
        r.gn2[...] = mm_nt(r.gproj[:, :width], r.win[0])
        r.gn2[...] += mm_nt(r.gproj[:, width : 2 * width], r.win[1])
        r.gn2[...] += mm_nt(r.gproj[:, 2 * width :], r.win[2])

        reduce_next(1, up_refs)
        drain(("za", 2))
        load(r.load_sem.at[0], r.tokens, r.tok).wait()

        def norm1_back(at, total):
            rows = pl.ds(pl.multiple_of(at * 32, 32), 32)
            grad, inverse = r.gn2[rows, :], r.inv1[rows, 0:1]
            xhat = (r.tok[rows, :].astype(F32) - r.mean1[rows, 0:1]) * inverse
            r.res[rows, :] = r.gres[rows, :] + norm_back(grad, r.gain1[...], xhat, inverse)
            return total + jnp.sum((grad * xhat).reshape(4, 8, width), axis=0)

        total = lax.fori_loop(0, tokens // 32, norm1_back, jnp.zeros((8, width), F32))
        r.sum_gain1[...] = jnp.sum(total, axis=0, keepdims=True)
        r.small_send[...] = jnp.zeros((groups, 16, share), F32)
        for group in range(groups):
            cols = slice(group * share, (group + 1) * share)
            r.small_send[group, 0:1, :] = r.sum_gain1[:, cols]
            r.small_send[group, 1:2, :] = r.sum_gain2[:, cols]
            r.small_send[group, 2:3, :] = r.sum_bias[:, cols]
            for lag in range(3):
                for third in range(3):
                    at = group * inc + third * share
                    row = 3 + 3 * lag + third
                    r.small_send[group, row : row + 1, :] = r.sum_short[lag : lag + 1, at : at + share]
        small_send(3, lambda to: r.small_send.at[to], lambda at: r.small_land.at[b])
        r.small_land[b] = r.small_send[b]
        store_tokens = load(r.local_sem.at[13], r.res, r.tokens_grad)
        reduce_finish(0, down_refs)
        store_down = load(r.local_sem.at[9], down_refs[4], r.grad_w_down)
        for way in range(chips - 1):
            out_copy(way).wait_recv()
        total = r.xhat2[share : 2 * share, :]
        for step in range(chips - 1):
            total = total + r.out_land[step].astype(F32)
        r.xhat2[share : 2 * share, :] = total
        r.outz_send[...] = total.astype(BF16)
        for step in range(1, blocks):
            send("outz", outz_copy(step, block_at(step)))
        r.outz_own[...] = r.xhat2[pl.ds(pl.multiple_of(share + z * rows_out, rows_out), rows_out), :]

        for at in range(peers):
            source = group_at(groups - 1 - at)
            dst = r.small_land.at[source]
            small_copy(3, dst, dst, at, source).wait_recv()
        small = r.small_land[0]
        for group in range(1, groups):
            small = small + r.small_land[group]
        r.small_sum[...] = small
        small_z_send(2, r.small_sum, lambda step: r.small_z.at[step - 1])
        reduce_finish(1, up_refs)
        spread_up = spread(0, up_refs[4], r.grad_w_up, ffc)
        for step in range(1, blocks):
            outz_copy(step, block_at(blocks - step)).wait_recv()
        total = r.outz_own[...]
        for step in range(zpeers):
            total = total + r.outz_land[step].astype(F32)
        r.outz_own[...] = total
        store_out = load(r.local_sem.at[11], r.outz_own, r.grad_w_out)
        def chosen(value, size):
            picked = value[:, :size]
            for block in range(1, blocks):
                picked = jnp.where(z == block, value[:, block * size : (block + 1) * size], picked)
            return picked

        @pl.when(z == holder)
        def _():
            for step in range(1, blocks):
                w3_copy(step, block_at(step)).wait_send()

        @pl.when(z != holder)
        def _():
            w3_copy(lax.rem(z + blocks - holder, blocks), holder).wait_recv()

        r.grad_w3[...] = chosen(r.w3_half[...], rows_out)
        small_z_wait(2, lambda step: r.small_z.at[step - 1])
        small = r.small_sum[...]
        for step in range(zpeers):
            small = small + r.small_z[step]
        r.grad_gain1[...] = chosen(small[0:1], rows_out)
        r.grad_gain2[...] = chosen(small[1:2], rows_out)
        r.grad_bias[...] = chosen(small[2:3], rows_out)
        for lag in range(3):
            for third in range(3):
                row = 3 + 3 * lag + third
                r.short_all[lag : lag + 1, third * share : (third + 1) * share] = small[row : row + 1]
        r.grad_short[...] = chosen(r.short_all[0:3, :], 3 * rows_out)
        spread_finish(0, spread_up, r.grad_w_up, ffc)
        for part in range(3):
            for step in range(1, blocks):
                source = block_at(blocks - step)
                in_spread(step, part, source, source).wait_recv()
            in_spread(0, part, z, z).wait()
        store_layer.wait()
        for down in range(2):
            for step in range(zpeers):

                @pl.when(seq_sends(down, step))
                def _():
                    seq_copy(down, step).wait_send()

        store_down.wait()
        store_out.wait()
        store_tokens.wait()
        for key in list(sent):
            drain(key)

    def call(args):
        result = pl.pallas_call(
            kernel,
            out_shape=[jax.ShapeDtypeStruct(shape, dtype) for shape, dtype, _ in outputs.values()],
            in_specs=[pl.BlockSpec(memory_space=space) for space in inputs.values()],
            out_specs=[pl.BlockSpec(memory_space=space) for *_, space in outputs.values()],
            scratch_shapes=list(scratch.values()),
            compiler_params=pltpu.CompilerParams(
                collective_id=0, has_side_effects=True, vmem_limit_bytes=KERNEL_VMEM
            ),
        )(*[args[name] for name in inputs])
        return settled(result[:13])

    return call


def settled(values):
    count = len(values)
    large = [at for at, value in enumerate(values) if value.size >= 1 << 15]

    def copy_all(*refs):
        sources, targets, held = refs[:count], refs[count : 2 * count], refs[2 * count : -1]
        sems = refs[-1]
        copies = [
            pltpu.make_async_copy(sources[at], held[k], sems.at[0, k]) for k, at in enumerate(large)
        ]
        for copy in copies:
            copy.start()
        for at in range(count):
            if at not in large:
                if at == count - 1:
                    targets[at][...] = sources[at][...].T
                else:
                    targets[at][...] = sources[at][...].reshape(targets[at].shape)
        stores = []
        for k, at in enumerate(large):
            copies[k].wait()
            stores.append(pltpu.make_async_copy(held[k], targets[at], sems.at[1, k]))
            stores[-1].start()
        for copy in stores:
            copy.wait()

    specs = [
        pl.BlockSpec(memory_space=pl.ANY if at in large else pltpu.VMEM) for at in range(count)
    ]
    return pl.pallas_call(
        copy_all,
        out_shape=[
            jax.ShapeDtypeStruct(value.shape[1:] if value.shape[0] == 1 else value.shape, value.dtype)
            for value in values[:-1]
        ]
        + [jax.ShapeDtypeStruct(values[-1].shape[::-1], values[-1].dtype)        ],
        in_specs=specs,
        out_specs=specs,
        scratch_shapes=[pltpu.VMEM(values[at].shape, values[at].dtype) for at in large]
        + [pltpu.SemaphoreType.DMA((2, len(large)))],
    )(*values)


def small_sums(gain1, bias, gain2, short, w1, w2, w3_own):
    blocks, position = lax.axis_size("seq"), lax.axis_index("seq")
    dests = lax.axis_size("batch") * blocks
    width, (filt_dim, own), emb = gain1.shape[0], w3_own.shape, w1.shape[0]
    w3_all = lax.dynamic_update_slice_in_dim(
        jnp.zeros((filt_dim, width), F32), w3_own, position * own, 1
    )
    share = width // dests
    small = jnp.concatenate(
        [
            gain1.reshape(dests, share),
            bias.reshape(dests, share),
            gain2.reshape(dests, share),
            short.reshape(3, dests, 3 * share).transpose(1, 0, 2).reshape(dests, 9 * share),
            w3_all.reshape(filt_dim, dests, share).transpose(1, 0, 2).reshape(dests, filt_dim * share),
        ],
        axis=1,
    )
    small = scatter_sum(small, wire=F32)[0]
    filters = all_sum(jnp.concatenate([w1, w2], axis=0))
    return (
        small[:share],
        small[3 * share : 12 * share].reshape(3, 3 * share),
        filters[:emb],
        filters[emb:],
        small[12 * share :].reshape(filt_dim, share),
        small[share : 2 * share],
        small[2 * share : 3 * share],
    )


def kernel_layer(
    tokens,
    norm_gain1,
    w_in,
    short_kernel,
    filt_w1,
    filt_w2,
    filt_w3,
    decay_rate,
    conv_bias,
    w_out,
    norm_gain2,
    w_up,
    w_down,
    cotangent,
):
    _, block_len, width = tokens.shape
    groups, blocks = lax.axis_size("batch"), lax.axis_size("seq")
    emb, filt = filt_w1.shape
    (cosine, sine), phase = symmetric_tables(block_len * blocks)
    features = lag_features(emb, block_len * blocks)
    call = kernel_plan(groups, blocks, block_len, width, w_up.shape[1], filt, emb)
    out = call(
        dict(
            tokens=tokens[0],
            cot=cotangent[0],
            w_in=w_in,
            w_out=w_out,
            w_up=w_up,
            w_down=w_down,
            cosine=jnp.asarray(cosine),
            sine=jnp.asarray(sine),
            filt_w3=filt_w3,
            decay=decay_rate[None],
            gain1=norm_gain1[None],
            gain2=norm_gain2[None],
            bias=conv_bias[None],
            short=short_kernel,
            filt_w1=filt_w1,
            filt_w2=filt_w2,
            features_t=jnp.asarray(features.T),
            phase=jnp.asarray(phase),
        )
    )
    layer_out, tokens_grad, w_in, w_out, w_up, w_down, gain1, gain2, bias, short, w1, w2, w3 = out
    return layer_out[None], tokens_grad[None], (gain1, short, w1, w2, w3.T, bias, gain2), (w_in, w_out, w_up, w_down)


def on_device(*args):
    tokens = args[0]
    fits = lax.axis_size("batch") == 8 and lax.axis_size("seq") == 4 and tokens.shape[1] * lax.axis_size("seq") <= 1024
    layer = kernel_layer if fits else plain_layer
    layer_out, tokens_grad, small, large = layer(*args)
    gain1, short, w1, w2, w3, bias, gain2 = small
    grad_w_in, grad_w_out, grad_w_up, grad_w_down = large
    return (
        layer_out, tokens_grad, gain1, grad_w_in, short, w1, w2, w3, bias, grad_w_out, gain2,
        grad_w_up, grad_w_down,
    )


def solution(mesh):
    split = P("batch", "seq", None)
    both = ("batch", "seq")
    return jax.shard_map(
        on_device,
        mesh=mesh,
        in_specs=(split,) + (P(),) * 12 + (split,),
        out_specs=(
            split,
            split,
            P(both),
            P(both, None),
            P(None, both),
            P(),
            P(),
            P(None, both),
            P(both),
            P(both, None),
            P(both),
            P(both, None),
            P(both, None),
        ),
        check_vma=False,
    )
```
